32 devices in a mesh: dp: 4 (over y, x), expert: 8 (over z, core).
Axes of the slice: x: 2, y: 2, z: 4, core: 2. Of those that a mesh axis runs over, the one named last changes fastest.
Arguments:
- tokens: bfloat16 [8, 1408, 1536], P('expert', 'dp'), may hold values from -6 to 6
- cotangent: bfloat16 [8, 1408, 1536], P('expert', 'dp'), may hold values from -6 to 6
- parents: int32 [8, 44], P('expert'), may hold values from 0 to 35, as said below
- routes: int32 [8, 1408, 4], P('expert', 'dp'), may hold values from 0 to 7, all different within a row; in each aligned block of 352 rows (0 to 351, 352 to 703, ..., all dimensions but the last counted through in order) at most 264 rows name the same one
- first_gain: bfloat16 [1536], P(('dp', 'expert')), may hold values from 0.099609375 to 1.8984375
- second_gain: bfloat16 [1536], P(('dp', 'expert')), may hold values from 0.099609375 to 1.8984375
- query_weight: bfloat16 [1536, 1536], P(('dp', 'expert')), may hold values from -0.15625 to 0.15625
- key_matrix: bfloat16 [1536, 256], P(('dp', 'expert')), may hold values from -0.15625 to 0.15625
- value_matrix: bfloat16 [1536, 256], P(('dp', 'expert')), may hold values from -0.15625 to 0.15625
- out_weight: bfloat16 [1536, 1536], P(('dp', 'expert')), may hold values from -2.5 to 2.5
- router_weight: bfloat16 [1536, 8], P(('dp', 'expert')), may hold values from -0.078125 to 0.078125
- gate_weight: bfloat16 [8, 1536, 768], P('expert'), may hold values from -0.15625 to 0.15625
- up_weight: bfloat16 [8, 1536, 768], P('expert'), may hold values from -0.15625 to 0.15625
- down_weight: bfloat16 [8, 768, 1536], P('expert'), may hold values from -0.625 to 0.625
Outputs:
- output: bfloat16 [8, 1408, 1536], P('expert', 'dp')
- grad_tokens: float32 [8, 1408, 1536], P('expert', 'dp')
- grad_first_gain: float32 [1536], P(('dp', 'expert'))
- grad_second_gain: float32 [1536], P(('dp', 'expert'))
- grad_query: float32 [1536, 1536], P(('dp', 'expert'))
- grad_key: float32 [1536, 256], P(('dp', 'expert'))
- grad_value: float32 [1536, 256], P(('dp', 'expert'))
- grad_out: float32 [1536, 1536], P(('dp', 'expert'))
- grad_router: float32 [1536, 8], P(('dp', 'expert'))
- grad_gate: float32 [8, 1536, 768], P('expert')
- grad_up: float32 [8, 1536, 768], P('expert')
- grad_down: float32 [8, 768, 1536], P('expert')
The draws below stay inside these ranges and needn't reach their ends.
Inputs may be any that keep to these rules, and one draw needn't show every extreme that they name: `parents`: block 0 has parent 0; each other trunk block b < 32 has parent b - 1; the next 4 blocks are branches with parent 1024 // 32 - 1; the last 8 blocks are leaves, two to each branch, whose parent is a branch. `routes`: the 4 experts of a token are distinct. Among the 352 tokens of one device at most 264 name the same expert, a bound that some block reaches.
All inputs are finite; a program needn't handle non-finite values.
Results may differ from the reference program's by a relative error of at most 0.019.
Values may be sent and summed in bfloat16 or wider, within the bound.
A program may use at most 320 MiB of HBM per device.

```python
import math
import jax
import jax.numpy as jnp
import numpy as np
from jax import lax

MODEL_WIDTH = 1536
QUERY_HEADS = 12
KEY_VALUE_HEADS = 2
HEAD_SIZE = 128
FF = 768
TOPK = 4
TRUNK = 1024
SEG = 32
EXPERTS = 8
TLEN = 1408
TOK_DEV = 352
NTREES = 8
CAP = 264
N_DP = 4


def draw_parents(key, part):
    key = jax.random.fold_in(key, 11)
    trunk_blocks = TRUNK // SEG
    block_ids = jnp.arange(trunk_blocks, dtype=jnp.int32)
    trunk_parents = jnp.maximum(block_ids - 1, 0)

    def tree_parents(tree_key):
        leaf_order = jax.random.permutation(tree_key, 8).astype(jnp.int32)
        leaf_parents = trunk_blocks + leaf_order // 2
        branch_parents = jnp.full((4,), trunk_blocks - 1, jnp.int32)
        return jnp.concatenate([trunk_parents, branch_parents, leaf_parents]).astype(jnp.int32)
    tree_keys = jax.random.split(key, NTREES)
    return jax.vmap(tree_parents)(tree_keys)


def block_levels(own_key, dims, shards, smallest, largest):
    loudness, own = 1.0, jax.random.fold_in(own_key, 6)
    for dim, shards_of in shards:
        draws = jnp.exp(jax.random.uniform(jax.random.fold_in(own, dim), (shards_of,), jnp.float32, smallest / len(shards), largest / len(shards)))
        loudness = loudness * jnp.repeat(draws, dims[dim] // shards_of).reshape([-1 if axis == dim else 1 for axis in range(len(dims))])
    return loudness


def routed_block(rng, own, number, rows, count, top, reach, skew):
    ranking = jax.random.permutation(rng, count)
    packed, ordinary = shares(count, rows * top, reach, skew, True), shares(count, rows * top, reach, skew, False)
    places = jnp.arange(count)

    def named(lengths, turn):
        used = int((lengths > 0).sum())
        fixed = max(1, used // 4)
        shifted = fixed + (places - fixed + turn * (used - fixed)) % max(1, count - fixed)
        return jnp.zeros((count,), jnp.int32).at[ranking[jnp.where(places < fixed, places, shifted)]].set(jnp.asarray(lengths, jnp.int32))

    lengths = jnp.where(number % 4 == 0, named(packed, number // 4), named(ordinary, number - number // 4 - 1))
    mixed = jax.random.permutation(jax.random.fold_in(own, 3), count)
    giver, receiver = mixed[0:count // 2 * 2:2], mixed[1:count // 2 * 2:2]
    margin = jnp.minimum(lengths[giver] - 1, reach - lengths[receiver]) // 2
    margin = jnp.where((giver == ranking[0]) | (receiver == ranking[0]) | (lengths[receiver] == 0), 0, jnp.maximum(margin, 0))
    shifted = jax.random.randint(jax.random.fold_in(own, 4), (count // 2,), 0, 1 << 20) % (margin + 1)
    lengths = lengths.at[giver].add(-shifted).at[receiver].add(shifted)
    labels = jnp.searchsorted(jnp.cumsum(lengths), jnp.arange(rows * top), side="right").astype(jnp.int32)
    grid = labels.reshape(top, rows).T
    grid = grid[jax.random.permutation(jax.random.fold_in(own, 1), rows)]
    turn = jax.random.randint(jax.random.fold_in(own, 2), (rows, 1), 0, top)
    return jnp.take_along_axis(grid, (jnp.arange(top)[None, :] + turn) % top, axis=1)


def shares(amount, total, most, slope, full):
    portions = [(1 << 20) // math.isqrt(grade ** slope) + 1 for grade in range(1, amount + 1)]
    largest = most if full else min(most, max(-(-total // amount), total * portions[0] // sum(portions)))
    least = 1 if total - largest >= amount - 1 else 0
    counts, spare = [largest] + [least] * (amount - 1), total - largest - least * (amount - 1)
    while spare > 0:
        movable = [i for i in range(1, amount) if counts[i] < largest] or [i for i in range(1, amount) if counts[i] < most]
        pool, remaining = sum([portions[i] for i in movable]), spare
        for i in movable:
            addition = min(most - counts[i], max(1, remaining * portions[i] // pool), spare)
            counts[i] = counts[i] + addition
            spare = spare - addition
    return np.array(counts)


def noise(own_key, dims, deviation, limit, cuts=(), kind=jnp.bfloat16):
    array = jax.random.normal(own_key, dims, jnp.float32) * deviation
    if len(cuts) > 0:
        array = block_levels(own_key, dims, cuts, -0.22, 0.18) * array
    return jnp.clip(array, min=-limit, max=limit).astype(kind)


def setup_inputs(seed: int = 0) -> dict:
    key_list = jax.random.split(jax.random.key(seed), 15)
    tokens = noise(key_list[0], (NTREES, TLEN, MODEL_WIDTH), 1.0, 6.0, ((0, 8), (1, 4)))
    cotangent = noise(key_list[1], (NTREES, TLEN, MODEL_WIDTH), 1.0, 6.0, ((0, 8), (1, 4)))
    parents = draw_parents(jax.random.fold_in(key_list[14], 71), 0)
    routes_keys = jax.random.split(jax.random.fold_in(key_list[3], 1), NTREES * TLEN // TOK_DEV)
    routes_turns = jax.random.permutation(jax.random.fold_in(key_list[3], 3), NTREES * TLEN // TOK_DEV)
    routes = jax.vmap(lambda own, number: routed_block(jax.random.fold_in(key_list[3], 2), own, number, TOK_DEV, EXPERTS, TOPK, CAP, 1))(routes_keys, routes_turns).reshape((NTREES, TLEN, TOPK))
    first_gain = jnp.clip(1.0 + 0.18 * jax.random.normal(key_list[4], (MODEL_WIDTH,), jnp.float32), 0.099609375, 1.8984375).astype(jnp.bfloat16)
    second_gain = jnp.clip(1.0 + 0.18 * jax.random.normal(key_list[5], (MODEL_WIDTH,), jnp.float32), 0.099609375, 1.8984375).astype(jnp.bfloat16)
    query_weight = noise(key_list[6], (MODEL_WIDTH, QUERY_HEADS * HEAD_SIZE), MODEL_WIDTH ** -0.5, 0.15625, ((0, 32),))
    key_matrix = noise(key_list[7], (MODEL_WIDTH, KEY_VALUE_HEADS * HEAD_SIZE), MODEL_WIDTH ** -0.5, 0.15625, ((0, 32),))
    value_matrix = noise(key_list[8], (MODEL_WIDTH, KEY_VALUE_HEADS * HEAD_SIZE), MODEL_WIDTH ** -0.5, 0.15625, ((0, 32),))
    out_weight = noise(key_list[9], (QUERY_HEADS * HEAD_SIZE, MODEL_WIDTH), (max(QUERY_HEADS * HEAD_SIZE // 256, 1)) ** -0.5, 2.5, ((0, 32),))
    router_weight = noise(key_list[10], (MODEL_WIDTH, EXPERTS), (4 * MODEL_WIDTH) ** -0.5, 0.078125, ((0, 32),))
    gate_weight = noise(key_list[11], (EXPERTS, MODEL_WIDTH, FF), MODEL_WIDTH ** -0.5, 0.15625, ((0, 8),))
    up_weight = noise(key_list[12], (EXPERTS, MODEL_WIDTH, FF), MODEL_WIDTH ** -0.5, 0.15625, ((0, 8),))
    down_weight = noise(key_list[13], (EXPERTS, FF, MODEL_WIDTH), (FF // 8) ** -0.5, 0.625, ((0, 8),))
    return {"tokens": tokens, "cotangent": cotangent, "parents": parents, "routes": routes, "first_gain": first_gain, "second_gain": second_gain, "query_weight": query_weight, "key_matrix": key_matrix, "value_matrix": value_matrix, "out_weight": out_weight, "router_weight": router_weight, "gate_weight": gate_weight, "up_weight": up_weight, "down_weight": down_weight}


EPS = 1e-06
THETA = 10000.0
HIGH_PRECISION = lax.Precision.HIGHEST
NEGATIVE = -1e+30

@jax.custom_vjp
def low(v):
    return lax.optimization_barrier(v.astype(jnp.bfloat16)).astype(jnp.float32)

@jax.custom_vjp
def low_back(v):
    return v

def low_keep(v):
    return (low(v), None)

def low_pass(kept, grad):
    return (grad,)

def back_keep(v):
    return (v, None)

def back_low(kept, grad):
    return (low(grad),)
low.defvjp(low_keep, low_pass)
low_back.defvjp(back_keep, back_low)

def ancestry(parent_row):
    block_count = parent_row.shape[0]
    block_ids = jnp.arange(block_count, dtype=jnp.int32)

    def advance(counter, carried):
        current, ancestors = carried
        ancestors = jnp.maximum(ancestors, (current[:, None] == block_ids[None, :]).astype(jnp.float32))
        return (jnp.take(parent_row, current).astype(jnp.int32), ancestors)
    start_pair = (block_ids, jnp.zeros((block_count, block_count), jnp.float32))
    current, ancestors = lax.fori_loop(0, block_count, advance, start_pair)
    depths = (lax.optimization_barrier(jnp.sum(ancestors, axis=1)) - 1.0).astype(jnp.int32)
    return (ancestors, depths)

def apply_rotation(values, positions):
    half_width = values.shape[-1] // 2
    frequency = jnp.power(THETA, -(jnp.arange(half_width, dtype=jnp.float32) * 2.0 / values.shape[-1]))
    angles = positions.astype(jnp.float32)[:, None] * frequency[None, :]
    cosine = jnp.cos(angles)[:, None, :]
    sine_part = jnp.sin(angles)[:, None, :]
    first_half = values[..., :half_width]
    second_half = values[..., half_width:]
    return jnp.concatenate([first_half * cosine - second_half * sine_part, second_half * cosine + first_half * sine_part], axis=-1)

def normalize(values, scales):
    return values * lax.rsqrt(lax.optimization_barrier(jnp.mean(values * values, axis=-1, keepdims=True)) + EPS) * scales

def place(route_ids, experts, capacity):
    one_hot = (route_ids[..., None] == jnp.arange(experts, dtype=jnp.int32)).astype(jnp.int32)
    earlier = jnp.cumsum(one_hot, axis=-2) - one_hot
    slot_rank = lax.optimization_barrier(jnp.sum(earlier * one_hot, axis=-1))
    return (route_ids * capacity + slot_rank).astype(jnp.int32)

def slot_sources(slot_index, pair_count, buffer_size):
    empty = jnp.full((buffer_size,), pair_count, jnp.int32)
    return empty.at[slot_index].set(jnp.arange(pair_count, dtype=jnp.int32))

def tree_layer(weights, tree_tokens, tree_parents, tree_routes):
    gain_one, gain_two, query_full, key_complete, value_complete, out_full, router_full, gate_full, up_full, down_full = weights
    sequence_length = tree_tokens.shape[0]
    ancestors, depths = ancestry(tree_parents)
    token_ids = jnp.arange(sequence_length, dtype=jnp.int32)
    block_of = token_ids // SEG
    positions = depths[block_of] * SEG + token_ids % SEG
    visible = (ancestors[block_of][:, block_of] > 0.5) & (positions[None, :] <= positions[:, None])
    first_normed = low(normalize(tree_tokens, gain_one))
    query_proj = jnp.dot(first_normed, query_full, precision=HIGH_PRECISION).reshape(sequence_length, QUERY_HEADS, HEAD_SIZE)
    key_projected = jnp.dot(first_normed, key_complete, precision=HIGH_PRECISION).reshape(sequence_length, KEY_VALUE_HEADS, HEAD_SIZE)
    value_projected = jnp.dot(first_normed, value_complete, precision=HIGH_PRECISION).reshape(sequence_length, KEY_VALUE_HEADS, HEAD_SIZE)
    query_rotated = low(apply_rotation(low_back(query_proj), positions))
    key_rotated = low(apply_rotation(low_back(key_projected), positions))
    value_low = low_back(low(value_projected))
    query_group_width = QUERY_HEADS // KEY_VALUE_HEADS
    grouped_queries = query_rotated.reshape(sequence_length, KEY_VALUE_HEADS, query_group_width, HEAD_SIZE)
    scores = jnp.einsum('qhgd,khd->hgqk', grouped_queries, key_rotated, precision=HIGH_PRECISION) * HEAD_SIZE ** (-0.5)
    scores = jnp.where(visible[None, None], low_back(scores), NEGATIVE)
    row_max = lax.optimization_barrier(jnp.max(scores, axis=-1, keepdims=True))
    exponent = jnp.exp(scores - row_max)
    softmax_out = exponent / lax.optimization_barrier(jnp.sum(exponent, axis=-1, keepdims=True))
    mixed_out = jnp.einsum('hgqk,khd->qhgd', low(softmax_out), value_low, precision=HIGH_PRECISION)
    mixed_out = low_back(low(mixed_out.reshape(sequence_length, QUERY_HEADS * HEAD_SIZE)))
    middle = tree_tokens + low_back(jnp.dot(mixed_out, out_full, precision=HIGH_PRECISION))
    normed_two = low(normalize(middle, gain_two))
    logits = jnp.dot(normed_two, router_full, precision=HIGH_PRECISION)
    chosen = jnp.take_along_axis(logits, tree_routes, axis=1)
    chosen_max = lax.optimization_barrier(jnp.max(chosen, axis=1, keepdims=True))
    chosen_exp = jnp.exp(chosen - chosen_max)
    gate_weights = chosen_exp / lax.optimization_barrier(jnp.sum(chosen_exp, axis=1, keepdims=True))
    experts = gate_full.shape[0]
    pair_count = TOK_DEV * TOPK
    block_rows = normed_two.reshape(N_DP, TOK_DEV, MODEL_WIDTH)
    route_ids = tree_routes.reshape(N_DP, pair_count)
    slot_index = place(route_ids, experts, CAP)
    sources = jax.vmap(lambda entry: slot_sources(entry, pair_count, experts * CAP))(slot_index)
    slot_used = sources < pair_count
    slot_token = jnp.where(slot_used, sources // TOPK, 0)
    sent_rows = jnp.take_along_axis(block_rows, slot_token[..., None], axis=1)
    sent_rows = low_back(sent_rows) * slot_used[..., None].astype(jnp.float32)
    sent_rows = sent_rows.reshape(N_DP, experts, CAP, MODEL_WIDTH)
    gate_pre = low_back(jnp.einsum('becd,edf->becf', sent_rows, gate_full, precision=HIGH_PRECISION))
    up_pre = low_back(jnp.einsum('becd,edf->becf', sent_rows, up_full, precision=HIGH_PRECISION))
    hidden = low(jax.nn.gelu(gate_pre, approximate=True) * up_pre)
    expert_out = low_back(low(jnp.einsum('becf,efd->becd', hidden, down_full, precision=HIGH_PRECISION)))
    combined = jnp.take_along_axis(expert_out.reshape(N_DP, experts * CAP, MODEL_WIDTH), slot_index[..., None], axis=1)
    combined = combined.reshape(sequence_length, TOPK, MODEL_WIDTH)
    return middle + lax.optimization_barrier(jnp.sum(gate_weights[..., None] * combined, axis=1))

def reference(tokens, cotangent, parents, routes, first_gain, second_gain, query_weight, key_matrix, value_matrix, out_weight, router_weight, gate_weight, up_weight, down_weight):
    weights = tuple((entry.astype(jnp.float32) for entry in (first_gain, second_gain, query_weight, key_matrix, value_matrix, out_weight, router_weight, gate_weight, up_weight, down_weight)))
    inputs = tokens.astype(jnp.float32)

    def forward(layer_inputs, layer_weights):

        def step(carried, tree_item):
            tree_tokens, tree_parents, tree_routes = tree_item
            return (carried, tree_layer(layer_weights, tree_tokens, tree_parents, tree_routes))
        start_value = jnp.zeros((), jnp.float32)
        carried, result = lax.scan(jax.checkpoint(step), start_value, (layer_inputs, parents, routes))
        return result
    result, pullback = jax.vjp(forward, inputs, weights)
    input_grad, weight_grads = pullback(cotangent.astype(jnp.float32))
    return (result.astype(jnp.bfloat16), input_grad, weight_grads[0], weight_grads[1], weight_grads[2], weight_grads[3], weight_grads[4], weight_grads[5], weight_grads[6], weight_grads[7], weight_grads[8], weight_grads[9])
```

```python
import jax
import jax.numpy as jnp
from jax import lax
from jax.sharding import PartitionSpec as P

MODEL_WIDTH = 1536
QUERY_HEADS = 12
KEY_VALUE_HEADS = 2
HEAD_SIZE = 128
FF = 768
TOPK = 4
SEG = 32


EPS = 1e-06
THETA = 10000.0
HIGH_PRECISION = lax.Precision.HIGHEST
NEGATIVE = -1e30


def ancestry(parent_row):
    block_count = parent_row.shape[0]
    block_ids = jnp.arange(block_count, dtype=jnp.int32)

    def advance(counter, carried):
        current, ancestors = carried
        ancestors = jnp.maximum(
            ancestors, (current[:, None] == block_ids[None, :]).astype(jnp.float32)
        )
        return (jnp.take(parent_row, current), ancestors)

    start_pair = (block_ids, jnp.zeros((block_count, block_count), jnp.float32))
    current, ancestors = lax.fori_loop(0, block_count, advance, start_pair)
    depths = (jnp.sum(ancestors, axis=1) - 1.0).astype(jnp.int32)
    return (ancestors, depths)


def apply_rotation(values, positions):
    half_width = values.shape[-1] // 2
    frequency = jnp.power(
        THETA, -(jnp.arange(half_width, dtype=jnp.float32) * 2.0 / values.shape[-1])
    )
    angles = positions.astype(jnp.float32)[:, None] * frequency[None, :]
    cosine = jnp.cos(angles)[:, None, :]
    sine_part = jnp.sin(angles)[:, None, :]
    first_half = values[..., :half_width]
    second_half = values[..., half_width:]
    return jnp.concatenate(
        [
            first_half * cosine - second_half * sine_part,
            second_half * cosine + first_half * sine_part,
        ],
        axis=-1,
    )


def normalize(values, scales):
    return values * lax.rsqrt(jnp.mean(values * values, axis=-1, keepdims=True) + EPS) * scales


def place(route_ids, experts, capacity):
    one_hot = (route_ids[..., None] == jnp.arange(experts, dtype=jnp.int32)).astype(jnp.int32)
    pairs = one_hot.shape[-2]
    before = jnp.tri(pairs, pairs, -1, dtype=jnp.bfloat16)
    earlier = jnp.dot(before, one_hot.astype(jnp.bfloat16), preferred_element_type=jnp.float32)
    slot_rank = jnp.sum(earlier.astype(jnp.int32) * one_hot, axis=-1)
    return route_ids * capacity + slot_rank


def visibility(ancestors, depths, query_ids, key_ids):
    block_ids = jnp.arange(ancestors.shape[0], dtype=jnp.int32)
    query_hit = (query_ids // SEG)[:, None] == block_ids[None, :]
    key_hit = (key_ids // SEG)[:, None] == block_ids[None, :]
    query_positions = (
        jnp.sum(jnp.where(query_hit, depths[None, :], 0), axis=1) * SEG + query_ids % SEG
    )
    key_pos = jnp.sum(jnp.where(key_hit, depths[None, :], 0), axis=1) * SEG + key_ids % SEG
    reach = jnp.dot(query_hit.astype(jnp.float32), ancestors, precision=HIGH_PRECISION)
    reach_keys = jnp.repeat(reach, SEG, axis=1)
    visible = (reach_keys > 0.5) & (key_pos[None, :] <= query_positions[:, None])
    return (visible, query_positions)


def head_scores(query_rotated, keys_all, visible, key_value_head, query_group_width):
    query_part = query_rotated[
        :, key_value_head * query_group_width : (key_value_head + 1) * query_group_width, :
    ]
    key_part = keys_all[:, key_value_head * HEAD_SIZE : (key_value_head + 1) * HEAD_SIZE]
    scores = jnp.einsum(
        "rgd,kd->grk", query_part, key_part, preferred_element_type=jnp.float32
    ) * HEAD_SIZE ** (-0.5)
    return jnp.where(visible[None], scores, NEGATIVE)


def gelu_product(gate_pre, up_pre):
    return jax.nn.gelu(gate_pre, approximate=True) * up_pre


def expert_hidden(received, local_gate, local_up):
    local_count = local_gate.shape[0]
    slot_count = received.shape[1]
    grouped_queries = received.reshape(-1, local_count, slot_count, MODEL_WIDTH)
    gate_pre = jnp.einsum(
        "sjcd,jdf->sjcf", grouped_queries, local_gate, preferred_element_type=jnp.float32
    )
    up_pre = jnp.einsum(
        "sjcd,jdf->sjcf", grouped_queries, local_up, preferred_element_type=jnp.float32
    )
    hidden = gelu_product(gate_pre, up_pre).astype(jnp.bfloat16)
    flat_shape = (received.shape[0], slot_count, FF)
    return (gate_pre.reshape(flat_shape), up_pre.reshape(flat_shape), hidden.reshape(flat_shape))


def expert_result(hidden, local_down):
    local_count = local_down.shape[0]
    grouped_queries = hidden.reshape(-1, local_count, hidden.shape[1], FF)
    result = jnp.einsum(
        "sjcf,jfd->sjcd", grouped_queries, local_down, preferred_element_type=jnp.float32
    )
    return result.astype(jnp.bfloat16).reshape(hidden.shape[0], hidden.shape[1], MODEL_WIDTH)


def on_device_routed(
    tokens,
    cotangent,
    parents,
    routes,
    first_gain,
    second_gain,
    query_weight,
    key_matrix,
    value_matrix,
    out_weight,
    router_weight,
    gate_weight,
    up_weight,
    down_weight,
):
    gathered = (
        lax.all_gather(query_weight, ("dp", "expert"), axis=0, tiled=True),
        lax.all_gather(key_matrix, ("dp", "expert"), axis=0, tiled=True),
        lax.all_gather(value_matrix, ("dp", "expert"), axis=0, tiled=True),
        lax.all_gather(out_weight, ("dp", "expert"), axis=0, tiled=True),
        lax.all_gather(router_weight, ("dp", "expert"), axis=0, tiled=True),
        lax.all_gather(first_gain, ("dp", "expert"), axis=0, tiled=True),
        lax.all_gather(second_gain, ("dp", "expert"), axis=0, tiled=True),
    )
    query_full, key_complete, value_complete, out_full, router_full, gain_one, gain_two = gathered
    scale_one = gain_one.astype(jnp.float32)
    scale_two = gain_two.astype(jnp.float32)
    inputs = tokens[0].astype(jnp.float32)
    total_rows = inputs.shape[0]
    query_group_width = QUERY_HEADS // KEY_VALUE_HEADS
    ancestors, depths = ancestry(parents[0])
    tree_length = ancestors.shape[0] * SEG
    query_ids = lax.axis_index("dp") * total_rows + jnp.arange(total_rows, dtype=jnp.int32)
    key_ids = jnp.arange(tree_length, dtype=jnp.int32)
    visible, query_positions = visibility(ancestors, depths, query_ids, key_ids)
    first_normed = normalize(inputs, scale_one).astype(jnp.bfloat16)
    query_proj = jnp.dot(first_normed, query_full, preferred_element_type=jnp.float32).reshape(
        total_rows, QUERY_HEADS, HEAD_SIZE
    )
    key_projected = jnp.dot(first_normed, key_complete, preferred_element_type=jnp.float32).reshape(
        total_rows, KEY_VALUE_HEADS, HEAD_SIZE
    )
    value_projected = jnp.dot(first_normed, value_complete, preferred_element_type=jnp.float32)
    query_rotated = apply_rotation(query_proj, query_positions).astype(jnp.bfloat16)
    key_rotated = (
        apply_rotation(key_projected, query_positions)
        .astype(jnp.bfloat16)
        .reshape(total_rows, KEY_VALUE_HEADS * HEAD_SIZE)
    )
    value_low = value_projected.astype(jnp.bfloat16)
    keys_all, values_all = (
        lax.all_gather(key_rotated, "dp", axis=0, tiled=True),
        lax.all_gather(value_low, "dp", axis=0, tiled=True),
    )
    mixed_parts = []
    log_totals = []
    for key_value_head in range(KEY_VALUE_HEADS):
        scores = head_scores(query_rotated, keys_all, visible, key_value_head, query_group_width)
        row_max = jnp.max(scores, axis=-1, keepdims=True)
        exponent = jnp.exp(scores - row_max)
        row_total = jnp.sum(exponent, axis=-1, keepdims=True)
        log_totals.append(row_max + jnp.log(row_total))
        softmax_out = (exponent / row_total).astype(jnp.bfloat16)
        value_part = values_all[:, key_value_head * HEAD_SIZE : (key_value_head + 1) * HEAD_SIZE]
        mixed_parts.append(
            jnp.einsum("grk,kd->rgd", softmax_out, value_part, preferred_element_type=jnp.float32)
        )
    mixed_out = (
        jnp.concatenate(mixed_parts, axis=1)
        .reshape(total_rows, QUERY_HEADS * HEAD_SIZE)
        .astype(jnp.bfloat16)
    )
    middle = inputs + jnp.dot(mixed_out, out_full, preferred_element_type=jnp.float32)
    normed_two = normalize(middle, scale_two).astype(jnp.bfloat16)
    logits = jnp.dot(normed_two, router_full, preferred_element_type=jnp.float32)
    route_ids = routes[0]
    experts = gate_weight.shape[0] * lax.axis_size("expert")
    capacity = 3 * total_rows * TOPK // (2 * experts)
    expert_ids = jnp.arange(experts, dtype=jnp.int32)
    route_hits = route_ids[:, :, None] == expert_ids[None, None, :]
    chosen = jnp.sum(jnp.where(route_hits, logits[:, None, :], 0.0), axis=2)
    chosen_max = jnp.max(chosen, axis=1, keepdims=True)
    chosen_exp = jnp.exp(chosen - chosen_max)
    gate_weights = chosen_exp / jnp.sum(chosen_exp, axis=1, keepdims=True)
    pair_count = total_rows * TOPK
    slot_index = place(route_ids.reshape(pair_count), experts, capacity)
    slot_source = (
        jnp.full((experts * capacity,), pair_count, jnp.int32)
        .at[slot_index]
        .set(jnp.arange(pair_count, dtype=jnp.int32))
    )
    slot_used = slot_source < pair_count
    slot_pair = jnp.where(slot_used, slot_source, 0)
    slot_token = slot_pair // TOPK
    zero_low = jnp.zeros((), jnp.bfloat16)
    outgoing = jnp.where(slot_used[:, None], normed_two[slot_token], zero_low).reshape(
        experts, capacity, MODEL_WIDTH
    )
    gate_pre, up_pre, hidden = expert_hidden(
        lax.all_to_all(outgoing, "expert", split_axis=0, concat_axis=0, tiled=True),
        gate_weight,
        up_weight,
    )
    dispatched = expert_result(hidden, down_weight)
    returned = lax.all_to_all(dispatched, "expert", split_axis=0, concat_axis=0, tiled=True)
    expert_rows = (
        returned.reshape(experts * capacity, MODEL_WIDTH)[slot_index]
        .astype(jnp.float32)
        .reshape(total_rows, TOPK, MODEL_WIDTH)
    )
    final = middle + jnp.sum(gate_weights[:, :, None] * expert_rows, axis=1)
    output = final.astype(jnp.bfloat16)[None]
    upstream = cotangent[0].astype(jnp.float32)
    gate_grad = jnp.sum(upstream[:, None, :] * expert_rows, axis=2)
    chosen_grad = gate_weights * (
        gate_grad - jnp.sum(gate_weights * gate_grad, axis=1, keepdims=True)
    )
    logit_grad = jnp.sum(jnp.where(route_hits, chosen_grad[:, :, None], 0.0), axis=1)
    pair_grad = (
        (gate_weights[:, :, None] * upstream[:, None, :])
        .astype(jnp.bfloat16)
        .reshape(pair_count, MODEL_WIDTH)
    )
    grad_outgoing = jnp.where(slot_used[:, None], pair_grad[slot_pair], zero_low).reshape(
        experts, capacity, MODEL_WIDTH
    )
    received, grad_in = (
        lax.all_to_all(outgoing, "expert", split_axis=0, concat_axis=0, tiled=True),
        lax.all_to_all(grad_outgoing, "expert", split_axis=0, concat_axis=0, tiled=True),
    )
    gate_pre, up_pre, hidden = expert_hidden(received, gate_weight, up_weight)
    local_count = gate_weight.shape[0]
    slot_count = received.shape[1]
    grouped_rows = received.reshape(-1, local_count, slot_count, MODEL_WIDTH)
    grouped_hidden = hidden.reshape(-1, local_count, slot_count, FF)
    grouped_grad = grad_in.reshape(-1, local_count, slot_count, MODEL_WIDTH)
    down_grad = jnp.einsum(
        "sjcf,sjcd->jfd", grouped_hidden, grouped_grad, preferred_element_type=jnp.float32
    )
    hidden_grad = jnp.einsum(
        "sjcd,jfd->sjcf", grouped_grad, down_weight, preferred_element_type=jnp.float32
    )
    _, product_pull = jax.vjp(gelu_product, gate_pre, up_pre)
    gate_pre_grad, up_pre_grad = product_pull(hidden_grad.reshape(gate_pre.shape))
    gate_low = gate_pre_grad.astype(jnp.bfloat16).reshape(-1, local_count, slot_count, FF)
    up_low = up_pre_grad.astype(jnp.bfloat16).reshape(-1, local_count, slot_count, FF)
    gate_w_grad = jnp.einsum(
        "sjcd,sjcf->jdf", grouped_rows, gate_low, preferred_element_type=jnp.float32
    )
    up_w_grad = jnp.einsum(
        "sjcd,sjcf->jdf", grouped_rows, up_low, preferred_element_type=jnp.float32
    )
    row_grad = jnp.einsum(
        "sjcf,jdf->sjcd", gate_low, gate_weight, preferred_element_type=jnp.float32
    ) + jnp.einsum("sjcf,jdf->sjcd", up_low, up_weight, preferred_element_type=jnp.float32)
    row_grad = row_grad.astype(jnp.bfloat16).reshape(received.shape)
    returned_grad = lax.all_to_all(row_grad, "expert", split_axis=0, concat_axis=0, tiled=True)
    pair_rows = (
        returned_grad.reshape(experts * capacity, MODEL_WIDTH)[slot_index]
        .astype(jnp.float32)
        .reshape(total_rows, TOPK, MODEL_WIDTH)
    )
    summed_experts = (
        lax.psum(gate_w_grad.astype(jnp.bfloat16), "dp").astype(jnp.float32),
        lax.psum(up_w_grad.astype(jnp.bfloat16), "dp").astype(jnp.float32),
        lax.psum(down_grad.astype(jnp.bfloat16), "dp").astype(jnp.float32),
    )
    router_wide = router_full.astype(jnp.float32)
    normed_two_grad = jnp.dot(logit_grad, router_wide.T, precision=HIGH_PRECISION) + jnp.sum(
        pair_rows, axis=1
    )
    router_grad = jnp.dot(normed_two.astype(jnp.float32).T, logit_grad, precision=HIGH_PRECISION)
    _, second_pull = jax.vjp(normalize, middle, scale_two)
    middle_norm_grad, second_gain_grad = second_pull(normed_two_grad)
    middle_grad = upstream + middle_norm_grad
    attended_low = middle_grad.astype(jnp.bfloat16)
    out_grad = jnp.einsum("rd,re->de", mixed_out, attended_low, preferred_element_type=jnp.float32)
    mixed_grad = jnp.einsum("re,de->rd", attended_low, out_full, preferred_element_type=jnp.float32)
    mixed_grad = mixed_grad.astype(jnp.bfloat16).reshape(total_rows, QUERY_HEADS, HEAD_SIZE)
    query_parts = []
    key_parts = []
    value_parts = []
    for key_value_head in range(KEY_VALUE_HEADS):
        scores = head_scores(query_rotated, keys_all, visible, key_value_head, query_group_width)
        softmax_out = jnp.exp(scores - log_totals[key_value_head])
        query_part = query_rotated[
            :, key_value_head * query_group_width : (key_value_head + 1) * query_group_width, :
        ]
        key_part = keys_all[:, key_value_head * HEAD_SIZE : (key_value_head + 1) * HEAD_SIZE]
        value_part = values_all[:, key_value_head * HEAD_SIZE : (key_value_head + 1) * HEAD_SIZE]
        grad_part = mixed_grad[
            :, key_value_head * query_group_width : (key_value_head + 1) * query_group_width, :
        ]
        value_parts.append(
            jnp.einsum(
                "grk,rgd->kd",
                softmax_out.astype(jnp.bfloat16),
                grad_part,
                preferred_element_type=jnp.float32,
            )
        )
        attn_grad = jnp.einsum(
            "rgd,kd->grk", grad_part, value_part, preferred_element_type=jnp.float32
        )
        score_grad = softmax_out * (
            attn_grad - jnp.sum(softmax_out * attn_grad, axis=-1, keepdims=True)
        )
        score_low = score_grad.astype(jnp.bfloat16)
        query_parts.append(
            jnp.einsum("grk,kd->rgd", score_low, key_part, preferred_element_type=jnp.float32)
            * HEAD_SIZE ** (-0.5)
        )
        key_parts.append(
            jnp.einsum("grk,rgd->kd", score_low, query_part, preferred_element_type=jnp.float32)
            * HEAD_SIZE ** (-0.5)
        )
    key_total_sum, value_sum = (
        lax.psum_scatter(
            jnp.concatenate(key_parts, axis=1).astype(jnp.bfloat16),
            "dp",
            scatter_dimension=0,
            tiled=True,
        ).astype(jnp.float32),
        lax.psum_scatter(
            jnp.concatenate(value_parts, axis=1).astype(jnp.bfloat16),
            "dp",
            scatter_dimension=0,
            tiled=True,
        ).astype(jnp.float32),
    )
    _, query_pull = jax.vjp(lambda values: apply_rotation(values, query_positions), query_proj)
    _, key_pullback = jax.vjp(lambda values: apply_rotation(values, query_positions), key_projected)
    query_grad = (
        query_pull(jnp.concatenate(query_parts, axis=1))[0]
        .astype(jnp.bfloat16)
        .reshape(total_rows, QUERY_HEADS * HEAD_SIZE)
    )
    key_grad = (
        key_pullback(key_total_sum.reshape(total_rows, KEY_VALUE_HEADS, HEAD_SIZE))[0]
        .astype(jnp.bfloat16)
        .reshape(total_rows, KEY_VALUE_HEADS * HEAD_SIZE)
    )
    value_grad = value_sum.astype(jnp.bfloat16)
    query_w_grad = jnp.einsum(
        "rd,re->de", first_normed, query_grad, preferred_element_type=jnp.float32
    )
    key_w_grad = jnp.einsum("rd,re->de", first_normed, key_grad, preferred_element_type=jnp.float32)
    value_w_grad = jnp.einsum(
        "rd,re->de", first_normed, value_grad, preferred_element_type=jnp.float32
    )
    normed_one_grad = (
        jnp.einsum("re,de->rd", query_grad, query_full, preferred_element_type=jnp.float32)
        + jnp.einsum("re,de->rd", key_grad, key_complete, preferred_element_type=jnp.float32)
        + jnp.einsum("re,de->rd", value_grad, value_complete, preferred_element_type=jnp.float32)
    )
    _, first_pull = jax.vjp(normalize, inputs, scale_one)
    input_norm_grad, first_gain_grad = first_pull(normed_one_grad)
    input_grad = (middle_grad + input_norm_grad)[None]
    shares = (
        lax.psum_scatter(query_w_grad, ("dp", "expert"), scatter_dimension=0, tiled=True),
        lax.psum_scatter(key_w_grad, ("dp", "expert"), scatter_dimension=0, tiled=True),
        lax.psum_scatter(value_w_grad, ("dp", "expert"), scatter_dimension=0, tiled=True),
        lax.psum_scatter(out_grad, ("dp", "expert"), scatter_dimension=0, tiled=True),
        lax.psum_scatter(router_grad, ("dp", "expert"), scatter_dimension=0, tiled=True),
        lax.psum_scatter(first_gain_grad, ("dp", "expert"), scatter_dimension=0, tiled=True),
        lax.psum_scatter(second_gain_grad, ("dp", "expert"), scatter_dimension=0, tiled=True),
    )
    return (
        output,
        input_grad,
        shares[5],
        shares[6],
        shares[0],
        shares[1],
        shares[2],
        shares[3],
        shares[4],
        summed_experts[0],
        summed_experts[1],
        summed_experts[2],
    )


def rows_to_gather(parts):
    return jnp.concatenate(parts, axis=1)


def dense_on_device(
    tokens,
    cotangent,
    parents,
    routes,
    first_gain,
    second_gain,
    query_weight,
    key_matrix,
    value_matrix,
    out_weight,
    router_weight,
    gate_weight,
    up_weight,
    down_weight,
):
    everyone = ("dp", "expert")
    experts = router_weight.shape[1]
    shard = rows_to_gather(
        [query_weight, key_matrix, value_matrix, out_weight, router_weight,
         first_gain[:, None], second_gain[:, None]]
    )
    width = shard.shape[1]
    shard = jnp.pad(shard, ((0, 0), (0, -width % 128)))
    full = lax.all_gather(shard, everyone, axis=0, tiled=True)
    heads_width = QUERY_HEADS * HEAD_SIZE
    kv_width = KEY_VALUE_HEADS * HEAD_SIZE
    qkv_width = heads_width + 2 * kv_width
    qkv_full = full[:, :qkv_width]
    out_full = full[:, qkv_width : qkv_width + MODEL_WIDTH]
    rest = full[:, qkv_width + MODEL_WIDTH :]
    router_full = rest[:, :experts]
    scale_one = rest[:, experts].astype(jnp.float32)
    scale_two = rest[:, experts + 1].astype(jnp.float32)
    inputs = tokens[0].astype(jnp.float32)
    dy_low = cotangent[0]
    dy_all = lax.all_gather(dy_low, "expert", axis=0)
    total_rows = inputs.shape[0]
    group = QUERY_HEADS // KEY_VALUE_HEADS
    ancestors, depths = ancestry(parents[0])
    tree_length = ancestors.shape[0] * SEG
    query_ids = lax.axis_index("dp") * total_rows + jnp.arange(total_rows, dtype=jnp.int32)
    key_ids = jnp.arange(tree_length, dtype=jnp.int32)
    visible, query_positions = visibility(ancestors, depths, query_ids, key_ids)
    n1 = normalize(inputs, scale_one).astype(jnp.bfloat16)
    qkv = jnp.dot(n1, qkv_full, preferred_element_type=jnp.float32)
    qk = qkv[:, : heads_width + kv_width].reshape(
        total_rows, QUERY_HEADS + KEY_VALUE_HEADS, HEAD_SIZE
    )
    qk_rot = apply_rotation(qk, query_positions).astype(jnp.bfloat16)
    query_rotated = qk_rot[:, :QUERY_HEADS]
    kv_own = jnp.concatenate(
        [
            qk_rot[:, QUERY_HEADS:].reshape(total_rows, kv_width),
            qkv[:, heads_width + kv_width :].astype(jnp.bfloat16),
        ],
        axis=1,
    )
    kv_all = lax.all_gather(kv_own, "dp", axis=0, tiled=True)
    keys_all = kv_all[:, :kv_width]
    values_all = kv_all[:, kv_width:]
    mixed_parts = []
    log_totals = []
    for head in range(KEY_VALUE_HEADS):
        scores = head_scores(query_rotated, keys_all, visible, head, group)
        row_max = jnp.max(scores, axis=-1, keepdims=True)
        exponent = jnp.exp(scores - row_max)
        row_total = jnp.sum(exponent, axis=-1, keepdims=True)
        log_totals.append(row_max + jnp.log(row_total))
        softmax_out = (exponent / row_total).astype(jnp.bfloat16)
        value_part = values_all[:, head * HEAD_SIZE : (head + 1) * HEAD_SIZE]
        mixed_parts.append(
            jnp.einsum("grk,kd->rgd", softmax_out, value_part, preferred_element_type=jnp.float32)
        )
    mixed = (
        jnp.concatenate(mixed_parts, axis=1).reshape(total_rows, heads_width).astype(jnp.bfloat16)
    )
    middle = inputs + jnp.dot(mixed, out_full, preferred_element_type=jnp.float32)
    n2 = normalize(middle, scale_two).astype(jnp.bfloat16)
    logits = jnp.dot(n2, router_full, preferred_element_type=jnp.float32)
    expert_ids = jnp.arange(experts, dtype=jnp.int32)
    hits = jnp.any(routes[0][:, :, None] == expert_ids[None, None, :], axis=1)
    chosen = jnp.where(hits, logits, NEGATIVE)
    chosen_exp = jnp.where(hits, jnp.exp(chosen - jnp.max(chosen, axis=1, keepdims=True)), 0.0)
    gates = chosen_exp / jnp.sum(chosen_exp, axis=1, keepdims=True)
    me = lax.axis_index("expert")
    n2_all = lax.all_gather(n2, "expert", axis=0)
    gates_all = lax.all_gather(gates, "expert", axis=0)
    own_gate = jnp.sum(jnp.where(expert_ids == me, gates_all, 0.0), axis=2)[:, :, None]
    gate_w, up_w, down_w = gate_weight[0], up_weight[0], down_weight[0]
    gate_pre = jnp.einsum("scd,df->scf", n2_all, gate_w, preferred_element_type=jnp.float32)
    up_pre = jnp.einsum("scd,df->scf", n2_all, up_w, preferred_element_type=jnp.float32)
    hidden, product_pull = jax.vjp(gelu_product, gate_pre, up_pre)
    scaled = (own_gate * hidden).astype(jnp.bfloat16)
    expert_sum = jnp.einsum("scf,fd->scd", scaled, down_w, preferred_element_type=jnp.float32)
    combined = lax.psum_scatter(
        expert_sum.astype(jnp.bfloat16), "expert", scatter_dimension=0, tiled=True
    )[0]
    output = (middle + combined.astype(jnp.float32)).astype(jnp.bfloat16)[None]
    back = jnp.einsum("scd,fd->scf", dy_all, down_w, preferred_element_type=jnp.float32)
    gate_grad_own = jnp.sum(back * hidden, axis=2)
    gate_grad = lax.all_to_all(gate_grad_own[:, None, :], "expert", 0, 1, tiled=True)[0].T
    chosen_grad = gates * (gate_grad - jnp.sum(gates * gate_grad, axis=1, keepdims=True))
    logit_grad = jnp.where(hits, chosen_grad, 0.0)
    down_grad = jnp.einsum("scf,scd->fd", scaled, dy_all, preferred_element_type=jnp.float32)
    gate_pre_grad, up_pre_grad = product_pull(own_gate * back)
    gate_low = gate_pre_grad.astype(jnp.bfloat16)
    up_low = up_pre_grad.astype(jnp.bfloat16)
    gate_w_grad = jnp.einsum("scd,scf->df", n2_all, gate_low, preferred_element_type=jnp.float32)
    up_w_grad = jnp.einsum("scd,scf->df", n2_all, up_low, preferred_element_type=jnp.float32)
    row_grad = jnp.einsum(
        "scf,df->scd", gate_low, gate_w, preferred_element_type=jnp.float32
    ) + jnp.einsum("scf,df->scd", up_low, up_w, preferred_element_type=jnp.float32)
    row_sum = lax.psum_scatter(
        row_grad.astype(jnp.bfloat16), "expert", scatter_dimension=0, tiled=True
    )[0].astype(jnp.float32)
    summed = tuple(
        lax.psum(grad.astype(jnp.bfloat16), "dp").astype(jnp.float32)[None]
        for grad in (gate_w_grad, up_w_grad, down_grad)
    )
    router_wide = router_full.astype(jnp.float32)
    n2_grad = jnp.dot(logit_grad, router_wide.T, precision=HIGH_PRECISION) + row_sum
    router_grad = jnp.dot(n2.astype(jnp.float32).T, logit_grad, precision=HIGH_PRECISION)
    upstream = dy_low.astype(jnp.float32)
    _, second_pull = jax.vjp(normalize, middle, scale_two)
    middle_norm_grad, second_gain_grad = second_pull(n2_grad)
    middle_grad = upstream + middle_norm_grad
    attended_low = middle_grad.astype(jnp.bfloat16)
    out_grad = jnp.einsum("rd,re->de", mixed, attended_low, preferred_element_type=jnp.float32)
    mixed_grad = jnp.einsum("re,de->rd", attended_low, out_full, preferred_element_type=jnp.float32)
    mixed_grad = mixed_grad.astype(jnp.bfloat16).reshape(total_rows, QUERY_HEADS, HEAD_SIZE)
    query_parts = []
    key_parts = []
    value_parts = []
    for head in range(KEY_VALUE_HEADS):
        scores = head_scores(query_rotated, keys_all, visible, head, group)
        softmax_out = jnp.exp(scores - log_totals[head])
        query_part = query_rotated[:, head * group : (head + 1) * group, :]
        key_part = keys_all[:, head * HEAD_SIZE : (head + 1) * HEAD_SIZE]
        value_part = values_all[:, head * HEAD_SIZE : (head + 1) * HEAD_SIZE]
        grad_part = mixed_grad[:, head * group : (head + 1) * group, :]
        value_parts.append(
            jnp.einsum(
                "grk,rgd->kd",
                softmax_out.astype(jnp.bfloat16),
                grad_part,
                preferred_element_type=jnp.float32,
            )
        )
        attn_grad = jnp.einsum(
            "rgd,kd->grk", grad_part, value_part, preferred_element_type=jnp.float32
        )
        score_grad = softmax_out * (
            attn_grad - jnp.sum(softmax_out * attn_grad, axis=-1, keepdims=True)
        )
        score_low = score_grad.astype(jnp.bfloat16)
        query_parts.append(
            jnp.einsum("grk,kd->rgd", score_low, key_part, preferred_element_type=jnp.float32)
            * HEAD_SIZE ** (-0.5)
        )
        key_parts.append(
            jnp.einsum("grk,rgd->kd", score_low, query_part, preferred_element_type=jnp.float32)
            * HEAD_SIZE ** (-0.5)
        )
    kv_sum = lax.psum_scatter(
        jnp.concatenate(key_parts + value_parts, axis=1).astype(jnp.bfloat16),
        "dp",
        scatter_dimension=0,
        tiled=True,
    )
    _, rotation_pull = jax.vjp(lambda values: apply_rotation(values, query_positions), qk)
    key_sum = kv_sum[:, :kv_width].astype(jnp.float32)
    qk_grad = rotation_pull(
        jnp.concatenate(
            query_parts + [key_sum.reshape(total_rows, KEY_VALUE_HEADS, HEAD_SIZE)], axis=1
        )
    )[0]
    qkv_grad = jnp.concatenate(
        [
            qk_grad.astype(jnp.bfloat16).reshape(total_rows, heads_width + kv_width),
            kv_sum[:, kv_width:],
        ],
        axis=1,
    )
    qkv_w_grad = jnp.einsum("rd,re->de", n1, qkv_grad, preferred_element_type=jnp.float32)
    n1_grad = jnp.einsum("re,de->rd", qkv_grad, qkv_full, preferred_element_type=jnp.float32)
    _, first_pull = jax.vjp(normalize, inputs, scale_one)
    input_norm_grad, first_gain_grad = first_pull(n1_grad)
    input_grad = (middle_grad + input_norm_grad)[None]
    small = jnp.concatenate(
        [router_grad, first_gain_grad[:, None], second_gain_grad[:, None]], axis=1
    )
    small = jnp.pad(small, ((0, 0), (0, -small.shape[1] % 128)))
    share = lax.psum_scatter(
        jnp.concatenate([qkv_w_grad, out_grad, small], axis=1).astype(jnp.bfloat16),
        everyone,
        scatter_dimension=0,
        tiled=True,
    ).astype(jnp.float32)
    query_share = share[:, :heads_width]
    key_share = share[:, heads_width : heads_width + kv_width]
    value_share = share[:, heads_width + kv_width : qkv_width]
    out_share = share[:, qkv_width : qkv_width + MODEL_WIDTH]
    small_share = share[:, qkv_width + MODEL_WIDTH :]
    return (
        output,
        input_grad,
        small_share[:, experts],
        small_share[:, experts + 1],
        query_share,
        key_share,
        value_share,
        out_share,
        small_share[:, :experts],
        *summed,
    )


def solution(mesh):
    dense = mesh.shape["expert"] <= 2 * TOPK
    return jax.shard_map(
        dense_on_device if dense else on_device_routed,
        mesh=mesh,
        in_specs=(
            P("expert", "dp", None),
            P("expert", "dp", None),
            P("expert", None),
            P("expert", "dp", None),
            P(("dp", "expert")),
            P(("dp", "expert")),
            P(("dp", "expert"), None),
            P(("dp", "expert"), None),
            P(("dp", "expert"), None),
            P(("dp", "expert"), None),
            P(("dp", "expert"), None),
            P("expert", None, None),
            P("expert", None, None),
            P("expert", None, None),
        ),
        out_specs=(
            P("expert", "dp", None),
            P("expert", "dp", None),
            P(("dp", "expert")),
            P(("dp", "expert")),
            P(("dp", "expert"), None),
            P(("dp", "expert"), None),
            P(("dp", "expert"), None),
            P(("dp", "expert"), None),
            P(("dp", "expert"), None),
            P("expert", None, None),
            P("expert", None, None),
            P("expert", None, None),
        ),
        check_vma=False,
    )
```

```python
import jax
import jax.numpy as jnp
from jax import lax
from jax.experimental import pallas as pl
from jax.experimental.pallas import tpu as pltpu
from jax.sharding import PartitionSpec as P

MESH = pl.DeviceIdType.MESH
BF = jnp.bfloat16
F32 = jnp.float32
MODEL_WIDTH = 1536
QUERY_HEADS = 12
KEY_VALUE_HEADS = 2
HEAD_SIZE = 128
FF = 768
TOPK = 4
SEG = 32
BRANCHES = 4
LEAVES = 8


EPS = 1e-06
THETA = 10000.0
HIGH_PRECISION = lax.Precision.HIGHEST
NEGATIVE = -1e30
LOG2E = 1.4426950408889634


def ancestry(parent_row):
    block_count = parent_row.shape[0]
    block_ids = jnp.arange(block_count, dtype=jnp.int32)

    def advance(counter, carried):
        current, ancestors = carried
        ancestors = jnp.maximum(
            ancestors, (current[:, None] == block_ids[None, :]).astype(jnp.float32)
        )
        return (jnp.take(parent_row, current), ancestors)

    start_pair = (block_ids, jnp.zeros((block_count, block_count), jnp.float32))
    current, ancestors = lax.fori_loop(0, block_count, advance, start_pair)
    depths = (jnp.sum(ancestors, axis=1) - 1.0).astype(jnp.int32)
    return (ancestors, depths)


def apply_rotation(values, positions):
    half_width = values.shape[-1] // 2
    frequency = jnp.power(
        THETA, -(jnp.arange(half_width, dtype=jnp.float32) * 2.0 / values.shape[-1])
    )
    angles = positions.astype(jnp.float32)[:, None] * frequency[None, :]
    cosine = jnp.cos(angles)[:, None, :]
    sine_part = jnp.sin(angles)[:, None, :]
    first_half = values[..., :half_width]
    second_half = values[..., half_width:]
    return jnp.concatenate(
        [
            first_half * cosine - second_half * sine_part,
            second_half * cosine + first_half * sine_part,
        ],
        axis=-1,
    )


def normalize(values, scales):
    return values * lax.rsqrt(jnp.mean(values * values, axis=-1, keepdims=True) + EPS) * scales


def place(route_ids, experts, capacity):
    one_hot = (route_ids[..., None] == jnp.arange(experts, dtype=jnp.int32)).astype(jnp.int32)
    pairs = one_hot.shape[-2]
    before = jnp.tri(pairs, pairs, -1, dtype=jnp.bfloat16)
    earlier = jnp.dot(before, one_hot.astype(jnp.bfloat16), preferred_element_type=jnp.float32)
    slot_rank = jnp.sum(earlier.astype(jnp.int32) * one_hot, axis=-1)
    return route_ids * capacity + slot_rank


def visibility(ancestors, depths, query_ids, key_ids):
    block_ids = jnp.arange(ancestors.shape[0], dtype=jnp.int32)
    query_hit = (query_ids // SEG)[:, None] == block_ids[None, :]
    key_hit = (key_ids // SEG)[:, None] == block_ids[None, :]
    query_positions = (
        jnp.sum(jnp.where(query_hit, depths[None, :], 0), axis=1) * SEG + query_ids % SEG
    )
    key_pos = jnp.sum(jnp.where(key_hit, depths[None, :], 0), axis=1) * SEG + key_ids % SEG
    reach = jnp.dot(query_hit.astype(jnp.float32), ancestors, precision=HIGH_PRECISION)
    reach_keys = jnp.repeat(reach, SEG, axis=1)
    visible = (reach_keys > 0.5) & (key_pos[None, :] <= query_positions[:, None])
    return (visible, query_positions)


def head_scores(query_rotated, keys_all, visible, key_value_head, query_group_width):
    query_part = query_rotated[
        :, key_value_head * query_group_width : (key_value_head + 1) * query_group_width, :
    ]
    key_part = keys_all[:, key_value_head * HEAD_SIZE : (key_value_head + 1) * HEAD_SIZE]
    scores = jnp.einsum(
        "rgd,kd->grk", query_part, key_part, preferred_element_type=jnp.float32
    ) * HEAD_SIZE ** (-0.5)
    return jnp.where(visible[None], scores, NEGATIVE)


def gelu_product(gate_pre, up_pre):
    return jax.nn.gelu(gate_pre, approximate=True) * up_pre


def expert_hidden(received, local_gate, local_up):
    local_count = local_gate.shape[0]
    slot_count = received.shape[1]
    grouped_queries = received.reshape(-1, local_count, slot_count, MODEL_WIDTH)
    gate_pre = jnp.einsum(
        "sjcd,jdf->sjcf", grouped_queries, local_gate, preferred_element_type=jnp.float32
    )
    up_pre = jnp.einsum(
        "sjcd,jdf->sjcf", grouped_queries, local_up, preferred_element_type=jnp.float32
    )
    hidden = gelu_product(gate_pre, up_pre).astype(jnp.bfloat16)
    flat_shape = (received.shape[0], slot_count, FF)
    return (gate_pre.reshape(flat_shape), up_pre.reshape(flat_shape), hidden.reshape(flat_shape))


def expert_result(hidden, local_down):
    local_count = local_down.shape[0]
    grouped_queries = hidden.reshape(-1, local_count, hidden.shape[1], FF)
    result = jnp.einsum(
        "sjcf,jfd->sjcd", grouped_queries, local_down, preferred_element_type=jnp.float32
    )
    return result.astype(jnp.bfloat16).reshape(hidden.shape[0], hidden.shape[1], MODEL_WIDTH)


def on_device_routed(
    tokens,
    cotangent,
    parents,
    routes,
    first_gain,
    second_gain,
    query_weight,
    key_matrix,
    value_matrix,
    out_weight,
    router_weight,
    gate_weight,
    up_weight,
    down_weight,
):
    gathered = (
        lax.all_gather(query_weight, ("dp", "expert"), axis=0, tiled=True),
        lax.all_gather(key_matrix, ("dp", "expert"), axis=0, tiled=True),
        lax.all_gather(value_matrix, ("dp", "expert"), axis=0, tiled=True),
        lax.all_gather(out_weight, ("dp", "expert"), axis=0, tiled=True),
        lax.all_gather(router_weight, ("dp", "expert"), axis=0, tiled=True),
        lax.all_gather(first_gain, ("dp", "expert"), axis=0, tiled=True),
        lax.all_gather(second_gain, ("dp", "expert"), axis=0, tiled=True),
    )
    query_full, key_complete, value_complete, out_full, router_full, gain_one, gain_two = gathered
    scale_one = gain_one.astype(jnp.float32)
    scale_two = gain_two.astype(jnp.float32)
    inputs = tokens[0].astype(jnp.float32)
    total_rows = inputs.shape[0]
    query_group_width = QUERY_HEADS // KEY_VALUE_HEADS
    ancestors, depths = ancestry(parents[0])
    tree_length = ancestors.shape[0] * SEG
    query_ids = lax.axis_index("dp") * total_rows + jnp.arange(total_rows, dtype=jnp.int32)
    key_ids = jnp.arange(tree_length, dtype=jnp.int32)
    visible, query_positions = visibility(ancestors, depths, query_ids, key_ids)
    first_normed = normalize(inputs, scale_one).astype(jnp.bfloat16)
    query_proj = jnp.dot(first_normed, query_full, preferred_element_type=jnp.float32).reshape(
        total_rows, QUERY_HEADS, HEAD_SIZE
    )
    key_projected = jnp.dot(first_normed, key_complete, preferred_element_type=jnp.float32).reshape(
        total_rows, KEY_VALUE_HEADS, HEAD_SIZE
    )
    value_projected = jnp.dot(first_normed, value_complete, preferred_element_type=jnp.float32)
    query_rotated = apply_rotation(query_proj, query_positions).astype(jnp.bfloat16)
    key_rotated = (
        apply_rotation(key_projected, query_positions)
        .astype(jnp.bfloat16)
        .reshape(total_rows, KEY_VALUE_HEADS * HEAD_SIZE)
    )
    value_low = value_projected.astype(jnp.bfloat16)
    keys_all, values_all = (
        lax.all_gather(key_rotated, "dp", axis=0, tiled=True),
        lax.all_gather(value_low, "dp", axis=0, tiled=True),
    )
    mixed_parts = []
    log_totals = []
    for key_value_head in range(KEY_VALUE_HEADS):
        scores = head_scores(query_rotated, keys_all, visible, key_value_head, query_group_width)
        row_max = jnp.max(scores, axis=-1, keepdims=True)
        exponent = jnp.exp(scores - row_max)
        row_total = jnp.sum(exponent, axis=-1, keepdims=True)
        log_totals.append(row_max + jnp.log(row_total))
        softmax_out = (exponent / row_total).astype(jnp.bfloat16)
        value_part = values_all[:, key_value_head * HEAD_SIZE : (key_value_head + 1) * HEAD_SIZE]
        mixed_parts.append(
            jnp.einsum("grk,kd->rgd", softmax_out, value_part, preferred_element_type=jnp.float32)
        )
    mixed_out = (
        jnp.concatenate(mixed_parts, axis=1)
        .reshape(total_rows, QUERY_HEADS * HEAD_SIZE)
        .astype(jnp.bfloat16)
    )
    middle = inputs + jnp.dot(mixed_out, out_full, preferred_element_type=jnp.float32)
    normed_two = normalize(middle, scale_two).astype(jnp.bfloat16)
    logits = jnp.dot(normed_two, router_full, preferred_element_type=jnp.float32)
    route_ids = routes[0]
    experts = gate_weight.shape[0] * lax.axis_size("expert")
    capacity = 3 * total_rows * TOPK // (2 * experts)
    expert_ids = jnp.arange(experts, dtype=jnp.int32)
    route_hits = route_ids[:, :, None] == expert_ids[None, None, :]
    chosen = jnp.sum(jnp.where(route_hits, logits[:, None, :], 0.0), axis=2)
    chosen_max = jnp.max(chosen, axis=1, keepdims=True)
    chosen_exp = jnp.exp(chosen - chosen_max)
    gate_weights = chosen_exp / jnp.sum(chosen_exp, axis=1, keepdims=True)
    pair_count = total_rows * TOPK
    slot_index = place(route_ids.reshape(pair_count), experts, capacity)
    slot_source = (
        jnp.full((experts * capacity,), pair_count, jnp.int32)
        .at[slot_index]
        .set(jnp.arange(pair_count, dtype=jnp.int32))
    )
    slot_used = slot_source < pair_count
    slot_pair = jnp.where(slot_used, slot_source, 0)
    slot_token = slot_pair // TOPK
    zero_low = jnp.zeros((), jnp.bfloat16)
    outgoing = jnp.where(slot_used[:, None], normed_two[slot_token], zero_low).reshape(
        experts, capacity, MODEL_WIDTH
    )
    gate_pre, up_pre, hidden = expert_hidden(
        lax.all_to_all(outgoing, "expert", split_axis=0, concat_axis=0, tiled=True),
        gate_weight,
        up_weight,
    )
    dispatched = expert_result(hidden, down_weight)
    returned = lax.all_to_all(dispatched, "expert", split_axis=0, concat_axis=0, tiled=True)
    expert_rows = (
        returned.reshape(experts * capacity, MODEL_WIDTH)[slot_index]
        .astype(jnp.float32)
        .reshape(total_rows, TOPK, MODEL_WIDTH)
    )
    final = middle + jnp.sum(gate_weights[:, :, None] * expert_rows, axis=1)
    output = final.astype(jnp.bfloat16)[None]
    upstream = cotangent[0].astype(jnp.float32)
    gate_grad = jnp.sum(upstream[:, None, :] * expert_rows, axis=2)
    chosen_grad = gate_weights * (
        gate_grad - jnp.sum(gate_weights * gate_grad, axis=1, keepdims=True)
    )
    logit_grad = jnp.sum(jnp.where(route_hits, chosen_grad[:, :, None], 0.0), axis=1)
    pair_grad = (
        (gate_weights[:, :, None] * upstream[:, None, :])
        .astype(jnp.bfloat16)
        .reshape(pair_count, MODEL_WIDTH)
    )
    grad_outgoing = jnp.where(slot_used[:, None], pair_grad[slot_pair], zero_low).reshape(
        experts, capacity, MODEL_WIDTH
    )
    received, grad_in = (
        lax.all_to_all(outgoing, "expert", split_axis=0, concat_axis=0, tiled=True),
        lax.all_to_all(grad_outgoing, "expert", split_axis=0, concat_axis=0, tiled=True),
    )
    gate_pre, up_pre, hidden = expert_hidden(received, gate_weight, up_weight)
    local_count = gate_weight.shape[0]
    slot_count = received.shape[1]
    grouped_rows = received.reshape(-1, local_count, slot_count, MODEL_WIDTH)
    grouped_hidden = hidden.reshape(-1, local_count, slot_count, FF)
    grouped_grad = grad_in.reshape(-1, local_count, slot_count, MODEL_WIDTH)
    down_grad = jnp.einsum(
        "sjcf,sjcd->jfd", grouped_hidden, grouped_grad, preferred_element_type=jnp.float32
    )
    hidden_grad = jnp.einsum(
        "sjcd,jfd->sjcf", grouped_grad, down_weight, preferred_element_type=jnp.float32
    )
    _, product_pull = jax.vjp(gelu_product, gate_pre, up_pre)
    gate_pre_grad, up_pre_grad = product_pull(hidden_grad.reshape(gate_pre.shape))
    gate_low = gate_pre_grad.astype(jnp.bfloat16).reshape(-1, local_count, slot_count, FF)
    up_low = up_pre_grad.astype(jnp.bfloat16).reshape(-1, local_count, slot_count, FF)
    gate_w_grad = jnp.einsum(
        "sjcd,sjcf->jdf", grouped_rows, gate_low, preferred_element_type=jnp.float32
    )
    up_w_grad = jnp.einsum(
        "sjcd,sjcf->jdf", grouped_rows, up_low, preferred_element_type=jnp.float32
    )
    row_grad = jnp.einsum(
        "sjcf,jdf->sjcd", gate_low, gate_weight, preferred_element_type=jnp.float32
    ) + jnp.einsum("sjcf,jdf->sjcd", up_low, up_weight, preferred_element_type=jnp.float32)
    row_grad = row_grad.astype(jnp.bfloat16).reshape(received.shape)
    returned_grad = lax.all_to_all(row_grad, "expert", split_axis=0, concat_axis=0, tiled=True)
    pair_rows = (
        returned_grad.reshape(experts * capacity, MODEL_WIDTH)[slot_index]
        .astype(jnp.float32)
        .reshape(total_rows, TOPK, MODEL_WIDTH)
    )
    summed_experts = (
        lax.psum(gate_w_grad.astype(jnp.bfloat16), "dp").astype(jnp.float32),
        lax.psum(up_w_grad.astype(jnp.bfloat16), "dp").astype(jnp.float32),
        lax.psum(down_grad.astype(jnp.bfloat16), "dp").astype(jnp.float32),
    )
    router_wide = router_full.astype(jnp.float32)
    normed_two_grad = jnp.dot(logit_grad, router_wide.T, precision=HIGH_PRECISION) + jnp.sum(
        pair_rows, axis=1
    )
    router_grad = jnp.dot(normed_two.astype(jnp.float32).T, logit_grad, precision=HIGH_PRECISION)
    _, second_pull = jax.vjp(normalize, middle, scale_two)
    middle_norm_grad, second_gain_grad = second_pull(normed_two_grad)
    middle_grad = upstream + middle_norm_grad
    attended_low = middle_grad.astype(jnp.bfloat16)
    out_grad = jnp.einsum("rd,re->de", mixed_out, attended_low, preferred_element_type=jnp.float32)
    mixed_grad = jnp.einsum("re,de->rd", attended_low, out_full, preferred_element_type=jnp.float32)
    mixed_grad = mixed_grad.astype(jnp.bfloat16).reshape(total_rows, QUERY_HEADS, HEAD_SIZE)
    query_parts = []
    key_parts = []
    value_parts = []
    for key_value_head in range(KEY_VALUE_HEADS):
        scores = head_scores(query_rotated, keys_all, visible, key_value_head, query_group_width)
        softmax_out = jnp.exp(scores - log_totals[key_value_head])
        query_part = query_rotated[
            :, key_value_head * query_group_width : (key_value_head + 1) * query_group_width, :
        ]
        key_part = keys_all[:, key_value_head * HEAD_SIZE : (key_value_head + 1) * HEAD_SIZE]
        value_part = values_all[:, key_value_head * HEAD_SIZE : (key_value_head + 1) * HEAD_SIZE]
        grad_part = mixed_grad[
            :, key_value_head * query_group_width : (key_value_head + 1) * query_group_width, :
        ]
        value_parts.append(
            jnp.einsum(
                "grk,rgd->kd",
                softmax_out.astype(jnp.bfloat16),
                grad_part,
                preferred_element_type=jnp.float32,
            )
        )
        attn_grad = jnp.einsum(
            "rgd,kd->grk", grad_part, value_part, preferred_element_type=jnp.float32
        )
        score_grad = softmax_out * (
            attn_grad - jnp.sum(softmax_out * attn_grad, axis=-1, keepdims=True)
        )
        score_low = score_grad.astype(jnp.bfloat16)
        query_parts.append(
            jnp.einsum("grk,kd->rgd", score_low, key_part, preferred_element_type=jnp.float32)
            * HEAD_SIZE ** (-0.5)
        )
        key_parts.append(
            jnp.einsum("grk,rgd->kd", score_low, query_part, preferred_element_type=jnp.float32)
            * HEAD_SIZE ** (-0.5)
        )
    key_total_sum, value_sum = (
        lax.psum_scatter(
            jnp.concatenate(key_parts, axis=1).astype(jnp.bfloat16),
            "dp",
            scatter_dimension=0,
            tiled=True,
        ).astype(jnp.float32),
        lax.psum_scatter(
            jnp.concatenate(value_parts, axis=1).astype(jnp.bfloat16),
            "dp",
            scatter_dimension=0,
            tiled=True,
        ).astype(jnp.float32),
    )
    _, query_pull = jax.vjp(lambda values: apply_rotation(values, query_positions), query_proj)
    _, key_pullback = jax.vjp(lambda values: apply_rotation(values, query_positions), key_projected)
    query_grad = (
        query_pull(jnp.concatenate(query_parts, axis=1))[0]
        .astype(jnp.bfloat16)
        .reshape(total_rows, QUERY_HEADS * HEAD_SIZE)
    )
    key_grad = (
        key_pullback(key_total_sum.reshape(total_rows, KEY_VALUE_HEADS, HEAD_SIZE))[0]
        .astype(jnp.bfloat16)
        .reshape(total_rows, KEY_VALUE_HEADS * HEAD_SIZE)
    )
    value_grad = value_sum.astype(jnp.bfloat16)
    query_w_grad = jnp.einsum(
        "rd,re->de", first_normed, query_grad, preferred_element_type=jnp.float32
    )
    key_w_grad = jnp.einsum("rd,re->de", first_normed, key_grad, preferred_element_type=jnp.float32)
    value_w_grad = jnp.einsum(
        "rd,re->de", first_normed, value_grad, preferred_element_type=jnp.float32
    )
    normed_one_grad = (
        jnp.einsum("re,de->rd", query_grad, query_full, preferred_element_type=jnp.float32)
        + jnp.einsum("re,de->rd", key_grad, key_complete, preferred_element_type=jnp.float32)
        + jnp.einsum("re,de->rd", value_grad, value_complete, preferred_element_type=jnp.float32)
    )
    _, first_pull = jax.vjp(normalize, inputs, scale_one)
    input_norm_grad, first_gain_grad = first_pull(normed_one_grad)
    input_grad = (middle_grad + input_norm_grad)[None]
    shares = (
        lax.psum_scatter(query_w_grad, ("dp", "expert"), scatter_dimension=0, tiled=True),
        lax.psum_scatter(key_w_grad, ("dp", "expert"), scatter_dimension=0, tiled=True),
        lax.psum_scatter(value_w_grad, ("dp", "expert"), scatter_dimension=0, tiled=True),
        lax.psum_scatter(out_grad, ("dp", "expert"), scatter_dimension=0, tiled=True),
        lax.psum_scatter(router_grad, ("dp", "expert"), scatter_dimension=0, tiled=True),
        lax.psum_scatter(first_gain_grad, ("dp", "expert"), scatter_dimension=0, tiled=True),
        lax.psum_scatter(second_gain_grad, ("dp", "expert"), scatter_dimension=0, tiled=True),
    )
    return (
        output,
        input_grad,
        shares[5],
        shares[6],
        shares[0],
        shares[1],
        shares[2],
        shares[3],
        shares[4],
        summed_experts[0],
        summed_experts[1],
        summed_experts[2],
    )


def mm(a, b):
    return jnp.dot(a, b, preferred_element_type=F32)


def mm_nt(a, b):
    return lax.dot_general(a, b, (((1,), (1,)), ((), ())), preferred_element_type=F32)


def mm_tn(a, b):
    return lax.dot_general(a, b, (((0,), (0,)), ((), ())), preferred_element_type=F32)


def gelu_both(value):
    scale = 0.7978845608028654
    square = value * value
    bend = jnp.tanh(scale * value * (1.0 + 0.044715 * square))
    half = 0.5 * (1.0 + bend)
    slope = half + 0.5 * value * (1.0 - bend * bend) * scale * (1.0 + 0.134145 * square)
    return value * half, slope


def expert_kernel(
    n2_ref, gate_ref, dy_ref, gw_ref, uw_ref, dw_ref,
    row_ref, gg_ref, sum_ref, dgw_ref, duw_ref, ddw_ref,
    n2_all, gate_all, dy_buf, dy_cols, hs_all, gl_all, ul_all, own, sib, zin, gg_out, gg_in, stage, down_stage,
    n2_send, n2_recv, gt_send, gt_recv, own_send, sib_recv, zin_send, zin_recv,
    gg_send, gg_recv, dy_sem, cols_sem, sum_sem, stage_sem,
):
    count = lax.axis_size("expert")
    depth = count // 2
    rows = n2_ref.shape[0]
    half = rows // 2
    width = n2_ref.shape[1]
    ff = gw_ref.shape[1]
    me = lax.axis_index("expert")
    z, core = me // 2, me % 2
    sibling = z * 2 + 1 - core

    def at(zz):
        return {"expert": zz * 2 + core}

    barrier = pltpu.get_barrier_semaphore()
    for other in range(1, count):
        pl.semaphore_signal(
            barrier, 1, device_id={"expert": lax.rem(me + other, count)}, device_id_type=MESH
        )
    pl.semaphore_wait(barrier, count - 1)

    def chunk(k):
        return pl.ds(pl.multiple_of(k * rows, 16), rows)

    def n2_copy(k, lane, target):
        return pltpu.make_async_remote_copy(
            n2_all.at[chunk(k)], n2_all.at[chunk(k)], n2_send.at[k, lane], n2_recv.at[k],
            device_id=target, device_id_type=MESH,
        )

    def gt_copy(k, lane, target):
        return pltpu.make_async_remote_copy(
            gate_all.at[k], gate_all.at[k], gt_send.at[k, lane], gt_recv.at[k],
            device_id=target, device_id_type=MESH,
        )

    def send_chunk(k, lane, target):
        n2_copy(k, lane, target).start()
        gt_copy(k, lane, target).start()

    def sent_chunk(k, lane, target):
        n2_copy(k, lane, target).wait_send()
        gt_copy(k, lane, target).wait_send()

    def arrived(k):
        n2_copy(k, 0, at(z)).wait_recv()
        gt_copy(k, 0, at(z)).wait_recv()

    def dy_copy(k, slot):
        return pltpu.make_async_copy(dy_ref.at[k], dy_buf.at[slot], dy_sem.at[slot])

    def gg_copy(k):
        return pltpu.make_async_remote_copy(
            gg_out.at[k], gg_in.at[me], gg_send.at[k], gg_recv.at[me],
            device_id={"expert": k}, device_id_type=MESH,
        )

    def own_copy(zs):
        return pltpu.make_async_remote_copy(
            own.at[2 * zs + 1 - core], sib.at[zs], own_send.at[zs], sib_recv.at[zs],
            device_id={"expert": sibling}, device_id_type=MESH,
        )

    def part(h):
        return pl.ds(h * half, half)

    def zin_copy(zd, h, nxt, slot):
        return pltpu.make_async_remote_copy(
            own.at[2 * zd + core, part(h)], zin.at[slot, part(h)],
            zin_send.at[zd, h], zin_recv.at[slot, h],
            device_id=at(nxt), device_id_type=MESH,
        )

    n2_all[chunk(me), :] = n2_ref[...]
    gate_all[me] = gate_ref[...]

    @pl.when(z < depth - 1)
    def _():
        send_chunk(me, 0, at(z + 1))

    @pl.when(z > 0)
    def _():
        send_chunk(me, 1, at(z - 1))

    send_chunk(me, 2, {"expert": sibling})

    row_ids = lax.broadcasted_iota(jnp.int32, (count, gate_ref.shape[1]), 0)

    def compute(k, slot):
        r = chunk(k)
        gate_row = jnp.sum(jnp.where(row_ids == me, gate_all[k], 0.0), axis=0, keepdims=True)
        gate_col = jnp.transpose(jnp.broadcast_to(gate_row, (128, gate_row.shape[1])))[:rows]
        tile = 256
        gate_wide = jnp.concatenate([gate_col] * (tile // 128), axis=1)
        total = jnp.zeros((rows, 128), F32)
        for j in range(ff // tile):
            cols = slice(j * tile, (j + 1) * tile)
            back = mm_nt(dy_buf[slot], dw_ref[cols, :])
            gate_pre = mm(n2_all[r, :], gw_ref[:, cols])
            up_pre = mm(n2_all[r, :], uw_ref[:, cols])
            act, slope = gelu_both(gate_pre)
            hidden = act * up_pre
            hs_all[r, cols] = (gate_wide * hidden).astype(BF)
            product = hidden * back
            for i in range(tile // 128):
                total = total + product[:, i * 128 : (i + 1) * 128]
            back = gate_wide * back
            gl_all[r, cols] = (back * up_pre * slope).astype(BF)
            ul_all[r, cols] = (back * act).astype(BF)
        padded = jnp.concatenate(
            [total, jnp.zeros((gate_ref.shape[1] - rows, 128), F32)], axis=0
        )
        gg_row = jnp.sum(jnp.transpose(padded), axis=0, keepdims=True)
        gg_tile = jnp.where(row_ids == me, gg_row, 0.0)
        gg_out[k] = gg_tile

        @pl.when(k == me)
        def _():
            gg_in[me] = gg_tile

        @pl.when(k != me)
        def _():
            gg_copy(k).start()

        wide = 512
        for j in range(width // wide):
            cols = slice(j * wide, (j + 1) * wide)
            own[k, :, cols] = (
                mm_nt(gl_all[r, :], gw_ref[cols, :]) + mm_nt(ul_all[r, :], uw_ref[cols, :])
            ).astype(BF)

    block = 16

    def combine(zd, h, with_in):
        def step(i, _):
            rr = pl.ds(pl.multiple_of(h * half + i * block, block), block)
            value = own[2 * zd + core, rr, :].astype(F32) + sib[zd, rr, :].astype(F32)
            if with_in:
                value = value + zin[zd, rr, :].astype(F32)
            own[2 * zd + core, rr, :] = value.astype(BF)
            return 0

        lax.fori_loop(0, half // block, step, 0)

    def slot_for(zd, nxt):
        return jnp.where((nxt == zd) & (nxt < z), depth, zd)

    def pass_on(zd, h, nxt, with_in):
        if h == 0:
            own_copy(zd).wait_recv()
        if with_in:
            zin_copy(zd, h, nxt, zd).wait_recv()
        combine(zd, h, with_in)
        zin_copy(zd, h, nxt, slot_for(zd, nxt)).start()

    def pair(zs):
        def one(w, _):
            k = 2 * zs + jnp.where(w == 0, 1 - core, core)

            @pl.when(w == 0)
            def _():
                arrived(k)

            dy_copy(k, w).wait()
            compute(k, w)

            @pl.when(w == 0)
            def _():
                own_copy(zs).start()

            return 0

        lax.fori_loop(0, 2, one, 0)

    def start_dy(zs):
        dy_copy(2 * zs + 1 - core, 0).start()
        dy_copy(2 * zs + core, 1).start()

    def by_distance(d, _):
        left, right = z - d, z + d
        has_left, has_right = left >= 0, (right < depth) & (d > 0)

        @pl.when(has_left)
        def _():
            start_dy(left)

        @pl.when(has_left & (d > 0))
        def _():
            k = 2 * left + core
            arrived(k)

            @pl.when(z < depth - 1)
            def _():
                send_chunk(k, 0, at(z + 1))

            send_chunk(k, 2, {"expert": sibling})

        @pl.when(has_right)
        def _():
            k = 2 * right + core
            arrived(k)

            @pl.when(z > 0)
            def _():
                send_chunk(k, 1, at(z - 1))

            send_chunk(k, 2, {"expert": sibling})

        def side(s, _):
            zs = jnp.where(s == 0, left, right)

            @pl.when(jnp.where(s == 0, has_left, has_right))
            def _():
                @pl.when(s == 1)
                def _():
                    start_dy(right)

                pair(zs)

                @pl.when((d > 0) & ((z == 0) | (z == depth - 1)))
                def _():
                    nxt = jnp.where(z == 0, 1, depth - 2)
                    for h in range(2):
                        pass_on(zs, h, nxt, False)

            return 0

        lax.fori_loop(0, 2, side, 0)
        return 0

    lax.fori_loop(0, depth, by_distance, 0)

    def sum_copy(k, slot):
        return pltpu.make_async_copy(own.at[slot], sum_ref.at[k], sum_sem.at[slot])

    def sums(i, _):
        slot = 2 * lax.rem(i, depth) + 1 - core

        @pl.when(i < depth)
        def _():
            own_copy(i).wait_send()

        @pl.when(i >= depth)
        def _():
            sum_copy(i, slot).wait()

        wide = 512
        for j in range(width // wide):
            cols = slice(j * wide, (j + 1) * wide)
            own[slot, :, cols] = mm(hs_all[chunk(i), :], dw_ref[:, cols]).astype(BF)
        sum_copy(i, slot).start()
        return 0

    lax.fori_loop(0, count, sums, 0)

    tile = 256

    def stage_copy(ref, i, slot):
        return pltpu.make_async_copy(
            stage.at[slot], ref.at[pl.ds(pl.multiple_of(i * tile, 16), tile)], stage_sem.at[slot]
        )

    def col_copy(i, slot):
        return pltpu.make_async_copy(
            dy_ref.at[:, :, pl.ds(pl.multiple_of(i * tile, 128), tile)], dy_cols.at[slot], cols_sem.at[slot]
        )

    def weight_tiles(ref, grads, low, high, fresh):
        def step(i, _):
            slot = lax.rem(i, 2)

            @pl.when(i >= 2 if fresh else i >= 0)
            def _():
                stage_copy(ref, i, slot).wait()

            cols = pl.ds(pl.multiple_of(i * tile, 128), tile)
            stage[slot] = mm_tn(n2_all[:, cols], grads[...]).astype(BF)
            stage_copy(ref, i, slot).start()
            return 0

        lax.fori_loop(low, high, step, 0)

    def down_copy(i, slot):
        return pltpu.make_async_copy(
            down_stage.at[slot],
            ddw_ref.at[:, pl.ds(pl.multiple_of(i * tile, 128), tile)],
            stage_sem.at[slot],
        )

    def down_tiles(low, high):
        def step(i, _):
            slot = lax.rem(i, 2)
            down_copy(i, slot).wait()
            col_copy(i, slot).wait()
            cols = dy_cols[slot].reshape(count * rows, tile)
            down_stage[slot] = mm_tn(hs_all[...], cols).astype(BF)
            down_copy(i, slot).start()

            @pl.when(i + 2 < width // tile)
            def _():
                col_copy(i + 2, slot).start()

            return 0

        lax.fori_loop(low, high, step, 0)

    def flow(r, first, h):
        right = (z < depth - 1 - z) if first else (z >= depth - 1 - z)
        zd = jnp.where(right, r, depth - 1 - r)
        valid = jnp.where(right, (z < zd) & (z > 0), (z > zd) & (z < depth - 1))

        @pl.when(valid)
        def _():
            pass_on(zd, h, jnp.where(right, z + 1, z - 1), True)

    col_copy(0, 0).start()
    col_copy(1, 1).start()
    tiles = width // tile
    jobs = [
        lambda: weight_tiles(dgw_ref, gl_all, 0, tiles // 2, True),
        lambda: weight_tiles(dgw_ref, gl_all, tiles // 2, tiles, True),
        lambda: weight_tiles(duw_ref, ul_all, 0, tiles // 2, False),
        lambda: weight_tiles(duw_ref, ul_all, tiles // 2, tiles, False),
        lambda: down_tiles(0, tiles // 2),
        lambda: down_tiles(tiles // 2, tiles),
    ]
    for r in range(2, depth):
        for first in (True, False):
            for h in range(2):
                flow(r, first, h)
                if jobs and (first or r == depth - 1):
                    jobs.pop(0)()
    while jobs:
        jobs.pop(0)()

    own_copy(z).wait_recv()
    for h in range(2):

        @pl.when(z > 0)
        def _():
            zin_copy(z, h, z, z).wait_recv()

        @pl.when(z < depth - 1)
        def _():
            zin_copy(z, h, z, depth).wait_recv()

    def last(i, _):
        rr = pl.ds(pl.multiple_of(i * block, block), block)
        row_ref[rr, :] = own[me, rr, :].astype(F32) + sib[z, rr, :].astype(F32)

        @pl.when(z > 0)
        def _():
            row_ref[rr, :] += zin[z, rr, :].astype(F32)

        @pl.when(z < depth - 1)
        def _():
            row_ref[rr, :] += zin[depth, rr, :].astype(F32)

        return 0

    lax.fori_loop(0, rows // block, last, 0)

    for e in range(count):

        @pl.when(e != me)
        def _():
            pltpu.make_async_remote_copy(
                gg_out.at[e], gg_in.at[e], gg_send.at[e], gg_recv.at[e],
                device_id={"expert": e}, device_id_type=MESH,
            ).wait_recv()

    gg_ref[...] = jnp.sum(gg_in[...], axis=0)

    for e in range(count):

        @pl.when(e != me)
        def _():
            gg_copy(e).wait_send()

        zs = e // 2

        @pl.when((e == me) | ((zs < z) & (e % 2 == core)))
        def _():
            @pl.when(z < depth - 1)
            def _():
                sent_chunk(e, 0, at(z + 1))

        @pl.when((e == me) | ((zs > z) & (e % 2 == core)))
        def _():
            @pl.when(z > 0)
            def _():
                sent_chunk(e, 1, at(z - 1))

        @pl.when(e % 2 == core)
        def _():
            sent_chunk(e, 2, {"expert": sibling})

    for zd in range(depth):
        sum_copy(zd, 2 * zd + 1 - core).wait()
        for h in range(2):

            @pl.when(zd != z)
            def _():
                zin_copy(zd, h, z, zd).wait_send()

    for slot in range(2):
        down_copy(0, slot).wait()


def expert_pass(n2, gate_rows, dy_all, gate_w, up_w, down_w):
    count = lax.axis_size("expert")
    depth = count // 2
    rows, width = n2.shape
    ff = gate_w.shape[1]
    lanes = gate_rows.shape[1]
    dma = pltpu.SemaphoreType.DMA
    vmem = pl.BlockSpec(memory_space=pltpu.VMEM)
    anywhere = pl.BlockSpec(memory_space=pl.ANY)
    outs = (
        jax.ShapeDtypeStruct((rows, width), F32),
        jax.ShapeDtypeStruct((count, lanes), F32),
        jax.ShapeDtypeStruct((count, rows, width), BF),
        jax.ShapeDtypeStruct((width, ff), BF),
        jax.ShapeDtypeStruct((width, ff), BF),
        jax.ShapeDtypeStruct((ff, width), BF),
    )
    return pl.pallas_call(
        expert_kernel,
        name="expert_pass",
        out_shape=outs,
        in_specs=[vmem, vmem, anywhere, vmem, vmem, vmem],
        out_specs=(vmem, vmem, anywhere, anywhere, anywhere, anywhere),
        scratch_shapes=[
            pltpu.VMEM((count * rows, width), BF),
            pltpu.VMEM((count, count, lanes), F32),
            pltpu.VMEM((2, rows, width), BF),
            pltpu.VMEM((2, count, rows, 256), BF),
            pltpu.VMEM((count * rows, ff), BF),
            pltpu.VMEM((count * rows, ff), BF),
            pltpu.VMEM((count * rows, ff), BF),
            pltpu.VMEM((count, rows, width), BF),
            pltpu.VMEM((depth, rows, width), BF),
            pltpu.VMEM((depth + 1, rows, width), BF),
            pltpu.VMEM((count, count, lanes), F32),
            pltpu.VMEM((count, count, lanes), F32),
            pltpu.VMEM((2, 256, ff), BF),
            pltpu.VMEM((2, ff, 256), BF),
            dma((count, 3)), dma((count,)), dma((count, 3)), dma((count,)),
            dma((depth,)), dma((depth,)), dma((depth, 2)), dma((depth + 1, 2)),
            dma((count,)), dma((count,)), dma((2,)), dma((2,)), dma((count,)), dma((2,)),
        ],
        compiler_params=pltpu.CompilerParams(
            collective_id=2, has_side_effects=True, vmem_limit_bytes=62 * 2**20
        ),
        cost_estimate=pl.CostEstimate(
            flops=18 * count * rows * width * ff, bytes_accessed=60 * 2**20, transcendentals=0
        ),
    )(n2, gate_rows, dy_all, gate_w, up_w, down_w)


def scatter_kernel(
    w_ref, es_ref,
    share_ref, sum_ref,
    w, es, wsib, ra, rb, ra2, rb2, wz, esib, ez,
    ws_send, ws_recv, a_send, a_recv, b_send, b_recv, a2_send, a2_recv, b2_send, b2_recv,
    wz_send, wz_recv, es_send, es_recv, ez_send, ez_recv, w_sem, e_sem,
):
    depth = es_ref.shape[0] // 2
    rows, width = es_ref.shape[1:]
    shard, total = w_ref.shape[3:]
    cut = ra.shape[3]
    half = rows // 2
    me, mine = lax.axis_index("expert"), lax.axis_index("dp")
    z, core = me // 2, me % 2
    y, x = mine // 2, mine % 2
    xn, yn, diag = y * 2 + 1 - x, (1 - y) * 2 + x, (1 - y) * 2 + 1 - x
    sibling = {"expert": z * 2 + 1 - core}

    def at(zz):
        return {"expert": zz * 2 + core}

    greet(depth, z, at, (sibling, {"dp": xn}, {"dp": yn}))

    def remote(src, dst, send, recv, target):
        return pltpu.make_async_remote_copy(
            src, dst, send, recv, device_id=target, device_id_type=MESH
        )

    def ws_copy(dp):
        return remote(w_ref.at[dp, :, 1 - core], wsib.at[dp], ws_send.at[dp], ws_recv.at[dp], sibling)

    def w_load(dp):
        return pltpu.make_async_copy(w_ref.at[dp, :, core], w.at[dp], w_sem.at[dp])

    def es_copy(zd):
        return remote(es_ref.at[2 * zd + 1 - core], esib.at[zd], es_send.at[zd], es_recv.at[zd], sibling)

    def es_load(zd):
        return pltpu.make_async_copy(es_ref.at[2 * zd + core], es.at[zd], e_sem.at[zd])

    first_cols, last_cols = slice(0, cut), slice(cut, total)

    def a_copy(yy):
        return remote(
            w.at[yy * 2 + 1 - x, :, :, first_cols], ra.at[yy], a_send.at[yy], a_recv.at[yy], {"dp": xn}
        )

    def b_copy(xx):
        return remote(
            w.at[(1 - y) * 2 + xx, :, :, last_cols], rb.at[xx], b_send.at[xx], b_recv.at[xx], {"dp": yn}
        )

    def a2_copy():
        return remote(w.at[yn, :, :, first_cols], ra2, a2_send, a2_recv, {"dp": yn})

    def b2_copy():
        return remote(w.at[xn, :, :, last_cols], rb2, b2_send, b2_recv, {"dp": xn})

    def wz_copy(zd, nxt, slot):
        return remote(w.at[mine, zd], wz.at[slot], wz_send.at[zd], wz_recv.at[slot], at(nxt))

    def part(h):
        return pl.ds(h * half, half)

    def ez_copy(zd, h, nxt, slot):
        return remote(
            es.at[zd, part(h)], ez.at[slot, part(h)], ez_send.at[zd, h], ez_recv.at[slot, h], at(nxt)
        )

    for dp in (xn, diag, yn, mine):
        ws_copy(dp).start()
        w_load(dp).start()
    for zd in range(depth):
        es_copy(zd).start()
        es_load(zd).start()

    block = 16

    def add(into, term):
        def step(i, _):
            zz, rr = i // (shard // block), pl.ds(pl.multiple_of(lax.rem(i, shard // block) * block, block), block)
            into[zz, rr, :] = (into[zz, rr, :].astype(F32) + term[zz, rr, :].astype(F32)).astype(BF)
            return 0

        lax.fori_loop(0, depth * (shard // block), step, 0)

    def combine(dp):
        w_load(dp).wait()
        ws_copy(dp).wait_recv()
        add(w.at[dp], wsib.at[dp])

    combine(xn)
    a_copy(y).start()
    combine(diag)
    a_copy(1 - y).start()
    b_copy(1 - x).start()
    combine(yn)
    b_copy(x).start()

    def slot_for(zd, nxt):
        return jnp.where((nxt == zd) & (nxt < z), depth, zd)

    def rows_on(zd, h, nxt, with_in):
        if h == 0:
            es_load(zd).wait()
            es_copy(zd).wait_recv()
        if with_in:
            ez_copy(zd, h, nxt, zd).wait_recv()

        def step(i, _):
            rr = pl.ds(pl.multiple_of(h * half + i * block, block), block)
            value = es[zd, rr, :].astype(F32) + esib[zd, rr, :].astype(F32)
            if with_in:
                value = value + ez[zd, rr, :].astype(F32)
            es[zd, rr, :] = value.astype(BF)
            return 0

        lax.fori_loop(0, half // block, step, 0)
        ez_copy(zd, h, nxt, slot_for(zd, nxt)).start()

    def shard_on(zd, nxt, with_in):
        if with_in:
            wz_copy(zd, nxt, zd).wait_recv()

            def step(i, _):
                rr = pl.ds(pl.multiple_of(i * block, block), block)
                w[mine, zd, rr, :] = (w[mine, zd, rr, :].astype(F32) + wz[zd, rr, :].astype(F32)).astype(BF)
                return 0

            lax.fori_loop(0, shard // block, step, 0)
        wz_copy(zd, nxt, slot_for(zd, nxt)).start()

    end = (z == 0) | (z == depth - 1)

    def from_end(d, action):
        @pl.when(end)
        def _():
            action(jnp.where(z == 0, d, depth - 1 - d), jnp.where(z == 0, 1, depth - 2))

    def flow(r, first, action):
        right = (z < depth - 1 - z) if first else (z >= depth - 1 - z)
        zd = jnp.where(right, r, depth - 1 - r)
        valid = jnp.where(right, (z < zd) & (z > 0), (z > zd) & (z < depth - 1))

        @pl.when(valid)
        def _():
            action(zd, jnp.where(right, z + 1, z - 1))

    for d in range(1, depth):
        for h in range(2):
            from_end(d, lambda zd, nxt, h=h: rows_on(zd, h, nxt, False))
    combine(mine)
    for h in range(2):
        flow(2, True, lambda zd, nxt, h=h: rows_on(zd, h, nxt, True))

    a_copy(1 - y).wait_recv()
    add(w.at[yn, :, :, first_cols], ra.at[1 - y])
    a2_copy().start()
    b_copy(1 - x).wait_recv()
    add(w.at[xn, :, :, last_cols], rb.at[1 - x])
    b2_copy().start()
    a_copy(y).wait_recv()
    add(w.at[mine, :, :, first_cols], ra.at[y])
    b_copy(x).wait_recv()
    add(w.at[mine, :, :, last_cols], rb.at[x])
    for r in range(2, depth):
        for first in (True, False):
            if (r, first) == (2, True):
                continue
            for h in range(2):
                flow(r, first, lambda zd, nxt, h=h: rows_on(zd, h, nxt, True))
    a2_copy().wait_recv()
    add(w.at[mine, :, :, first_cols], ra2)
    b2_copy().wait_recv()
    add(w.at[mine, :, :, last_cols], rb2)
    for d in range(1, depth):
        from_end(d, lambda zd, nxt: shard_on(zd, nxt, False))
    for r in range(2, depth):
        for first in (True, False):
            flow(r, first, lambda zd, nxt: shard_on(zd, nxt, True))

    es_load(z).wait()
    es_copy(z).wait_recv()

    @pl.when(z > 0)
    def _():
        for h in range(2):
            ez_copy(z, h, z, z).wait_recv()

    @pl.when(z < depth - 1)
    def _():
        for h in range(2):
            ez_copy(z, h, z, depth).wait_recv()

    def last_rows(i, _):
        rr = pl.ds(pl.multiple_of(i * block, block), block)
        sum_ref[rr, :] = es[z, rr, :].astype(F32) + esib[z, rr, :].astype(F32)

        @pl.when(z > 0)
        def _():
            sum_ref[rr, :] += ez[z, rr, :].astype(F32)

        @pl.when(z < depth - 1)
        def _():
            sum_ref[rr, :] += ez[depth, rr, :].astype(F32)

        return 0

    lax.fori_loop(0, rows // block, last_rows, 0)

    @pl.when(z > 0)
    def _():
        wz_copy(z, z, z).wait_recv()

    @pl.when(z < depth - 1)
    def _():
        wz_copy(z, z, depth).wait_recv()

    share_ref[...] = w[mine, z].astype(F32)

    @pl.when(z > 0)
    def _():
        share_ref[...] += wz[z].astype(F32)

    @pl.when(z < depth - 1)
    def _():
        share_ref[...] += wz[depth].astype(F32)

    for dp in range(w.shape[0]):
        ws_copy(dp).wait_send()
    for i in range(2):
        a_copy(i).wait_send()
        b_copy(i).wait_send()
    a2_copy().wait_send()
    b2_copy().wait_send()
    for zd in range(depth):
        es_copy(zd).wait_send()

        @pl.when(zd != z)
        def _():
            wz_copy(zd, z, zd).wait_send()
            for h in range(2):
                ez_copy(zd, h, z, zd).wait_send()


def scatter_pass(w_grads, sums):
    planes = lax.axis_size("dp")
    count = lax.axis_size("expert")
    depth = count // 2
    shard, total = w_grads.shape[1:]
    rows, width = sums.shape[1:]
    cut = total // 2 // 128 * 128 + 128
    dma = pltpu.SemaphoreType.DMA
    vmem = pl.BlockSpec(memory_space=pltpu.VMEM)
    anywhere = pl.BlockSpec(memory_space=pl.ANY)
    return pl.pallas_call(
        scatter_kernel,
        name="scatter_pass",
        out_shape=(
            jax.ShapeDtypeStruct((shard, total), F32),
            jax.ShapeDtypeStruct((rows, width), F32),
        ),
        in_specs=[anywhere, anywhere],
        out_specs=(vmem, vmem),
        scratch_shapes=[
            pltpu.VMEM((planes, depth, shard, total), BF),
            pltpu.VMEM((depth, rows, width), BF),
            pltpu.VMEM((planes, depth, shard, total), BF),
            pltpu.VMEM((2, depth, shard, cut), BF),
            pltpu.VMEM((2, depth, shard, total - cut), BF),
            pltpu.VMEM((depth, shard, cut), BF),
            pltpu.VMEM((depth, shard, total - cut), BF),
            pltpu.VMEM((depth + 1, shard, total), BF),
            pltpu.VMEM((depth, rows, width), BF),
            pltpu.VMEM((depth + 1, rows, width), BF),
            dma((planes,)), dma((planes,)), dma((2,)), dma((2,)), dma((2,)), dma((2,)),
            dma, dma, dma, dma,
            dma((depth,)), dma((depth + 1,)), dma((depth,)), dma((depth,)),
            dma((depth, 2)), dma((depth + 1, 2)), dma((planes,)), dma((depth,)),
        ],
        compiler_params=pltpu.CompilerParams(
            collective_id=3, has_side_effects=True, vmem_limit_bytes=60 * 2**20
        ),
        cost_estimate=pl.CostEstimate(
            flops=10**9, bytes_accessed=200 * 2**20, transcendentals=0
        ),
    )(w_grads.reshape(planes, depth, 2, shard, total), sums)


def greet(depth, z, at, targets):
    barrier = pltpu.get_barrier_semaphore()
    for target in targets:
        pl.semaphore_signal(barrier, 1, device_id=target, device_id_type=MESH)

    @pl.when(z > 0)
    def _():
        pl.semaphore_signal(barrier, 1, device_id=at(z - 1), device_id_type=MESH)

    @pl.when(z < depth - 1)
    def _():
        pl.semaphore_signal(barrier, 1, device_id=at(z + 1), device_id_type=MESH)

    ends = (z > 0).astype(jnp.int32) + (z < depth - 1).astype(jnp.int32)
    pl.semaphore_wait(barrier, len(targets) + ends)


def attention_kernel(
    x_ref, shard_ref, cos_ref, sin_ref, bias_ref, hits_ref,
    n1_ref, q_ref, kv_ref, mixed_ref, lse_ref, middle_ref, n2_ref, gate_ref, w_out,
    w, n1, q, kv, mixed,
    z_send, z_recv, x_send, x_recv, y_send, y_recv, a_send, a_recv, b_send, b_recv, s_send, s_recv,
    kx_send, kx_recv, ky_send, ky_recv, ka_send, ka_recv, kb_send, kb_recv, out_sem, keep_sem,
):
    count = lax.axis_size("expert")
    depth = count // 2
    shard, total = shard_ref.shape
    rows, width = x_ref.shape
    heads = q.shape[1] // HEAD_SIZE
    kv_width = kv.shape[1]
    groups = kv_width // (2 * HEAD_SIZE)
    group = heads // groups
    wide = heads * HEAD_SIZE
    qkv_width = wide + kv_width
    split = qkv_width + 128
    me, mine = lax.axis_index("expert"), lax.axis_index("dp")
    z, core = me // 2, me % 2
    y, x = mine // 2, mine % 2
    xn, yn, diag = y * 2 + 1 - x, (1 - y) * 2 + x, (1 - y) * 2 + 1 - x
    sibling = {"expert": z * 2 + 1 - core}

    def at(zz):
        return {"expert": zz * 2 + core}

    greet(depth, z, at, (sibling, {"dp": xn}, {"dp": yn}))

    def remote(src, dst, send, recv, target):
        return pltpu.make_async_remote_copy(
            src, dst, send, recv, device_id=target, device_id_type=MESH
        )

    bounds = ((0, split), (split, total))
    cuts = (bounds[0][1] // 256 * 128, split + (total - split) // 256 * 128)

    def place(dp, zz, cc):
        return pl.ds(pl.multiple_of((dp * count + 2 * zz + cc) * shard, 16), shard)

    def w_copy(dp, zz, low, high, send, recv, target, cc=core):
        ref = w.at[place(dp, zz, cc), pl.ds(low, high - low)]
        return remote(ref, ref, send, recv, target)

    def z_copy(p, zz, lane, target):
        return w_copy(mine, zz, *bounds[p], z_send.at[p, zz, lane], z_recv.at[p, zz], target)

    def x_copy(p, zz, dp):
        return w_copy(dp, zz, *bounds[p], x_send.at[p, zz], x_recv.at[p, zz], {"dp": xn})

    def y_copy(p, zz, dp):
        return w_copy(dp, zz, *bounds[p], y_send.at[p, zz], y_recv.at[p, zz], {"dp": yn})

    def a_copy(p, zz, dp):
        return w_copy(dp, zz, bounds[p][0], cuts[p], a_send.at[p, zz], a_recv.at[p, zz], {"dp": yn})

    def b_copy(p, zz, dp):
        return w_copy(dp, zz, cuts[p], bounds[p][1], b_send.at[p, zz], b_recv.at[p, zz], {"dp": xn})

    def s_copy(p, dp, zz, cc=core):
        return w_copy(dp, zz, *bounds[p], s_send.at[p, dp, zz], s_recv.at[p, dp, zz], sibling, cc)

    def spread(p, zz):
        x_copy(p, zz, mine).start()
        y_copy(p, zz, mine).start()
        s_copy(p, mine, zz).start()

    def on_sides(d, action):
        @pl.when(z - d >= 0)
        def _():
            action(z - d, True)

        if d > 0:

            @pl.when(z + d < depth)
            def _():
                action(z + d, False)

    def z_step(p, d):
        if d == 0:

            @pl.when(z < depth - 1)
            def _():
                z_copy(p, z, 0, at(z + 1)).start()

            @pl.when(z > 0)
            def _():
                z_copy(p, z, 1, at(z - 1)).start()

            spread(p, z)
            return

        def action(zz, from_left):
            z_copy(p, zz, 0, at(z)).wait_recv()
            if from_left:

                @pl.when(z < depth - 1)
                def _():
                    z_copy(p, zz, 0, at(z + 1)).start()
            else:

                @pl.when(z > 0)
                def _():
                    z_copy(p, zz, 1, at(z - 1)).start()

            spread(p, zz)

        on_sides(d, action)

    def xy_step(p, d):
        def action(zz, _):
            x_copy(p, zz, xn).wait_recv()
            a_copy(p, zz, xn).start()
            s_copy(p, xn, zz).start()
            y_copy(p, zz, yn).wait_recv()
            b_copy(p, zz, yn).start()
            s_copy(p, yn, zz).start()

        on_sides(d, action)

    def diag_step(p, d):
        def action(zz, _):
            a_copy(p, zz, diag).wait_recv()
            b_copy(p, zz, diag).wait_recv()
            s_copy(p, diag, zz).start()

        on_sides(d, action)

    def all_here(p):
        for dp in range(4):
            for zz in range(depth):
                s_copy(p, dp, zz, 1 - core).wait_recv()

    def all_sent(p):
        for zz in range(depth):

            @pl.when((zz <= z) & (z < depth - 1))
            def _():
                z_copy(p, zz, 0, at(z)).wait_send()

            @pl.when((zz >= z) & (z > 0))
            def _():
                z_copy(p, zz, 1, at(z)).wait_send()

            x_copy(p, zz, mine).wait_send()
            y_copy(p, zz, mine).wait_send()
            a_copy(p, zz, xn).wait_send()
            b_copy(p, zz, yn).wait_send()
            for dp in range(4):
                s_copy(p, dp, zz).wait_send()

    w[place(mine, z, core), :] = shard_ref[...]
    z_step(0, 0)
    z_step(0, 1)
    xy_step(0, 0)
    for d in range(2, depth):
        z_step(0, d)
        xy_step(0, d - 1)
    xy_step(0, depth - 1)
    for d in range(depth):
        diag_step(0, d)
    all_here(0)
    z_step(1, 0)

    def keep(p):
        low, high = bounds[p]
        return pltpu.make_async_copy(
            w.at[:, pl.ds(low, high - low)], w_out.at[:, pl.ds(low, high - low)], keep_sem.at[p]
        )

    keep(0).start()
    small = jnp.transpose(w[:, qkv_width:split].astype(F32))
    experts = hits_ref.shape[0]
    gain_one, gain_two = small[experts : experts + 1], small[experts + 1 : experts + 2]

    block = 32

    def first_norm(i, _):
        rr = pl.ds(pl.multiple_of(i * block, block), block)
        value = x_ref[rr, :].astype(F32)
        scale = lax.rsqrt(jnp.mean(value * value, axis=1, keepdims=True) + EPS)
        n1[rr, :] = (value * scale * gain_one).astype(BF)
        return 0

    lax.fori_loop(0, rows // block, first_norm, 0)

    def turn(value):
        return value * cos_ref[...] + pltpu.roll(value, HEAD_SIZE // 2, 1) * sin_ref[...]

    own = pl.ds(pl.multiple_of(mine * rows, 16), rows)
    projected = mm(n1[...], w[:, wide:qkv_width])
    for g in range(groups):
        low = 2 * g * HEAD_SIZE
        kv[own, low : low + HEAD_SIZE] = turn(projected[:, low : low + HEAD_SIZE]).astype(BF)
        kv[own, low + HEAD_SIZE : low + 2 * HEAD_SIZE] = projected[
            :, low + HEAD_SIZE : low + 2 * HEAD_SIZE
        ].astype(BF)

    def kv_copy(g, dp, low, high, send, recv, target):
        ref = kv.at[
            pl.ds(pl.multiple_of(dp * rows, 16), rows),
            pl.ds((2 * g + low) * HEAD_SIZE, (high - low) * HEAD_SIZE),
        ]
        return remote(ref, ref, send.at[g], recv.at[g], target)

    def kx(g, dp):
        return kv_copy(g, dp, 0, 2, kx_send, kx_recv, {"dp": xn})

    def ky(g, dp):
        return kv_copy(g, dp, 0, 2, ky_send, ky_recv, {"dp": yn})

    def ka(g, dp):
        return kv_copy(g, dp, 0, 1, ka_send, ka_recv, {"dp": yn})

    def kb(g, dp):
        return kv_copy(g, dp, 1, 2, kb_send, kb_recv, {"dp": xn})

    def kv_on(g):
        kx(g, xn).wait_recv()
        ka(g, xn).start()
        ky(g, yn).wait_recv()
        kb(g, yn).start()

    def kv_here(g):
        ka(g, diag).wait_recv()
        kb(g, diag).wait_recv()

    for g in range(groups):
        kx(g, mine).start()
        ky(g, mine).start()

    def project(h, _):
        cols = pl.ds(pl.multiple_of(h * 2 * HEAD_SIZE, 2 * HEAD_SIZE), 2 * HEAD_SIZE)
        value = mm(n1[...], w[:, cols])
        q[:, cols] = jnp.concatenate(
            [turn(value[:, :HEAD_SIZE]), turn(value[:, HEAD_SIZE:])], axis=1
        ).astype(BF)
        return 0

    lax.fori_loop(0, heads // 2, project, 0)
    kv_on(0)
    z_step(1, 1)
    kv_here(0)
    later = [
        lambda: (kv_on(1), xy_step(1, 0), z_step(1, 2)),
        lambda: (xy_step(1, 1), z_step(1, 3)),
        lambda: xy_step(1, 2),
        lambda: xy_step(1, 3),
        lambda: (diag_step(1, 0), diag_step(1, 1)),
        lambda: (diag_step(1, 2), diag_step(1, 3)),
        lambda: kv_here(1),
    ]
    lse_ref[...] = jnp.zeros_like(lse_ref)
    lanes = lax.broadcasted_iota(jnp.int32, lse_ref.shape, 1)

    def attend(h, _):
        for i, job in enumerate(later):
            pl.when(h == i)(lambda job=job: (job(), None)[1])
        g = h // group
        cols = pl.ds(pl.multiple_of(h * HEAD_SIZE, HEAD_SIZE), HEAD_SIZE)
        k_cols = pl.ds(pl.multiple_of(g * 2 * HEAD_SIZE, HEAD_SIZE), HEAD_SIZE)
        v_cols = pl.ds(pl.multiple_of(g * 2 * HEAD_SIZE + HEAD_SIZE, HEAD_SIZE), HEAD_SIZE)
        scores = mm_nt(q[:, cols], kv[:, k_cols]) * (HEAD_SIZE**-0.5 * LOG2E) + bias_ref[...]
        top = jnp.max(scores, axis=1, keepdims=True)
        power = jnp.exp2(scores - top)
        sums = jnp.sum(power, axis=1, keepdims=True)
        mixed[:, cols] = (mm(power.astype(BF), kv[:, v_cols]) / sums).astype(BF)
        lse_ref[...] = jnp.where(lanes == h, top + jnp.log2(sums), lse_ref[...])
        return 0

    lax.fori_loop(0, heads, attend, 0)
    keeps = [
        pltpu.make_async_copy(src, dst, out_sem.at[i])
        for i, (src, dst) in enumerate(
            ((n1, n1_ref), (q, q_ref), (kv, kv_ref), (mixed, mixed_ref))
        )
    ]
    for copy in keeps:
        copy.start()
    all_here(1)
    keep(1).start()
    tile = 512

    def project_out(i, _):
        cols = pl.ds(pl.multiple_of(i * tile, tile), tile)
        w_cols = pl.ds(pl.multiple_of(split + i * tile, 128), tile)
        middle_ref[:, cols] = x_ref[:, cols].astype(F32) + mm(mixed[...], w[:, w_cols])
        return 0

    lax.fori_loop(0, width // tile, project_out, 0)

    def second_norm(i, _):
        rr = pl.ds(pl.multiple_of(i * block, block), block)
        value = middle_ref[rr, :]
        scale = lax.rsqrt(jnp.mean(value * value, axis=1, keepdims=True) + EPS)
        n2_ref[rr, :] = (value * scale * gain_two).astype(BF)
        return 0

    lax.fori_loop(0, rows // block, second_norm, 0)
    logits = mm_nt(small.astype(BF), n2_ref[...])[:experts]
    hits = hits_ref[...] > 0.5
    chosen = jnp.where(hits, logits, NEGATIVE)
    power = jnp.where(hits, jnp.exp(chosen - jnp.max(chosen, axis=0, keepdims=True)), 0.0)
    gate_ref[...] = jnp.zeros_like(gate_ref)
    gate_ref[:, :rows] = power / jnp.sum(power, axis=0, keepdims=True)

    for g in range(groups):
        kx(g, mine).wait_send()
        ky(g, mine).wait_send()
        ka(g, xn).wait_send()
        kb(g, yn).wait_send()
    for p in range(2):
        all_sent(p)
        keep(p).wait()
    for copy in keeps:
        copy.wait()


def attention_pass(x, shard, cos, sin, bias, hits, kv_width):
    count = lax.axis_size("expert")
    depth = count // 2
    rows, width = x.shape
    lanes = rows + -rows % 128
    devices = 4 * count
    wide = width
    dma = pltpu.SemaphoreType.DMA
    vmem = pl.BlockSpec(memory_space=pltpu.VMEM)
    anywhere = pl.BlockSpec(memory_space=pl.ANY)
    shape = jax.ShapeDtypeStruct
    pair = dma((2, depth))
    groups = kv_width // (2 * HEAD_SIZE)
    tree = 4 * rows
    total = shard.shape[1]
    return pl.pallas_call(
        attention_kernel,
        name="attention_pass",
        out_shape=(
            shape((rows, width), BF),
            shape((rows, wide), BF),
            shape((tree, kv_width), BF),
            shape((rows, wide), BF),
            shape((rows, 128), F32),
            shape((rows, width), F32),
            shape((rows, width), BF),
            shape((hits.shape[0], lanes), F32),
            shape((devices * shard.shape[0], total), BF),
        ),
        in_specs=[vmem] * 6,
        out_specs=(anywhere,) * 4 + (vmem,) * 4 + (anywhere,),
        scratch_shapes=[
            pltpu.VMEM((devices * shard.shape[0], total), BF),
            pltpu.VMEM((rows, width), BF),
            pltpu.VMEM((rows, wide), BF),
            pltpu.VMEM((tree, kv_width), BF),
            pltpu.VMEM((rows, wide), BF),
            dma((2, depth, 2)), pair, pair, pair, pair, pair, pair, pair, pair, pair,
            dma((2, 4, depth)), dma((2, 4, depth)),
            *[dma((groups,)) for _ in range(8)],
            dma((4,)), dma((2,)),
        ],
        compiler_params=pltpu.CompilerParams(
            collective_id=1, has_side_effects=True, vmem_limit_bytes=56 * 2**20
        ),
        cost_estimate=pl.CostEstimate(
            flops=10**10, bytes_accessed=300 * 2**20, transcendentals=0
        ),
    )(x, shard, cos, sin, bias, hits)


def rotation_rows(positions):
    half = HEAD_SIZE // 2
    frequency = jnp.power(THETA, -(jnp.arange(half, dtype=jnp.float32) * 2.0 / HEAD_SIZE))
    angles = positions.astype(jnp.float32)[:, None] * frequency[None, :]
    cosine, sine = jnp.cos(angles), jnp.sin(angles)
    return jnp.concatenate([cosine, cosine], axis=1), jnp.concatenate([-sine, sine], axis=1)


def turn_back(values, cos, sin):
    half = HEAD_SIZE // 2
    swapped = jnp.concatenate([values[..., half:], values[..., :half]], axis=-1)
    return values * cos - swapped * sin


def tree_visibility(parent_row, query_ids, tree_length):
    blocks = parent_row.shape[0]
    trunk = blocks - BRANCHES - LEAVES
    leaf_from = trunk + BRANCHES
    query_block = query_ids // SEG
    block_ids = jnp.arange(blocks, dtype=jnp.int32)
    depth_of = jnp.minimum(query_block, trunk) + (query_block >= leaf_from).astype(jnp.int32)
    positions = depth_of * SEG + query_ids % SEG
    parent = jnp.sum(jnp.where(query_block[:, None] == block_ids, parent_row, 0), axis=1)
    above = jnp.where(query_block >= leaf_from, parent, query_block)
    key_ids = jnp.arange(tree_length, dtype=jnp.int32)[None, :]
    key_block = key_ids // SEG
    related = (
        (key_block < trunk) | (key_block == query_block[:, None]) | (key_block == above[:, None])
    )
    return related & (key_ids <= query_ids[:, None]), positions


def rows_to_gather(parts):
    return jnp.concatenate(parts, axis=1)


def dense_on_device(
    tokens,
    cotangent,
    parents,
    routes,
    first_gain,
    second_gain,
    query_weight,
    key_matrix,
    value_matrix,
    out_weight,
    router_weight,
    gate_weight,
    up_weight,
    down_weight,
):
    experts = router_weight.shape[1]
    group = QUERY_HEADS // KEY_VALUE_HEADS
    heads_width = QUERY_HEADS * HEAD_SIZE
    kv_width = 2 * KEY_VALUE_HEADS * HEAD_SIZE
    qkv_width = heads_width + kv_width
    kv_shards = []
    for head in range(KEY_VALUE_HEADS):
        cols = slice(head * HEAD_SIZE, (head + 1) * HEAD_SIZE)
        kv_shards += [key_matrix[:, cols], value_matrix[:, cols]]
    small_shard = jnp.concatenate(
        [router_weight, first_gain[:, None], second_gain[:, None]], axis=1
    )
    small_shard = jnp.pad(small_shard, ((0, 0), (0, -small_shard.shape[1] % 128)))
    small_width = small_shard.shape[1]
    shard = jnp.concatenate([query_weight, *kv_shards, small_shard, out_weight], axis=1)
    dy_low = cotangent[0]
    dy_all = lax.all_gather(dy_low, "expert", axis=0)
    inputs_low = tokens[0]
    total_rows = inputs_low.shape[0]
    tree_length = parents.shape[1] * SEG
    query_ids = lax.axis_index("dp") * total_rows + jnp.arange(total_rows, dtype=jnp.int32)
    visible, query_positions = tree_visibility(parents[0], query_ids, tree_length)
    bias = jnp.where(visible, 0.0, NEGATIVE)
    cos, sin = rotation_rows(query_positions)
    expert_ids = jnp.arange(experts, dtype=jnp.int32)
    hit_rows = jnp.any(routes[0][None, :, :] == expert_ids[:, None, None], axis=2)
    n1, query_low, kv_all, mixed, logs, middle, n2, gate_rows, full = attention_pass(
        inputs_low, shard, cos, sin, bias, hit_rows.astype(F32), kv_width
    )
    row_sum, gate_grad_rows, sums, gate_w_grad, up_w_grad, down_grad = expert_pass(
        n2, gate_rows, dy_all, gate_weight[0], up_weight[0], down_weight[0]
    )
    gates = gate_rows[:, :total_rows]
    gate_grad = gate_grad_rows[:, :total_rows]
    logit_grad = gates * (gate_grad - jnp.sum(gates * gate_grad, axis=0, keepdims=True))
    qkv_full = full[:, :qkv_width]
    small_full = full[:, qkv_width : qkv_width + small_width]
    out_full = full[:, qkv_width + small_width :]
    router_full = small_full[:, :experts]
    scale_one = small_full[:, experts].astype(F32)
    scale_two = small_full[:, experts + 1].astype(F32)
    inputs = inputs_low.astype(F32)
    summed = tuple(
        lax.psum(grad, "dp").astype(jnp.float32)[None]
        for grad in (gate_w_grad, up_w_grad, down_grad)
    )
    router_wide = router_full.astype(jnp.float32)
    n2_grad = (
        jnp.einsum("er,de->rd", logit_grad, router_wide, precision=HIGH_PRECISION) + row_sum
    )
    router_grad = jnp.einsum(
        "rd,er->de", n2.astype(jnp.float32), logit_grad, precision=HIGH_PRECISION
    )
    upstream = dy_low.astype(jnp.float32)
    _, second_pull = jax.vjp(normalize, middle, scale_two)
    middle_norm_grad, second_gain_grad = second_pull(n2_grad)
    middle_grad = upstream + middle_norm_grad
    attended_low = middle_grad.astype(jnp.bfloat16)
    out_grad = jnp.einsum("rd,re->de", mixed, attended_low, preferred_element_type=jnp.float32)
    mixed_grad = jnp.einsum("re,de->rd", attended_low, out_full, preferred_element_type=jnp.float32)
    mixed_grad = mixed_grad.astype(jnp.bfloat16).reshape(total_rows, QUERY_HEADS, HEAD_SIZE)
    query_rotated = query_low.reshape(total_rows, QUERY_HEADS, HEAD_SIZE)
    query_parts = []
    kv_parts = []
    for head in range(KEY_VALUE_HEADS):
        query_part = query_rotated[:, head * group : (head + 1) * group, :]
        key_part = kv_all[:, 2 * head * HEAD_SIZE : (2 * head + 1) * HEAD_SIZE]
        value_part = kv_all[:, (2 * head + 1) * HEAD_SIZE : (2 * head + 2) * HEAD_SIZE]
        grad_part = mixed_grad[:, head * group : (head + 1) * group, :]
        scores = jnp.einsum("rgd,kd->grk", query_part, key_part, preferred_element_type=F32)
        scores = scores * (HEAD_SIZE**-0.5 * LOG2E) + bias
        log_rows = logs[:, head * group : (head + 1) * group].T[:, :, None]
        softmax_out = jnp.exp2(scores - log_rows)
        value_grad = jnp.einsum(
            "grk,rgd->kd", softmax_out.astype(BF), grad_part, preferred_element_type=F32
        )
        attn_grad = jnp.einsum("rgd,kd->grk", grad_part, value_part, preferred_element_type=F32)
        score_grad = softmax_out * (
            attn_grad - jnp.sum(softmax_out * attn_grad, axis=-1, keepdims=True)
        )
        score_low = score_grad.astype(BF)
        query_parts.append(
            jnp.einsum("grk,kd->rgd", score_low, key_part, preferred_element_type=F32)
            * HEAD_SIZE ** (-0.5)
        )
        key_grad = jnp.einsum("grk,rgd->kd", score_low, query_part, preferred_element_type=F32)
        kv_parts += [key_grad * HEAD_SIZE ** (-0.5), value_grad]
    kv_sum = lax.psum_scatter(
        jnp.concatenate(kv_parts, axis=1).astype(BF), "dp", scatter_dimension=0, tiled=True
    ).astype(F32)
    query_grad = turn_back(
        jnp.concatenate(query_parts, axis=1), cos[:, None, :], sin[:, None, :]
    ).reshape(total_rows, heads_width)
    kv_grads = []
    for head in range(KEY_VALUE_HEADS):
        key_sum = kv_sum[:, 2 * head * HEAD_SIZE : (2 * head + 1) * HEAD_SIZE]
        kv_grads += [
            turn_back(key_sum, cos, sin),
            kv_sum[:, (2 * head + 1) * HEAD_SIZE : (2 * head + 2) * HEAD_SIZE],
        ]
    qkv_grad = jnp.concatenate([query_grad, *kv_grads], axis=1).astype(BF)
    qkv_w_grad = jnp.einsum("rd,re->de", n1, qkv_grad, preferred_element_type=F32)
    n1_grad = jnp.einsum("re,de->rd", qkv_grad, qkv_full, preferred_element_type=F32)
    _, first_pull = jax.vjp(normalize, inputs, scale_one)
    input_norm_grad, first_gain_grad = first_pull(n1_grad)
    input_grad = (middle_grad + input_norm_grad)[None]
    small = jnp.concatenate(
        [router_grad, first_gain_grad[:, None], second_gain_grad[:, None]], axis=1
    )
    small = jnp.pad(small, ((0, 0), (0, small_width - small.shape[1])))
    all_grads = jnp.concatenate([qkv_w_grad, small, out_grad], axis=1).astype(BF)
    shards = lax.axis_size("dp") * lax.axis_size("expert")
    share, combined = scatter_pass(all_grads.reshape(shards, -1, all_grads.shape[1]), sums)
    output = (middle + combined).astype(BF)[None]
    heads_of = [
        share[:, heads_width + i * HEAD_SIZE : heads_width + (i + 1) * HEAD_SIZE]
        for i in range(2 * KEY_VALUE_HEADS)
    ]
    query_share = share[:, :heads_width]
    key_share = jnp.concatenate(heads_of[0::2], axis=1)
    value_share = jnp.concatenate(heads_of[1::2], axis=1)
    small_share = share[:, qkv_width : qkv_width + small_width]
    out_share = share[:, qkv_width + small_width :]
    return (
        output,
        input_grad,
        small_share[:, experts],
        small_share[:, experts + 1],
        query_share,
        key_share,
        value_share,
        out_share,
        small_share[:, :experts],
        *summed,
    )


def solution(mesh):
    dense = mesh.shape["expert"] <= 2 * TOPK and mesh.shape["dp"] == 4
    return jax.shard_map(
        dense_on_device if dense else on_device_routed,
        mesh=mesh,
        in_specs=(
            P("expert", "dp", None),
            P("expert", "dp", None),
            P("expert", None),
            P("expert", "dp", None),
            P(("dp", "expert")),
            P(("dp", "expert")),
            P(("dp", "expert"), None),
            P(("dp", "expert"), None),
            P(("dp", "expert"), None),
            P(("dp", "expert"), None),
            P(("dp", "expert"), None),
            P("expert", None, None),
            P("expert", None, None),
            P("expert", None, None),
        ),
        out_specs=(
            P("expert", "dp", None),
            P("expert", "dp", None),
            P(("dp", "expert")),
            P(("dp", "expert")),
            P(("dp", "expert"), None),
            P(("dp", "expert"), None),
            P(("dp", "expert"), None),
            P(("dp", "expert"), None),
            P(("dp", "expert"), None),
            P("expert", None, None),
            P("expert", None, None),
            P("expert", None, None),
        ),
        check_vma=False,
    )
```

```python
import jax
import jax.numpy as jnp
from jax import lax
from jax.experimental import pallas as pl
from jax.experimental.pallas import tpu as pltpu
from jax.sharding import PartitionSpec as P

MESH = pl.DeviceIdType.MESH
BF = jnp.bfloat16
F32 = jnp.float32
MODEL_WIDTH = 1536
QUERY_HEADS = 12
KEY_VALUE_HEADS = 2
HEAD_SIZE = 128
FF = 768
TOPK = 4
SEG = 32
BRANCHES = 4
LEAVES = 8


EPS = 1e-06
THETA = 10000.0
HIGH_PRECISION = lax.Precision.HIGHEST
NEGATIVE = -1e30
LOG2E = 1.4426950408889634


def ancestry(parent_row):
    block_count = parent_row.shape[0]
    block_ids = jnp.arange(block_count, dtype=jnp.int32)

    def advance(counter, carried):
        current, ancestors = carried
        ancestors = jnp.maximum(
            ancestors, (current[:, None] == block_ids[None, :]).astype(jnp.float32)
        )
        return (jnp.take(parent_row, current), ancestors)

    start_pair = (block_ids, jnp.zeros((block_count, block_count), jnp.float32))
    current, ancestors = lax.fori_loop(0, block_count, advance, start_pair)
    depths = (jnp.sum(ancestors, axis=1) - 1.0).astype(jnp.int32)
    return (ancestors, depths)


def apply_rotation(values, positions):
    half_width = values.shape[-1] // 2
    frequency = jnp.power(
        THETA, -(jnp.arange(half_width, dtype=jnp.float32) * 2.0 / values.shape[-1])
    )
    angles = positions.astype(jnp.float32)[:, None] * frequency[None, :]
    cosine = jnp.cos(angles)[:, None, :]
    sine_part = jnp.sin(angles)[:, None, :]
    first_half = values[..., :half_width]
    second_half = values[..., half_width:]
    return jnp.concatenate(
        [
            first_half * cosine - second_half * sine_part,
            second_half * cosine + first_half * sine_part,
        ],
        axis=-1,
    )


def normalize(values, scales):
    return values * lax.rsqrt(jnp.mean(values * values, axis=-1, keepdims=True) + EPS) * scales


def place(route_ids, experts, capacity):
    one_hot = (route_ids[..., None] == jnp.arange(experts, dtype=jnp.int32)).astype(jnp.int32)
    pairs = one_hot.shape[-2]
    before = jnp.tri(pairs, pairs, -1, dtype=jnp.bfloat16)
    earlier = jnp.dot(before, one_hot.astype(jnp.bfloat16), preferred_element_type=jnp.float32)
    slot_rank = jnp.sum(earlier.astype(jnp.int32) * one_hot, axis=-1)
    return route_ids * capacity + slot_rank


def visibility(ancestors, depths, query_ids, key_ids):
    block_ids = jnp.arange(ancestors.shape[0], dtype=jnp.int32)
    query_hit = (query_ids // SEG)[:, None] == block_ids[None, :]
    key_hit = (key_ids // SEG)[:, None] == block_ids[None, :]
    query_positions = (
        jnp.sum(jnp.where(query_hit, depths[None, :], 0), axis=1) * SEG + query_ids % SEG
    )
    key_pos = jnp.sum(jnp.where(key_hit, depths[None, :], 0), axis=1) * SEG + key_ids % SEG
    reach = jnp.dot(query_hit.astype(jnp.float32), ancestors, precision=HIGH_PRECISION)
    reach_keys = jnp.repeat(reach, SEG, axis=1)
    visible = (reach_keys > 0.5) & (key_pos[None, :] <= query_positions[:, None])
    return (visible, query_positions)


def head_scores(query_rotated, keys_all, visible, key_value_head, query_group_width):
    query_part = query_rotated[
        :, key_value_head * query_group_width : (key_value_head + 1) * query_group_width, :
    ]
    key_part = keys_all[:, key_value_head * HEAD_SIZE : (key_value_head + 1) * HEAD_SIZE]
    scores = jnp.einsum(
        "rgd,kd->grk", query_part, key_part, preferred_element_type=jnp.float32
    ) * HEAD_SIZE ** (-0.5)
    return jnp.where(visible[None], scores, NEGATIVE)


def gelu_product(gate_pre, up_pre):
    return jax.nn.gelu(gate_pre, approximate=True) * up_pre


def expert_hidden(received, local_gate, local_up):
    local_count = local_gate.shape[0]
    slot_count = received.shape[1]
    grouped_queries = received.reshape(-1, local_count, slot_count, MODEL_WIDTH)
    gate_pre = jnp.einsum(
        "sjcd,jdf->sjcf", grouped_queries, local_gate, preferred_element_type=jnp.float32
    )
    up_pre = jnp.einsum(
        "sjcd,jdf->sjcf", grouped_queries, local_up, preferred_element_type=jnp.float32
    )
    hidden = gelu_product(gate_pre, up_pre).astype(jnp.bfloat16)
    flat_shape = (received.shape[0], slot_count, FF)
    return (gate_pre.reshape(flat_shape), up_pre.reshape(flat_shape), hidden.reshape(flat_shape))


def expert_result(hidden, local_down):
    local_count = local_down.shape[0]
    grouped_queries = hidden.reshape(-1, local_count, hidden.shape[1], FF)
    result = jnp.einsum(
        "sjcf,jfd->sjcd", grouped_queries, local_down, preferred_element_type=jnp.float32
    )
    return result.astype(jnp.bfloat16).reshape(hidden.shape[0], hidden.shape[1], MODEL_WIDTH)


def on_device_routed(
    tokens,
    cotangent,
    parents,
    routes,
    first_gain,
    second_gain,
    query_weight,
    key_matrix,
    value_matrix,
    out_weight,
    router_weight,
    gate_weight,
    up_weight,
    down_weight,
):
    gathered = (
        lax.all_gather(query_weight, ("dp", "expert"), axis=0, tiled=True),
        lax.all_gather(key_matrix, ("dp", "expert"), axis=0, tiled=True),
        lax.all_gather(value_matrix, ("dp", "expert"), axis=0, tiled=True),
        lax.all_gather(out_weight, ("dp", "expert"), axis=0, tiled=True),
        lax.all_gather(router_weight, ("dp", "expert"), axis=0, tiled=True),
        lax.all_gather(first_gain, ("dp", "expert"), axis=0, tiled=True),
        lax.all_gather(second_gain, ("dp", "expert"), axis=0, tiled=True),
    )
    query_full, key_complete, value_complete, out_full, router_full, gain_one, gain_two = gathered
    scale_one = gain_one.astype(jnp.float32)
    scale_two = gain_two.astype(jnp.float32)
    inputs = tokens[0].astype(jnp.float32)
    total_rows = inputs.shape[0]
    query_group_width = QUERY_HEADS // KEY_VALUE_HEADS
    ancestors, depths = ancestry(parents[0])
    tree_length = ancestors.shape[0] * SEG
    query_ids = lax.axis_index("dp") * total_rows + jnp.arange(total_rows, dtype=jnp.int32)
    key_ids = jnp.arange(tree_length, dtype=jnp.int32)
    visible, query_positions = visibility(ancestors, depths, query_ids, key_ids)
    first_normed = normalize(inputs, scale_one).astype(jnp.bfloat16)
    query_proj = jnp.dot(first_normed, query_full, preferred_element_type=jnp.float32).reshape(
        total_rows, QUERY_HEADS, HEAD_SIZE
    )
    key_projected = jnp.dot(first_normed, key_complete, preferred_element_type=jnp.float32).reshape(
        total_rows, KEY_VALUE_HEADS, HEAD_SIZE
    )
    value_projected = jnp.dot(first_normed, value_complete, preferred_element_type=jnp.float32)
    query_rotated = apply_rotation(query_proj, query_positions).astype(jnp.bfloat16)
    key_rotated = (
        apply_rotation(key_projected, query_positions)
        .astype(jnp.bfloat16)
        .reshape(total_rows, KEY_VALUE_HEADS * HEAD_SIZE)
    )
    value_low = value_projected.astype(jnp.bfloat16)
    keys_all, values_all = (
        lax.all_gather(key_rotated, "dp", axis=0, tiled=True),
        lax.all_gather(value_low, "dp", axis=0, tiled=True),
    )
    mixed_parts = []
    log_totals = []
    for key_value_head in range(KEY_VALUE_HEADS):
        scores = head_scores(query_rotated, keys_all, visible, key_value_head, query_group_width)
        row_max = jnp.max(scores, axis=-1, keepdims=True)
        exponent = jnp.exp(scores - row_max)
        row_total = jnp.sum(exponent, axis=-1, keepdims=True)
        log_totals.append(row_max + jnp.log(row_total))
        softmax_out = (exponent / row_total).astype(jnp.bfloat16)
        value_part = values_all[:, key_value_head * HEAD_SIZE : (key_value_head + 1) * HEAD_SIZE]
        mixed_parts.append(
            jnp.einsum("grk,kd->rgd", softmax_out, value_part, preferred_element_type=jnp.float32)
        )
    mixed_out = (
        jnp.concatenate(mixed_parts, axis=1)
        .reshape(total_rows, QUERY_HEADS * HEAD_SIZE)
        .astype(jnp.bfloat16)
    )
    middle = inputs + jnp.dot(mixed_out, out_full, preferred_element_type=jnp.float32)
    normed_two = normalize(middle, scale_two).astype(jnp.bfloat16)
    logits = jnp.dot(normed_two, router_full, preferred_element_type=jnp.float32)
    route_ids = routes[0]
    experts = gate_weight.shape[0] * lax.axis_size("expert")
    capacity = 3 * total_rows * TOPK // (2 * experts)
    expert_ids = jnp.arange(experts, dtype=jnp.int32)
    route_hits = route_ids[:, :, None] == expert_ids[None, None, :]
    chosen = jnp.sum(jnp.where(route_hits, logits[:, None, :], 0.0), axis=2)
    chosen_max = jnp.max(chosen, axis=1, keepdims=True)
    chosen_exp = jnp.exp(chosen - chosen_max)
    gate_weights = chosen_exp / jnp.sum(chosen_exp, axis=1, keepdims=True)
    pair_count = total_rows * TOPK
    slot_index = place(route_ids.reshape(pair_count), experts, capacity)
    slot_source = (
        jnp.full((experts * capacity,), pair_count, jnp.int32)
        .at[slot_index]
        .set(jnp.arange(pair_count, dtype=jnp.int32))
    )
    slot_used = slot_source < pair_count
    slot_pair = jnp.where(slot_used, slot_source, 0)
    slot_token = slot_pair // TOPK
    zero_low = jnp.zeros((), jnp.bfloat16)
    outgoing = jnp.where(slot_used[:, None], normed_two[slot_token], zero_low).reshape(
        experts, capacity, MODEL_WIDTH
    )
    gate_pre, up_pre, hidden = expert_hidden(
        lax.all_to_all(outgoing, "expert", split_axis=0, concat_axis=0, tiled=True),
        gate_weight,
        up_weight,
    )
    dispatched = expert_result(hidden, down_weight)
    returned = lax.all_to_all(dispatched, "expert", split_axis=0, concat_axis=0, tiled=True)
    expert_rows = (
        returned.reshape(experts * capacity, MODEL_WIDTH)[slot_index]
        .astype(jnp.float32)
        .reshape(total_rows, TOPK, MODEL_WIDTH)
    )
    final = middle + jnp.sum(gate_weights[:, :, None] * expert_rows, axis=1)
    output = final.astype(jnp.bfloat16)[None]
    upstream = cotangent[0].astype(jnp.float32)
    gate_grad = jnp.sum(upstream[:, None, :] * expert_rows, axis=2)
    chosen_grad = gate_weights * (
        gate_grad - jnp.sum(gate_weights * gate_grad, axis=1, keepdims=True)
    )
    logit_grad = jnp.sum(jnp.where(route_hits, chosen_grad[:, :, None], 0.0), axis=1)
    pair_grad = (
        (gate_weights[:, :, None] * upstream[:, None, :])
        .astype(jnp.bfloat16)
        .reshape(pair_count, MODEL_WIDTH)
    )
    grad_outgoing = jnp.where(slot_used[:, None], pair_grad[slot_pair], zero_low).reshape(
        experts, capacity, MODEL_WIDTH
    )
    received, grad_in = (
        lax.all_to_all(outgoing, "expert", split_axis=0, concat_axis=0, tiled=True),
        lax.all_to_all(grad_outgoing, "expert", split_axis=0, concat_axis=0, tiled=True),
    )
    gate_pre, up_pre, hidden = expert_hidden(received, gate_weight, up_weight)
    local_count = gate_weight.shape[0]
    slot_count = received.shape[1]
    grouped_rows = received.reshape(-1, local_count, slot_count, MODEL_WIDTH)
    grouped_hidden = hidden.reshape(-1, local_count, slot_count, FF)
    grouped_grad = grad_in.reshape(-1, local_count, slot_count, MODEL_WIDTH)
    down_grad = jnp.einsum(
        "sjcf,sjcd->jfd", grouped_hidden, grouped_grad, preferred_element_type=jnp.float32
    )
    hidden_grad = jnp.einsum(
        "sjcd,jfd->sjcf", grouped_grad, down_weight, preferred_element_type=jnp.float32
    )
    _, product_pull = jax.vjp(gelu_product, gate_pre, up_pre)
    gate_pre_grad, up_pre_grad = product_pull(hidden_grad.reshape(gate_pre.shape))
    gate_low = gate_pre_grad.astype(jnp.bfloat16).reshape(-1, local_count, slot_count, FF)
    up_low = up_pre_grad.astype(jnp.bfloat16).reshape(-1, local_count, slot_count, FF)
    gate_w_grad = jnp.einsum(
        "sjcd,sjcf->jdf", grouped_rows, gate_low, preferred_element_type=jnp.float32
    )
    up_w_grad = jnp.einsum(
        "sjcd,sjcf->jdf", grouped_rows, up_low, preferred_element_type=jnp.float32
    )
    row_grad = jnp.einsum(
        "sjcf,jdf->sjcd", gate_low, gate_weight, preferred_element_type=jnp.float32
    ) + jnp.einsum("sjcf,jdf->sjcd", up_low, up_weight, preferred_element_type=jnp.float32)
    row_grad = row_grad.astype(jnp.bfloat16).reshape(received.shape)
    returned_grad = lax.all_to_all(row_grad, "expert", split_axis=0, concat_axis=0, tiled=True)
    pair_rows = (
        returned_grad.reshape(experts * capacity, MODEL_WIDTH)[slot_index]
        .astype(jnp.float32)
        .reshape(total_rows, TOPK, MODEL_WIDTH)
    )
    summed_experts = (
        lax.psum(gate_w_grad.astype(jnp.bfloat16), "dp").astype(jnp.float32),
        lax.psum(up_w_grad.astype(jnp.bfloat16), "dp").astype(jnp.float32),
        lax.psum(down_grad.astype(jnp.bfloat16), "dp").astype(jnp.float32),
    )
    router_wide = router_full.astype(jnp.float32)
    normed_two_grad = jnp.dot(logit_grad, router_wide.T, precision=HIGH_PRECISION) + jnp.sum(
        pair_rows, axis=1
    )
    router_grad = jnp.dot(normed_two.astype(jnp.float32).T, logit_grad, precision=HIGH_PRECISION)
    _, second_pull = jax.vjp(normalize, middle, scale_two)
    middle_norm_grad, second_gain_grad = second_pull(normed_two_grad)
    middle_grad = upstream + middle_norm_grad
    attended_low = middle_grad.astype(jnp.bfloat16)
    out_grad = jnp.einsum("rd,re->de", mixed_out, attended_low, preferred_element_type=jnp.float32)
    mixed_grad = jnp.einsum("re,de->rd", attended_low, out_full, preferred_element_type=jnp.float32)
    mixed_grad = mixed_grad.astype(jnp.bfloat16).reshape(total_rows, QUERY_HEADS, HEAD_SIZE)
    query_parts = []
    key_parts = []
    value_parts = []
    for key_value_head in range(KEY_VALUE_HEADS):
        scores = head_scores(query_rotated, keys_all, visible, key_value_head, query_group_width)
        softmax_out = jnp.exp(scores - log_totals[key_value_head])
        query_part = query_rotated[
            :, key_value_head * query_group_width : (key_value_head + 1) * query_group_width, :
        ]
        key_part = keys_all[:, key_value_head * HEAD_SIZE : (key_value_head + 1) * HEAD_SIZE]
        value_part = values_all[:, key_value_head * HEAD_SIZE : (key_value_head + 1) * HEAD_SIZE]
        grad_part = mixed_grad[
            :, key_value_head * query_group_width : (key_value_head + 1) * query_group_width, :
        ]
        value_parts.append(
            jnp.einsum(
                "grk,rgd->kd",
                softmax_out.astype(jnp.bfloat16),
                grad_part,
                preferred_element_type=jnp.float32,
            )
        )
        attn_grad = jnp.einsum(
            "rgd,kd->grk", grad_part, value_part, preferred_element_type=jnp.float32
        )
        score_grad = softmax_out * (
            attn_grad - jnp.sum(softmax_out * attn_grad, axis=-1, keepdims=True)
        )
        score_low = score_grad.astype(jnp.bfloat16)
        query_parts.append(
            jnp.einsum("grk,kd->rgd", score_low, key_part, preferred_element_type=jnp.float32)
            * HEAD_SIZE ** (-0.5)
        )
        key_parts.append(
            jnp.einsum("grk,rgd->kd", score_low, query_part, preferred_element_type=jnp.float32)
            * HEAD_SIZE ** (-0.5)
        )
    key_total_sum, value_sum = (
        lax.psum_scatter(
            jnp.concatenate(key_parts, axis=1).astype(jnp.bfloat16),
            "dp",
            scatter_dimension=0,
            tiled=True,
        ).astype(jnp.float32),
        lax.psum_scatter(
            jnp.concatenate(value_parts, axis=1).astype(jnp.bfloat16),
            "dp",
            scatter_dimension=0,
            tiled=True,
        ).astype(jnp.float32),
    )
    _, query_pull = jax.vjp(lambda values: apply_rotation(values, query_positions), query_proj)
    _, key_pullback = jax.vjp(lambda values: apply_rotation(values, query_positions), key_projected)
    query_grad = (
        query_pull(jnp.concatenate(query_parts, axis=1))[0]
        .astype(jnp.bfloat16)
        .reshape(total_rows, QUERY_HEADS * HEAD_SIZE)
    )
    key_grad = (
        key_pullback(key_total_sum.reshape(total_rows, KEY_VALUE_HEADS, HEAD_SIZE))[0]
        .astype(jnp.bfloat16)
        .reshape(total_rows, KEY_VALUE_HEADS * HEAD_SIZE)
    )
    value_grad = value_sum.astype(jnp.bfloat16)
    query_w_grad = jnp.einsum(
        "rd,re->de", first_normed, query_grad, preferred_element_type=jnp.float32
    )
    key_w_grad = jnp.einsum("rd,re->de", first_normed, key_grad, preferred_element_type=jnp.float32)
    value_w_grad = jnp.einsum(
        "rd,re->de", first_normed, value_grad, preferred_element_type=jnp.float32
    )
    normed_one_grad = (
        jnp.einsum("re,de->rd", query_grad, query_full, preferred_element_type=jnp.float32)
        + jnp.einsum("re,de->rd", key_grad, key_complete, preferred_element_type=jnp.float32)
        + jnp.einsum("re,de->rd", value_grad, value_complete, preferred_element_type=jnp.float32)
    )
    _, first_pull = jax.vjp(normalize, inputs, scale_one)
    input_norm_grad, first_gain_grad = first_pull(normed_one_grad)
    input_grad = (middle_grad + input_norm_grad)[None]
    shares = (
        lax.psum_scatter(query_w_grad, ("dp", "expert"), scatter_dimension=0, tiled=True),
        lax.psum_scatter(key_w_grad, ("dp", "expert"), scatter_dimension=0, tiled=True),
        lax.psum_scatter(value_w_grad, ("dp", "expert"), scatter_dimension=0, tiled=True),
        lax.psum_scatter(out_grad, ("dp", "expert"), scatter_dimension=0, tiled=True),
        lax.psum_scatter(router_grad, ("dp", "expert"), scatter_dimension=0, tiled=True),
        lax.psum_scatter(first_gain_grad, ("dp", "expert"), scatter_dimension=0, tiled=True),
        lax.psum_scatter(second_gain_grad, ("dp", "expert"), scatter_dimension=0, tiled=True),
    )
    return (
        output,
        input_grad,
        shares[5],
        shares[6],
        shares[0],
        shares[1],
        shares[2],
        shares[3],
        shares[4],
        summed_experts[0],
        summed_experts[1],
        summed_experts[2],
    )


def mm(a, b):
    return jnp.dot(a, b, preferred_element_type=F32)


def mm_nt(a, b):
    return lax.dot_general(a, b, (((1,), (1,)), ((), ())), preferred_element_type=F32)


def mm_tn(a, b):
    return lax.dot_general(a, b, (((0,), (0,)), ((), ())), preferred_element_type=F32)


def gelu_both(value):
    scale = 0.7978845608028654
    square = value * value
    bend = jnp.tanh(scale * value * (1.0 + 0.044715 * square))
    half = 0.5 * (1.0 + bend)
    slope = half + 0.5 * value * (1.0 - bend * bend) * scale * (1.0 + 0.134145 * square)
    return value * half, slope


def expert_kernel(
    n2_ref, gate_ref, dy_ref, gw_ref, uw_ref, dw_ref,
    row_ref, gg_ref, sum_ref, wide_ref, down_ref, landing,
    n2_all, gate_all, dy_buf, dy_cols, hs_all, gl_all, ul_all, own, sib, zin, gg_out, gg_in,
    stage, kept, down_kept,
    n2_send, n2_recv, gt_send, gt_recv, own_send, sib_recv, zin_send, zin_recv,
    gg_send, gg_recv, dy_sem, cols_sem, sum_sem, tile_send, tile_recv, load_sem, keep_sem,
):
    count = lax.axis_size("expert")
    depth = count // 2
    rows = n2_ref.shape[0]
    half = rows // 2
    width = n2_ref.shape[1]
    ff = gw_ref.shape[1]
    me = lax.axis_index("expert")
    z, core = me // 2, me % 2
    sibling = z * 2 + 1 - core
    mine = lax.axis_index("dp")
    y, x = mine // 2, mine % 2
    others = (y * 2 + 1 - x, (1 - y) * 2 + 1 - x, (1 - y) * 2 + x)

    def at(zz):
        return {"expert": zz * 2 + core}

    barrier = pltpu.get_barrier_semaphore()
    for other in range(1, count):
        pl.semaphore_signal(
            barrier, 1, device_id={"expert": lax.rem(me + other, count)}, device_id_type=MESH
        )
    for dp in others:
        pl.semaphore_signal(barrier, 1, device_id={"dp": dp}, device_id_type=MESH)
    pl.semaphore_wait(barrier, count - 1 + len(others))

    def chunk(k):
        return pl.ds(pl.multiple_of(k * rows, 16), rows)

    def n2_copy(k, lane, target):
        return pltpu.make_async_remote_copy(
            n2_all.at[chunk(k)], n2_all.at[chunk(k)], n2_send.at[k, lane], n2_recv.at[k],
            device_id=target, device_id_type=MESH,
        )

    def gt_copy(k, lane, target):
        return pltpu.make_async_remote_copy(
            gate_all.at[k], gate_all.at[k], gt_send.at[k, lane], gt_recv.at[k],
            device_id=target, device_id_type=MESH,
        )

    def send_chunk(k, lane, target):
        n2_copy(k, lane, target).start()
        gt_copy(k, lane, target).start()

    def sent_chunk(k, lane, target):
        n2_copy(k, lane, target).wait_send()
        gt_copy(k, lane, target).wait_send()

    def arrived(k):
        n2_copy(k, 0, at(z)).wait_recv()
        gt_copy(k, 0, at(z)).wait_recv()

    def dy_copy(k, slot):
        return pltpu.make_async_copy(dy_ref.at[k], dy_buf.at[slot], dy_sem.at[slot])

    def gg_copy(k):
        return pltpu.make_async_remote_copy(
            gg_out.at[k], gg_in.at[me], gg_send.at[k], gg_recv.at[me],
            device_id={"expert": k}, device_id_type=MESH,
        )

    def own_copy(zs):
        return pltpu.make_async_remote_copy(
            own.at[2 * zs + 1 - core], sib.at[zs], own_send.at[zs], sib_recv.at[zs],
            device_id={"expert": sibling}, device_id_type=MESH,
        )

    def part(h):
        return pl.ds(h * half, half)

    def zin_copy(zd, h, nxt, slot):
        return pltpu.make_async_remote_copy(
            own.at[2 * zd + core, part(h)], zin.at[slot, part(h)],
            zin_send.at[zd, h], zin_recv.at[slot, h],
            device_id=at(nxt), device_id_type=MESH,
        )

    n2_all[chunk(me), :] = n2_ref[...]
    gate_all[me] = gate_ref[...]

    @pl.when(z < depth - 1)
    def _():
        send_chunk(me, 0, at(z + 1))

    @pl.when(z > 0)
    def _():
        send_chunk(me, 1, at(z - 1))

    send_chunk(me, 2, {"expert": sibling})

    row_ids = lax.broadcasted_iota(jnp.int32, (count, gate_ref.shape[1]), 0)

    def compute(k, slot):
        r = chunk(k)
        gate_row = jnp.sum(jnp.where(row_ids == me, gate_all[k], 0.0), axis=0, keepdims=True)
        gate_col = jnp.transpose(jnp.broadcast_to(gate_row, (128, gate_row.shape[1])))[:rows]
        tile = 256
        gate_wide = jnp.concatenate([gate_col] * (tile // 128), axis=1)
        total = jnp.zeros((rows, 128), F32)
        for j in range(ff // tile):
            cols = slice(j * tile, (j + 1) * tile)
            back = mm_nt(dy_buf[slot], dw_ref[cols, :])
            gate_pre = mm(n2_all[r, :], gw_ref[:, cols])
            up_pre = mm(n2_all[r, :], uw_ref[:, cols])
            act, slope = gelu_both(gate_pre)
            hidden = act * up_pre
            hs_all[r, cols] = (gate_wide * hidden).astype(BF)
            product = hidden * back
            for i in range(tile // 128):
                total = total + product[:, i * 128 : (i + 1) * 128]
            back = gate_wide * back
            gl_all[r, cols] = (back * up_pre * slope).astype(BF)
            ul_all[r, cols] = (back * act).astype(BF)
        padded = jnp.concatenate(
            [total, jnp.zeros((gate_ref.shape[1] - rows, 128), F32)], axis=0
        )
        gg_row = jnp.sum(jnp.transpose(padded), axis=0, keepdims=True)
        gg_tile = jnp.where(row_ids == me, gg_row, 0.0)
        gg_out[k] = gg_tile

        @pl.when(k == me)
        def _():
            gg_in[me] = gg_tile

        @pl.when(k != me)
        def _():
            gg_copy(k).start()

        wide = 512
        for j in range(width // wide):
            cols = slice(j * wide, (j + 1) * wide)
            own[k, :, cols] = (
                mm_nt(gl_all[r, :], gw_ref[cols, :]) + mm_nt(ul_all[r, :], uw_ref[cols, :])
            ).astype(BF)

    block = 16

    def combine(zd, h, with_in):
        def step(i, _):
            rr = pl.ds(pl.multiple_of(h * half + i * block, block), block)
            value = own[2 * zd + core, rr, :].astype(F32) + sib[zd, rr, :].astype(F32)
            if with_in:
                value = value + zin[zd, rr, :].astype(F32)
            own[2 * zd + core, rr, :] = value.astype(BF)
            return 0

        lax.fori_loop(0, half // block, step, 0)

    def slot_for(zd, nxt):
        return jnp.where((nxt == zd) & (nxt < z), depth, zd)

    def pass_on(zd, h, nxt, with_in):
        if h == 0:
            own_copy(zd).wait_recv()
        if with_in:
            zin_copy(zd, h, nxt, zd).wait_recv()
        combine(zd, h, with_in)
        zin_copy(zd, h, nxt, slot_for(zd, nxt)).start()

    def pair(zs):
        def one(w, _):
            k = 2 * zs + jnp.where(w == 0, 1 - core, core)

            @pl.when(w == 0)
            def _():
                arrived(k)

            dy_copy(k, w).wait()
            compute(k, w)

            @pl.when(w == 0)
            def _():
                own_copy(zs).start()

            return 0

        lax.fori_loop(0, 2, one, 0)

    def start_dy(zs):
        dy_copy(2 * zs + 1 - core, 0).start()
        dy_copy(2 * zs + core, 1).start()

    def by_distance(d, _):
        left, right = z - d, z + d
        has_left, has_right = left >= 0, (right < depth) & (d > 0)

        @pl.when(has_left)
        def _():
            start_dy(left)

        @pl.when(has_left & (d > 0))
        def _():
            k = 2 * left + core
            arrived(k)

            @pl.when(z < depth - 1)
            def _():
                send_chunk(k, 0, at(z + 1))

            send_chunk(k, 2, {"expert": sibling})

        @pl.when(has_right)
        def _():
            k = 2 * right + core
            arrived(k)

            @pl.when(z > 0)
            def _():
                send_chunk(k, 1, at(z - 1))

            send_chunk(k, 2, {"expert": sibling})

        def side(s, _):
            zs = jnp.where(s == 0, left, right)

            @pl.when(jnp.where(s == 0, has_left, has_right))
            def _():
                @pl.when(s == 1)
                def _():
                    start_dy(right)

                pair(zs)

                @pl.when((d > 0) & ((z == 0) | (z == depth - 1)))
                def _():
                    nxt = jnp.where(z == 0, 1, depth - 2)
                    for h in range(2):
                        pass_on(zs, h, nxt, False)

            return 0

        lax.fori_loop(0, 2, side, 0)
        return 0

    lax.fori_loop(0, depth, by_distance, 0)

    def sum_copy(k, slot):
        return pltpu.make_async_copy(own.at[slot], sum_ref.at[k], sum_sem.at[slot])

    def sums(low, high):
        def step(i, _):
            slot = 2 * lax.rem(i, depth) + 1 - core

            @pl.when(i < depth)
            def _():
                own_copy(i).wait_send()

            @pl.when(i >= depth)
            def _():
                sum_copy(i, slot).wait()

            wide = 512
            for j in range(width // wide):
                cols = slice(j * wide, (j + 1) * wide)
                own[slot, :, cols] = mm(hs_all[chunk(i), :], dw_ref[:, cols]).astype(BF)
            sum_copy(i, slot).start()
            return 0

        lax.fori_loop(low, high, step, 0)

    quarter = width // 4

    def owner(j):
        return jnp.where(
            j == 0, others[0], jnp.where(j == 1, others[1], jnp.where(j == 2, others[2], mine))
        )

    def cols_of(dp):
        return pl.ds(pl.multiple_of(dp * quarter, 128), quarter)

    def tile_slot(kind, j):
        if kind == 0:
            return stage.at[j]
        return (gl_all, ul_all)[kind - 1].at[pl.ds(pl.multiple_of(j * quarter, 16), quarter)]

    def tile_copy(kind, j):
        return pltpu.make_async_remote_copy(
            tile_slot(kind, j), landing.at[mine, kind], tile_send.at[kind, j],
            tile_recv.at[mine, kind], device_id={"dp": owner(j)}, device_id_type=MESH,
        )

    def col_copy(j):
        return pltpu.make_async_copy(dy_ref.at[:, :, cols_of(owner(j))], dy_cols, cols_sem)

    def tiles(kind, low, high):
        def step(j, _):
            cols = cols_of(owner(j))
            if kind == 2:
                col_copy(j).wait()
                tile = mm_tn(dy_cols[...].reshape(count * rows, quarter), hs_all[...])

                @pl.when(j < 3)
                def _():
                    col_copy(j + 1).start()
            else:
                tile = mm_tn(n2_all[:, cols], (gl_all, ul_all)[kind][...])
            tile = tile.astype(BF)

            @pl.when(j < 3)
            def _():
                tile_slot(kind, j)[...] = tile
                tile_copy(kind, j).start()

            @pl.when(j == 3)
            def _():
                kept[kind] = tile

            return 0

        lax.fori_loop(low, high, step, 0)

    def flow(r, first, h):
        right = (z < depth - 1 - z) if first else (z >= depth - 1 - z)
        zd = jnp.where(right, r, depth - 1 - r)
        valid = jnp.where(right, (z < zd) & (z > 0), (z > zd) & (z < depth - 1))

        @pl.when(valid)
        def _():
            pass_on(zd, h, jnp.where(right, z + 1, z - 1), True)

    col_copy(0).start()
    jobs = [lambda k=kind, i=i: tiles(k, i, i + 2) for kind in range(3) for i in (0, 2)]
    eighth = count // 4
    jobs += [lambda i=i: sums(i * eighth, (i + 1) * eighth) for i in range(4)]
    for r in range(2, depth):
        for first in (True, False):
            for h in range(2):
                if first or r == depth - 1:
                    for _ in range(2 if r == 2 else 1):
                        if jobs:
                            jobs.pop(0)()
                flow(r, first, h)
    while jobs:
        jobs.pop(0)()

    own_copy(z).wait_recv()
    for h in range(2):

        @pl.when(z > 0)
        def _():
            zin_copy(z, h, z, z).wait_recv()

        @pl.when(z < depth - 1)
        def _():
            zin_copy(z, h, z, depth).wait_recv()

    def last(i, _):
        rr = pl.ds(pl.multiple_of(i * block, block), block)
        row_ref[rr, :] = own[me, rr, :].astype(F32) + sib[z, rr, :].astype(F32)

        @pl.when(z > 0)
        def _():
            row_ref[rr, :] += zin[z, rr, :].astype(F32)

        @pl.when(z < depth - 1)
        def _():
            row_ref[rr, :] += zin[depth, rr, :].astype(F32)

        return 0

    lax.fori_loop(0, rows // block, last, 0)

    for e in range(count):

        @pl.when(e != me)
        def _():
            pltpu.make_async_remote_copy(
                gg_out.at[e], gg_in.at[e], gg_send.at[e], gg_recv.at[e],
                device_id={"expert": e}, device_id_type=MESH,
            ).wait_recv()

    gg_ref[...] = jnp.sum(gg_in[...], axis=0)

    def tile_load(kind, i):
        into = (gl_all, ul_all, hs_all)[kind]
        return pltpu.make_async_copy(
            landing.at[others[i], kind], into.at[pl.ds((3 + i) * quarter, quarter)], load_sem.at[kind, i]
        )

    keeps = [
        pltpu.make_async_copy(kept.at[pl.ds(0, 2)], wide_ref, keep_sem.at[0]),
        pltpu.make_async_copy(down_kept, down_ref, keep_sem.at[1]),
    ]
    for kind in range(3):
        for i in range(3):
            pltpu.make_async_remote_copy(
                stage.at[0], landing.at[others[i], kind], tile_send.at[kind, i],
                tile_recv.at[others[i], kind], device_id={"dp": others[i]}, device_id_type=MESH,
            ).wait_recv()
            tile_load(kind, i).start()
    for kind in range(3):
        for i in range(3):
            tile_load(kind, i).wait()
        into = (gl_all, ul_all, hs_all)[kind]

        def add_up(i, _):
            rr = pl.ds(pl.multiple_of(i * 128, 128), 128)
            total = kept[kind, rr, :].astype(F32)
            for j in range(3):
                total = total + into[pl.ds(pl.multiple_of((3 + j) * quarter + i * 128, 128), 128), :].astype(F32)
            if kind == 2:
                down_kept[:, rr] = jnp.transpose(total).astype(BF)
            else:
                kept[kind, rr, :] = total.astype(BF)
            return 0

        lax.fori_loop(0, quarter // 128, add_up, 0)
        if kind > 0:
            keeps[kind - 1].start()

    for e in range(count):

        @pl.when(e != me)
        def _():
            gg_copy(e).wait_send()

        zs = e // 2

        @pl.when((e == me) | ((zs < z) & (e % 2 == core)))
        def _():
            @pl.when(z < depth - 1)
            def _():
                sent_chunk(e, 0, at(z + 1))

        @pl.when((e == me) | ((zs > z) & (e % 2 == core)))
        def _():
            @pl.when(z > 0)
            def _():
                sent_chunk(e, 1, at(z - 1))

        @pl.when(e % 2 == core)
        def _():
            sent_chunk(e, 2, {"expert": sibling})

    for zd in range(depth):
        sum_copy(zd, 2 * zd + 1 - core).wait()
        for h in range(2):

            @pl.when(zd != z)
            def _():
                zin_copy(zd, h, z, zd).wait_send()

    for kind in range(3):
        for j in range(3):
            tile_copy(kind, j).wait_send()
    for keep in keeps:
        keep.wait()


def expert_pass(n2, gate_rows, dy_all, gate_w, up_w, down_w):
    count = lax.axis_size("expert")
    depth = count // 2
    rows, width = n2.shape
    ff = gate_w.shape[1]
    lanes = gate_rows.shape[1]
    dma = pltpu.SemaphoreType.DMA
    vmem = pl.BlockSpec(memory_space=pltpu.VMEM)
    anywhere = pl.BlockSpec(memory_space=pl.ANY)
    outs = (
        jax.ShapeDtypeStruct((rows, width), F32),
        jax.ShapeDtypeStruct((count, lanes), F32),
        jax.ShapeDtypeStruct((count, rows, width), BF),
        jax.ShapeDtypeStruct((2, width // 4, ff), BF),
        jax.ShapeDtypeStruct((ff, width // 4), BF),
        jax.ShapeDtypeStruct((4, 3, width // 4, ff), BF),
    )
    return pl.pallas_call(
        expert_kernel,
        name="expert_pass",
        out_shape=outs,
        in_specs=[vmem, vmem, anywhere, vmem, vmem, vmem],
        out_specs=(vmem, vmem, anywhere, anywhere, anywhere, anywhere),
        scratch_shapes=[
            pltpu.VMEM((count * rows, width), BF),
            pltpu.VMEM((count, count, lanes), F32),
            pltpu.VMEM((2, rows, width), BF),
            pltpu.VMEM((count, rows, width // 4), BF),
            pltpu.VMEM((count * rows, ff), BF),
            pltpu.VMEM((count * rows, ff), BF),
            pltpu.VMEM((count * rows, ff), BF),
            pltpu.VMEM((count, rows, width), BF),
            pltpu.VMEM((depth, rows, width), BF),
            pltpu.VMEM((depth + 1, rows, width), BF),
            pltpu.VMEM((count, count, lanes), F32),
            pltpu.VMEM((count, count, lanes), F32),
            pltpu.VMEM((3, width // 4, ff), BF),
            pltpu.VMEM((3, width // 4, ff), BF),
            pltpu.VMEM((ff, width // 4), BF),
            dma((count, 3)), dma((count,)), dma((count, 3)), dma((count,)),
            dma((depth,)), dma((depth,)), dma((depth, 2)), dma((depth + 1, 2)),
            dma((count,)), dma((count,)), dma((2,)), dma, dma((count,)), dma((3, 3)), dma((4, 3)),
            dma((3, 3)), dma((2,)),
        ],
        compiler_params=pltpu.CompilerParams(
            collective_id=2, has_side_effects=True, vmem_limit_bytes=62 * 2**20
        ),
        cost_estimate=pl.CostEstimate(
            flops=18 * count * rows * width * ff, bytes_accessed=60 * 2**20, transcendentals=0
        ),
    )(n2, gate_rows, dy_all, gate_w, up_w, down_w)


def greet(depth, z, at, targets):
    barrier = pltpu.get_barrier_semaphore()
    for target in targets:
        pl.semaphore_signal(barrier, 1, device_id=target, device_id_type=MESH)

    @pl.when(z > 0)
    def _():
        pl.semaphore_signal(barrier, 1, device_id=at(z - 1), device_id_type=MESH)

    @pl.when(z < depth - 1)
    def _():
        pl.semaphore_signal(barrier, 1, device_id=at(z + 1), device_id_type=MESH)

    ends = (z > 0).astype(jnp.int32) + (z < depth - 1).astype(jnp.int32)
    pl.semaphore_wait(barrier, len(targets) + ends)


def attention_kernel(
    x_ref, shard_ref, cos_ref, sin_ref, bias_ref, hits_ref,
    n1_ref, q_ref, kv_ref, mixed_ref, lse_ref, middle_ref, n2_ref, gate_ref, w_out,
    w, n1, q, kv, mixed,
    z_send, z_recv, x_send, x_recv, y_send, y_recv, a_send, a_recv, b_send, b_recv, s_send, s_recv,
    kx_send, kx_recv, ky_send, ky_recv, ka_send, ka_recv, kb_send, kb_recv, out_sem, keep_sem,
):
    count = lax.axis_size("expert")
    depth = count // 2
    shard, total = shard_ref.shape
    rows, width = x_ref.shape
    heads = q.shape[1] // HEAD_SIZE
    kv_width = kv.shape[1]
    groups = kv_width // (2 * HEAD_SIZE)
    group = heads // groups
    wide = heads * HEAD_SIZE
    qkv_width = wide + kv_width
    split = qkv_width + 128
    me, mine = lax.axis_index("expert"), lax.axis_index("dp")
    z, core = me // 2, me % 2
    y, x = mine // 2, mine % 2
    xn, yn, diag = y * 2 + 1 - x, (1 - y) * 2 + x, (1 - y) * 2 + 1 - x
    sibling = {"expert": z * 2 + 1 - core}

    def at(zz):
        return {"expert": zz * 2 + core}

    greet(depth, z, at, (sibling, {"dp": xn}, {"dp": yn}))

    def remote(src, dst, send, recv, target):
        return pltpu.make_async_remote_copy(
            src, dst, send, recv, device_id=target, device_id_type=MESH
        )

    bounds = ((0, split), (split, total))
    cuts = (bounds[0][1] // 256 * 128, split + (total - split) // 256 * 128)

    def place(dp, zz, cc):
        return pl.ds(pl.multiple_of((dp * count + 2 * zz + cc) * shard, 16), shard)

    def w_copy(dp, zz, low, high, send, recv, target, cc=core):
        ref = w.at[place(dp, zz, cc), pl.ds(low, high - low)]
        return remote(ref, ref, send, recv, target)

    def z_copy(p, zz, lane, target):
        return w_copy(mine, zz, *bounds[p], z_send.at[p, zz, lane], z_recv.at[p, zz], target)

    def x_copy(p, zz, dp):
        return w_copy(dp, zz, *bounds[p], x_send.at[p, zz], x_recv.at[p, zz], {"dp": xn})

    def y_copy(p, zz, dp):
        return w_copy(dp, zz, *bounds[p], y_send.at[p, zz], y_recv.at[p, zz], {"dp": yn})

    def a_copy(p, zz, dp):
        return w_copy(dp, zz, bounds[p][0], cuts[p], a_send.at[p, zz], a_recv.at[p, zz], {"dp": yn})

    def b_copy(p, zz, dp):
        return w_copy(dp, zz, cuts[p], bounds[p][1], b_send.at[p, zz], b_recv.at[p, zz], {"dp": xn})

    def s_copy(p, dp, zz, cc=core):
        return w_copy(dp, zz, *bounds[p], s_send.at[p, dp, zz], s_recv.at[p, dp, zz], sibling, cc)

    def spread(p, zz):
        x_copy(p, zz, mine).start()
        y_copy(p, zz, mine).start()
        s_copy(p, mine, zz).start()

    def on_sides(d, action):
        @pl.when(z - d >= 0)
        def _():
            action(z - d, True)

        if d > 0:

            @pl.when(z + d < depth)
            def _():
                action(z + d, False)

    def z_step(p, d):
        if d == 0:

            @pl.when(z < depth - 1)
            def _():
                z_copy(p, z, 0, at(z + 1)).start()

            @pl.when(z > 0)
            def _():
                z_copy(p, z, 1, at(z - 1)).start()

            spread(p, z)
            return

        def action(zz, from_left):
            z_copy(p, zz, 0, at(z)).wait_recv()
            if from_left:

                @pl.when(z < depth - 1)
                def _():
                    z_copy(p, zz, 0, at(z + 1)).start()
            else:

                @pl.when(z > 0)
                def _():
                    z_copy(p, zz, 1, at(z - 1)).start()

            spread(p, zz)

        on_sides(d, action)

    def xy_step(p, d):
        def action(zz, _):
            x_copy(p, zz, xn).wait_recv()
            a_copy(p, zz, xn).start()
            s_copy(p, xn, zz).start()
            y_copy(p, zz, yn).wait_recv()
            b_copy(p, zz, yn).start()
            s_copy(p, yn, zz).start()

        on_sides(d, action)

    def diag_step(p, d):
        def action(zz, _):
            a_copy(p, zz, diag).wait_recv()
            b_copy(p, zz, diag).wait_recv()
            s_copy(p, diag, zz).start()

        on_sides(d, action)

    def all_here(p):
        for dp in range(4):
            for zz in range(depth):
                s_copy(p, dp, zz, 1 - core).wait_recv()

    def all_sent(p):
        for zz in range(depth):

            @pl.when((zz <= z) & (z < depth - 1))
            def _():
                z_copy(p, zz, 0, at(z)).wait_send()

            @pl.when((zz >= z) & (z > 0))
            def _():
                z_copy(p, zz, 1, at(z)).wait_send()

            x_copy(p, zz, mine).wait_send()
            y_copy(p, zz, mine).wait_send()
            a_copy(p, zz, xn).wait_send()
            b_copy(p, zz, yn).wait_send()
            for dp in range(4):
                s_copy(p, dp, zz).wait_send()

    w[place(mine, z, core), :] = shard_ref[...]
    z_step(0, 0)
    z_step(0, 1)
    xy_step(0, 0)
    for d in range(2, depth):
        z_step(0, d)
        xy_step(0, d - 1)
    xy_step(0, depth - 1)
    for d in range(depth):
        diag_step(0, d)
    all_here(0)
    z_step(1, 0)

    def keep(p):
        low, high = bounds[p]
        return pltpu.make_async_copy(
            w.at[:, pl.ds(low, high - low)], w_out.at[:, pl.ds(low, high - low)], keep_sem.at[p]
        )

    keep(0).start()
    small = jnp.transpose(w[:, qkv_width:split].astype(F32))
    experts = hits_ref.shape[0]
    gain_one, gain_two = small[experts : experts + 1], small[experts + 1 : experts + 2]

    block = 32

    def first_norm(i, _):
        rr = pl.ds(pl.multiple_of(i * block, block), block)
        value = x_ref[rr, :].astype(F32)
        scale = lax.rsqrt(jnp.mean(value * value, axis=1, keepdims=True) + EPS)
        n1[rr, :] = (value * scale * gain_one).astype(BF)
        return 0

    lax.fori_loop(0, rows // block, first_norm, 0)

    def turn(value):
        return value * cos_ref[...] + pltpu.roll(value, HEAD_SIZE // 2, 1) * sin_ref[...]

    own = pl.ds(pl.multiple_of(mine * rows, 16), rows)
    projected = mm(n1[...], w[:, wide:qkv_width])
    for g in range(groups):
        low = 2 * g * HEAD_SIZE
        kv[own, low : low + HEAD_SIZE] = turn(projected[:, low : low + HEAD_SIZE]).astype(BF)
        kv[own, low + HEAD_SIZE : low + 2 * HEAD_SIZE] = projected[
            :, low + HEAD_SIZE : low + 2 * HEAD_SIZE
        ].astype(BF)

    def kv_copy(g, dp, low, high, send, recv, target):
        ref = kv.at[
            pl.ds(pl.multiple_of(dp * rows, 16), rows),
            pl.ds((2 * g + low) * HEAD_SIZE, (high - low) * HEAD_SIZE),
        ]
        return remote(ref, ref, send.at[g], recv.at[g], target)

    def kx(g, dp):
        return kv_copy(g, dp, 0, 2, kx_send, kx_recv, {"dp": xn})

    def ky(g, dp):
        return kv_copy(g, dp, 0, 2, ky_send, ky_recv, {"dp": yn})

    def ka(g, dp):
        return kv_copy(g, dp, 0, 1, ka_send, ka_recv, {"dp": yn})

    def kb(g, dp):
        return kv_copy(g, dp, 1, 2, kb_send, kb_recv, {"dp": xn})

    def kv_on(g):
        kx(g, xn).wait_recv()
        ka(g, xn).start()
        ky(g, yn).wait_recv()
        kb(g, yn).start()

    def kv_here(g):
        ka(g, diag).wait_recv()
        kb(g, diag).wait_recv()

    for g in range(groups):
        kx(g, mine).start()
        ky(g, mine).start()

    def project(h, _):
        cols = pl.ds(pl.multiple_of(h * 2 * HEAD_SIZE, 2 * HEAD_SIZE), 2 * HEAD_SIZE)
        value = mm(n1[...], w[:, cols])
        q[:, cols] = jnp.concatenate(
            [turn(value[:, :HEAD_SIZE]), turn(value[:, HEAD_SIZE:])], axis=1
        ).astype(BF)
        return 0

    lax.fori_loop(0, heads // 2, project, 0)
    kv_on(0)
    z_step(1, 1)
    kv_here(0)
    later = [
        lambda: (kv_on(1), xy_step(1, 0), z_step(1, 2)),
        lambda: (xy_step(1, 1), z_step(1, 3)),
        lambda: xy_step(1, 2),
        lambda: xy_step(1, 3),
        lambda: (diag_step(1, 0), diag_step(1, 1)),
        lambda: (diag_step(1, 2), diag_step(1, 3)),
        lambda: kv_here(1),
    ]
    lse_ref[...] = jnp.zeros_like(lse_ref)
    lanes = lax.broadcasted_iota(jnp.int32, lse_ref.shape, 1)

    def attend(h, _):
        for i, job in enumerate(later):
            pl.when(h == i)(lambda job=job: (job(), None)[1])
        g = h // group
        cols = pl.ds(pl.multiple_of(h * HEAD_SIZE, HEAD_SIZE), HEAD_SIZE)
        k_cols = pl.ds(pl.multiple_of(g * 2 * HEAD_SIZE, HEAD_SIZE), HEAD_SIZE)
        v_cols = pl.ds(pl.multiple_of(g * 2 * HEAD_SIZE + HEAD_SIZE, HEAD_SIZE), HEAD_SIZE)
        scores = mm_nt(q[:, cols], kv[:, k_cols]) * (HEAD_SIZE**-0.5 * LOG2E) + bias_ref[...]
        top = jnp.max(scores, axis=1, keepdims=True)
        power = jnp.exp2(scores - top)
        sums = jnp.sum(power, axis=1, keepdims=True)
        mixed[:, cols] = (mm(power.astype(BF), kv[:, v_cols]) / sums).astype(BF)
        lse_ref[...] = jnp.where(lanes == h, top + jnp.log2(sums), lse_ref[...])
        return 0

    lax.fori_loop(0, heads, attend, 0)
    keeps = [
        pltpu.make_async_copy(src, dst, out_sem.at[i])
        for i, (src, dst) in enumerate(
            ((n1, n1_ref), (q, q_ref), (kv, kv_ref), (mixed, mixed_ref))
        )
    ]
    for copy in keeps:
        copy.start()
    all_here(1)
    keep(1).start()
    tile = 512

    def project_out(i, _):
        cols = pl.ds(pl.multiple_of(i * tile, tile), tile)
        w_cols = pl.ds(pl.multiple_of(split + i * tile, 128), tile)
        middle_ref[:, cols] = x_ref[:, cols].astype(F32) + mm(mixed[...], w[:, w_cols])
        return 0

    lax.fori_loop(0, width // tile, project_out, 0)

    def second_norm(i, _):
        rr = pl.ds(pl.multiple_of(i * block, block), block)
        value = middle_ref[rr, :]
        scale = lax.rsqrt(jnp.mean(value * value, axis=1, keepdims=True) + EPS)
        n2_ref[rr, :] = (value * scale * gain_two).astype(BF)
        return 0

    lax.fori_loop(0, rows // block, second_norm, 0)
    logits = mm_nt(small.astype(BF), n2_ref[...])[:experts]
    hits = hits_ref[...] > 0.5
    chosen = jnp.where(hits, logits, NEGATIVE)
    power = jnp.where(hits, jnp.exp(chosen - jnp.max(chosen, axis=0, keepdims=True)), 0.0)
    gate_ref[...] = jnp.zeros_like(gate_ref)
    gate_ref[:, :rows] = power / jnp.sum(power, axis=0, keepdims=True)

    for g in range(groups):
        kx(g, mine).wait_send()
        ky(g, mine).wait_send()
        ka(g, xn).wait_send()
        kb(g, yn).wait_send()
    for p in range(2):
        all_sent(p)
        keep(p).wait()
    for copy in keeps:
        copy.wait()


def attention_pass(x, shard, cos, sin, bias, hits, kv_width):
    count = lax.axis_size("expert")
    depth = count // 2
    rows, width = x.shape
    lanes = rows + -rows % 128
    devices = 4 * count
    wide = width
    dma = pltpu.SemaphoreType.DMA
    vmem = pl.BlockSpec(memory_space=pltpu.VMEM)
    anywhere = pl.BlockSpec(memory_space=pl.ANY)
    shape = jax.ShapeDtypeStruct
    pair = dma((2, depth))
    groups = kv_width // (2 * HEAD_SIZE)
    tree = 4 * rows
    total = shard.shape[1]
    return pl.pallas_call(
        attention_kernel,
        name="attention_pass",
        out_shape=(
            shape((rows, width), BF),
            shape((rows, wide), BF),
            shape((tree, kv_width), BF),
            shape((rows, wide), BF),
            shape((rows, 128), F32),
            shape((rows, width), F32),
            shape((rows, width), BF),
            shape((hits.shape[0], lanes), F32),
            shape((devices * shard.shape[0], total), BF),
        ),
        in_specs=[vmem] * 6,
        out_specs=(anywhere,) * 4 + (vmem,) * 4 + (anywhere,),
        scratch_shapes=[
            pltpu.VMEM((devices * shard.shape[0], total), BF),
            pltpu.VMEM((rows, width), BF),
            pltpu.VMEM((rows, wide), BF),
            pltpu.VMEM((tree, kv_width), BF),
            pltpu.VMEM((rows, wide), BF),
            dma((2, depth, 2)), pair, pair, pair, pair, pair, pair, pair, pair, pair,
            dma((2, 4, depth)), dma((2, 4, depth)),
            *[dma((groups,)) for _ in range(8)],
            dma((4,)), dma((2,)),
        ],
        compiler_params=pltpu.CompilerParams(
            collective_id=1, has_side_effects=True, vmem_limit_bytes=56 * 2**20
        ),
        cost_estimate=pl.CostEstimate(
            flops=10**10, bytes_accessed=300 * 2**20, transcendentals=0
        ),
    )(x, shard, cos, sin, bias, hits)


def backward_kernel(
    x_ref, dy_ref, gate_ref, gg_ref, n1_ref, q_ref, kv_ref, mixed_ref, n2_ref, lse_ref,
    cos_ref, sin_ref, bias_ref, middle_any, row_ref, w_full, wide_ref, down_ref,
    tok_ref, share_ref, wide_all, down_all,
    middle, wbuf, wsmall, attended, mixed_grad, qg, dkv, kv_low, kv_in, w, wsib, legs, legs2, wz,
    load_sem, ag_local, ag_xs, ag_xr, ag_ys, ag_yr, ag_fs, ag_fr, kv_send, kv_recv,
    ws_send, ws_recv, a_send, a_recv, b_send, b_recv, a2_send, a2_recv, b2_send, b2_recv,
    wz_send, wz_recv,
):
    depth = lax.axis_size("expert") // 2
    rows, width = x_ref.shape
    heads = q_ref.shape[1] // HEAD_SIZE
    kv_width = kv_ref.shape[1]
    groups = kv_width // (2 * HEAD_SIZE)
    group = heads // groups
    wide = heads * HEAD_SIZE
    qkv_width = wide + kv_width
    split = qkv_width + 128
    shard, total = share_ref.shape
    me, mine = lax.axis_index("expert"), lax.axis_index("dp")
    z, core = me // 2, me % 2
    y, x = mine // 2, mine % 2
    xn, yn, diag = y * 2 + 1 - x, (1 - y) * 2 + x, (1 - y) * 2 + 1 - x
    sibling = {"expert": z * 2 + 1 - core}

    def at(zz):
        return {"expert": zz * 2 + core}

    greet(depth, z, at, (sibling, {"dp": xn}, {"dp": yn}, {"dp": diag}))

    def remote(src, dst, send, recv, target):
        return pltpu.make_async_remote_copy(
            src, dst, send, recv, device_id=target, device_id_type=MESH
        )

    def load(src, dst, i):
        return pltpu.make_async_copy(src, dst, load_sem.at[i])

    load_rows = load(row_ref, tok_ref, 0)
    load_out = load(w_full.at[:, pl.ds(split, width)], wbuf.at[:, pl.ds(0, width)], 1)
    load_small = load(w_full.at[:, pl.ds(qkv_width, 128)], wsmall, 2)
    load_qkv = load(w_full.at[:, pl.ds(0, qkv_width)], wbuf, 3)
    load_middle = load(middle_any, middle, 4)
    load_small.start()
    load_rows.start()
    load_middle.start()
    load_out.start()

    quarter = wide_ref.shape[1]
    down_half = down_ref.shape[0] // 2

    def quarter_of(piece, dp):
        span = pl.ds(pl.multiple_of(dp * quarter, 128), quarter)
        if piece < 2:
            return wide_all.at[piece, span]
        return down_all.at[pl.ds((piece - 2) * down_half, down_half), span]

    def own_quarter(piece):
        if piece < 2:
            return wide_ref.at[piece]
        return down_ref.at[pl.ds((piece - 2) * down_half, down_half)]

    def keep_quarter(piece):
        return pltpu.make_async_copy(own_quarter(piece), quarter_of(piece, mine), ag_local.at[piece])

    def quarter_x(piece, dp):
        return remote(own_quarter(piece), quarter_of(piece, dp), ag_xs.at[piece], ag_xr.at[piece], {"dp": xn})

    def quarter_y(piece, dp):
        return remote(own_quarter(piece), quarter_of(piece, dp), ag_ys.at[piece], ag_yr.at[piece], {"dp": yn})

    def quarter_on(piece, dp, target):
        ref = quarter_of(piece, dp)
        return remote(ref, ref, ag_fs.at[piece], ag_fr.at[piece], target)

    for piece in range(4):
        quarter_x(piece, mine).start()
        quarter_y(piece, mine).start()
        keep_quarter(piece).start()

    def quarters_on(first):
        for piece in (0, 1) if first else (2, 3):
            if piece % 2 == 0:
                quarter_x(piece, xn).wait_recv()
                quarter_on(piece, xn, {"dp": yn}).start()
            else:
                quarter_y(piece, yn).wait_recv()
                quarter_on(piece, yn, {"dp": xn}).start()

    bounds = ((split, total), (0, wide // 2), (wide // 2, wide), (wide, split))
    cuts = tuple(low + ((high - low) // 128 + 1) // 2 * 128 for low, high in bounds)

    def span(low, high):
        return pl.ds(low, high - low)

    def ws_copy(p, dp):
        cols = span(*bounds[p])
        return remote(
            w.at[dp, :, 1 - core, :, cols], wsib.at[dp, :, :, cols],
            ws_send.at[p, dp], ws_recv.at[p, dp], sibling,
        )

    def a_cols(p):
        return span(bounds[p][0], cuts[p])

    def b_cols(p):
        return span(cuts[p], bounds[p][1])

    def a_copy(p, yy):
        return remote(
            w.at[yy * 2 + 1 - x, :, core, :, a_cols(p)], legs.at[yy, :, :, a_cols(p)],
            a_send.at[p, yy], a_recv.at[p, yy], {"dp": xn},
        )

    def b_copy(p, xx):
        return remote(
            w.at[(1 - y) * 2 + xx, :, core, :, b_cols(p)], legs.at[xx, :, :, b_cols(p)],
            b_send.at[p, xx], b_recv.at[p, xx], {"dp": yn},
        )

    def a2_copy(p):
        return remote(
            w.at[yn, :, core, :, a_cols(p)], legs2.at[:, :, a_cols(p)], a2_send.at[p], a2_recv.at[p], {"dp": yn}
        )

    def b2_copy(p):
        return remote(
            w.at[xn, :, core, :, b_cols(p)], legs2.at[:, :, b_cols(p)], b2_send.at[p], b2_recv.at[p], {"dp": xn}
        )

    def wz_copy(p, zd, nxt, slot):
        cols = span(*bounds[p])
        return remote(
            w.at[mine, zd, core, :, cols], wz.at[slot, :, cols], wz_send.at[p, zd], wz_recv.at[p, slot], at(nxt)
        )

    block = 16
    steps = shard // block

    def add(dp, term, cols):
        def step(i, _):
            zz, rr = i // steps, pl.ds(pl.multiple_of(lax.rem(i, steps) * block, block), block)
            value = w[dp, zz, core, rr, cols].astype(F32) + term[zz, rr, cols].astype(F32)
            w[dp, zz, core, rr, cols] = value.astype(BF)
            return 0

        lax.fori_loop(0, depth * steps, step, 0)

    def begin(p):
        for dp in (xn, diag, yn, mine):
            ws_copy(p, dp).start()

    def first_legs(p):
        def combine(dp):
            ws_copy(p, dp).wait_recv()
            add(dp, wsib.at[dp], span(*bounds[p]))

        combine(xn)
        a_copy(p, y).start()
        combine(diag)
        a_copy(p, 1 - y).start()
        b_copy(p, 1 - x).start()
        combine(yn)
        b_copy(p, x).start()
        combine(mine)

    def second_legs(p):
        a_copy(p, 1 - y).wait_recv()
        add(yn, legs.at[1 - y], a_cols(p))
        a2_copy(p).start()
        b_copy(p, 1 - x).wait_recv()
        add(xn, legs.at[1 - x], b_cols(p))
        b2_copy(p).start()
        a_copy(p, y).wait_recv()
        add(mine, legs.at[y], a_cols(p))
        b_copy(p, x).wait_recv()
        add(mine, legs.at[x], b_cols(p))

    def slot_for(zd, nxt):
        return jnp.where((nxt == zd) & (nxt < z), depth, zd)

    def line(p):
        a2_copy(p).wait_recv()
        add(mine, legs2, a_cols(p))
        b2_copy(p).wait_recv()
        add(mine, legs2, b_cols(p))

        @pl.when((z == 0) | (z == depth - 1))
        def _():
            nxt = jnp.where(z == 0, 1, depth - 2)
            for d in range(1, depth):
                zd = jnp.where(z == 0, depth - d, d - 1)
                wz_copy(p, zd, nxt, slot_for(zd, nxt)).start()

    def line_on(p):
        cols = span(*bounds[p])
        for r in range(depth - 1, 1, -1):
            for first in (True, False):
                right = (z < depth - 1 - z) if first else (z >= depth - 1 - z)
                zd = jnp.where(right, r, depth - 1 - r)
                nxt = jnp.where(right, z + 1, z - 1)
                valid = jnp.where(right, (z < zd) & (z > 0), (z > zd) & (z < depth - 1))

                @pl.when(valid)
                def _():
                    wz_copy(p, zd, nxt, zd).wait_recv()

                    def step(i, _):
                        rr = pl.ds(pl.multiple_of(i * block, block), block)
                        value = w[mine, zd, core, rr, cols].astype(F32) + wz[zd, rr, cols].astype(F32)
                        w[mine, zd, core, rr, cols] = value.astype(BF)
                        return 0

                    lax.fori_loop(0, steps, step, 0)
                    wz_copy(p, zd, nxt, slot_for(zd, nxt)).start()

    def line_end(p):
        cols = span(*bounds[p])
        share_ref[:, cols] = w[mine, z, core, :, cols].astype(F32)

        @pl.when(z > 0)
        def _():
            wz_copy(p, z, z, z).wait_recv()
            share_ref[:, cols] += wz[z, :, cols].astype(F32)

        @pl.when(z < depth - 1)
        def _():
            wz_copy(p, z, z, depth).wait_recv()
            share_ref[:, cols] += wz[depth, :, cols].astype(F32)

    def weight_rows(left, right, low, size):
        quarter_rows = width // 4

        def step(i, _):
            cols = pl.ds(pl.multiple_of(i * quarter_rows, 128), quarter_rows)
            tile = mm_tn(left[:, cols], right).astype(BF)
            w[i, :, :, :, low : low + size] = tile.reshape(depth, 2, shard, size)
            return 0

        lax.fori_loop(0, 4, step, 0)

    experts = gate_ref.shape[0]
    gates, gate_grad = gate_ref[:, :rows], gg_ref[:, :rows]
    logit_grad = gates * (gate_grad - jnp.sum(gates * gate_grad, axis=0, keepdims=True))
    high = logit_grad.astype(BF)
    logit_two = jnp.concatenate([high.astype(F32), logit_grad - high.astype(F32)], axis=0).astype(BF)
    load_small.wait()
    small = jnp.transpose(wsmall[...].astype(F32))
    router = small[:experts].astype(BF).astype(F32)
    router_two = jnp.concatenate([router, router], axis=0).astype(BF)
    gain_one, gain_two = small[experts : experts + 1], small[experts + 1 : experts + 2]
    router_grad = mm(logit_two, n2_ref[...])
    router_grad = router_grad[:experts] + router_grad[experts:]
    load_rows.wait()
    load_middle.wait()
    tok_ref[...] += mm_tn(logit_two, router_two)

    def norm_back(value, grad, gain):
        scale = lax.rsqrt(jnp.mean(value * value, axis=1, keepdims=True) + EPS)
        unit = value * scale
        scaled = grad * gain
        back = scale * (scaled - unit * jnp.mean(scaled * unit, axis=1, keepdims=True))
        return back, jnp.sum(grad * unit, axis=0, keepdims=True)

    def second_norm(i, carry):
        rr = pl.ds(pl.multiple_of(i * block, block), block)
        back, gain = norm_back(middle[rr, :], tok_ref[rr, :], gain_two)
        back = back + dy_ref[rr, :].astype(F32)
        tok_ref[rr, :] = back
        attended[rr, :] = back.astype(BF)
        return carry + gain

    gain_two_grad = lax.fori_loop(0, rows // block, second_norm, jnp.zeros((1, width), F32))
    weight_rows(mixed_ref, attended[...], split, width)
    begin(0)
    load_out.wait()
    tile = 512

    def mixed_step(i, _):
        out_rows = pl.ds(pl.multiple_of(i * tile, tile), tile)
        mixed_grad[:, out_rows] = mm_nt(attended[...], wbuf[out_rows, :width]).astype(BF)
        return 0

    lax.fori_loop(0, wide // tile, mixed_step, 0)
    load_qkv.start()
    first_legs(0)

    lanes = lax.broadcasted_iota(jnp.int32, lse_ref.shape, 1)

    def turn_back(value):
        return value * cos_ref[...] - pltpu.roll(value, HEAD_SIZE // 2, 1) * sin_ref[...]

    def kv_copy(g, i):
        dp = (xn, diag, yn)[i]
        return remote(
            kv_low.at[g, pl.ds(pl.multiple_of(dp * rows, 16), rows)], kv_in.at[g, mine],
            kv_send.at[g, i], kv_recv.at[g, mine], {"dp": dp},
        )

    def attend_group(g, polls):
        low = 2 * g * HEAD_SIZE
        key, value = kv_ref[:, low : low + HEAD_SIZE], kv_ref[:, low + HEAD_SIZE : low + 2 * HEAD_SIZE]

        def attend(i, _):
            for j, job in polls.items():
                pl.when(i == j)(lambda job=job: (job(), None)[1])
            h = g * group + i
            cols = pl.ds(pl.multiple_of(h * HEAD_SIZE, HEAD_SIZE), HEAD_SIZE)
            query, grad = q_ref[:, cols], mixed_grad[:, cols]
            level = jnp.sum(jnp.where(lanes == h, lse_ref[...], 0.0), axis=1, keepdims=True)
            scores = mm_nt(query, key) * (HEAD_SIZE**-0.5 * LOG2E) + bias_ref[...]
            attn = jnp.exp2(scores - level)
            attn_grad = mm_nt(grad, value)
            mean = jnp.sum(attn * attn_grad, axis=1, keepdims=True)
            score_grad = (attn * (attn_grad - mean)).astype(BF)
            value_term = mm_tn(attn.astype(BF), grad)
            key_term = mm_tn(score_grad, query)
            qg[:, cols] = turn_back(mm(score_grad, key) * HEAD_SIZE**-0.5).astype(BF)

            @pl.when(i == 0)
            def _():
                dkv[:, :HEAD_SIZE] = key_term
                dkv[:, HEAD_SIZE:] = value_term

            @pl.when(i > 0)
            def _():
                dkv[:, :HEAD_SIZE] += key_term
                dkv[:, HEAD_SIZE:] += value_term

            return 0

        lax.fori_loop(0, group, attend, 0)
        kv_low[g, :, :HEAD_SIZE] = (dkv[:, :HEAD_SIZE] * HEAD_SIZE**-0.5).astype(BF)
        kv_low[g, :, HEAD_SIZE:] = dkv[:, HEAD_SIZE:].astype(BF)
        for i in range(3):
            kv_copy(g, i).start()
        weight_rows(n1_ref, qg[:, g * wide // 2 : (g + 1) * wide // 2], g * wide // 2, wide // 2)
        begin(1 + g)
        first_legs(1 + g)

    attend_group(0, {})
    attend_group(1, {2: lambda: second_legs(0)})

    def kv_sum(g):
        for i in range(3):
            dp = (xn, diag, yn)[i]
            remote(
                kv_low.at[g, pl.ds(0, rows)], kv_in.at[g, dp], kv_send.at[g, i], kv_recv.at[g, dp], {"dp": dp}
            ).wait_recv()
        terms = kv_low[g, pl.ds(pl.multiple_of(mine * rows, 16), rows), :].astype(F32)
        for dp in (xn, diag, yn):
            terms = terms + kv_in[g, dp].astype(F32)
        low = wide + 2 * g * HEAD_SIZE
        qg[:, low : low + HEAD_SIZE] = turn_back(terms[:, :HEAD_SIZE]).astype(BF)
        qg[:, low + HEAD_SIZE : low + 2 * HEAD_SIZE] = terms[:, HEAD_SIZE:].astype(BF)

    for g in range(groups):
        kv_sum(g)
    weight_rows(n1_ref, qg[:, wide:], wide, kv_width)
    load_qkv.wait()

    def first_grad(i, _):
        out_rows = pl.ds(pl.multiple_of(i * tile, tile), tile)
        middle[:, out_rows] = mm_nt(qg[...], wbuf[out_rows, :])
        return 0

    lax.fori_loop(0, width // tile, first_grad, 0)

    def first_norm(i, carry):
        rr = pl.ds(pl.multiple_of(i * block, block), block)
        back, gain = norm_back(x_ref[rr, :].astype(F32), middle[rr, :], gain_one)
        tok_ref[rr, :] += back
        return carry + gain

    gain_one_grad = lax.fori_loop(0, rows // block, first_norm, jnp.zeros((1, width), F32))
    small_grad = jnp.concatenate(
        [
            router_grad,
            gain_one_grad,
            gain_two_grad,
            jnp.zeros((128 - experts - 2, width), F32),
        ],
        axis=0,
    )
    small_grad = jnp.transpose(small_grad).astype(BF)
    for i in range(4):
        part = small_grad[i * width // 4 : (i + 1) * width // 4]
        w[i, :, :, :, qkv_width:split] = part.reshape(depth, 2, shard, 128)
    begin(3)
    quarters_on(True)
    first_legs(3)
    second_legs(1)
    quarters_on(False)
    line(0)
    second_legs(2)
    line_on(0)
    line(1)
    second_legs(3)
    line_on(1)
    line(2)
    line_on(2)
    line(3)
    line_on(3)
    for p in range(4):
        line_end(p)

    for piece in range(4):
        keep_quarter(piece).wait()
        quarter_x(piece, mine).wait_send()
        quarter_y(piece, mine).wait_send()
        if piece % 2 == 0:
            quarter_y(piece, yn).wait_recv()
        else:
            quarter_x(piece, xn).wait_recv()
        quarter_on(piece, diag, {"dp": xn}).wait()
    for g in range(groups):
        for i in range(3):
            kv_copy(g, i).wait_send()
    for p in range(4):
        for dp in range(4):
            ws_copy(p, dp).wait_send()
        for i in range(2):
            a_copy(p, i).wait_send()
            b_copy(p, i).wait_send()
        a2_copy(p).wait_send()
        b2_copy(p).wait_send()
        for zd in range(depth):

            @pl.when(zd != z)
            def _():
                wz_copy(p, zd, z, zd).wait_send()


def backward_pass(
    x, dy, middle, gates, gate_grads, n1, q, kv, mixed, n2, logs, cos, sin, bias, row_sum, w_full,
    wide_part, down_part,
):
    depth = lax.axis_size("expert") // 2
    rows, width = x.shape
    total = w_full.shape[1]
    shard = w_full.shape[0] // (4 * 2 * depth)
    kv_width = kv.shape[1]
    groups = kv_width // (2 * HEAD_SIZE)
    qkv_width = q.shape[1] + kv_width
    dma = pltpu.SemaphoreType.DMA
    vmem = pl.BlockSpec(memory_space=pltpu.VMEM)
    anywhere = pl.BlockSpec(memory_space=pl.ANY)
    shape = jax.ShapeDtypeStruct
    parts = 4
    return pl.pallas_call(
        backward_kernel,
        name="backward_pass",
        out_shape=(
            shape((rows, width), F32),
            shape((shard, total), F32),
            shape((2, 4 * wide_part.shape[1], wide_part.shape[2]), BF),
            shape((down_part.shape[0], 4 * down_part.shape[1]), BF),
        ),
        in_specs=[vmem] * 13 + [anywhere] * 5,
        out_specs=(vmem, vmem, anywhere, anywhere),
        scratch_shapes=[
            pltpu.VMEM((rows, width), F32),
            pltpu.VMEM((width, qkv_width), BF),
            pltpu.VMEM((width, 128), BF),
            pltpu.VMEM((rows, width), BF),
            pltpu.VMEM((rows, q.shape[1]), BF),
            pltpu.VMEM((rows, qkv_width), BF),
            pltpu.VMEM((kv.shape[0], 2 * HEAD_SIZE), F32),
            pltpu.VMEM((groups, kv.shape[0], 2 * HEAD_SIZE), BF),
            pltpu.VMEM((groups, 4, rows, 2 * HEAD_SIZE), BF),
            pltpu.VMEM((4, depth, 2, shard, total), BF),
            pltpu.VMEM((4, depth, shard, total), BF),
            pltpu.VMEM((2, depth, shard, total), BF),
            pltpu.VMEM((depth, shard, total), BF),
            pltpu.VMEM((depth + 1, shard, total), BF),
            dma((5,)), dma((4,)), dma((4,)), dma((4,)), dma((4,)), dma((4,)), dma((4,)), dma((4,)),
            dma((groups, 3)), dma((groups, 4)),
            dma((parts, 4)), dma((parts, 4)), dma((parts, 2)), dma((parts, 2)), dma((parts, 2)), dma((parts, 2)),
            dma((parts,)), dma((parts,)), dma((parts,)), dma((parts,)),
            dma((parts, depth)), dma((parts, depth + 1)),
        ],
        compiler_params=pltpu.CompilerParams(
            collective_id=3, has_side_effects=True, vmem_limit_bytes=63 * 2**20
        ),
        cost_estimate=pl.CostEstimate(
            flops=2 * 10**10, bytes_accessed=200 * 2**20, transcendentals=0
        ),
    )(
        x, dy, gates, gate_grads, n1, q, kv, mixed, n2, logs, cos, sin, bias,
        middle, row_sum, w_full, wide_part, down_part,
    )


def rotation_rows(positions):
    half = HEAD_SIZE // 2
    frequency = jnp.power(THETA, -(jnp.arange(half, dtype=jnp.float32) * 2.0 / HEAD_SIZE))
    angles = positions.astype(jnp.float32)[:, None] * frequency[None, :]
    cosine, sine = jnp.cos(angles), jnp.sin(angles)
    return jnp.concatenate([cosine, cosine], axis=1), jnp.concatenate([-sine, sine], axis=1)


def tree_visibility(parent_row, query_ids, tree_length):
    blocks = parent_row.shape[0]
    trunk = blocks - BRANCHES - LEAVES
    leaf_from = trunk + BRANCHES
    query_block = query_ids // SEG
    block_ids = jnp.arange(blocks, dtype=jnp.int32)
    depth_of = jnp.minimum(query_block, trunk) + (query_block >= leaf_from).astype(jnp.int32)
    positions = depth_of * SEG + query_ids % SEG
    parent = jnp.sum(jnp.where(query_block[:, None] == block_ids, parent_row, 0), axis=1)
    above = jnp.where(query_block >= leaf_from, parent, query_block)
    key_ids = jnp.arange(tree_length, dtype=jnp.int32)[None, :]
    key_block = key_ids // SEG
    related = (
        (key_block < trunk) | (key_block == query_block[:, None]) | (key_block == above[:, None])
    )
    return related & (key_ids <= query_ids[:, None]), positions


def dense_on_device(
    tokens,
    cotangent,
    parents,
    routes,
    first_gain,
    second_gain,
    query_weight,
    key_matrix,
    value_matrix,
    out_weight,
    router_weight,
    gate_weight,
    up_weight,
    down_weight,
):
    experts = router_weight.shape[1]
    heads_width = QUERY_HEADS * HEAD_SIZE
    kv_width = 2 * KEY_VALUE_HEADS * HEAD_SIZE
    qkv_width = heads_width + kv_width
    kv_shards = []
    for head in range(KEY_VALUE_HEADS):
        cols = slice(head * HEAD_SIZE, (head + 1) * HEAD_SIZE)
        kv_shards += [key_matrix[:, cols], value_matrix[:, cols]]
    small_shard = jnp.concatenate(
        [router_weight, first_gain[:, None], second_gain[:, None]], axis=1
    )
    small_shard = jnp.pad(small_shard, ((0, 0), (0, -small_shard.shape[1] % 128)))
    small_width = small_shard.shape[1]
    shard = jnp.concatenate([query_weight, *kv_shards, small_shard, out_weight], axis=1)
    dy_low = cotangent[0]
    dy_all = lax.all_gather(dy_low, "expert", axis=0)
    inputs_low = tokens[0]
    total_rows = inputs_low.shape[0]
    tree_length = parents.shape[1] * SEG
    query_ids = lax.axis_index("dp") * total_rows + jnp.arange(total_rows, dtype=jnp.int32)
    visible, query_positions = tree_visibility(parents[0], query_ids, tree_length)
    bias = jnp.where(visible, 0.0, NEGATIVE)
    cos, sin = rotation_rows(query_positions)
    expert_ids = jnp.arange(experts, dtype=jnp.int32)
    hit_rows = jnp.any(routes[0][None, :, :] == expert_ids[:, None, None], axis=2)
    n1, query_low, kv_all, mixed, logs, middle, n2, gate_rows, full = attention_pass(
        inputs_low, shard, cos, sin, bias, hit_rows.astype(F32), kv_width
    )
    row_sum, gate_grads, sums, wide_part, down_part, _ = expert_pass(
        n2, gate_rows, dy_all, gate_weight[0], up_weight[0], down_weight[0]
    )
    combined = lax.psum_scatter(sums, "expert", scatter_dimension=0, tiled=True)[0]
    input_grad, share, wide_grads, down_grad = backward_pass(
        inputs_low, dy_low, middle, gate_rows, gate_grads, n1, query_low, kv_all, mixed, n2, logs,
        cos, sin, bias, row_sum, full, wide_part, down_part,
    )
    output = (middle + combined.astype(F32)).astype(BF)[None]
    heads_of = [
        share[:, heads_width + i * HEAD_SIZE : heads_width + (i + 1) * HEAD_SIZE]
        for i in range(2 * KEY_VALUE_HEADS)
    ]
    query_share = share[:, :heads_width]
    key_share = jnp.concatenate(heads_of[0::2], axis=1)
    value_share = jnp.concatenate(heads_of[1::2], axis=1)
    small_share = share[:, qkv_width : qkv_width + small_width]
    out_share = share[:, qkv_width + small_width :]
    return (
        output,
        input_grad[None],
        small_share[:, experts],
        small_share[:, experts + 1],
        query_share,
        key_share,
        value_share,
        out_share,
        small_share[:, :experts],
        wide_grads[0].astype(F32)[None],
        wide_grads[1].astype(F32)[None],
        down_grad.astype(F32)[None],
    )


def solution(mesh):
    dense = mesh.shape["expert"] <= 2 * TOPK and mesh.shape["dp"] == 4
    return jax.shard_map(
        dense_on_device if dense else on_device_routed,
        mesh=mesh,
        in_specs=(
            P("expert", "dp", None),
            P("expert", "dp", None),
            P("expert", None),
            P("expert", "dp", None),
            P(("dp", "expert")),
            P(("dp", "expert")),
            P(("dp", "expert"), None),
            P(("dp", "expert"), None),
            P(("dp", "expert"), None),
            P(("dp", "expert"), None),
            P(("dp", "expert"), None),
            P("expert", None, None),
            P("expert", None, None),
            P("expert", None, None),
        ),
        out_specs=(
            P("expert", "dp", None),
            P("expert", "dp", None),
            P(("dp", "expert")),
            P(("dp", "expert")),
            P(("dp", "expert"), None),
            P(("dp", "expert"), None),
            P(("dp", "expert"), None),
            P(("dp", "expert"), None),
            P(("dp", "expert"), None),
            P("expert", None, None),
            P("expert", None, None),
            P("expert", None, None),
        ),
        check_vma=False,
    )
```

```python
import jax
import jax.numpy as jnp
import numpy as np
from jax import lax
from jax.experimental import pallas as pl
from jax.experimental.pallas import tpu as pltpu
from jax.sharding import PartitionSpec as P

MESH = pl.DeviceIdType.MESH
BF = jnp.bfloat16
F32 = jnp.float32
MODEL_WIDTH = 1536
QUERY_HEADS = 12
KEY_VALUE_HEADS = 2
HEAD_SIZE = 128
FF = 768
TOPK = 4
SEG = 32
BRANCHES = 4
LEAVES = 8


EPS = 1e-06
THETA = 10000.0
HIGH_PRECISION = lax.Precision.HIGHEST
NEGATIVE = -1e30
LOG2E = 1.4426950408889634


def ancestry(parent_row):
    block_count = parent_row.shape[0]
    block_ids = jnp.arange(block_count, dtype=jnp.int32)

    def advance(counter, carried):
        current, ancestors = carried
        ancestors = jnp.maximum(
            ancestors, (current[:, None] == block_ids[None, :]).astype(jnp.float32)
        )
        return (jnp.take(parent_row, current), ancestors)

    start_pair = (block_ids, jnp.zeros((block_count, block_count), jnp.float32))
    current, ancestors = lax.fori_loop(0, block_count, advance, start_pair)
    depths = (jnp.sum(ancestors, axis=1) - 1.0).astype(jnp.int32)
    return (ancestors, depths)


def apply_rotation(values, positions):
    half_width = values.shape[-1] // 2
    frequency = jnp.power(
        THETA, -(jnp.arange(half_width, dtype=jnp.float32) * 2.0 / values.shape[-1])
    )
    angles = positions.astype(jnp.float32)[:, None] * frequency[None, :]
    cosine = jnp.cos(angles)[:, None, :]
    sine_part = jnp.sin(angles)[:, None, :]
    first_half = values[..., :half_width]
    second_half = values[..., half_width:]
    return jnp.concatenate(
        [
            first_half * cosine - second_half * sine_part,
            second_half * cosine + first_half * sine_part,
        ],
        axis=-1,
    )


def normalize(values, scales):
    return values * lax.rsqrt(jnp.mean(values * values, axis=-1, keepdims=True) + EPS) * scales


def place(route_ids, experts, capacity):
    one_hot = (route_ids[..., None] == jnp.arange(experts, dtype=jnp.int32)).astype(jnp.int32)
    pairs = one_hot.shape[-2]
    before = jnp.tri(pairs, pairs, -1, dtype=jnp.bfloat16)
    earlier = jnp.dot(before, one_hot.astype(jnp.bfloat16), preferred_element_type=jnp.float32)
    slot_rank = jnp.sum(earlier.astype(jnp.int32) * one_hot, axis=-1)
    return route_ids * capacity + slot_rank


def visibility(ancestors, depths, query_ids, key_ids):
    block_ids = jnp.arange(ancestors.shape[0], dtype=jnp.int32)
    query_hit = (query_ids // SEG)[:, None] == block_ids[None, :]
    key_hit = (key_ids // SEG)[:, None] == block_ids[None, :]
    query_positions = (
        jnp.sum(jnp.where(query_hit, depths[None, :], 0), axis=1) * SEG + query_ids % SEG
    )
    key_pos = jnp.sum(jnp.where(key_hit, depths[None, :], 0), axis=1) * SEG + key_ids % SEG
    reach = jnp.dot(query_hit.astype(jnp.float32), ancestors, precision=HIGH_PRECISION)
    reach_keys = jnp.repeat(reach, SEG, axis=1)
    visible = (reach_keys > 0.5) & (key_pos[None, :] <= query_positions[:, None])
    return (visible, query_positions)


def head_scores(query_rotated, keys_all, visible, key_value_head, query_group_width):
    query_part = query_rotated[
        :, key_value_head * query_group_width : (key_value_head + 1) * query_group_width, :
    ]
    key_part = keys_all[:, key_value_head * HEAD_SIZE : (key_value_head + 1) * HEAD_SIZE]
    scores = jnp.einsum(
        "rgd,kd->grk", query_part, key_part, preferred_element_type=jnp.float32
    ) * HEAD_SIZE ** (-0.5)
    return jnp.where(visible[None], scores, NEGATIVE)


def gelu_product(gate_pre, up_pre):
    return jax.nn.gelu(gate_pre, approximate=True) * up_pre


def expert_hidden(received, local_gate, local_up):
    local_count = local_gate.shape[0]
    slot_count = received.shape[1]
    grouped_queries = received.reshape(-1, local_count, slot_count, MODEL_WIDTH)
    gate_pre = jnp.einsum(
        "sjcd,jdf->sjcf", grouped_queries, local_gate, preferred_element_type=jnp.float32
    )
    up_pre = jnp.einsum(
        "sjcd,jdf->sjcf", grouped_queries, local_up, preferred_element_type=jnp.float32
    )
    hidden = gelu_product(gate_pre, up_pre).astype(jnp.bfloat16)
    flat_shape = (received.shape[0], slot_count, FF)
    return (gate_pre.reshape(flat_shape), up_pre.reshape(flat_shape), hidden.reshape(flat_shape))


def expert_result(hidden, local_down):
    local_count = local_down.shape[0]
    grouped_queries = hidden.reshape(-1, local_count, hidden.shape[1], FF)
    result = jnp.einsum(
        "sjcf,jfd->sjcd", grouped_queries, local_down, preferred_element_type=jnp.float32
    )
    return result.astype(jnp.bfloat16).reshape(hidden.shape[0], hidden.shape[1], MODEL_WIDTH)


def on_device_routed(
    tokens,
    cotangent,
    parents,
    routes,
    first_gain,
    second_gain,
    query_weight,
    key_matrix,
    value_matrix,
    out_weight,
    router_weight,
    gate_weight,
    up_weight,
    down_weight,
):
    gathered = (
        lax.all_gather(query_weight, ("dp", "expert"), axis=0, tiled=True),
        lax.all_gather(key_matrix, ("dp", "expert"), axis=0, tiled=True),
        lax.all_gather(value_matrix, ("dp", "expert"), axis=0, tiled=True),
        lax.all_gather(out_weight, ("dp", "expert"), axis=0, tiled=True),
        lax.all_gather(router_weight, ("dp", "expert"), axis=0, tiled=True),
        lax.all_gather(first_gain, ("dp", "expert"), axis=0, tiled=True),
        lax.all_gather(second_gain, ("dp", "expert"), axis=0, tiled=True),
    )
    query_full, key_complete, value_complete, out_full, router_full, gain_one, gain_two = gathered
    scale_one = gain_one.astype(jnp.float32)
    scale_two = gain_two.astype(jnp.float32)
    inputs = tokens[0].astype(jnp.float32)
    total_rows = inputs.shape[0]
    query_group_width = QUERY_HEADS // KEY_VALUE_HEADS
    ancestors, depths = ancestry(parents[0])
    tree_length = ancestors.shape[0] * SEG
    query_ids = lax.axis_index("dp") * total_rows + jnp.arange(total_rows, dtype=jnp.int32)
    key_ids = jnp.arange(tree_length, dtype=jnp.int32)
    visible, query_positions = visibility(ancestors, depths, query_ids, key_ids)
    first_normed = normalize(inputs, scale_one).astype(jnp.bfloat16)
    query_proj = jnp.dot(first_normed, query_full, preferred_element_type=jnp.float32).reshape(
        total_rows, QUERY_HEADS, HEAD_SIZE
    )
    key_projected = jnp.dot(first_normed, key_complete, preferred_element_type=jnp.float32).reshape(
        total_rows, KEY_VALUE_HEADS, HEAD_SIZE
    )
    value_projected = jnp.dot(first_normed, value_complete, preferred_element_type=jnp.float32)
    query_rotated = apply_rotation(query_proj, query_positions).astype(jnp.bfloat16)
    key_rotated = (
        apply_rotation(key_projected, query_positions)
        .astype(jnp.bfloat16)
        .reshape(total_rows, KEY_VALUE_HEADS * HEAD_SIZE)
    )
    value_low = value_projected.astype(jnp.bfloat16)
    keys_all, values_all = (
        lax.all_gather(key_rotated, "dp", axis=0, tiled=True),
        lax.all_gather(value_low, "dp", axis=0, tiled=True),
    )
    mixed_parts = []
    log_totals = []
    for key_value_head in range(KEY_VALUE_HEADS):
        scores = head_scores(query_rotated, keys_all, visible, key_value_head, query_group_width)
        row_max = jnp.max(scores, axis=-1, keepdims=True)
        exponent = jnp.exp(scores - row_max)
        row_total = jnp.sum(exponent, axis=-1, keepdims=True)
        log_totals.append(row_max + jnp.log(row_total))
        softmax_out = (exponent / row_total).astype(jnp.bfloat16)
        value_part = values_all[:, key_value_head * HEAD_SIZE : (key_value_head + 1) * HEAD_SIZE]
        mixed_parts.append(
            jnp.einsum("grk,kd->rgd", softmax_out, value_part, preferred_element_type=jnp.float32)
        )
    mixed_out = (
        jnp.concatenate(mixed_parts, axis=1)
        .reshape(total_rows, QUERY_HEADS * HEAD_SIZE)
        .astype(jnp.bfloat16)
    )
    middle = inputs + jnp.dot(mixed_out, out_full, preferred_element_type=jnp.float32)
    normed_two = normalize(middle, scale_two).astype(jnp.bfloat16)
    logits = jnp.dot(normed_two, router_full, preferred_element_type=jnp.float32)
    route_ids = routes[0]
    experts = gate_weight.shape[0] * lax.axis_size("expert")
    capacity = 3 * total_rows * TOPK // (2 * experts)
    expert_ids = jnp.arange(experts, dtype=jnp.int32)
    route_hits = route_ids[:, :, None] == expert_ids[None, None, :]
    chosen = jnp.sum(jnp.where(route_hits, logits[:, None, :], 0.0), axis=2)
    chosen_max = jnp.max(chosen, axis=1, keepdims=True)
    chosen_exp = jnp.exp(chosen - chosen_max)
    gate_weights = chosen_exp / jnp.sum(chosen_exp, axis=1, keepdims=True)
    pair_count = total_rows * TOPK
    slot_index = place(route_ids.reshape(pair_count), experts, capacity)
    slot_source = (
        jnp.full((experts * capacity,), pair_count, jnp.int32)
        .at[slot_index]
        .set(jnp.arange(pair_count, dtype=jnp.int32))
    )
    slot_used = slot_source < pair_count
    slot_pair = jnp.where(slot_used, slot_source, 0)
    slot_token = slot_pair // TOPK
    zero_low = jnp.zeros((), jnp.bfloat16)
    outgoing = jnp.where(slot_used[:, None], normed_two[slot_token], zero_low).reshape(
        experts, capacity, MODEL_WIDTH
    )
    gate_pre, up_pre, hidden = expert_hidden(
        lax.all_to_all(outgoing, "expert", split_axis=0, concat_axis=0, tiled=True),
        gate_weight,
        up_weight,
    )
    dispatched = expert_result(hidden, down_weight)
    returned = lax.all_to_all(dispatched, "expert", split_axis=0, concat_axis=0, tiled=True)
    expert_rows = (
        returned.reshape(experts * capacity, MODEL_WIDTH)[slot_index]
        .astype(jnp.float32)
        .reshape(total_rows, TOPK, MODEL_WIDTH)
    )
    final = middle + jnp.sum(gate_weights[:, :, None] * expert_rows, axis=1)
    output = final.astype(jnp.bfloat16)[None]
    upstream = cotangent[0].astype(jnp.float32)
    gate_grad = jnp.sum(upstream[:, None, :] * expert_rows, axis=2)
    chosen_grad = gate_weights * (
        gate_grad - jnp.sum(gate_weights * gate_grad, axis=1, keepdims=True)
    )
    logit_grad = jnp.sum(jnp.where(route_hits, chosen_grad[:, :, None], 0.0), axis=1)
    pair_grad = (
        (gate_weights[:, :, None] * upstream[:, None, :])
        .astype(jnp.bfloat16)
        .reshape(pair_count, MODEL_WIDTH)
    )
    grad_outgoing = jnp.where(slot_used[:, None], pair_grad[slot_pair], zero_low).reshape(
        experts, capacity, MODEL_WIDTH
    )
    received, grad_in = (
        lax.all_to_all(outgoing, "expert", split_axis=0, concat_axis=0, tiled=True),
        lax.all_to_all(grad_outgoing, "expert", split_axis=0, concat_axis=0, tiled=True),
    )
    gate_pre, up_pre, hidden = expert_hidden(received, gate_weight, up_weight)
    local_count = gate_weight.shape[0]
    slot_count = received.shape[1]
    grouped_rows = received.reshape(-1, local_count, slot_count, MODEL_WIDTH)
    grouped_hidden = hidden.reshape(-1, local_count, slot_count, FF)
    grouped_grad = grad_in.reshape(-1, local_count, slot_count, MODEL_WIDTH)
    down_grad = jnp.einsum(
        "sjcf,sjcd->jfd", grouped_hidden, grouped_grad, preferred_element_type=jnp.float32
    )
    hidden_grad = jnp.einsum(
        "sjcd,jfd->sjcf", grouped_grad, down_weight, preferred_element_type=jnp.float32
    )
    _, product_pull = jax.vjp(gelu_product, gate_pre, up_pre)
    gate_pre_grad, up_pre_grad = product_pull(hidden_grad.reshape(gate_pre.shape))
    gate_low = gate_pre_grad.astype(jnp.bfloat16).reshape(-1, local_count, slot_count, FF)
    up_low = up_pre_grad.astype(jnp.bfloat16).reshape(-1, local_count, slot_count, FF)
    gate_w_grad = jnp.einsum(
        "sjcd,sjcf->jdf", grouped_rows, gate_low, preferred_element_type=jnp.float32
    )
    up_w_grad = jnp.einsum(
        "sjcd,sjcf->jdf", grouped_rows, up_low, preferred_element_type=jnp.float32
    )
    row_grad = jnp.einsum(
        "sjcf,jdf->sjcd", gate_low, gate_weight, preferred_element_type=jnp.float32
    ) + jnp.einsum("sjcf,jdf->sjcd", up_low, up_weight, preferred_element_type=jnp.float32)
    row_grad = row_grad.astype(jnp.bfloat16).reshape(received.shape)
    returned_grad = lax.all_to_all(row_grad, "expert", split_axis=0, concat_axis=0, tiled=True)
    pair_rows = (
        returned_grad.reshape(experts * capacity, MODEL_WIDTH)[slot_index]
        .astype(jnp.float32)
        .reshape(total_rows, TOPK, MODEL_WIDTH)
    )
    summed_experts = (
        lax.psum(gate_w_grad.astype(jnp.bfloat16), "dp").astype(jnp.float32),
        lax.psum(up_w_grad.astype(jnp.bfloat16), "dp").astype(jnp.float32),
        lax.psum(down_grad.astype(jnp.bfloat16), "dp").astype(jnp.float32),
    )
    router_wide = router_full.astype(jnp.float32)
    normed_two_grad = jnp.dot(logit_grad, router_wide.T, precision=HIGH_PRECISION) + jnp.sum(
        pair_rows, axis=1
    )
    router_grad = jnp.dot(normed_two.astype(jnp.float32).T, logit_grad, precision=HIGH_PRECISION)
    _, second_pull = jax.vjp(normalize, middle, scale_two)
    middle_norm_grad, second_gain_grad = second_pull(normed_two_grad)
    middle_grad = upstream + middle_norm_grad
    attended_low = middle_grad.astype(jnp.bfloat16)
    out_grad = jnp.einsum("rd,re->de", mixed_out, attended_low, preferred_element_type=jnp.float32)
    mixed_grad = jnp.einsum("re,de->rd", attended_low, out_full, preferred_element_type=jnp.float32)
    mixed_grad = mixed_grad.astype(jnp.bfloat16).reshape(total_rows, QUERY_HEADS, HEAD_SIZE)
    query_parts = []
    key_parts = []
    value_parts = []
    for key_value_head in range(KEY_VALUE_HEADS):
        scores = head_scores(query_rotated, keys_all, visible, key_value_head, query_group_width)
        softmax_out = jnp.exp(scores - log_totals[key_value_head])
        query_part = query_rotated[
            :, key_value_head * query_group_width : (key_value_head + 1) * query_group_width, :
        ]
        key_part = keys_all[:, key_value_head * HEAD_SIZE : (key_value_head + 1) * HEAD_SIZE]
        value_part = values_all[:, key_value_head * HEAD_SIZE : (key_value_head + 1) * HEAD_SIZE]
        grad_part = mixed_grad[
            :, key_value_head * query_group_width : (key_value_head + 1) * query_group_width, :
        ]
        value_parts.append(
            jnp.einsum(
                "grk,rgd->kd",
                softmax_out.astype(jnp.bfloat16),
                grad_part,
                preferred_element_type=jnp.float32,
            )
        )
        attn_grad = jnp.einsum(
            "rgd,kd->grk", grad_part, value_part, preferred_element_type=jnp.float32
        )
        score_grad = softmax_out * (
            attn_grad - jnp.sum(softmax_out * attn_grad, axis=-1, keepdims=True)
        )
        score_low = score_grad.astype(jnp.bfloat16)
        query_parts.append(
            jnp.einsum("grk,kd->rgd", score_low, key_part, preferred_element_type=jnp.float32)
            * HEAD_SIZE ** (-0.5)
        )
        key_parts.append(
            jnp.einsum("grk,rgd->kd", score_low, query_part, preferred_element_type=jnp.float32)
            * HEAD_SIZE ** (-0.5)
        )
    key_total_sum, value_sum = (
        lax.psum_scatter(
            jnp.concatenate(key_parts, axis=1).astype(jnp.bfloat16),
            "dp",
            scatter_dimension=0,
            tiled=True,
        ).astype(jnp.float32),
        lax.psum_scatter(
            jnp.concatenate(value_parts, axis=1).astype(jnp.bfloat16),
            "dp",
            scatter_dimension=0,
            tiled=True,
        ).astype(jnp.float32),
    )
    _, query_pull = jax.vjp(lambda values: apply_rotation(values, query_positions), query_proj)
    _, key_pullback = jax.vjp(lambda values: apply_rotation(values, query_positions), key_projected)
    query_grad = (
        query_pull(jnp.concatenate(query_parts, axis=1))[0]
        .astype(jnp.bfloat16)
        .reshape(total_rows, QUERY_HEADS * HEAD_SIZE)
    )
    key_grad = (
        key_pullback(key_total_sum.reshape(total_rows, KEY_VALUE_HEADS, HEAD_SIZE))[0]
        .astype(jnp.bfloat16)
        .reshape(total_rows, KEY_VALUE_HEADS * HEAD_SIZE)
    )
    value_grad = value_sum.astype(jnp.bfloat16)
    query_w_grad = jnp.einsum(
        "rd,re->de", first_normed, query_grad, preferred_element_type=jnp.float32
    )
    key_w_grad = jnp.einsum("rd,re->de", first_normed, key_grad, preferred_element_type=jnp.float32)
    value_w_grad = jnp.einsum(
        "rd,re->de", first_normed, value_grad, preferred_element_type=jnp.float32
    )
    normed_one_grad = (
        jnp.einsum("re,de->rd", query_grad, query_full, preferred_element_type=jnp.float32)
        + jnp.einsum("re,de->rd", key_grad, key_complete, preferred_element_type=jnp.float32)
        + jnp.einsum("re,de->rd", value_grad, value_complete, preferred_element_type=jnp.float32)
    )
    _, first_pull = jax.vjp(normalize, inputs, scale_one)
    input_norm_grad, first_gain_grad = first_pull(normed_one_grad)
    input_grad = (middle_grad + input_norm_grad)[None]
    shares = (
        lax.psum_scatter(query_w_grad, ("dp", "expert"), scatter_dimension=0, tiled=True),
        lax.psum_scatter(key_w_grad, ("dp", "expert"), scatter_dimension=0, tiled=True),
        lax.psum_scatter(value_w_grad, ("dp", "expert"), scatter_dimension=0, tiled=True),
        lax.psum_scatter(out_grad, ("dp", "expert"), scatter_dimension=0, tiled=True),
        lax.psum_scatter(router_grad, ("dp", "expert"), scatter_dimension=0, tiled=True),
        lax.psum_scatter(first_gain_grad, ("dp", "expert"), scatter_dimension=0, tiled=True),
        lax.psum_scatter(second_gain_grad, ("dp", "expert"), scatter_dimension=0, tiled=True),
    )
    return (
        output,
        input_grad,
        shares[5],
        shares[6],
        shares[0],
        shares[1],
        shares[2],
        shares[3],
        shares[4],
        summed_experts[0],
        summed_experts[1],
        summed_experts[2],
    )


def mm(a, b):
    return jnp.dot(a, b, preferred_element_type=F32)


def mm_nt(a, b):
    return lax.dot_general(a, b, (((1,), (1,)), ((), ())), preferred_element_type=F32)


def mm_tn(a, b):
    return lax.dot_general(a, b, (((0,), (0,)), ((), ())), preferred_element_type=F32)


def gelu_both(value):
    scale = 0.7978845608028654
    square = value * value
    bend = jnp.tanh(scale * value * (1.0 + 0.044715 * square))
    half = 0.5 * (1.0 + bend)
    slope = half + 0.5 * value * (1.0 - bend * bend) * scale * (1.0 + 0.134145 * square)
    return value * half, slope


def expert_kernel(
    n2_ref, gate_ref, dy_ref, gw_ref, uw_ref, dw_ref,
    row_ref, gg_ref, sum_ref, wide_ref, down_ref, landing,
    n2_all, gate_all, dy_buf, dy_cols, hs_all, gl_all, ul_all, own, sib, zin, gg_out, gg_in,
    gate_cols, gg_cols, stage, kept, down_kept,
    n2_send, n2_recv, gt_send, gt_recv, own_send, sib_recv, zin_send, zin_recv,
    gg_send, gg_recv, dy_sem, cols_sem, sum_sem, tile_send, tile_recv, load_sem, keep_sem,
):
    count = lax.axis_size("expert")
    depth = count // 2
    rows = n2_ref.shape[0]
    half = rows // 2
    width = n2_ref.shape[1]
    ff = gw_ref.shape[1]
    me = lax.axis_index("expert")
    z, core = me // 2, me % 2
    sibling = z * 2 + 1 - core
    mine = lax.axis_index("dp")
    y, x = mine // 2, mine % 2
    others = (y * 2 + 1 - x, (1 - y) * 2 + 1 - x, (1 - y) * 2 + x)

    def at(zz):
        return {"expert": zz * 2 + core}

    n2_load = pltpu.make_async_copy(
        n2_ref, n2_all.at[pl.ds(pl.multiple_of(me * rows, 16), rows)], cols_sem
    )
    n2_load.start()
    barrier = pltpu.get_barrier_semaphore()
    for other in range(1, count):
        pl.semaphore_signal(
            barrier, 1, device_id={"expert": lax.rem(me + other, count)}, device_id_type=MESH
        )
    for dp in others:
        pl.semaphore_signal(barrier, 1, device_id={"dp": dp}, device_id_type=MESH)
    pl.semaphore_wait(barrier, count - 1 + len(others))

    def chunk(k):
        return pl.ds(pl.multiple_of(k * rows, 16), rows)

    def piece(k, h):
        return pl.ds(pl.multiple_of(k * rows + h * half, 16), half)

    def part(h):
        return pl.ds(h * half, half)

    def n2_copy(k, h, lane, target):
        return pltpu.make_async_remote_copy(
            n2_all.at[piece(k, h)], n2_all.at[piece(k, h)], n2_send.at[k, h, lane], n2_recv.at[k, h],
            device_id=target, device_id_type=MESH,
        )

    def gt_copy(k, lane, target):
        return pltpu.make_async_remote_copy(
            gate_all.at[k], gate_all.at[k], gt_send.at[k, lane], gt_recv.at[k],
            device_id=target, device_id_type=MESH,
        )

    def send_chunk(k, h, lane, target):
        n2_copy(k, h, lane, target).start()
        if h == 0:
            gt_copy(k, lane, target).start()

    def sent_chunk(k, h, lane, target):
        n2_copy(k, h, lane, target).wait_send()
        if h == 0:
            gt_copy(k, lane, target).wait_send()

    def arrived(k, h):
        n2_copy(k, h, 0, at(z)).wait_recv()
        if h == 0:
            gt_copy(k, 0, at(z)).wait_recv()

    def dy_copy(k, h, w, s):
        return pltpu.make_async_copy(dy_ref.at[k, part(h)], dy_buf.at[w, s], dy_sem.at[w, s])

    def gg_copy(k):
        return pltpu.make_async_remote_copy(
            gg_out.at[k], gg_in.at[me], gg_send.at[k], gg_recv.at[me],
            device_id={"expert": k}, device_id_type=MESH,
        )

    def own_copy(zs, h):
        return pltpu.make_async_remote_copy(
            own.at[2 * zs + 1 - core, part(h)], sib.at[zs, part(h)],
            own_send.at[zs, h], sib_recv.at[zs, h],
            device_id={"expert": sibling}, device_id_type=MESH,
        )

    def zin_copy(zd, h, nxt, slot):
        return pltpu.make_async_remote_copy(
            own.at[2 * zd + core, part(h)], zin.at[slot, part(h)],
            zin_send.at[zd, h], zin_recv.at[slot, h],
            device_id=at(nxt), device_id_type=MESH,
        )

    n2_load.wait()
    gate_all[me] = gate_ref[...]

    for h in range(2):

        @pl.when(z < depth - 1)
        def _():
            send_chunk(me, h, 0, at(z + 1))

        @pl.when(z > 0)
        def _():
            send_chunk(me, h, 1, at(z - 1))

        send_chunk(me, h, 2, {"expert": sibling})

    row_ids = lax.broadcasted_iota(jnp.int32, (count, gate_ref.shape[1]), 0)

    def hidden_part(k, h, w, s):
        r = piece(k, h)
        place = 2 * s + w
        if h == 0:
            gate_row = jnp.sum(jnp.where(row_ids == me, gate_all[k], 0.0), axis=0, keepdims=True)
            gate_cols[place] = jnp.transpose(jnp.broadcast_to(gate_row, (128, gate_row.shape[1])))
            gg_cols[place, rows:, :] = jnp.zeros((gate_ref.shape[1] - rows, 128), F32)
        gate_col = gate_cols[place, part(h), :]
        tile = 256
        gate_wide = jnp.concatenate([gate_col] * (tile // 128), axis=1)
        total = jnp.zeros((half, 128), F32)
        for j in range(ff // tile):
            cols = slice(j * tile, (j + 1) * tile)
            back = mm_nt(dy_buf[w, s], dw_ref[cols, :])
            gate_pre = mm(n2_all[r, :], gw_ref[:, cols])
            up_pre = mm(n2_all[r, :], uw_ref[:, cols])
            act, slope = gelu_both(gate_pre)
            hidden = act * up_pre
            hs_all[r, cols] = (gate_wide * hidden).astype(BF)
            product = hidden * back
            for i in range(tile // 128):
                total = total + product[:, i * 128 : (i + 1) * 128]
            back = gate_wide * back
            gl_all[r, cols] = (back * up_pre * slope).astype(BF)
            ul_all[r, cols] = (back * act).astype(BF)
        gg_cols[place, part(h), :] = total
        if h == 1:
            gg_row = jnp.sum(jnp.transpose(gg_cols[place]), axis=0, keepdims=True)
            gg_tile = jnp.where(row_ids == me, gg_row, 0.0)
            gg_out[k] = gg_tile

            @pl.when(k == me)
            def _():
                gg_in[me] = gg_tile

            @pl.when(k != me)
            def _():
                gg_copy(k).start()

    def row_part(k, h):
        r = piece(k, h)
        wide = 512
        for j in range(width // wide):
            cols = slice(j * wide, (j + 1) * wide)
            own[k, part(h), cols] = (
                mm_nt(gl_all[r, :], gw_ref[cols, :]) + mm_nt(ul_all[r, :], uw_ref[cols, :])
            ).astype(BF)

    block = 16

    def combine(zd, h, with_in):
        def step(i, _):
            rr = pl.ds(pl.multiple_of(h * half + i * block, block), block)
            value = own[2 * zd + core, rr, :].astype(F32) + sib[zd, rr, :].astype(F32)
            if with_in:
                value = value + zin[zd, rr, :].astype(F32)
            own[2 * zd + core, rr, :] = value.astype(BF)
            return 0

        lax.fori_loop(0, half // block, step, 0)

    def slot_for(zd, nxt):
        return jnp.where((nxt == zd) & (nxt < z), depth, zd)

    def pass_on(zd, h, nxt, with_in):
        own_copy(zd, h).wait_recv()
        if with_in:
            zin_copy(zd, h, nxt, zd).wait_recv()
        combine(zd, h, with_in)
        zin_copy(zd, h, nxt, slot_for(zd, nxt)).start()

    quarter = width // 4
    cut = ff // 2
    order = (others[1], others[0], others[2], mine)

    def owner(j):
        return jnp.where(
            j == 0, order[0], jnp.where(j == 1, order[1], jnp.where(j == 2, order[2], mine))
        )

    def cols_of(dp):
        return pl.ds(pl.multiple_of(dp * quarter, 128), quarter)

    def tile_slot(kind, j):
        if kind == 0:
            return stage.at[j]
        return (gl_all, ul_all)[kind - 1].at[pl.ds(pl.multiple_of(j * quarter, 16), quarter)]

    sides = (slice(0, cut), slice(cut, ff))
    ends = ({"dp": others[0]}, {"dp": others[2]})
    hops = ((0, 0, 1, 0), (0, 1, 1, 1), (1, 0, 0, 0), (2, 1, 0, 1), (2, 0, 2, 1), (1, 1, 2, 0))

    def hop(kind, n):
        j, side, slot, way = hops[n]
        return pltpu.make_async_remote_copy(
            tile_slot(kind, j).at[:, sides[side]], landing.at[kind, slot, :, sides[side]],
            tile_send.at[kind, n], tile_recv.at[kind, slot, side],
            device_id=ends[way], device_id_type=MESH,
        )

    def col_copy(j):
        return pltpu.make_async_copy(dy_ref.at[:, :, cols_of(owner(j))], dy_cols, cols_sem)

    def tiles(kind, low, high):
        def step(j, _):
            cols = cols_of(owner(j))
            if kind == 2:
                col_copy(j).wait()
                tile = mm_tn(dy_cols[...].reshape(count * rows, quarter), hs_all[...])

                @pl.when(j < 3)
                def _():
                    col_copy(j + 1).start()
            else:
                tile = mm_tn(n2_all[:, cols], (gl_all, ul_all)[kind][...])
            tile = tile.astype(BF)

            @pl.when(j < 3)
            def _():
                tile_slot(kind, j)[...] = tile

            for n in range(4):

                @pl.when(j == hops[n][0])
                def _():
                    hop(kind, n).start()

            @pl.when(j == 3)
            def _():
                kept[kind] = tile

            return 0

        lax.fori_loop(low, high, step, 0)

    def spare(kind, i):
        return (gl_all, ul_all, gl_all)[kind].at[pl.ds(6 * quarter, quarter)]

    def second_leg(kind):
        for side in range(2):
            n = side
            hop(kind, n).wait_recv()
        load = pltpu.make_async_copy(landing.at[kind, 1], spare(kind, 6), load_sem.at[kind, 2])
        load.start()
        load.wait()
        for n in (4, 5):
            j, side, _, _ = hops[n]

            def step(i, _):
                rr = pl.ds(pl.multiple_of(i * 32, 32), 32)
                into = tile_slot(kind, j)
                value = into[rr, sides[side]].astype(F32) + spare(kind, 6)[rr, sides[side]].astype(F32)
                into[rr, sides[side]] = value.astype(BF)
                return 0

            lax.fori_loop(0, quarter // 32, step, 0)
            hop(kind, n).start()

    def by_distance(d, _):
        left, right = z - d, z + d
        has_left, has_right = left >= 0, (right < depth) & (d > 0)

        def other_chunk(zs):
            return 2 * zs + 1 - core

        for h in range(2):
            for s, zs, there in ((0, left, has_left), (1, right, has_right)):

                @pl.when(there)
                def _():
                    dy_copy(other_chunk(zs), h, 0, s).start()
                    dy_copy(2 * zs + core, h, 1, s).start()

            @pl.when(has_left & (d > 0))
            def _():
                k = 2 * left + core
                arrived(k, h)

                @pl.when(z < depth - 1)
                def _():
                    send_chunk(k, h, 0, at(z + 1))

                send_chunk(k, h, 2, {"expert": sibling})

            @pl.when(has_right)
            def _():
                k = 2 * right + core
                arrived(k, h)

                @pl.when(z > 0)
                def _():
                    send_chunk(k, h, 1, at(z - 1))

                send_chunk(k, h, 2, {"expert": sibling})

            def side(s, _):
                zs = jnp.where(s == 0, left, right)

                @pl.when(jnp.where(s == 0, has_left, has_right))
                def _():
                    def first(w, _):
                        k = 2 * zs + jnp.where(w == 0, 1 - core, core)

                        @pl.when(w == 0)
                        def _():
                            arrived(k, h)

                        dy_copy(k, h, w, s).wait()
                        hidden_part(k, h, w, s)
                        return 0

                    lax.fori_loop(0, 2, first, 0)
                    if h == 1:
                        @pl.when(d == jnp.maximum(z, depth - 1 - z))
                        def _():
                            tiles(0, 0, 3)

                    def second(w, _):
                        row_part(2 * zs + jnp.where(w == 0, 1 - core, core), h)

                        @pl.when(w == 0)
                        def _():
                            own_copy(zs, h).start()

                        return 0

                    lax.fori_loop(0, 2, second, 0)

                    @pl.when((d > 0) & ((z == 0) | (z == depth - 1)))
                    def _():
                        pass_on(zs, h, jnp.where(z == 0, 1, depth - 2), False)

                return 0

            lax.fori_loop(0, 2, side, 0)
        return 0

    col_copy(0).start()
    lax.fori_loop(0, depth, by_distance, 0)

    def sum_copy(k, slot):
        return pltpu.make_async_copy(own.at[slot], sum_ref.at[k], sum_sem.at[slot])

    def sums(low, high):
        def step(i, _):
            slot = 2 * lax.rem(i, depth) + 1 - core

            @pl.when(i < depth)
            def _():
                for h in range(2):
                    own_copy(i, h).wait_send()

            @pl.when(i >= depth)
            def _():
                sum_copy(i, slot).wait()

            wide = 512
            for j in range(width // wide):
                cols = slice(j * wide, (j + 1) * wide)
                own[slot, :, cols] = mm(hs_all[chunk(i), :], dw_ref[:, cols]).astype(BF)
            sum_copy(i, slot).start()
            return 0

        lax.fori_loop(low, high, step, 0)

    def flow(r, first, h):
        right = (z < depth - 1 - z) if first else (z >= depth - 1 - z)
        zd = jnp.where(right, r, depth - 1 - r)
        valid = jnp.where(right, (z < zd) & (z > 0), (z > zd) & (z < depth - 1))

        @pl.when(valid)
        def _():
            pass_on(zd, h, jnp.where(right, z + 1, z - 1), True)

    eighth = count // 4
    jobs = [
        lambda: tiles(0, 3, 4),
        lambda: tiles(1, 0, 2),
        lambda: tiles(1, 2, 4),
        lambda: second_leg(0),
        lambda: tiles(2, 0, 2),
        lambda: tiles(2, 2, 4),
        lambda: second_leg(1),
        *[lambda i=i: sums(i * eighth, (i + 1) * eighth) for i in range(4)],
        lambda: second_leg(2),
    ]
    for r in range(2, depth):
        for first in (True, False):
            for h in range(2):
                if first or r == depth - 1:
                    for _ in range(2):
                        if jobs:
                            jobs.pop(0)()
                flow(r, first, h)
    while jobs:
        jobs.pop(0)()

    for h in range(2):
        own_copy(z, h).wait_recv()

        @pl.when(z > 0)
        def _():
            zin_copy(z, h, z, z).wait_recv()

        @pl.when(z < depth - 1)
        def _():
            zin_copy(z, h, z, depth).wait_recv()

    def last(i, _):
        rr = pl.ds(pl.multiple_of(i * block, block), block)
        row_ref[rr, :] = own[me, rr, :].astype(F32) + sib[z, rr, :].astype(F32)

        @pl.when(z > 0)
        def _():
            row_ref[rr, :] += zin[z, rr, :].astype(F32)

        @pl.when(z < depth - 1)
        def _():
            row_ref[rr, :] += zin[depth, rr, :].astype(F32)

        return 0

    lax.fori_loop(0, rows // block, last, 0)

    for e in range(count):

        @pl.when(e != me)
        def _():
            pltpu.make_async_remote_copy(
                gg_out.at[e], gg_in.at[e], gg_send.at[e], gg_recv.at[e],
                device_id={"expert": e}, device_id_type=MESH,
            ).wait_recv()

    gg_ref[...] = jnp.sum(gg_in[...], axis=0)

    def tile_load(kind, i):
        into = (gl_all, ul_all, hs_all)[kind]
        return pltpu.make_async_copy(
            landing.at[kind, 2 * i], into.at[pl.ds((3 + i) * quarter, quarter)], load_sem.at[kind, i]
        )

    keeps = [
        pltpu.make_async_copy(kept.at[pl.ds(0, 2)], wide_ref, keep_sem.at[0]),
        pltpu.make_async_copy(down_kept, down_ref, keep_sem.at[1]),
    ]
    for kind in range(3):
        for n in (2, 3, 4, 5):
            hop(kind, n).wait_recv()
        for i in range(2):
            tile_load(kind, i).start()
    for kind in range(3):
        for i in range(2):
            tile_load(kind, i).wait()
        into = (gl_all, ul_all, hs_all)[kind]

        def add_up(i, _):
            rr = pl.ds(pl.multiple_of(i * 128, 128), 128)
            total = kept[kind, rr, :].astype(F32)
            for j in range(2):
                total = total + into[pl.ds(pl.multiple_of((3 + j) * quarter + i * 128, 128), 128), :].astype(F32)
            if kind == 2:
                down_kept[:, rr] = jnp.transpose(total).astype(BF)
            else:
                kept[kind, rr, :] = total.astype(BF)
            return 0

        lax.fori_loop(0, quarter // 128, add_up, 0)
        if kind > 0:
            keeps[kind - 1].start()

    for e in range(count):

        @pl.when(e != me)
        def _():
            gg_copy(e).wait_send()

        zs = e // 2

        for h in range(2):

            @pl.when(((e == me) | ((zs < z) & (e % 2 == core))) & (z < depth - 1))
            def _():
                sent_chunk(e, h, 0, at(z + 1))

            @pl.when(((e == me) | ((zs > z) & (e % 2 == core))) & (z > 0))
            def _():
                sent_chunk(e, h, 1, at(z - 1))

            @pl.when(e % 2 == core)
            def _():
                sent_chunk(e, h, 2, {"expert": sibling})

    for zd in range(depth):
        sum_copy(zd, 2 * zd + 1 - core).wait()
        for h in range(2):

            @pl.when(zd != z)
            def _():
                zin_copy(zd, h, z, zd).wait_send()

    for kind in range(3):
        for n in range(len(hops)):
            hop(kind, n).wait_send()
    for keep in keeps:
        keep.wait()


def expert_pass(n2, gate_rows, dy_all, gate_w, up_w, down_w):
    count = lax.axis_size("expert")
    depth = count // 2
    rows, width = n2.shape
    ff = gate_w.shape[1]
    lanes = gate_rows.shape[1]
    dma = pltpu.SemaphoreType.DMA
    vmem = pl.BlockSpec(memory_space=pltpu.VMEM)
    anywhere = pl.BlockSpec(memory_space=pl.ANY)
    outs = (
        jax.ShapeDtypeStruct((rows, width), F32),
        jax.ShapeDtypeStruct((count, lanes), F32),
        jax.ShapeDtypeStruct((count, rows, width), BF),
        jax.ShapeDtypeStruct((2, width // 4, ff), BF),
        jax.ShapeDtypeStruct((ff, width // 4), BF),
        jax.ShapeDtypeStruct((3, 3, width // 4, ff), BF),
    )
    return pl.pallas_call(
        expert_kernel,
        name="expert_pass",
        out_shape=outs,
        in_specs=[anywhere, vmem, anywhere, vmem, vmem, vmem],
        out_specs=(vmem, vmem, anywhere, anywhere, anywhere, anywhere),
        scratch_shapes=[
            pltpu.VMEM((count * rows, width), BF),
            pltpu.VMEM((count, count, lanes), F32),
            pltpu.VMEM((2, 2, rows // 2, width), BF),
            pltpu.VMEM((count, rows, width // 4), BF),
            pltpu.VMEM((count * rows, ff), BF),
            pltpu.VMEM((count * rows, ff), BF),
            pltpu.VMEM((count * rows, ff), BF),
            pltpu.VMEM((count, rows, width), BF),
            pltpu.VMEM((depth, rows, width), BF),
            pltpu.VMEM((depth + 1, rows, width), BF),
            pltpu.VMEM((count, count, lanes), F32),
            pltpu.VMEM((count, count, lanes), F32),
            pltpu.VMEM((4, lanes, 128), F32),
            pltpu.VMEM((4, lanes, 128), F32),
            pltpu.VMEM((3, width // 4, ff), BF),
            pltpu.VMEM((3, width // 4, ff), BF),
            pltpu.VMEM((ff, width // 4), BF),
            dma((count, 2, 3)), dma((count, 2)), dma((count, 3)), dma((count,)),
            dma((depth, 2)), dma((depth, 2)), dma((depth, 2)), dma((depth + 1, 2)),
            dma((count,)), dma((count,)), dma((2, 2)), dma, dma((count,)), dma((3, 6)), dma((3, 3, 2)),
            dma((3, 3)), dma((2,)),
        ],
        compiler_params=pltpu.CompilerParams(
            collective_id=2, has_side_effects=True, vmem_limit_bytes=62 * 2**20
        ),
        cost_estimate=pl.CostEstimate(
            flops=18 * count * rows * width * ff, bytes_accessed=60 * 2**20, transcendentals=0
        ),
    )(n2, gate_rows, dy_all, gate_w, up_w, down_w)


def greet(depth, z, at, targets):
    barrier = pltpu.get_barrier_semaphore()
    for target in targets:
        pl.semaphore_signal(barrier, 1, device_id=target, device_id_type=MESH)

    @pl.when(z > 0)
    def _():
        pl.semaphore_signal(barrier, 1, device_id=at(z - 1), device_id_type=MESH)

    @pl.when(z < depth - 1)
    def _():
        pl.semaphore_signal(barrier, 1, device_id=at(z + 1), device_id_type=MESH)

    ends = (z > 0).astype(jnp.int32) + (z < depth - 1).astype(jnp.int32)
    pl.semaphore_wait(barrier, len(targets) + ends)


def attention_kernel(
    x_ref, wq_ref, wk_ref, wv_ref, ws_ref, wo_ref, freq_ref, parent_ref, hits_ref, dy_ref,
    n1_ref, q_ref, kv_ref, mixed_ref, lse_ref, middle_ref, n2_ref, gate_ref, cos_ref, sin_ref,
    bias_ref, w_out, dy_all,
    w, n1, q, kv, mixed, bias,
    z_send, z_recv, x_send, x_recv, y_send, y_recv, a_send, a_recv, b_send, b_recv, s_send, s_recv,
    kx_send, kx_recv, ky_send, ky_recv, ka_send, ka_recv, kb_send, kb_recv, dy_send, dy_recv, out_sem, keep_sem, dy_sem,
):
    count = lax.axis_size("expert")
    depth = count // 2
    shard, total = wq_ref.shape[0], w.shape[1]
    rows, width = x_ref.shape
    heads = q.shape[1] // HEAD_SIZE
    kv_width = kv.shape[1]
    groups = kv_width // (2 * HEAD_SIZE)
    group = heads // groups
    wide = heads * HEAD_SIZE
    qkv_width = wide + kv_width
    split = qkv_width + 128
    me, mine = lax.axis_index("expert"), lax.axis_index("dp")
    z, core = me // 2, me % 2
    y, x = mine // 2, mine % 2
    xn, yn, diag = y * 2 + 1 - x, (1 - y) * 2 + x, (1 - y) * 2 + 1 - x
    sibling = {"expert": z * 2 + 1 - core}

    def at(zz):
        return {"expert": zz * 2 + core}

    greet(depth, z, at, (sibling, {"dp": xn}, {"dp": yn}))

    def remote(src, dst, send, recv, target):
        return pltpu.make_async_remote_copy(
            src, dst, send, recv, device_id=target, device_id_type=MESH
        )

    bounds = ((wide, split), (0, wide), (split, total))
    cuts = tuple(low + ((high - low) // 128 + 1) // 2 * 128 for low, high in bounds)

    def place(dp, zz, cc):
        return pl.ds(pl.multiple_of((dp * count + 2 * zz + cc) * shard, 16), shard)

    def w_copy(dp, zz, low, high, send, recv, target, cc=core):
        ref = w.at[place(dp, zz, cc), pl.ds(low, high - low)]
        return remote(ref, ref, send, recv, target)

    def z_copy(p, zz, lane, target):
        return w_copy(mine, zz, *bounds[p], z_send.at[p, zz, lane], z_recv.at[p, zz], target)

    def x_copy(p, zz, dp):
        return w_copy(dp, zz, *bounds[p], x_send.at[p, zz], x_recv.at[p, zz], {"dp": xn})

    def y_copy(p, zz, dp):
        return w_copy(dp, zz, *bounds[p], y_send.at[p, zz], y_recv.at[p, zz], {"dp": yn})

    def a_copy(p, zz, dp):
        return w_copy(dp, zz, bounds[p][0], cuts[p], a_send.at[p, zz], a_recv.at[p, zz], {"dp": yn})

    def b_copy(p, zz, dp):
        return w_copy(dp, zz, cuts[p], bounds[p][1], b_send.at[p, zz], b_recv.at[p, zz], {"dp": xn})

    def s_copy(p, dp, zz, cc=core):
        return w_copy(dp, zz, *bounds[p], s_send.at[p, dp, zz], s_recv.at[p, dp, zz], sibling, cc)

    def spread(p, zz):
        x_copy(p, zz, mine).start()
        y_copy(p, zz, mine).start()
        s_copy(p, mine, zz).start()

    def on_sides(d, action):
        @pl.when(z - d >= 0)
        def _():
            action(z - d, True)

        if d > 0:

            @pl.when(z + d < depth)
            def _():
                action(z + d, False)

    def z_step(p, d):
        if d == 0:

            @pl.when(z < depth - 1)
            def _():
                z_copy(p, z, 0, at(z + 1)).start()

            @pl.when(z > 0)
            def _():
                z_copy(p, z, 1, at(z - 1)).start()

            return

        def action(zz, from_left):
            z_copy(p, zz, 0, at(z)).wait_recv()
            if from_left:

                @pl.when(z < depth - 1)
                def _():
                    z_copy(p, zz, 0, at(z + 1)).start()
            else:

                @pl.when(z > 0)
                def _():
                    z_copy(p, zz, 1, at(z - 1)).start()

        on_sides(d, action)

    def spread_step(p, d):
        on_sides(d, lambda zz, _: spread(p, zz))

    def xy_step(p, d):
        def action(zz, _):
            x_copy(p, zz, xn).wait_recv()
            a_copy(p, zz, xn).start()
            s_copy(p, xn, zz).start()
            y_copy(p, zz, yn).wait_recv()
            b_copy(p, zz, yn).start()
            s_copy(p, yn, zz).start()

        on_sides(d, action)

    def diag_step(p, d):
        def action(zz, _):
            a_copy(p, zz, diag).wait_recv()
            b_copy(p, zz, diag).wait_recv()
            s_copy(p, diag, zz).start()

        on_sides(d, action)

    def all_here(p):
        for dp in range(4):
            for zz in range(depth):
                s_copy(p, dp, zz, 1 - core).wait_recv()

    def all_sent(p):
        for zz in range(depth):

            @pl.when((zz <= z) & (z < depth - 1))
            def _():
                z_copy(p, zz, 0, at(z)).wait_send()

            @pl.when((zz >= z) & (z > 0))
            def _():
                z_copy(p, zz, 1, at(z)).wait_send()

            x_copy(p, zz, mine).wait_send()
            y_copy(p, zz, mine).wait_send()
            a_copy(p, zz, xn).wait_send()
            b_copy(p, zz, yn).wait_send()
            for dp in range(4):
                s_copy(p, dp, zz).wait_send()

    def dy_copy(k, lane, target):
        return remote(dy_all.at[k], dy_all.at[k], dy_send.at[k, lane], dy_recv.at[k], target)

    def dy_own(lane, target):
        return remote(dy_ref, dy_all.at[me], dy_send.at[me, lane], dy_recv.at[me], target)

    dy_keep = pltpu.make_async_copy(dy_ref, dy_all.at[me], dy_sem)

    def dy_step(d):
        if d == 0:
            dy_own(2, sibling).start()
            dy_keep.start()

            @pl.when(z < depth - 1)
            def _():
                dy_own(0, at(z + 1)).start()

            @pl.when(z > 0)
            def _():
                dy_own(1, at(z - 1)).start()

            return

        def action(zz, from_left):
            k = 2 * zz + core
            dy_copy(k, 0, sibling).wait_recv()
            if from_left:

                @pl.when(z < depth - 1)
                def _():
                    dy_copy(k, 0, at(z + 1)).start()
            else:

                @pl.when(z > 0)
                def _():
                    dy_copy(k, 1, at(z - 1)).start()

            dy_copy(k, 2, sibling).start()

        on_sides(d, action)

    def dy_end():
        dy_keep.wait()
        for zz in range(depth):
            dy_copy(2 * zz + 1 - core, 2, sibling).wait_recv()
            k = 2 * zz + core
            dy_copy(k, 2, sibling).wait_send()

            @pl.when((zz <= z) & (z < depth - 1))
            def _():
                dy_copy(k, 0, sibling).wait_send()

            @pl.when((zz >= z) & (z > 0))
            def _():
                dy_copy(k, 1, sibling).wait_send()

    home = place(mine, z, core)
    w[home, 0:wide] = wq_ref[...]
    for g in range(groups):
        low, head = wide + 2 * g * HEAD_SIZE, slice(g * HEAD_SIZE, (g + 1) * HEAD_SIZE)
        w[home, low : low + HEAD_SIZE] = wk_ref[:, head]
        w[home, low + HEAD_SIZE : low + 2 * HEAD_SIZE] = wv_ref[:, head]
    w[home, qkv_width:split] = ws_ref[...]
    w[home, split:total] = wo_ref[...]
    z_step(0, 0)
    spread_step(0, 0)

    blocks = parent_ref.shape[1]
    trunk = blocks - BRANCHES - LEAVES
    ids = mine * rows + lax.broadcasted_iota(jnp.int32, (rows, 1), 0)
    query_block = lax.div(ids, SEG)
    level = jnp.minimum(query_block, trunk) + (query_block >= trunk + BRANCHES).astype(jnp.int32)
    positions = (level * SEG + lax.rem(ids, SEG)).astype(F32)
    angles = positions * freq_ref[...]
    cos_ref[...] = jnp.cos(angles)
    turned = lax.broadcasted_iota(jnp.int32, angles.shape, 1) < HEAD_SIZE // 2
    sine = jnp.sin(angles)
    sin_ref[...] = jnp.where(turned, -sine, sine)
    z_step(0, 1)
    spread_step(0, 1)
    xy_step(0, 0)
    block_ids = lax.broadcasted_iota(jnp.int32, (rows, blocks), 1)
    parent = jnp.sum(jnp.where(block_ids == query_block, parent_ref[...], 0), axis=1, keepdims=True)
    above = jnp.where(query_block >= trunk + BRANCHES, parent, query_block)
    keys = bias.shape[1] // 128

    def visible(i, _):
        cols = pl.ds(pl.multiple_of(i * 128, 128), 128)
        key_ids = i * 128 + lax.broadcasted_iota(jnp.int32, (rows, 128), 1)
        key_block = lax.div(key_ids, SEG)
        related = (key_block < trunk) | (key_block == query_block) | (key_block == above)
        bias[:, cols] = jnp.where(related & (key_ids <= ids), 0.0, NEGATIVE)
        return 0

    z_step(0, 2)
    spread_step(0, 2)
    z_step(1, 0)
    xy_step(0, 1)
    lax.fori_loop(0, keys, visible, 0)
    z_step(0, 3)
    spread_step(0, 3)
    z_step(2, 0)
    spread_step(1, 0)
    z_step(1, 1)
    spread_step(1, 1)
    xy_step(0, 2)
    z_step(2, 1)
    xy_step(0, 3)
    z_step(1, 2)
    spread_step(1, 2)
    for d in range(depth):
        diag_step(0, d)
    z_step(2, 2)
    xy_step(1, 0)
    z_step(1, 3)
    spread_step(1, 3)
    z_step(2, 3)
    dy_step(0)
    all_here(0)

    def keep(p):
        low, high = bounds[p]
        return pltpu.make_async_copy(
            w.at[:, pl.ds(low, high - low)], w_out.at[:, pl.ds(low, high - low)], keep_sem.at[p]
        )

    keep(0).start()
    small = jnp.transpose(w[:, qkv_width:split].astype(F32))
    experts = hits_ref.shape[0]
    gain_one, gain_two = small[experts : experts + 1], small[experts + 1 : experts + 2]

    block = 32

    def first_norm(i, _):
        rr = pl.ds(pl.multiple_of(i * block, block), block)
        value = x_ref[rr, :].astype(F32)
        scale = lax.rsqrt(jnp.mean(value * value, axis=1, keepdims=True) + EPS)
        n1[rr, :] = (value * scale * gain_one).astype(BF)
        return 0

    lax.fori_loop(0, rows // block, first_norm, 0)

    def turn(value):
        return value * cos_ref[...] + pltpu.roll(value, HEAD_SIZE // 2, 1) * sin_ref[...]

    own = pl.ds(pl.multiple_of(mine * rows, 16), rows)
    projected = mm(n1[...], w[:, wide:qkv_width])
    for g in range(groups):
        low = 2 * g * HEAD_SIZE
        kv[own, low : low + HEAD_SIZE] = turn(projected[:, low : low + HEAD_SIZE]).astype(BF)
        kv[own, low + HEAD_SIZE : low + 2 * HEAD_SIZE] = projected[
            :, low + HEAD_SIZE : low + 2 * HEAD_SIZE
        ].astype(BF)

    def kv_copy(g, dp, low, high, send, recv, target):
        ref = kv.at[
            pl.ds(pl.multiple_of(dp * rows, 16), rows),
            pl.ds((2 * g + low) * HEAD_SIZE, (high - low) * HEAD_SIZE),
        ]
        return remote(ref, ref, send.at[g], recv.at[g], target)

    def kx(g, dp):
        return kv_copy(g, dp, 0, 2, kx_send, kx_recv, {"dp": xn})

    def ky(g, dp):
        return kv_copy(g, dp, 0, 2, ky_send, ky_recv, {"dp": yn})

    def ka(g, dp):
        return kv_copy(g, dp, 0, 1, ka_send, ka_recv, {"dp": yn})

    def kb(g, dp):
        return kv_copy(g, dp, 1, 2, kb_send, kb_recv, {"dp": xn})

    def kv_on(g):
        kx(g, xn).wait_recv()
        ka(g, xn).start()
        ky(g, yn).wait_recv()
        kb(g, yn).start()

    def kv_here(g):
        ka(g, diag).wait_recv()
        kb(g, diag).wait_recv()

    for g in range(groups):
        kx(g, mine).start()
        ky(g, mine).start()
    xy_step(1, 1)
    xy_step(1, 2)
    kv_on(0)
    xy_step(1, 3)
    kv_on(1)
    for d in range(depth):
        diag_step(1, d)
        spread_step(2, d)
    kv_here(0)
    all_here(1)
    keep(1).start()
    dy_step(1)

    def project(h, _):
        cols = pl.ds(pl.multiple_of(h * 2 * HEAD_SIZE, 2 * HEAD_SIZE), 2 * HEAD_SIZE)
        value = mm(n1[...], w[:, cols])
        q[:, cols] = jnp.concatenate(
            [turn(value[:, :HEAD_SIZE]), turn(value[:, HEAD_SIZE:])], axis=1
        ).astype(BF)
        return 0

    lax.fori_loop(0, heads // 2, project, 0)
    later = [
        lambda: xy_step(2, 0),
        lambda: xy_step(2, 1),
        lambda: xy_step(2, 2),
        lambda: xy_step(2, 3),
        lambda: kv_here(1),
        lambda: (diag_step(2, 0), diag_step(2, 1)),
        lambda: (diag_step(2, 2), diag_step(2, 3)),
    ]
    lse_ref[...] = jnp.zeros_like(lse_ref)
    lanes = lax.broadcasted_iota(jnp.int32, lse_ref.shape, 1)

    def attend(h, _):
        for i, job in enumerate(later):
            pl.when(h == i)(lambda job=job: (job(), None)[1])
        g = h // group
        cols = pl.ds(pl.multiple_of(h * HEAD_SIZE, HEAD_SIZE), HEAD_SIZE)
        k_cols = pl.ds(pl.multiple_of(g * 2 * HEAD_SIZE, HEAD_SIZE), HEAD_SIZE)
        v_cols = pl.ds(pl.multiple_of(g * 2 * HEAD_SIZE + HEAD_SIZE, HEAD_SIZE), HEAD_SIZE)
        scores = mm_nt(q[:, cols], kv[:, k_cols]) * (HEAD_SIZE**-0.5 * LOG2E) + bias[...]
        top = jnp.max(scores, axis=1, keepdims=True)
        power = jnp.exp2(scores - top)
        sums = jnp.sum(power, axis=1, keepdims=True)
        mixed[:, cols] = (mm(power.astype(BF), kv[:, v_cols]) / sums).astype(BF)
        lse_ref[...] = jnp.where(lanes == h, top + jnp.log2(sums), lse_ref[...])
        return 0

    lax.fori_loop(0, heads, attend, 0)
    keeps = [
        pltpu.make_async_copy(src, dst, out_sem.at[i])
        for i, (src, dst) in enumerate(
            ((n1, n1_ref), (q, q_ref), (kv, kv_ref), (mixed, mixed_ref), (bias, bias_ref))
        )
    ]
    for copy in keeps:
        copy.start()
    all_here(2)
    keep(2).start()
    dy_step(2)
    tile = 512

    def project_out(i, _):
        cols = pl.ds(pl.multiple_of(i * tile, tile), tile)
        w_cols = pl.ds(pl.multiple_of(split + i * tile, 128), tile)
        middle_ref[:, cols] = x_ref[:, cols].astype(F32) + mm(mixed[...], w[:, w_cols])
        return 0

    lax.fori_loop(0, width // tile, project_out, 0)

    def second_norm(i, _):
        rr = pl.ds(pl.multiple_of(i * block, block), block)
        value = middle_ref[rr, :]
        scale = lax.rsqrt(jnp.mean(value * value, axis=1, keepdims=True) + EPS)
        n2_ref[rr, :] = (value * scale * gain_two).astype(BF)
        return 0

    lax.fori_loop(0, rows // block, second_norm, 0)
    logits = mm_nt(small.astype(BF), n2_ref[...])[:experts]
    hits = hits_ref[...] > 0.5
    chosen = jnp.where(hits, logits, NEGATIVE)
    power = jnp.where(hits, jnp.exp(chosen - jnp.max(chosen, axis=0, keepdims=True)), 0.0)
    gate_ref[...] = jnp.zeros_like(gate_ref)
    gate_ref[:, :rows] = power / jnp.sum(power, axis=0, keepdims=True)

    dy_step(3)
    dy_end()
    for g in range(groups):
        kx(g, mine).wait_send()
        ky(g, mine).wait_send()
        ka(g, xn).wait_send()
        kb(g, yn).wait_send()
    for p in range(3):
        all_sent(p)
        keep(p).wait()
    for copy in keeps:
        copy.wait()


def attention_pass(x, shards, freq, parent, hits, dy):
    count = lax.axis_size("expert")
    depth = count // 2
    rows, width = x.shape
    lanes = rows + -rows % 128
    shard = shards[0].shape[0]
    devices = 4 * count
    wide = shards[0].shape[1]
    kv_width = 2 * shards[1].shape[1]
    dma = pltpu.SemaphoreType.DMA
    vmem = pl.BlockSpec(memory_space=pltpu.VMEM)
    anywhere = pl.BlockSpec(memory_space=pl.ANY)
    shape = jax.ShapeDtypeStruct
    parts = 3
    pair = dma((parts, depth))
    groups = kv_width // (2 * HEAD_SIZE)
    tree = 4 * rows
    total = kv_width + sum(part.shape[1] for part in (shards[0], *shards[3:]))
    return pl.pallas_call(
        attention_kernel,
        name="attention_pass",
        out_shape=(
            shape((rows, width), BF),
            shape((rows, wide), BF),
            shape((tree, kv_width), BF),
            shape((rows, wide), BF),
            shape((rows, 128), F32),
            shape((rows, width), F32),
            shape((rows, width), BF),
            shape((hits.shape[0], lanes), F32),
            shape((rows, HEAD_SIZE), F32),
            shape((rows, HEAD_SIZE), F32),
            shape((rows, tree), F32),
            shape((devices * shard, total), BF),
            shape((count, rows, width), BF),
        ),
        in_specs=[vmem] * 9 + [anywhere],
        out_specs=(anywhere,) * 4 + (vmem,) * 6 + (anywhere,) * 3,
        scratch_shapes=[
            pltpu.VMEM((devices * shard, total), BF),
            pltpu.VMEM((rows, width), BF),
            pltpu.VMEM((rows, wide), BF),
            pltpu.VMEM((tree, kv_width), BF),
            pltpu.VMEM((rows, wide), BF),
            pltpu.VMEM((rows, tree), F32),
            dma((parts, depth, 2)), pair, pair, pair, pair, pair, pair, pair, pair, pair,
            dma((parts, 4, depth)), dma((parts, 4, depth)),
            *[dma((groups,)) for _ in range(8)],
            dma((count, 3)), dma((count,)), dma((5,)), dma((parts,)), dma,
        ],
        compiler_params=pltpu.CompilerParams(
            collective_id=1, has_side_effects=True, vmem_limit_bytes=56 * 2**20
        ),
        cost_estimate=pl.CostEstimate(
            flops=10**10, bytes_accessed=300 * 2**20, transcendentals=0
        ),
    )(x, *shards, freq, parent, hits, dy)


def backward_kernel(
    x_ref, dy_ref, gate_ref, gg_ref, n1_ref, q_ref, kv_ref, mixed_ref, n2_ref, lse_ref,
    cos_ref, sin_ref, bias_ref, middle_any, row_ref, w_full, wide_ref, down_ref,
    tok_ref, share_ref, wide_all, down_all,
    middle, wbuf, wsmall, attended, mixed_grad, qg, dkv, kv_low, kv_in, w, wsib, legs, legs2, wz,
    load_sem, ag_local, ag_xs, ag_xr, ag_ys, ag_yr, ag_fs, ag_fr, kv_send, kv_recv,
    ws_send, ws_recv, a_send, a_recv, b_send, b_recv, a2_send, a2_recv, b2_send, b2_recv,
    wz_send, wz_recv,
):
    depth = lax.axis_size("expert") // 2
    rows, width = x_ref.shape
    heads = q_ref.shape[1] // HEAD_SIZE
    kv_width = kv_ref.shape[1]
    groups = kv_width // (2 * HEAD_SIZE)
    group = heads // groups
    wide = heads * HEAD_SIZE
    qkv_width = wide + kv_width
    split = qkv_width + 128
    shard, total = share_ref.shape
    me, mine = lax.axis_index("expert"), lax.axis_index("dp")
    z, core = me // 2, me % 2
    y, x = mine // 2, mine % 2
    xn, yn, diag = y * 2 + 1 - x, (1 - y) * 2 + x, (1 - y) * 2 + 1 - x
    sibling = {"expert": z * 2 + 1 - core}

    def at(zz):
        return {"expert": zz * 2 + core}

    greet(depth, z, at, (sibling, {"dp": xn}, {"dp": yn}, {"dp": diag}))

    def remote(src, dst, send, recv, target):
        return pltpu.make_async_remote_copy(
            src, dst, send, recv, device_id=target, device_id_type=MESH
        )

    def load(src, dst, i):
        return pltpu.make_async_copy(src, dst, load_sem.at[i])

    load_rows = load(row_ref, tok_ref, 0)
    load_out = load(w_full.at[:, pl.ds(split, width)], wbuf.at[:, pl.ds(0, width)], 1)
    load_small = load(w_full.at[:, pl.ds(qkv_width, 128)], wsmall, 2)
    load_qkv = load(w_full.at[:, pl.ds(0, qkv_width)], wbuf, 3)
    load_middle = load(middle_any, middle, 4)
    load_small.start()
    load_rows.start()
    load_middle.start()
    load_out.start()

    quarter = wide_ref.shape[1]
    down_half = down_ref.shape[0] // 2

    def quarter_of(piece, dp):
        span = pl.ds(pl.multiple_of(dp * quarter, 128), quarter)
        if piece < 2:
            return wide_all.at[piece, span]
        return down_all.at[pl.ds((piece - 2) * down_half, down_half), span]

    def own_quarter(piece):
        if piece < 2:
            return wide_ref.at[piece]
        return down_ref.at[pl.ds((piece - 2) * down_half, down_half)]

    def keep_quarter(piece):
        return pltpu.make_async_copy(own_quarter(piece), quarter_of(piece, mine), ag_local.at[piece])

    def quarter_x(piece, dp):
        return remote(own_quarter(piece), quarter_of(piece, dp), ag_xs.at[piece], ag_xr.at[piece], {"dp": xn})

    def quarter_y(piece, dp):
        return remote(own_quarter(piece), quarter_of(piece, dp), ag_ys.at[piece], ag_yr.at[piece], {"dp": yn})

    def quarter_on(piece, dp, target):
        ref = quarter_of(piece, dp)
        return remote(ref, ref, ag_fs.at[piece], ag_fr.at[piece], target)

    def quarters(piece):
        quarter_x(piece, mine).start()
        quarter_y(piece, mine).start()
        keep_quarter(piece).start()

    def quarters_on(piece):
        if piece % 2 == 0:
            quarter_x(piece, xn).wait_recv()
            quarter_on(piece, xn, {"dp": yn}).start()
        else:
            quarter_y(piece, yn).wait_recv()
            quarter_on(piece, yn, {"dp": xn}).start()

    quarters(0)

    bounds = ((split, total), (0, wide // 2), (wide // 2, wide), (wide, split))
    cuts = tuple(low + ((high - low) // 128 + 1) // 2 * 128 for low, high in bounds)

    def span(low, high):
        return pl.ds(low, high - low)

    def ws_copy(p, dp):
        cols = span(*bounds[p])
        return remote(
            w.at[dp, :, 1 - core, :, cols], wsib.at[dp, :, :, cols],
            ws_send.at[p, dp], ws_recv.at[p, dp], sibling,
        )

    def a_cols(p):
        return span(bounds[p][0], cuts[p])

    def b_cols(p):
        return span(cuts[p], bounds[p][1])

    def a_copy(p, yy):
        return remote(
            w.at[yy * 2 + 1 - x, :, core, :, a_cols(p)], legs.at[yy, :, :, a_cols(p)],
            a_send.at[p, yy], a_recv.at[p, yy], {"dp": xn},
        )

    def b_copy(p, xx):
        return remote(
            w.at[(1 - y) * 2 + xx, :, core, :, b_cols(p)], legs.at[xx, :, :, b_cols(p)],
            b_send.at[p, xx], b_recv.at[p, xx], {"dp": yn},
        )

    def a2_copy(p):
        return remote(
            w.at[yn, :, core, :, a_cols(p)], legs2.at[:, :, a_cols(p)], a2_send.at[p], a2_recv.at[p], {"dp": yn}
        )

    def b2_copy(p):
        return remote(
            w.at[xn, :, core, :, b_cols(p)], legs2.at[:, :, b_cols(p)], b2_send.at[p], b2_recv.at[p], {"dp": xn}
        )

    def wz_copy(p, zd, nxt, slot):
        cols = span(*bounds[p])
        return remote(
            w.at[mine, zd, core, :, cols], wz.at[slot, :, cols], wz_send.at[p, zd], wz_recv.at[p, slot], at(nxt)
        )

    block = 16
    steps = shard // block

    def add(dp, term, cols):
        def step(i, _):
            zz, rr = i // steps, pl.ds(pl.multiple_of(lax.rem(i, steps) * block, block), block)
            value = w[dp, zz, core, rr, cols].astype(F32) + term[zz, rr, cols].astype(F32)
            w[dp, zz, core, rr, cols] = value.astype(BF)
            return 0

        lax.fori_loop(0, depth * steps, step, 0)

    def begin(p):
        for dp in (xn, diag, yn, mine):
            ws_copy(p, dp).start()

    def first_legs(p):
        def combine(dp):
            ws_copy(p, dp).wait_recv()
            add(dp, wsib.at[dp], span(*bounds[p]))

        combine(xn)
        a_copy(p, y).start()
        combine(diag)
        a_copy(p, 1 - y).start()
        b_copy(p, 1 - x).start()
        combine(yn)
        b_copy(p, x).start()
        combine(mine)

    def second_legs(p):
        a_copy(p, 1 - y).wait_recv()
        add(yn, legs.at[1 - y], a_cols(p))
        a2_copy(p).start()
        b_copy(p, 1 - x).wait_recv()
        add(xn, legs.at[1 - x], b_cols(p))
        b2_copy(p).start()
        a_copy(p, y).wait_recv()
        add(mine, legs.at[y], a_cols(p))
        b_copy(p, x).wait_recv()
        add(mine, legs.at[x], b_cols(p))

    def slot_for(zd, nxt):
        return jnp.where((nxt == zd) & (nxt < z), depth, zd)

    def line(p):
        a2_copy(p).wait_recv()
        add(mine, legs2, a_cols(p))
        b2_copy(p).wait_recv()
        add(mine, legs2, b_cols(p))

        @pl.when((z == 0) | (z == depth - 1))
        def _():
            nxt = jnp.where(z == 0, 1, depth - 2)
            for d in range(1, depth):
                zd = jnp.where(z == 0, depth - d, d - 1)
                wz_copy(p, zd, nxt, slot_for(zd, nxt)).start()

    def line_on(p):
        cols = span(*bounds[p])
        for r in range(depth - 1, 1, -1):
            for first in (True, False):
                right = (z < depth - 1 - z) if first else (z >= depth - 1 - z)
                zd = jnp.where(right, r, depth - 1 - r)
                nxt = jnp.where(right, z + 1, z - 1)
                valid = jnp.where(right, (z < zd) & (z > 0), (z > zd) & (z < depth - 1))

                @pl.when(valid)
                def _():
                    wz_copy(p, zd, nxt, zd).wait_recv()

                    def step(i, _):
                        rr = pl.ds(pl.multiple_of(i * block, block), block)
                        value = w[mine, zd, core, rr, cols].astype(F32) + wz[zd, rr, cols].astype(F32)
                        w[mine, zd, core, rr, cols] = value.astype(BF)
                        return 0

                    lax.fori_loop(0, steps, step, 0)
                    wz_copy(p, zd, nxt, slot_for(zd, nxt)).start()

    def line_end(p):
        cols = span(*bounds[p])
        share_ref[:, cols] = w[mine, z, core, :, cols].astype(F32)

        @pl.when(z > 0)
        def _():
            wz_copy(p, z, z, z).wait_recv()
            share_ref[:, cols] += wz[z, :, cols].astype(F32)

        @pl.when(z < depth - 1)
        def _():
            wz_copy(p, z, z, depth).wait_recv()
            share_ref[:, cols] += wz[depth, :, cols].astype(F32)

    def weight_rows(left, right, low, size):
        quarter_rows = width // 4

        def step(i, _):
            cols = pl.ds(pl.multiple_of(i * quarter_rows, 128), quarter_rows)
            tile = mm_tn(left[:, cols], right).astype(BF)
            w[i, :, :, :, low : low + size] = tile.reshape(depth, 2, shard, size)
            return 0

        lax.fori_loop(0, 4, step, 0)

    experts = gate_ref.shape[0]
    gates, gate_grad = gate_ref[:, :rows], gg_ref[:, :rows]
    logit_grad = gates * (gate_grad - jnp.sum(gates * gate_grad, axis=0, keepdims=True))
    high = logit_grad.astype(BF)
    logit_two = jnp.concatenate([high.astype(F32), logit_grad - high.astype(F32)], axis=0).astype(BF)
    load_small.wait()
    small = jnp.transpose(wsmall[...].astype(F32))
    router = small[:experts].astype(BF).astype(F32)
    router_two = jnp.concatenate([router, router], axis=0).astype(BF)
    gain_one, gain_two = small[experts : experts + 1], small[experts + 1 : experts + 2]
    router_grad = mm(logit_two, n2_ref[...])
    router_grad = router_grad[:experts] + router_grad[experts:]
    load_rows.wait()
    load_middle.wait()
    tok_ref[...] += mm_tn(logit_two, router_two)

    def norm_back(value, grad, gain):
        scale = lax.rsqrt(jnp.mean(value * value, axis=1, keepdims=True) + EPS)
        unit = value * scale
        scaled = grad * gain
        back = scale * (scaled - unit * jnp.mean(scaled * unit, axis=1, keepdims=True))
        return back, jnp.sum(grad * unit, axis=0, keepdims=True)

    def second_norm(i, carry):
        rr = pl.ds(pl.multiple_of(i * block, block), block)
        back, gain = norm_back(middle[rr, :], tok_ref[rr, :], gain_two)
        back = back + dy_ref[rr, :].astype(F32)
        tok_ref[rr, :] = back
        attended[rr, :] = back.astype(BF)
        return carry + gain

    gain_two_grad = lax.fori_loop(0, rows // block, second_norm, jnp.zeros((1, width), F32))
    weight_rows(mixed_ref, attended[...], split, width)
    begin(0)
    load_out.wait()
    tile = 512

    def mixed_step(i, _):
        out_rows = pl.ds(pl.multiple_of(i * tile, tile), tile)
        mixed_grad[:, out_rows] = mm_nt(attended[...], wbuf[out_rows, :width]).astype(BF)
        return 0

    lax.fori_loop(0, wide // tile, mixed_step, 0)
    load_qkv.start()
    first_legs(0)
    quarters(1)

    lanes = lax.broadcasted_iota(jnp.int32, lse_ref.shape, 1)

    def turn_back(value):
        return value * cos_ref[...] - pltpu.roll(value, HEAD_SIZE // 2, 1) * sin_ref[...]

    def kv_copy(g, i):
        dp = (xn, diag, yn)[i]
        return remote(
            kv_low.at[g, pl.ds(pl.multiple_of(dp * rows, 16), rows)], kv_in.at[g, mine],
            kv_send.at[g, i], kv_recv.at[g, mine], {"dp": dp},
        )

    def attend_group(g, polls):
        low = 2 * g * HEAD_SIZE
        key, value = kv_ref[:, low : low + HEAD_SIZE], kv_ref[:, low + HEAD_SIZE : low + 2 * HEAD_SIZE]

        def attend(i, _):
            for j, job in polls.items():
                pl.when(i == j)(lambda job=job: (job(), None)[1])
            h = g * group + i
            cols = pl.ds(pl.multiple_of(h * HEAD_SIZE, HEAD_SIZE), HEAD_SIZE)
            query, grad = q_ref[:, cols], mixed_grad[:, cols]
            level = jnp.sum(jnp.where(lanes == h, lse_ref[...], 0.0), axis=1, keepdims=True)
            scores = mm_nt(query, key) * (HEAD_SIZE**-0.5 * LOG2E) + bias_ref[...]
            attn = jnp.exp2(scores - level)
            attn_grad = mm_nt(grad, value)
            mean = jnp.sum(attn * attn_grad, axis=1, keepdims=True)
            score_grad = (attn * (attn_grad - mean)).astype(BF)
            value_term = mm_tn(attn.astype(BF), grad)
            key_term = mm_tn(score_grad, query)
            qg[:, cols] = turn_back(mm(score_grad, key) * HEAD_SIZE**-0.5).astype(BF)

            @pl.when(i == 0)
            def _():
                dkv[:, :HEAD_SIZE] = key_term
                dkv[:, HEAD_SIZE:] = value_term

            @pl.when(i > 0)
            def _():
                dkv[:, :HEAD_SIZE] += key_term
                dkv[:, HEAD_SIZE:] += value_term

            return 0

        lax.fori_loop(0, group, attend, 0)
        kv_low[g, :, :HEAD_SIZE] = (dkv[:, :HEAD_SIZE] * HEAD_SIZE**-0.5).astype(BF)
        kv_low[g, :, HEAD_SIZE:] = dkv[:, HEAD_SIZE:].astype(BF)
        for i in range(3):
            kv_copy(g, i).start()
        weight_rows(n1_ref, qg[:, g * wide // 2 : (g + 1) * wide // 2], g * wide // 2, wide // 2)
        begin(1 + g)
        first_legs(1 + g)
        quarters(2 + g)

    attend_group(0, {3: lambda: quarters_on(0)})
    attend_group(1, {1: lambda: second_legs(0), 4: lambda: quarters_on(1)})

    def kv_sum(g):
        for i in range(3):
            dp = (xn, diag, yn)[i]
            remote(
                kv_low.at[g, pl.ds(0, rows)], kv_in.at[g, dp], kv_send.at[g, i], kv_recv.at[g, dp], {"dp": dp}
            ).wait_recv()
        terms = kv_low[g, pl.ds(pl.multiple_of(mine * rows, 16), rows), :].astype(F32)
        for dp in (xn, diag, yn):
            terms = terms + kv_in[g, dp].astype(F32)
        low = wide + 2 * g * HEAD_SIZE
        qg[:, low : low + HEAD_SIZE] = turn_back(terms[:, :HEAD_SIZE]).astype(BF)
        qg[:, low + HEAD_SIZE : low + 2 * HEAD_SIZE] = terms[:, HEAD_SIZE:].astype(BF)

    for g in range(groups):
        kv_sum(g)
    second_legs(1)
    weight_rows(n1_ref, qg[:, wide:], wide, kv_width)
    load_qkv.wait()

    def first_grad(i, _):
        out_rows = pl.ds(pl.multiple_of(i * tile, tile), tile)
        middle[:, out_rows] = mm_nt(qg[...], wbuf[out_rows, :])
        return 0

    lax.fori_loop(0, width // tile, first_grad, 0)
    quarters_on(2)

    def first_norm(i, carry):
        rr = pl.ds(pl.multiple_of(i * block, block), block)
        back, gain = norm_back(x_ref[rr, :].astype(F32), middle[rr, :], gain_one)
        tok_ref[rr, :] += back
        return carry + gain

    gain_one_grad = lax.fori_loop(0, rows // block, first_norm, jnp.zeros((1, width), F32))
    small_grad = jnp.concatenate(
        [
            router_grad,
            gain_one_grad,
            gain_two_grad,
            jnp.zeros((128 - experts - 2, width), F32),
        ],
        axis=0,
    )
    small_grad = jnp.transpose(small_grad).astype(BF)
    for i in range(4):
        part = small_grad[i * width // 4 : (i + 1) * width // 4]
        w[i, :, :, :, qkv_width:split] = part.reshape(depth, 2, shard, 128)
    begin(3)
    first_legs(3)
    line(0)
    second_legs(2)
    quarters_on(3)
    line_on(0)
    line(1)
    second_legs(3)
    line_on(1)
    line(2)
    line_on(2)
    line(3)
    line_on(3)
    for p in range(4):
        line_end(p)

    for piece in range(4):
        keep_quarter(piece).wait()
        quarter_x(piece, mine).wait_send()
        quarter_y(piece, mine).wait_send()
        if piece % 2 == 0:
            quarter_y(piece, yn).wait_recv()
        else:
            quarter_x(piece, xn).wait_recv()
        quarter_on(piece, diag, {"dp": xn}).wait()
    for g in range(groups):
        for i in range(3):
            kv_copy(g, i).wait_send()
    for p in range(4):
        for dp in range(4):
            ws_copy(p, dp).wait_send()
        for i in range(2):
            a_copy(p, i).wait_send()
            b_copy(p, i).wait_send()
        a2_copy(p).wait_send()
        b2_copy(p).wait_send()
        for zd in range(depth):

            @pl.when(zd != z)
            def _():
                wz_copy(p, zd, z, zd).wait_send()


def backward_pass(
    x, dy, middle, gates, gate_grads, n1, q, kv, mixed, n2, logs, cos, sin, bias, row_sum, w_full,
    wide_part, down_part,
):
    depth = lax.axis_size("expert") // 2
    rows, width = x.shape
    total = w_full.shape[1]
    shard = w_full.shape[0] // (4 * 2 * depth)
    kv_width = kv.shape[1]
    groups = kv_width // (2 * HEAD_SIZE)
    qkv_width = q.shape[1] + kv_width
    dma = pltpu.SemaphoreType.DMA
    vmem = pl.BlockSpec(memory_space=pltpu.VMEM)
    anywhere = pl.BlockSpec(memory_space=pl.ANY)
    shape = jax.ShapeDtypeStruct
    parts = 4
    return pl.pallas_call(
        backward_kernel,
        name="backward_pass",
        out_shape=(
            shape((rows, width), F32),
            shape((shard, total), F32),
            shape((2, 4 * wide_part.shape[1], wide_part.shape[2]), BF),
            shape((down_part.shape[0], 4 * down_part.shape[1]), BF),
        ),
        in_specs=[vmem] * 13 + [anywhere] * 5,
        out_specs=(vmem, vmem, anywhere, anywhere),
        scratch_shapes=[
            pltpu.VMEM((rows, width), F32),
            pltpu.VMEM((width, qkv_width), BF),
            pltpu.VMEM((width, 128), BF),
            pltpu.VMEM((rows, width), BF),
            pltpu.VMEM((rows, q.shape[1]), BF),
            pltpu.VMEM((rows, qkv_width), BF),
            pltpu.VMEM((kv.shape[0], 2 * HEAD_SIZE), F32),
            pltpu.VMEM((groups, kv.shape[0], 2 * HEAD_SIZE), BF),
            pltpu.VMEM((groups, 4, rows, 2 * HEAD_SIZE), BF),
            pltpu.VMEM((4, depth, 2, shard, total), BF),
            pltpu.VMEM((4, depth, shard, total), BF),
            pltpu.VMEM((2, depth, shard, total), BF),
            pltpu.VMEM((depth, shard, total), BF),
            pltpu.VMEM((depth + 1, shard, total), BF),
            dma((5,)), dma((4,)), dma((4,)), dma((4,)), dma((4,)), dma((4,)), dma((4,)), dma((4,)),
            dma((groups, 3)), dma((groups, 4)),
            dma((parts, 4)), dma((parts, 4)), dma((parts, 2)), dma((parts, 2)), dma((parts, 2)), dma((parts, 2)),
            dma((parts,)), dma((parts,)), dma((parts,)), dma((parts,)),
            dma((parts, depth)), dma((parts, depth + 1)),
        ],
        compiler_params=pltpu.CompilerParams(
            collective_id=3, has_side_effects=True, vmem_limit_bytes=63 * 2**20
        ),
        cost_estimate=pl.CostEstimate(
            flops=2 * 10**10, bytes_accessed=200 * 2**20, transcendentals=0
        ),
    )(
        x, dy, gates, gate_grads, n1, q, kv, mixed, n2, logs, cos, sin, bias,
        middle, row_sum, w_full, wide_part, down_part,
    )


def dense_on_device(
    tokens,
    cotangent,
    parents,
    routes,
    first_gain,
    second_gain,
    query_weight,
    key_matrix,
    value_matrix,
    out_weight,
    router_weight,
    gate_weight,
    up_weight,
    down_weight,
):
    experts = router_weight.shape[1]
    heads_width = QUERY_HEADS * HEAD_SIZE
    kv_width = 2 * KEY_VALUE_HEADS * HEAD_SIZE
    qkv_width = heads_width + kv_width
    small_shard = jnp.concatenate(
        [router_weight, first_gain[:, None], second_gain[:, None]], axis=1
    )
    small_shard = jnp.pad(small_shard, ((0, 0), (0, -small_shard.shape[1] % 128)))
    small_width = small_shard.shape[1]
    shards = (query_weight, key_matrix, value_matrix, small_shard, out_weight)
    dy_low = cotangent[0]
    inputs_low = tokens[0]
    total_rows = inputs_low.shape[0]
    half = HEAD_SIZE // 2
    frequency = THETA ** -(np.arange(half, dtype=np.float64) * 2.0 / HEAD_SIZE)
    freq = np.concatenate([frequency, frequency]).astype(np.float32)[None]
    expert_ids = jnp.arange(experts, dtype=jnp.int32)
    hit_rows = jnp.any(routes[0][None, :, :] == expert_ids[:, None, None], axis=2).astype(F32)
    n1, query_low, kv_all, mixed, logs, middle, n2, gate_rows, cos, sin, bias, full, dy_all = (
        attention_pass(inputs_low, shards, freq, parents, hit_rows, dy_low)
    )
    row_sum, gate_grads, sums, wide_part, down_part, _ = expert_pass(
        n2, gate_rows, dy_all, gate_weight[0], up_weight[0], down_weight[0]
    )
    combined = lax.psum_scatter(sums, "expert", scatter_dimension=0, tiled=True)[0]
    input_grad, share, wide_grads, down_grad = backward_pass(
        inputs_low, dy_low, middle, gate_rows, gate_grads, n1, query_low, kv_all, mixed, n2, logs,
        cos, sin, bias, row_sum, full, wide_part, down_part,
    )
    output = (middle + combined.astype(F32)).astype(BF)[None]
    heads_of = [
        share[:, heads_width + i * HEAD_SIZE : heads_width + (i + 1) * HEAD_SIZE]
        for i in range(2 * KEY_VALUE_HEADS)
    ]
    query_share = share[:, :heads_width]
    key_share = jnp.concatenate(heads_of[0::2], axis=1)
    value_share = jnp.concatenate(heads_of[1::2], axis=1)
    small_share = share[:, qkv_width : qkv_width + small_width]
    out_share = share[:, qkv_width + small_width :]
    return (
        output,
        input_grad[None],
        small_share[:, experts],
        small_share[:, experts + 1],
        query_share,
        key_share,
        value_share,
        out_share,
        small_share[:, :experts],
        wide_grads[0].astype(F32)[None],
        wide_grads[1].astype(F32)[None],
        down_grad.astype(F32)[None],
    )


def solution(mesh):
    dense = mesh.shape["expert"] <= 2 * TOPK and mesh.shape["dp"] == 4
    return jax.shard_map(
        dense_on_device if dense else on_device_routed,
        mesh=mesh,
        in_specs=(
            P("expert", "dp", None),
            P("expert", "dp", None),
            P("expert", None),
            P("expert", "dp", None),
            P(("dp", "expert")),
            P(("dp", "expert")),
            P(("dp", "expert"), None),
            P(("dp", "expert"), None),
            P(("dp", "expert"), None),
            P(("dp", "expert"), None),
            P(("dp", "expert"), None),
            P("expert", None, None),
            P("expert", None, None),
            P("expert", None, None),
        ),
        out_specs=(
            P("expert", "dp", None),
            P("expert", "dp", None),
            P(("dp", "expert")),
            P(("dp", "expert")),
            P(("dp", "expert"), None),
            P(("dp", "expert"), None),
            P(("dp", "expert"), None),
            P(("dp", "expert"), None),
            P(("dp", "expert"), None),
            P("expert", None, None),
            P("expert", None, None),
            P("expert", None, None),
        ),
        check_vma=False,
    )
```

```python
import jax
import jax.numpy as jnp
import numpy as np
from jax import lax
from jax.experimental import pallas as pl
from jax.experimental.pallas import tpu as pltpu
from jax.sharding import PartitionSpec as P

MESH = pl.DeviceIdType.MESH
BF = jnp.bfloat16
F32 = jnp.float32
MODEL_WIDTH = 1536
QUERY_HEADS = 12
KEY_VALUE_HEADS = 2
HEAD_SIZE = 128
FF = 768
TOPK = 4
SEG = 32
BRANCHES = 4
LEAVES = 8


EPS = 1e-06
THETA = 10000.0
HIGH_PRECISION = lax.Precision.HIGHEST
NEGATIVE = -1e30
LOG2E = 1.4426950408889634


def ancestry(parent_row):
    block_count = parent_row.shape[0]
    block_ids = jnp.arange(block_count, dtype=jnp.int32)

    def advance(counter, carried):
        current, ancestors = carried
        ancestors = jnp.maximum(
            ancestors, (current[:, None] == block_ids[None, :]).astype(jnp.float32)
        )
        return (jnp.take(parent_row, current), ancestors)

    start_pair = (block_ids, jnp.zeros((block_count, block_count), jnp.float32))
    current, ancestors = lax.fori_loop(0, block_count, advance, start_pair)
    depths = (jnp.sum(ancestors, axis=1) - 1.0).astype(jnp.int32)
    return (ancestors, depths)


def apply_rotation(values, positions):
    half_width = values.shape[-1] // 2
    frequency = jnp.power(
        THETA, -(jnp.arange(half_width, dtype=jnp.float32) * 2.0 / values.shape[-1])
    )
    angles = positions.astype(jnp.float32)[:, None] * frequency[None, :]
    cosine = jnp.cos(angles)[:, None, :]
    sine_part = jnp.sin(angles)[:, None, :]
    first_half = values[..., :half_width]
    second_half = values[..., half_width:]
    return jnp.concatenate(
        [
            first_half * cosine - second_half * sine_part,
            second_half * cosine + first_half * sine_part,
        ],
        axis=-1,
    )


def normalize(values, scales):
    return values * lax.rsqrt(jnp.mean(values * values, axis=-1, keepdims=True) + EPS) * scales


def place(route_ids, experts, capacity):
    one_hot = (route_ids[..., None] == jnp.arange(experts, dtype=jnp.int32)).astype(jnp.int32)
    pairs = one_hot.shape[-2]
    before = jnp.tri(pairs, pairs, -1, dtype=jnp.bfloat16)
    earlier = jnp.dot(before, one_hot.astype(jnp.bfloat16), preferred_element_type=jnp.float32)
    slot_rank = jnp.sum(earlier.astype(jnp.int32) * one_hot, axis=-1)
    return route_ids * capacity + slot_rank


def visibility(ancestors, depths, query_ids, key_ids):
    block_ids = jnp.arange(ancestors.shape[0], dtype=jnp.int32)
    query_hit = (query_ids // SEG)[:, None] == block_ids[None, :]
    key_hit = (key_ids // SEG)[:, None] == block_ids[None, :]
    query_positions = (
        jnp.sum(jnp.where(query_hit, depths[None, :], 0), axis=1) * SEG + query_ids % SEG
    )
    key_pos = jnp.sum(jnp.where(key_hit, depths[None, :], 0), axis=1) * SEG + key_ids % SEG
    reach = jnp.dot(query_hit.astype(jnp.float32), ancestors, precision=HIGH_PRECISION)
    reach_keys = jnp.repeat(reach, SEG, axis=1)
    visible = (reach_keys > 0.5) & (key_pos[None, :] <= query_positions[:, None])
    return (visible, query_positions)


def head_scores(query_rotated, keys_all, visible, key_value_head, query_group_width):
    query_part = query_rotated[
        :, key_value_head * query_group_width : (key_value_head + 1) * query_group_width, :
    ]
    key_part = keys_all[:, key_value_head * HEAD_SIZE : (key_value_head + 1) * HEAD_SIZE]
    scores = jnp.einsum(
        "rgd,kd->grk", query_part, key_part, preferred_element_type=jnp.float32
    ) * HEAD_SIZE ** (-0.5)
    return jnp.where(visible[None], scores, NEGATIVE)


def gelu_product(gate_pre, up_pre):
    return jax.nn.gelu(gate_pre, approximate=True) * up_pre


def expert_hidden(received, local_gate, local_up):
    local_count = local_gate.shape[0]
    slot_count = received.shape[1]
    grouped_queries = received.reshape(-1, local_count, slot_count, MODEL_WIDTH)
    gate_pre = jnp.einsum(
        "sjcd,jdf->sjcf", grouped_queries, local_gate, preferred_element_type=jnp.float32
    )
    up_pre = jnp.einsum(
        "sjcd,jdf->sjcf", grouped_queries, local_up, preferred_element_type=jnp.float32
    )
    hidden = gelu_product(gate_pre, up_pre).astype(jnp.bfloat16)
    flat_shape = (received.shape[0], slot_count, FF)
    return (gate_pre.reshape(flat_shape), up_pre.reshape(flat_shape), hidden.reshape(flat_shape))


def expert_result(hidden, local_down):
    local_count = local_down.shape[0]
    grouped_queries = hidden.reshape(-1, local_count, hidden.shape[1], FF)
    result = jnp.einsum(
        "sjcf,jfd->sjcd", grouped_queries, local_down, preferred_element_type=jnp.float32
    )
    return result.astype(jnp.bfloat16).reshape(hidden.shape[0], hidden.shape[1], MODEL_WIDTH)


def on_device_routed(
    tokens,
    cotangent,
    parents,
    routes,
    first_gain,
    second_gain,
    query_weight,
    key_matrix,
    value_matrix,
    out_weight,
    router_weight,
    gate_weight,
    up_weight,
    down_weight,
):
    gathered = (
        lax.all_gather(query_weight, ("dp", "expert"), axis=0, tiled=True),
        lax.all_gather(key_matrix, ("dp", "expert"), axis=0, tiled=True),
        lax.all_gather(value_matrix, ("dp", "expert"), axis=0, tiled=True),
        lax.all_gather(out_weight, ("dp", "expert"), axis=0, tiled=True),
        lax.all_gather(router_weight, ("dp", "expert"), axis=0, tiled=True),
        lax.all_gather(first_gain, ("dp", "expert"), axis=0, tiled=True),
        lax.all_gather(second_gain, ("dp", "expert"), axis=0, tiled=True),
    )
    query_full, key_complete, value_complete, out_full, router_full, gain_one, gain_two = gathered
    scale_one = gain_one.astype(jnp.float32)
    scale_two = gain_two.astype(jnp.float32)
    inputs = tokens[0].astype(jnp.float32)
    total_rows = inputs.shape[0]
    query_group_width = QUERY_HEADS // KEY_VALUE_HEADS
    ancestors, depths = ancestry(parents[0])
    tree_length = ancestors.shape[0] * SEG
    query_ids = lax.axis_index("dp") * total_rows + jnp.arange(total_rows, dtype=jnp.int32)
    key_ids = jnp.arange(tree_length, dtype=jnp.int32)
    visible, query_positions = visibility(ancestors, depths, query_ids, key_ids)
    first_normed = normalize(inputs, scale_one).astype(jnp.bfloat16)
    query_proj = jnp.dot(first_normed, query_full, preferred_element_type=jnp.float32).reshape(
        total_rows, QUERY_HEADS, HEAD_SIZE
    )
    key_projected = jnp.dot(first_normed, key_complete, preferred_element_type=jnp.float32).reshape(
        total_rows, KEY_VALUE_HEADS, HEAD_SIZE
    )
    value_projected = jnp.dot(first_normed, value_complete, preferred_element_type=jnp.float32)
    query_rotated = apply_rotation(query_proj, query_positions).astype(jnp.bfloat16)
    key_rotated = (
        apply_rotation(key_projected, query_positions)
        .astype(jnp.bfloat16)
        .reshape(total_rows, KEY_VALUE_HEADS * HEAD_SIZE)
    )
    value_low = value_projected.astype(jnp.bfloat16)
    keys_all, values_all = (
        lax.all_gather(key_rotated, "dp", axis=0, tiled=True),
        lax.all_gather(value_low, "dp", axis=0, tiled=True),
    )
    mixed_parts = []
    log_totals = []
    for key_value_head in range(KEY_VALUE_HEADS):
        scores = head_scores(query_rotated, keys_all, visible, key_value_head, query_group_width)
        row_max = jnp.max(scores, axis=-1, keepdims=True)
        exponent = jnp.exp(scores - row_max)
        row_total = jnp.sum(exponent, axis=-1, keepdims=True)
        log_totals.append(row_max + jnp.log(row_total))
        softmax_out = (exponent / row_total).astype(jnp.bfloat16)
        value_part = values_all[:, key_value_head * HEAD_SIZE : (key_value_head + 1) * HEAD_SIZE]
        mixed_parts.append(
            jnp.einsum("grk,kd->rgd", softmax_out, value_part, preferred_element_type=jnp.float32)
        )
    mixed_out = (
        jnp.concatenate(mixed_parts, axis=1)
        .reshape(total_rows, QUERY_HEADS * HEAD_SIZE)
        .astype(jnp.bfloat16)
    )
    middle = inputs + jnp.dot(mixed_out, out_full, preferred_element_type=jnp.float32)
    normed_two = normalize(middle, scale_two).astype(jnp.bfloat16)
    logits = jnp.dot(normed_two, router_full, preferred_element_type=jnp.float32)
    route_ids = routes[0]
    experts = gate_weight.shape[0] * lax.axis_size("expert")
    capacity = 3 * total_rows * TOPK // (2 * experts)
    expert_ids = jnp.arange(experts, dtype=jnp.int32)
    route_hits = route_ids[:, :, None] == expert_ids[None, None, :]
    chosen = jnp.sum(jnp.where(route_hits, logits[:, None, :], 0.0), axis=2)
    chosen_max = jnp.max(chosen, axis=1, keepdims=True)
    chosen_exp = jnp.exp(chosen - chosen_max)
    gate_weights = chosen_exp / jnp.sum(chosen_exp, axis=1, keepdims=True)
    pair_count = total_rows * TOPK
    slot_index = place(route_ids.reshape(pair_count), experts, capacity)
    slot_source = (
        jnp.full((experts * capacity,), pair_count, jnp.int32)
        .at[slot_index]
        .set(jnp.arange(pair_count, dtype=jnp.int32))
    )
    slot_used = slot_source < pair_count
    slot_pair = jnp.where(slot_used, slot_source, 0)
    slot_token = slot_pair // TOPK
    zero_low = jnp.zeros((), jnp.bfloat16)
    outgoing = jnp.where(slot_used[:, None], normed_two[slot_token], zero_low).reshape(
        experts, capacity, MODEL_WIDTH
    )
    gate_pre, up_pre, hidden = expert_hidden(
        lax.all_to_all(outgoing, "expert", split_axis=0, concat_axis=0, tiled=True),
        gate_weight,
        up_weight,
    )
    dispatched = expert_result(hidden, down_weight)
    returned = lax.all_to_all(dispatched, "expert", split_axis=0, concat_axis=0, tiled=True)
    expert_rows = (
        returned.reshape(experts * capacity, MODEL_WIDTH)[slot_index]
        .astype(jnp.float32)
        .reshape(total_rows, TOPK, MODEL_WIDTH)
    )
    final = middle + jnp.sum(gate_weights[:, :, None] * expert_rows, axis=1)
    output = final.astype(jnp.bfloat16)[None]
    upstream = cotangent[0].astype(jnp.float32)
    gate_grad = jnp.sum(upstream[:, None, :] * expert_rows, axis=2)
    chosen_grad = gate_weights * (
        gate_grad - jnp.sum(gate_weights * gate_grad, axis=1, keepdims=True)
    )
    logit_grad = jnp.sum(jnp.where(route_hits, chosen_grad[:, :, None], 0.0), axis=1)
    pair_grad = (
        (gate_weights[:, :, None] * upstream[:, None, :])
        .astype(jnp.bfloat16)
        .reshape(pair_count, MODEL_WIDTH)
    )
    grad_outgoing = jnp.where(slot_used[:, None], pair_grad[slot_pair], zero_low).reshape(
        experts, capacity, MODEL_WIDTH
    )
    received, grad_in = (
        lax.all_to_all(outgoing, "expert", split_axis=0, concat_axis=0, tiled=True),
        lax.all_to_all(grad_outgoing, "expert", split_axis=0, concat_axis=0, tiled=True),
    )
    gate_pre, up_pre, hidden = expert_hidden(received, gate_weight, up_weight)
    local_count = gate_weight.shape[0]
    slot_count = received.shape[1]
    grouped_rows = received.reshape(-1, local_count, slot_count, MODEL_WIDTH)
    grouped_hidden = hidden.reshape(-1, local_count, slot_count, FF)
    grouped_grad = grad_in.reshape(-1, local_count, slot_count, MODEL_WIDTH)
    down_grad = jnp.einsum(
        "sjcf,sjcd->jfd", grouped_hidden, grouped_grad, preferred_element_type=jnp.float32
    )
    hidden_grad = jnp.einsum(
        "sjcd,jfd->sjcf", grouped_grad, down_weight, preferred_element_type=jnp.float32
    )
    _, product_pull = jax.vjp(gelu_product, gate_pre, up_pre)
    gate_pre_grad, up_pre_grad = product_pull(hidden_grad.reshape(gate_pre.shape))
    gate_low = gate_pre_grad.astype(jnp.bfloat16).reshape(-1, local_count, slot_count, FF)
    up_low = up_pre_grad.astype(jnp.bfloat16).reshape(-1, local_count, slot_count, FF)
    gate_w_grad = jnp.einsum(
        "sjcd,sjcf->jdf", grouped_rows, gate_low, preferred_element_type=jnp.float32
    )
    up_w_grad = jnp.einsum(
        "sjcd,sjcf->jdf", grouped_rows, up_low, preferred_element_type=jnp.float32
    )
    row_grad = jnp.einsum(
        "sjcf,jdf->sjcd", gate_low, gate_weight, preferred_element_type=jnp.float32
    ) + jnp.einsum("sjcf,jdf->sjcd", up_low, up_weight, preferred_element_type=jnp.float32)
    row_grad = row_grad.astype(jnp.bfloat16).reshape(received.shape)
    returned_grad = lax.all_to_all(row_grad, "expert", split_axis=0, concat_axis=0, tiled=True)
    pair_rows = (
        returned_grad.reshape(experts * capacity, MODEL_WIDTH)[slot_index]
        .astype(jnp.float32)
        .reshape(total_rows, TOPK, MODEL_WIDTH)
    )
    summed_experts = (
        lax.psum(gate_w_grad.astype(jnp.bfloat16), "dp").astype(jnp.float32),
        lax.psum(up_w_grad.astype(jnp.bfloat16), "dp").astype(jnp.float32),
        lax.psum(down_grad.astype(jnp.bfloat16), "dp").astype(jnp.float32),
    )
    router_wide = router_full.astype(jnp.float32)
    normed_two_grad = jnp.dot(logit_grad, router_wide.T, precision=HIGH_PRECISION) + jnp.sum(
        pair_rows, axis=1
    )
    router_grad = jnp.dot(normed_two.astype(jnp.float32).T, logit_grad, precision=HIGH_PRECISION)
    _, second_pull = jax.vjp(normalize, middle, scale_two)
    middle_norm_grad, second_gain_grad = second_pull(normed_two_grad)
    middle_grad = upstream + middle_norm_grad
    attended_low = middle_grad.astype(jnp.bfloat16)
    out_grad = jnp.einsum("rd,re->de", mixed_out, attended_low, preferred_element_type=jnp.float32)
    mixed_grad = jnp.einsum("re,de->rd", attended_low, out_full, preferred_element_type=jnp.float32)
    mixed_grad = mixed_grad.astype(jnp.bfloat16).reshape(total_rows, QUERY_HEADS, HEAD_SIZE)
    query_parts = []
    key_parts = []
    value_parts = []
    for key_value_head in range(KEY_VALUE_HEADS):
        scores = head_scores(query_rotated, keys_all, visible, key_value_head, query_group_width)
        softmax_out = jnp.exp(scores - log_totals[key_value_head])
        query_part = query_rotated[
            :, key_value_head * query_group_width : (key_value_head + 1) * query_group_width, :
        ]
        key_part = keys_all[:, key_value_head * HEAD_SIZE : (key_value_head + 1) * HEAD_SIZE]
        value_part = values_all[:, key_value_head * HEAD_SIZE : (key_value_head + 1) * HEAD_SIZE]
        grad_part = mixed_grad[
            :, key_value_head * query_group_width : (key_value_head + 1) * query_group_width, :
        ]
        value_parts.append(
            jnp.einsum(
                "grk,rgd->kd",
                softmax_out.astype(jnp.bfloat16),
                grad_part,
                preferred_element_type=jnp.float32,
            )
        )
        attn_grad = jnp.einsum(
            "rgd,kd->grk", grad_part, value_part, preferred_element_type=jnp.float32
        )
        score_grad = softmax_out * (
            attn_grad - jnp.sum(softmax_out * attn_grad, axis=-1, keepdims=True)
        )
        score_low = score_grad.astype(jnp.bfloat16)
        query_parts.append(
            jnp.einsum("grk,kd->rgd", score_low, key_part, preferred_element_type=jnp.float32)
            * HEAD_SIZE ** (-0.5)
        )
        key_parts.append(
            jnp.einsum("grk,rgd->kd", score_low, query_part, preferred_element_type=jnp.float32)
            * HEAD_SIZE ** (-0.5)
        )
    key_total_sum, value_sum = (
        lax.psum_scatter(
            jnp.concatenate(key_parts, axis=1).astype(jnp.bfloat16),
            "dp",
            scatter_dimension=0,
            tiled=True,
        ).astype(jnp.float32),
        lax.psum_scatter(
            jnp.concatenate(value_parts, axis=1).astype(jnp.bfloat16),
            "dp",
            scatter_dimension=0,
            tiled=True,
        ).astype(jnp.float32),
    )
    _, query_pull = jax.vjp(lambda values: apply_rotation(values, query_positions), query_proj)
    _, key_pullback = jax.vjp(lambda values: apply_rotation(values, query_positions), key_projected)
    query_grad = (
        query_pull(jnp.concatenate(query_parts, axis=1))[0]
        .astype(jnp.bfloat16)
        .reshape(total_rows, QUERY_HEADS * HEAD_SIZE)
    )
    key_grad = (
        key_pullback(key_total_sum.reshape(total_rows, KEY_VALUE_HEADS, HEAD_SIZE))[0]
        .astype(jnp.bfloat16)
        .reshape(total_rows, KEY_VALUE_HEADS * HEAD_SIZE)
    )
    value_grad = value_sum.astype(jnp.bfloat16)
    query_w_grad = jnp.einsum(
        "rd,re->de", first_normed, query_grad, preferred_element_type=jnp.float32
    )
    key_w_grad = jnp.einsum("rd,re->de", first_normed, key_grad, preferred_element_type=jnp.float32)
    value_w_grad = jnp.einsum(
        "rd,re->de", first_normed, value_grad, preferred_element_type=jnp.float32
    )
    normed_one_grad = (
        jnp.einsum("re,de->rd", query_grad, query_full, preferred_element_type=jnp.float32)
        + jnp.einsum("re,de->rd", key_grad, key_complete, preferred_element_type=jnp.float32)
        + jnp.einsum("re,de->rd", value_grad, value_complete, preferred_element_type=jnp.float32)
    )
    _, first_pull = jax.vjp(normalize, inputs, scale_one)
    input_norm_grad, first_gain_grad = first_pull(normed_one_grad)
    input_grad = (middle_grad + input_norm_grad)[None]
    shares = (
        lax.psum_scatter(query_w_grad, ("dp", "expert"), scatter_dimension=0, tiled=True),
        lax.psum_scatter(key_w_grad, ("dp", "expert"), scatter_dimension=0, tiled=True),
        lax.psum_scatter(value_w_grad, ("dp", "expert"), scatter_dimension=0, tiled=True),
        lax.psum_scatter(out_grad, ("dp", "expert"), scatter_dimension=0, tiled=True),
        lax.psum_scatter(router_grad, ("dp", "expert"), scatter_dimension=0, tiled=True),
        lax.psum_scatter(first_gain_grad, ("dp", "expert"), scatter_dimension=0, tiled=True),
        lax.psum_scatter(second_gain_grad, ("dp", "expert"), scatter_dimension=0, tiled=True),
    )
    return (
        output,
        input_grad,
        shares[5],
        shares[6],
        shares[0],
        shares[1],
        shares[2],
        shares[3],
        shares[4],
        summed_experts[0],
        summed_experts[1],
        summed_experts[2],
    )


def mm(a, b):
    return jnp.dot(a, b, preferred_element_type=F32)


def mm_nt(a, b):
    return lax.dot_general(a, b, (((1,), (1,)), ((), ())), preferred_element_type=F32)


def mm_tn(a, b):
    return lax.dot_general(a, b, (((0,), (0,)), ((), ())), preferred_element_type=F32)


def gelu_both(value):
    scale = 0.7978845608028654
    square = value * value
    bend = jnp.tanh(scale * value * (1.0 + 0.044715 * square))
    half = 0.5 * (1.0 + bend)
    slope = half + 0.5 * value * (1.0 - bend * bend) * scale * (1.0 + 0.134145 * square)
    return value * half, slope


def expert_kernel(
    n2_ref, gate_ref, dy_ref, gw_any, uw_any, dw_any,
    row_ref, gg_ref, sum_ref, wide_ref, down_ref, landing,
    gw_ref, uw_ref, dw_ref, n2_all, gate_all, dy_buf, dy_cols, hs_all, gl_all, ul_all, own, sib, zin, gg_out, gg_in,
    gate_cols, gg_cols, stage, kept, down_kept,
    n2_send, n2_recv, gt_send, gt_recv, own_send, sib_recv, zin_send, zin_recv,
    gg_send, gg_recv, dy_sem, cols_sem, sum_sem, tile_send, tile_recv, load_sem, keep_sem, weight_sem,
):
    count = lax.axis_size("expert")
    depth = count // 2
    rows = n2_ref.shape[0]
    half = rows // 2
    width = n2_ref.shape[1]
    ff = gw_ref.shape[1]
    me = lax.axis_index("expert")
    z, core = me // 2, me % 2
    sibling = z * 2 + 1 - core
    mine = lax.axis_index("dp")
    y, x = mine // 2, mine % 2
    others = (y * 2 + 1 - x, (1 - y) * 2 + 1 - x, (1 - y) * 2 + x)

    def at(zz):
        return {"expert": zz * 2 + core}

    n2_load = pltpu.make_async_copy(
        n2_ref, n2_all.at[pl.ds(pl.multiple_of(me * rows, 16), rows)], cols_sem
    )
    n2_load.start()
    weight_loads = [
        pltpu.make_async_copy(src, dst, weight_sem.at[i])
        for i, (src, dst) in enumerate(((dw_any, dw_ref), (gw_any, gw_ref), (uw_any, uw_ref)))
    ]
    for load in weight_loads:
        load.start()
    barrier = pltpu.get_barrier_semaphore()
    for other in range(1, count):
        pl.semaphore_signal(
            barrier, 1, device_id={"expert": lax.rem(me + other, count)}, device_id_type=MESH
        )
    for dp in others:
        pl.semaphore_signal(barrier, 1, device_id={"dp": dp}, device_id_type=MESH)
    pl.semaphore_wait(barrier, count - 1 + len(others))

    def chunk(k):
        return pl.ds(pl.multiple_of(k * rows, 16), rows)

    def piece(k, h):
        return pl.ds(pl.multiple_of(k * rows + h * half, 16), half)

    def part(h):
        return pl.ds(h * half, half)

    def n2_copy(k, h, lane, target):
        return pltpu.make_async_remote_copy(
            n2_all.at[piece(k, h)], n2_all.at[piece(k, h)], n2_send.at[k, h, lane], n2_recv.at[k, h],
            device_id=target, device_id_type=MESH,
        )

    def gt_copy(k, lane, target):
        return pltpu.make_async_remote_copy(
            gate_all.at[k], gate_all.at[k], gt_send.at[k, lane], gt_recv.at[k],
            device_id=target, device_id_type=MESH,
        )

    def send_chunk(k, h, lane, target):
        n2_copy(k, h, lane, target).start()
        if h == 0:
            gt_copy(k, lane, target).start()

    def sent_chunk(k, h, lane, target):
        n2_copy(k, h, lane, target).wait_send()
        if h == 0:
            gt_copy(k, lane, target).wait_send()

    def arrived(k, h):
        n2_copy(k, h, 0, at(z)).wait_recv()
        if h == 0:
            gt_copy(k, 0, at(z)).wait_recv()

    def dy_copy(k, h, w, s):
        return pltpu.make_async_copy(dy_ref.at[k, part(h)], dy_buf.at[w, s], dy_sem.at[w, s])

    def gg_copy(k):
        return pltpu.make_async_remote_copy(
            gg_out.at[k], gg_in.at[me], gg_send.at[k], gg_recv.at[me],
            device_id={"expert": k}, device_id_type=MESH,
        )

    def own_copy(zs, h):
        return pltpu.make_async_remote_copy(
            own.at[2 * zs + 1 - core, part(h)], sib.at[zs, part(h)],
            own_send.at[zs, h], sib_recv.at[zs, h],
            device_id={"expert": sibling}, device_id_type=MESH,
        )

    def zin_copy(zd, h, nxt, slot):
        return pltpu.make_async_remote_copy(
            own.at[2 * zd + core, part(h)], zin.at[slot, part(h)],
            zin_send.at[zd, h], zin_recv.at[slot, h],
            device_id=at(nxt), device_id_type=MESH,
        )

    n2_load.wait()
    gate_all[me] = gate_ref[...]

    for h in range(2):

        @pl.when(z < depth - 1)
        def _():
            send_chunk(me, h, 0, at(z + 1))

        @pl.when(z > 0)
        def _():
            send_chunk(me, h, 1, at(z - 1))

        send_chunk(me, h, 2, {"expert": sibling})

    row_ids = lax.broadcasted_iota(jnp.int32, (count, gate_ref.shape[1]), 0)

    def hidden_part(k, h, w, s):
        r = piece(k, h)
        place = 2 * s + w
        if h == 0:
            gate_row = jnp.sum(jnp.where(row_ids == me, gate_all[k], 0.0), axis=0, keepdims=True)
            gate_cols[place] = jnp.transpose(jnp.broadcast_to(gate_row, (128, gate_row.shape[1])))
            gg_cols[place, rows:, :] = jnp.zeros((gate_ref.shape[1] - rows, 128), F32)
        gate_col = gate_cols[place, part(h), :]
        tile = 256
        gate_wide = jnp.concatenate([gate_col] * (tile // 128), axis=1)
        total = jnp.zeros((half, 128), F32)
        for j in range(ff // tile):
            cols = slice(j * tile, (j + 1) * tile)
            back = mm_nt(dy_buf[w, s], dw_ref[cols, :])
            gate_pre = mm(n2_all[r, :], gw_ref[:, cols])
            up_pre = mm(n2_all[r, :], uw_ref[:, cols])
            act, slope = gelu_both(gate_pre)
            hidden = act * up_pre
            hs_all[r, cols] = (gate_wide * hidden).astype(BF)
            product = hidden * back
            for i in range(tile // 128):
                total = total + product[:, i * 128 : (i + 1) * 128]
            back = gate_wide * back
            gl_all[r, cols] = (back * up_pre * slope).astype(BF)
            ul_all[r, cols] = (back * act).astype(BF)
        gg_cols[place, part(h), :] = total
        if h == 1:
            gg_row = jnp.sum(jnp.transpose(gg_cols[place]), axis=0, keepdims=True)
            gg_tile = jnp.where(row_ids == me, gg_row, 0.0)
            gg_out[k] = gg_tile

            @pl.when(k == me)
            def _():
                gg_in[me] = gg_tile

            @pl.when(k != me)
            def _():
                gg_copy(k).start()

    def row_part(k, h):
        r = piece(k, h)
        wide = 512
        for j in range(width // wide):
            cols = slice(j * wide, (j + 1) * wide)
            own[k, part(h), cols] = (
                mm_nt(gl_all[r, :], gw_ref[cols, :]) + mm_nt(ul_all[r, :], uw_ref[cols, :])
            ).astype(BF)

    block = 16

    def combine(zd, h, with_in):
        def step(i, _):
            rr = pl.ds(pl.multiple_of(h * half + i * block, block), block)
            value = own[2 * zd + core, rr, :].astype(F32) + sib[zd, rr, :].astype(F32)
            if with_in:
                value = value + zin[zd, rr, :].astype(F32)
            own[2 * zd + core, rr, :] = value.astype(BF)
            return 0

        lax.fori_loop(0, half // block, step, 0)

    def slot_for(zd, nxt):
        return jnp.where((nxt == zd) & (nxt < z), depth, zd)

    def pass_on(zd, h, nxt, with_in):
        own_copy(zd, h).wait_recv()
        if with_in:
            zin_copy(zd, h, nxt, zd).wait_recv()
        combine(zd, h, with_in)
        zin_copy(zd, h, nxt, slot_for(zd, nxt)).start()

    quarter = width // 4
    cut = ff // 2
    order = (others[1], others[0], others[2], mine)

    def owner(j):
        return jnp.where(
            j == 0, order[0], jnp.where(j == 1, order[1], jnp.where(j == 2, order[2], mine))
        )

    def cols_of(dp):
        return pl.ds(pl.multiple_of(dp * quarter, 128), quarter)

    def tile_slot(kind, j):
        if kind == 0:
            return stage.at[j]
        return (gl_all, ul_all)[kind - 1].at[pl.ds(pl.multiple_of(j * quarter, 16), quarter)]

    sides = (slice(0, cut), slice(cut, ff))
    ends = ({"dp": others[0]}, {"dp": others[2]})
    hops = ((0, 0, 1, 0), (0, 1, 1, 1), (1, 0, 0, 0), (2, 1, 0, 1), (2, 0, 2, 1), (1, 1, 2, 0))

    def hop(kind, n):
        j, side, slot, way = hops[n]
        return pltpu.make_async_remote_copy(
            tile_slot(kind, j).at[:, sides[side]], landing.at[kind, slot, :, sides[side]],
            tile_send.at[kind, n], tile_recv.at[kind, slot, side],
            device_id=ends[way], device_id_type=MESH,
        )

    def col_copy(j):
        return pltpu.make_async_copy(dy_ref.at[:, :, cols_of(owner(j))], dy_cols, cols_sem)

    def tiles(kind, low, high):
        def step(j, _):
            cols = cols_of(owner(j))
            if kind == 2:
                col_copy(j).wait()
                tile = mm_tn(dy_cols[...].reshape(count * rows, quarter), hs_all[...])

                @pl.when(j < 3)
                def _():
                    col_copy(j + 1).start()
            else:
                tile = mm_tn(n2_all[:, cols], (gl_all, ul_all)[kind][...])
            tile = tile.astype(BF)

            @pl.when(j < 3)
            def _():
                tile_slot(kind, j)[...] = tile

            for n in range(4):

                @pl.when(j == hops[n][0])
                def _():
                    hop(kind, n).start()

            @pl.when(j == 3)
            def _():
                kept[kind] = tile

            return 0

        lax.fori_loop(low, high, step, 0)

    def spare(kind, i):
        return (gl_all, ul_all, gl_all)[kind].at[pl.ds(6 * quarter, quarter)]

    def second_leg(kind):
        for side in range(2):
            n = side
            hop(kind, n).wait_recv()
        load = pltpu.make_async_copy(landing.at[kind, 1], spare(kind, 6), load_sem.at[kind, 2])
        load.start()
        load.wait()
        for n in (4, 5):
            j, side, _, _ = hops[n]

            def step(i, _):
                rr = pl.ds(pl.multiple_of(i * 32, 32), 32)
                into = tile_slot(kind, j)
                value = into[rr, sides[side]].astype(F32) + spare(kind, 6)[rr, sides[side]].astype(F32)
                into[rr, sides[side]] = value.astype(BF)
                return 0

            lax.fori_loop(0, quarter // 32, step, 0)
            hop(kind, n).start()

    def by_distance(d, _):
        left, right = z - d, z + d
        has_left, has_right = left >= 0, (right < depth) & (d > 0)

        def other_chunk(zs):
            return 2 * zs + 1 - core

        for h in range(2):
            for s, zs, there in ((0, left, has_left), (1, right, has_right)):

                @pl.when(there)
                def _():
                    dy_copy(other_chunk(zs), h, 0, s).start()
                    dy_copy(2 * zs + core, h, 1, s).start()

            @pl.when(has_left & (d > 0))
            def _():
                k = 2 * left + core
                arrived(k, h)

                @pl.when(z < depth - 1)
                def _():
                    send_chunk(k, h, 0, at(z + 1))

                send_chunk(k, h, 2, {"expert": sibling})

            @pl.when(has_right)
            def _():
                k = 2 * right + core
                arrived(k, h)

                @pl.when(z > 0)
                def _():
                    send_chunk(k, h, 1, at(z - 1))

                send_chunk(k, h, 2, {"expert": sibling})

            def side(s, _):
                zs = jnp.where(s == 0, left, right)

                @pl.when(jnp.where(s == 0, has_left, has_right))
                def _():
                    def first(w, _):
                        k = 2 * zs + jnp.where(w == 0, 1 - core, core)

                        @pl.when(w == 0)
                        def _():
                            arrived(k, h)

                        dy_copy(k, h, w, s).wait()
                        hidden_part(k, h, w, s)
                        return 0

                    lax.fori_loop(0, 2, first, 0)
                    if h == 1:
                        @pl.when(d == jnp.maximum(z, depth - 1 - z))
                        def _():
                            tiles(0, 0, 3)

                    def second(w, _):
                        row_part(2 * zs + jnp.where(w == 0, 1 - core, core), h)

                        @pl.when(w == 0)
                        def _():
                            own_copy(zs, h).start()

                        return 0

                    lax.fori_loop(0, 2, second, 0)

                    @pl.when((d > 0) & ((z == 0) | (z == depth - 1)))
                    def _():
                        pass_on(zs, h, jnp.where(z == 0, 1, depth - 2), False)

                return 0

            lax.fori_loop(0, 2, side, 0)
        return 0

    for load in weight_loads:
        load.wait()
    col_copy(0).start()
    lax.fori_loop(0, depth, by_distance, 0)

    def sum_copy(k, slot):
        return pltpu.make_async_copy(own.at[slot], sum_ref.at[k], sum_sem.at[slot])

    def sums(low, high):
        def step(i, _):
            slot = 2 * lax.rem(i, depth) + 1 - core

            @pl.when(i < depth)
            def _():
                for h in range(2):
                    own_copy(i, h).wait_send()

            @pl.when(i >= depth)
            def _():
                sum_copy(i, slot).wait()

            wide = 512
            for j in range(width // wide):
                cols = slice(j * wide, (j + 1) * wide)
                own[slot, :, cols] = mm(hs_all[chunk(i), :], dw_ref[:, cols]).astype(BF)
            sum_copy(i, slot).start()
            return 0

        lax.fori_loop(low, high, step, 0)

    def flow(r, first, h):
        right = (z < depth - 1 - z) if first else (z >= depth - 1 - z)
        zd = jnp.where(right, r, depth - 1 - r)
        valid = jnp.where(right, (z < zd) & (z > 0), (z > zd) & (z < depth - 1))

        @pl.when(valid)
        def _():
            pass_on(zd, h, jnp.where(right, z + 1, z - 1), True)

    eighth = count // 4
    jobs = [
        lambda: tiles(0, 3, 4),
        lambda: tiles(1, 0, 2),
        lambda: tiles(1, 2, 4),
        lambda: second_leg(0),
        lambda: tiles(2, 0, 2),
        lambda: tiles(2, 2, 4),
        lambda: second_leg(1),
        *[lambda i=i: sums(i * eighth, (i + 1) * eighth) for i in range(4)],
        lambda: second_leg(2),
    ]
    for r in range(2, depth):
        for first in (True, False):
            for h in range(2):
                if first or r == depth - 1:
                    for _ in range(2):
                        if jobs:
                            jobs.pop(0)()
                flow(r, first, h)
    while jobs:
        jobs.pop(0)()

    for h in range(2):
        own_copy(z, h).wait_recv()

        @pl.when(z > 0)
        def _():
            zin_copy(z, h, z, z).wait_recv()

        @pl.when(z < depth - 1)
        def _():
            zin_copy(z, h, z, depth).wait_recv()

    def last(i, _):
        rr = pl.ds(pl.multiple_of(i * block, block), block)
        row_ref[rr, :] = own[me, rr, :].astype(F32) + sib[z, rr, :].astype(F32)

        @pl.when(z > 0)
        def _():
            row_ref[rr, :] += zin[z, rr, :].astype(F32)

        @pl.when(z < depth - 1)
        def _():
            row_ref[rr, :] += zin[depth, rr, :].astype(F32)

        return 0

    lax.fori_loop(0, rows // block, last, 0)

    for e in range(count):

        @pl.when(e != me)
        def _():
            pltpu.make_async_remote_copy(
                gg_out.at[e], gg_in.at[e], gg_send.at[e], gg_recv.at[e],
                device_id={"expert": e}, device_id_type=MESH,
            ).wait_recv()

    gg_ref[...] = jnp.sum(gg_in[...], axis=0)

    def tile_load(kind, i):
        into = (gl_all, ul_all, hs_all)[kind]
        return pltpu.make_async_copy(
            landing.at[kind, 2 * i], into.at[pl.ds((3 + i) * quarter, quarter)], load_sem.at[kind, i]
        )

    keeps = [
        pltpu.make_async_copy(kept.at[pl.ds(0, 2)], wide_ref, keep_sem.at[0]),
        pltpu.make_async_copy(down_kept, down_ref, keep_sem.at[1]),
    ]
    for kind in range(3):
        for n in (2, 3, 4, 5):
            hop(kind, n).wait_recv()
        for i in range(2):
            tile_load(kind, i).start()
    for kind in range(3):
        for i in range(2):
            tile_load(kind, i).wait()
        into = (gl_all, ul_all, hs_all)[kind]

        def add_up(i, _):
            rr = pl.ds(pl.multiple_of(i * 128, 128), 128)
            total = kept[kind, rr, :].astype(F32)
            for j in range(2):
                total = total + into[pl.ds(pl.multiple_of((3 + j) * quarter + i * 128, 128), 128), :].astype(F32)
            if kind == 2:
                down_kept[:, rr] = jnp.transpose(total).astype(BF)
            else:
                kept[kind, rr, :] = total.astype(BF)
            return 0

        lax.fori_loop(0, quarter // 128, add_up, 0)
        if kind > 0:
            keeps[kind - 1].start()

    for e in range(count):

        @pl.when(e != me)
        def _():
            gg_copy(e).wait_send()

        zs = e // 2

        for h in range(2):

            @pl.when(((e == me) | ((zs < z) & (e % 2 == core))) & (z < depth - 1))
            def _():
                sent_chunk(e, h, 0, at(z + 1))

            @pl.when(((e == me) | ((zs > z) & (e % 2 == core))) & (z > 0))
            def _():
                sent_chunk(e, h, 1, at(z - 1))

            @pl.when(e % 2 == core)
            def _():
                sent_chunk(e, h, 2, {"expert": sibling})

    for zd in range(depth):
        sum_copy(zd, 2 * zd + 1 - core).wait()
        for h in range(2):

            @pl.when(zd != z)
            def _():
                zin_copy(zd, h, z, zd).wait_send()

    for kind in range(3):
        for n in range(len(hops)):
            hop(kind, n).wait_send()
    for keep in keeps:
        keep.wait()


def expert_pass(n2, gate_rows, dy_all, gate_w, up_w, down_w):
    count = lax.axis_size("expert")
    depth = count // 2
    rows, width = n2.shape
    ff = gate_w.shape[1]
    lanes = gate_rows.shape[1]
    dma = pltpu.SemaphoreType.DMA
    vmem = pl.BlockSpec(memory_space=pltpu.VMEM)
    anywhere = pl.BlockSpec(memory_space=pl.ANY)
    outs = (
        jax.ShapeDtypeStruct((rows, width), F32),
        jax.ShapeDtypeStruct((count, lanes), F32),
        jax.ShapeDtypeStruct((count, rows, width), BF),
        jax.ShapeDtypeStruct((2, width // 4, ff), BF),
        jax.ShapeDtypeStruct((ff, width // 4), BF),
        jax.ShapeDtypeStruct((3, 3, width // 4, ff), BF),
    )
    return pl.pallas_call(
        expert_kernel,
        name="expert_pass",
        out_shape=outs,
        in_specs=[anywhere, vmem] + [anywhere] * 4,
        out_specs=(vmem, vmem, anywhere, anywhere, anywhere, anywhere),
        scratch_shapes=[
            pltpu.VMEM((width, ff), BF),
            pltpu.VMEM((width, ff), BF),
            pltpu.VMEM((ff, width), BF),
            pltpu.VMEM((count * rows, width), BF),
            pltpu.VMEM((count, count, lanes), F32),
            pltpu.VMEM((2, 2, rows // 2, width), BF),
            pltpu.VMEM((count, rows, width // 4), BF),
            pltpu.VMEM((count * rows, ff), BF),
            pltpu.VMEM((count * rows, ff), BF),
            pltpu.VMEM((count * rows, ff), BF),
            pltpu.VMEM((count, rows, width), BF),
            pltpu.VMEM((depth, rows, width), BF),
            pltpu.VMEM((depth + 1, rows, width), BF),
            pltpu.VMEM((count, count, lanes), F32),
            pltpu.VMEM((count, count, lanes), F32),
            pltpu.VMEM((4, lanes, 128), F32),
            pltpu.VMEM((4, lanes, 128), F32),
            pltpu.VMEM((3, width // 4, ff), BF),
            pltpu.VMEM((3, width // 4, ff), BF),
            pltpu.VMEM((ff, width // 4), BF),
            dma((count, 2, 3)), dma((count, 2)), dma((count, 3)), dma((count,)),
            dma((depth, 2)), dma((depth, 2)), dma((depth, 2)), dma((depth + 1, 2)),
            dma((count,)), dma((count,)), dma((2, 2)), dma, dma((count,)), dma((3, 6)), dma((3, 3, 2)),
            dma((3, 3)), dma((2,)), dma((3,)),
        ],
        compiler_params=pltpu.CompilerParams(
            collective_id=2, has_side_effects=True, vmem_limit_bytes=62 * 2**20
        ),
        cost_estimate=pl.CostEstimate(
            flops=18 * count * rows * width * ff, bytes_accessed=60 * 2**20, transcendentals=0
        ),
    )(n2, gate_rows, dy_all, gate_w, up_w, down_w)


def greet(depth, z, at, targets):
    barrier = pltpu.get_barrier_semaphore()
    for target in targets:
        pl.semaphore_signal(barrier, 1, device_id=target, device_id_type=MESH)

    @pl.when(z > 0)
    def _():
        pl.semaphore_signal(barrier, 1, device_id=at(z - 1), device_id_type=MESH)

    @pl.when(z < depth - 1)
    def _():
        pl.semaphore_signal(barrier, 1, device_id=at(z + 1), device_id_type=MESH)

    ends = (z > 0).astype(jnp.int32) + (z < depth - 1).astype(jnp.int32)
    pl.semaphore_wait(barrier, len(targets) + ends)


def attention_kernel(
    x_ref, wq_ref, wk_ref, wv_ref, ws_ref, wo_ref, freq_ref, parent_ref, hits_ref, dy_ref,
    n1_ref, q_ref, kv_ref, mixed_ref, lse_ref, middle_ref, n2_ref, gate_ref, cos_ref, sin_ref,
    bias_ref, w_out, dy_all,
    w, n1, q, kv, mixed, bias,
    z_send, z_recv, x_send, x_recv, y_send, y_recv, a_send, a_recv, b_send, b_recv, s_send, s_recv,
    kx_send, kx_recv, ky_send, ky_recv, ka_send, ka_recv, kb_send, kb_recv, dy_send, dy_recv, out_sem, keep_sem, dy_sem,
):
    count = lax.axis_size("expert")
    depth = count // 2
    shard, total = wq_ref.shape[0], w.shape[1]
    rows, width = x_ref.shape
    heads = q.shape[1] // HEAD_SIZE
    kv_width = kv.shape[1]
    groups = kv_width // (2 * HEAD_SIZE)
    group = heads // groups
    wide = heads * HEAD_SIZE
    qkv_width = wide + kv_width
    split = qkv_width + 128
    me, mine = lax.axis_index("expert"), lax.axis_index("dp")
    z, core = me // 2, me % 2
    y, x = mine // 2, mine % 2
    xn, yn, diag = y * 2 + 1 - x, (1 - y) * 2 + x, (1 - y) * 2 + 1 - x
    sibling = {"expert": z * 2 + 1 - core}

    def at(zz):
        return {"expert": zz * 2 + core}

    greet(depth, z, at, (sibling, {"dp": xn}, {"dp": yn}))

    def remote(src, dst, send, recv, target):
        return pltpu.make_async_remote_copy(
            src, dst, send, recv, device_id=target, device_id_type=MESH
        )

    bounds = ((wide, split), (0, wide), (split, total))
    cuts = tuple(low + ((high - low) // 128 + 1) // 2 * 128 for low, high in bounds)

    def place(dp, zz, cc):
        return pl.ds(pl.multiple_of((dp * count + 2 * zz + cc) * shard, 16), shard)

    def w_copy(dp, zz, low, high, send, recv, target, cc=core):
        ref = w.at[place(dp, zz, cc), pl.ds(low, high - low)]
        return remote(ref, ref, send, recv, target)

    def z_copy(p, zz, lane, target):
        return w_copy(mine, zz, *bounds[p], z_send.at[p, zz, lane], z_recv.at[p, zz], target)

    def x_copy(p, zz, dp):
        return w_copy(dp, zz, *bounds[p], x_send.at[p, zz], x_recv.at[p, zz], {"dp": xn})

    def y_copy(p, zz, dp):
        return w_copy(dp, zz, *bounds[p], y_send.at[p, zz], y_recv.at[p, zz], {"dp": yn})

    def a_copy(p, zz, dp):
        return w_copy(dp, zz, bounds[p][0], cuts[p], a_send.at[p, zz], a_recv.at[p, zz], {"dp": yn})

    def b_copy(p, zz, dp):
        return w_copy(dp, zz, cuts[p], bounds[p][1], b_send.at[p, zz], b_recv.at[p, zz], {"dp": xn})

    def s_copy(p, dp, zz, cc=core):
        return w_copy(dp, zz, *bounds[p], s_send.at[p, dp, zz], s_recv.at[p, dp, zz], sibling, cc)

    def spread(p, zz):
        x_copy(p, zz, mine).start()
        y_copy(p, zz, mine).start()
        s_copy(p, mine, zz).start()

    def on_sides(d, action):
        @pl.when(z - d >= 0)
        def _():
            action(z - d, True)

        if d > 0:

            @pl.when(z + d < depth)
            def _():
                action(z + d, False)

    def z_step(p, d):
        if d == 0:

            @pl.when(z < depth - 1)
            def _():
                z_copy(p, z, 0, at(z + 1)).start()

            @pl.when(z > 0)
            def _():
                z_copy(p, z, 1, at(z - 1)).start()

            return

        def action(zz, from_left):
            z_copy(p, zz, 0, at(z)).wait_recv()
            if from_left:

                @pl.when(z < depth - 1)
                def _():
                    z_copy(p, zz, 0, at(z + 1)).start()
            else:

                @pl.when(z > 0)
                def _():
                    z_copy(p, zz, 1, at(z - 1)).start()

        on_sides(d, action)

    def spread_step(p, d):
        on_sides(d, lambda zz, _: spread(p, zz))

    def xy_step(p, d):
        def action(zz, _):
            x_copy(p, zz, xn).wait_recv()
            a_copy(p, zz, xn).start()
            s_copy(p, xn, zz).start()
            y_copy(p, zz, yn).wait_recv()
            b_copy(p, zz, yn).start()
            s_copy(p, yn, zz).start()

        on_sides(d, action)

    def diag_step(p, d):
        def action(zz, _):
            a_copy(p, zz, diag).wait_recv()
            b_copy(p, zz, diag).wait_recv()
            s_copy(p, diag, zz).start()

        on_sides(d, action)

    def all_here(p):
        for dp in range(4):
            for zz in range(depth):
                s_copy(p, dp, zz, 1 - core).wait_recv()

    def all_sent(p):
        for zz in range(depth):

            @pl.when((zz <= z) & (z < depth - 1))
            def _():
                z_copy(p, zz, 0, at(z)).wait_send()

            @pl.when((zz >= z) & (z > 0))
            def _():
                z_copy(p, zz, 1, at(z)).wait_send()

            x_copy(p, zz, mine).wait_send()
            y_copy(p, zz, mine).wait_send()
            a_copy(p, zz, xn).wait_send()
            b_copy(p, zz, yn).wait_send()
            for dp in range(4):
                s_copy(p, dp, zz).wait_send()

    def dy_copy(k, lane, target):
        return remote(dy_all.at[k], dy_all.at[k], dy_send.at[k, lane], dy_recv.at[k], target)

    def dy_own(lane, target):
        return remote(dy_ref, dy_all.at[me], dy_send.at[me, lane], dy_recv.at[me], target)

    dy_keep = pltpu.make_async_copy(dy_ref, dy_all.at[me], dy_sem)

    def dy_step(d):
        if d == 0:
            dy_own(2, sibling).start()
            dy_keep.start()

            @pl.when(z < depth - 1)
            def _():
                dy_own(0, at(z + 1)).start()

            @pl.when(z > 0)
            def _():
                dy_own(1, at(z - 1)).start()

            return

        def action(zz, from_left):
            k = 2 * zz + core
            dy_copy(k, 0, sibling).wait_recv()
            if from_left:

                @pl.when(z < depth - 1)
                def _():
                    dy_copy(k, 0, at(z + 1)).start()
            else:

                @pl.when(z > 0)
                def _():
                    dy_copy(k, 1, at(z - 1)).start()

            dy_copy(k, 2, sibling).start()

        on_sides(d, action)

    def dy_end():
        dy_keep.wait()
        for zz in range(depth):
            dy_copy(2 * zz + 1 - core, 2, sibling).wait_recv()
            k = 2 * zz + core
            dy_copy(k, 2, sibling).wait_send()

            @pl.when((zz <= z) & (z < depth - 1))
            def _():
                dy_copy(k, 0, sibling).wait_send()

            @pl.when((zz >= z) & (z > 0))
            def _():
                dy_copy(k, 1, sibling).wait_send()

    home = place(mine, z, core)
    w[home, 0:wide] = wq_ref[...]
    for g in range(groups):
        low, head = wide + 2 * g * HEAD_SIZE, slice(g * HEAD_SIZE, (g + 1) * HEAD_SIZE)
        w[home, low : low + HEAD_SIZE] = wk_ref[:, head]
        w[home, low + HEAD_SIZE : low + 2 * HEAD_SIZE] = wv_ref[:, head]
    w[home, qkv_width:split] = ws_ref[...]
    w[home, split:total] = wo_ref[...]
    z_step(0, 0)
    spread_step(0, 0)

    blocks = parent_ref.shape[1]
    trunk = blocks - BRANCHES - LEAVES
    ids = mine * rows + lax.broadcasted_iota(jnp.int32, (rows, 1), 0)
    query_block = lax.div(ids, SEG)
    level = jnp.minimum(query_block, trunk) + (query_block >= trunk + BRANCHES).astype(jnp.int32)
    positions = (level * SEG + lax.rem(ids, SEG)).astype(F32)
    angles = positions * freq_ref[...]
    cos_ref[...] = jnp.cos(angles)
    turned = lax.broadcasted_iota(jnp.int32, angles.shape, 1) < HEAD_SIZE // 2
    sine = jnp.sin(angles)
    sin_ref[...] = jnp.where(turned, -sine, sine)
    z_step(0, 1)
    spread_step(0, 1)
    xy_step(0, 0)
    block_ids = lax.broadcasted_iota(jnp.int32, (rows, blocks), 1)
    parent = jnp.sum(jnp.where(block_ids == query_block, parent_ref[...], 0), axis=1, keepdims=True)
    above = jnp.where(query_block >= trunk + BRANCHES, parent, query_block)
    keys = bias.shape[1] // 128

    def visible(i, _):
        cols = pl.ds(pl.multiple_of(i * 128, 128), 128)
        key_ids = i * 128 + lax.broadcasted_iota(jnp.int32, (rows, 128), 1)
        key_block = lax.div(key_ids, SEG)
        related = (key_block < trunk) | (key_block == query_block) | (key_block == above)
        bias[:, cols] = jnp.where(related & (key_ids <= ids), 0.0, NEGATIVE)
        return 0

    z_step(0, 2)
    spread_step(0, 2)
    z_step(1, 0)
    xy_step(0, 1)
    lax.fori_loop(0, keys, visible, 0)
    z_step(0, 3)
    spread_step(0, 3)
    z_step(2, 0)
    spread_step(1, 0)
    z_step(1, 1)
    spread_step(1, 1)
    xy_step(0, 2)
    z_step(2, 1)
    xy_step(0, 3)
    z_step(1, 2)
    spread_step(1, 2)
    for d in range(depth):
        diag_step(0, d)
    z_step(2, 2)
    xy_step(1, 0)
    z_step(1, 3)
    spread_step(1, 3)
    z_step(2, 3)
    dy_step(0)
    all_here(0)

    def keep(p):
        low, high = bounds[p]
        return pltpu.make_async_copy(
            w.at[:, pl.ds(low, high - low)], w_out.at[:, pl.ds(low, high - low)], keep_sem.at[p]
        )

    keep(0).start()
    small = jnp.transpose(w[:, qkv_width:split].astype(F32))
    experts = hits_ref.shape[0]
    gain_one, gain_two = small[experts : experts + 1], small[experts + 1 : experts + 2]

    block = 32

    def first_norm(i, _):
        rr = pl.ds(pl.multiple_of(i * block, block), block)
        value = x_ref[rr, :].astype(F32)
        scale = lax.rsqrt(jnp.mean(value * value, axis=1, keepdims=True) + EPS)
        n1[rr, :] = (value * scale * gain_one).astype(BF)
        return 0

    lax.fori_loop(0, rows // block, first_norm, 0)

    def turn(value):
        return value * cos_ref[...] + pltpu.roll(value, HEAD_SIZE // 2, 1) * sin_ref[...]

    own = pl.ds(pl.multiple_of(mine * rows, 16), rows)
    projected = mm(n1[...], w[:, wide:qkv_width])
    for g in range(groups):
        low = 2 * g * HEAD_SIZE
        kv[own, low : low + HEAD_SIZE] = turn(projected[:, low : low + HEAD_SIZE]).astype(BF)
        kv[own, low + HEAD_SIZE : low + 2 * HEAD_SIZE] = projected[
            :, low + HEAD_SIZE : low + 2 * HEAD_SIZE
        ].astype(BF)

    def kv_copy(g, dp, low, high, send, recv, target):
        ref = kv.at[
            pl.ds(pl.multiple_of(dp * rows, 16), rows),
            pl.ds((2 * g + low) * HEAD_SIZE, (high - low) * HEAD_SIZE),
        ]
        return remote(ref, ref, send.at[g], recv.at[g], target)

    def kx(g, dp):
        return kv_copy(g, dp, 0, 2, kx_send, kx_recv, {"dp": xn})

    def ky(g, dp):
        return kv_copy(g, dp, 0, 2, ky_send, ky_recv, {"dp": yn})

    def ka(g, dp):
        return kv_copy(g, dp, 0, 1, ka_send, ka_recv, {"dp": yn})

    def kb(g, dp):
        return kv_copy(g, dp, 1, 2, kb_send, kb_recv, {"dp": xn})

    def kv_on(g):
        kx(g, xn).wait_recv()
        ka(g, xn).start()
        ky(g, yn).wait_recv()
        kb(g, yn).start()

    def kv_here(g):
        ka(g, diag).wait_recv()
        kb(g, diag).wait_recv()

    for g in range(groups):
        kx(g, mine).start()
        ky(g, mine).start()
    xy_step(1, 1)
    xy_step(1, 2)
    kv_on(0)
    xy_step(1, 3)
    kv_on(1)
    for d in range(depth):
        diag_step(1, d)
        spread_step(2, d)
    kv_here(0)
    all_here(1)
    keep(1).start()
    dy_step(1)

    def project(h, _):
        cols = pl.ds(pl.multiple_of(h * 2 * HEAD_SIZE, 2 * HEAD_SIZE), 2 * HEAD_SIZE)
        value = mm(n1[...], w[:, cols])
        q[:, cols] = jnp.concatenate(
            [turn(value[:, :HEAD_SIZE]), turn(value[:, HEAD_SIZE:])], axis=1
        ).astype(BF)
        return 0

    lax.fori_loop(0, heads // 2, project, 0)
    later = [
        lambda: xy_step(2, 0),
        lambda: xy_step(2, 1),
        lambda: xy_step(2, 2),
        lambda: xy_step(2, 3),
        lambda: kv_here(1),
        lambda: (diag_step(2, 0), diag_step(2, 1)),
        lambda: (diag_step(2, 2), diag_step(2, 3)),
    ]
    lse_ref[...] = jnp.zeros_like(lse_ref)
    lanes = lax.broadcasted_iota(jnp.int32, lse_ref.shape, 1)

    def attend(h, _):
        for i, job in enumerate(later):
            pl.when(h == i)(lambda job=job: (job(), None)[1])
        g = h // group
        cols = pl.ds(pl.multiple_of(h * HEAD_SIZE, HEAD_SIZE), HEAD_SIZE)
        k_cols = pl.ds(pl.multiple_of(g * 2 * HEAD_SIZE, HEAD_SIZE), HEAD_SIZE)
        v_cols = pl.ds(pl.multiple_of(g * 2 * HEAD_SIZE + HEAD_SIZE, HEAD_SIZE), HEAD_SIZE)
        scores = mm_nt(q[:, cols], kv[:, k_cols]) * (HEAD_SIZE**-0.5 * LOG2E) + bias[...]
        top = jnp.max(scores, axis=1, keepdims=True)
        power = jnp.exp2(scores - top)
        sums = jnp.sum(power, axis=1, keepdims=True)
        mixed[:, cols] = (mm(power.astype(BF), kv[:, v_cols]) / sums).astype(BF)
        lse_ref[...] = jnp.where(lanes == h, top + jnp.log2(sums), lse_ref[...])
        return 0

    lax.fori_loop(0, heads, attend, 0)
    keeps = [
        pltpu.make_async_copy(src, dst, out_sem.at[i])
        for i, (src, dst) in enumerate(
            ((n1, n1_ref), (q, q_ref), (kv, kv_ref), (mixed, mixed_ref), (bias, bias_ref))
        )
    ]
    for copy in keeps:
        copy.start()
    all_here(2)
    keep(2).start()
    dy_step(2)
    tile = 512

    def project_out(i, _):
        cols = pl.ds(pl.multiple_of(i * tile, tile), tile)
        w_cols = pl.ds(pl.multiple_of(split + i * tile, 128), tile)
        middle_ref[:, cols] = x_ref[:, cols].astype(F32) + mm(mixed[...], w[:, w_cols])
        return 0

    lax.fori_loop(0, width // tile, project_out, 0)

    def second_norm(i, _):
        rr = pl.ds(pl.multiple_of(i * block, block), block)
        value = middle_ref[rr, :]
        scale = lax.rsqrt(jnp.mean(value * value, axis=1, keepdims=True) + EPS)
        n2_ref[rr, :] = (value * scale * gain_two).astype(BF)
        return 0

    lax.fori_loop(0, rows // block, second_norm, 0)
    logits = mm_nt(small.astype(BF), n2_ref[...])[:experts]
    hits = hits_ref[...] > 0.5
    chosen = jnp.where(hits, logits, NEGATIVE)
    power = jnp.where(hits, jnp.exp(chosen - jnp.max(chosen, axis=0, keepdims=True)), 0.0)
    gate_ref[...] = jnp.zeros_like(gate_ref)
    gate_ref[:, :rows] = power / jnp.sum(power, axis=0, keepdims=True)

    dy_step(3)
    dy_end()
    for g in range(groups):
        kx(g, mine).wait_send()
        ky(g, mine).wait_send()
        ka(g, xn).wait_send()
        kb(g, yn).wait_send()
    for p in range(3):
        all_sent(p)
        keep(p).wait()
    for copy in keeps:
        copy.wait()


def attention_pass(x, shards, freq, parent, hits, dy):
    count = lax.axis_size("expert")
    depth = count // 2
    rows, width = x.shape
    lanes = rows + -rows % 128
    shard = shards[0].shape[0]
    devices = 4 * count
    wide = shards[0].shape[1]
    kv_width = 2 * shards[1].shape[1]
    dma = pltpu.SemaphoreType.DMA
    vmem = pl.BlockSpec(memory_space=pltpu.VMEM)
    anywhere = pl.BlockSpec(memory_space=pl.ANY)
    shape = jax.ShapeDtypeStruct
    parts = 3
    pair = dma((parts, depth))
    groups = kv_width // (2 * HEAD_SIZE)
    tree = 4 * rows
    total = kv_width + sum(part.shape[1] for part in (shards[0], *shards[3:]))
    return pl.pallas_call(
        attention_kernel,
        name="attention_pass",
        out_shape=(
            shape((rows, width), BF),
            shape((rows, wide), BF),
            shape((tree, kv_width), BF),
            shape((rows, wide), BF),
            shape((rows, 128), F32),
            shape((rows, width), F32),
            shape((rows, width), BF),
            shape((hits.shape[0], lanes), F32),
            shape((rows, HEAD_SIZE), F32),
            shape((rows, HEAD_SIZE), F32),
            shape((rows, tree), F32),
            shape((devices * shard, total), BF),
            shape((count, rows, width), BF),
        ),
        in_specs=[vmem] * 9 + [anywhere],
        out_specs=(anywhere,) * 4 + (vmem,) * 6 + (anywhere,) * 3,
        scratch_shapes=[
            pltpu.VMEM((devices * shard, total), BF),
            pltpu.VMEM((rows, width), BF),
            pltpu.VMEM((rows, wide), BF),
            pltpu.VMEM((tree, kv_width), BF),
            pltpu.VMEM((rows, wide), BF),
            pltpu.VMEM((rows, tree), F32),
            dma((parts, depth, 2)), pair, pair, pair, pair, pair, pair, pair, pair, pair,
            dma((parts, 4, depth)), dma((parts, 4, depth)),
            *[dma((groups,)) for _ in range(8)],
            dma((count, 3)), dma((count,)), dma((5,)), dma((parts,)), dma,
        ],
        compiler_params=pltpu.CompilerParams(
            collective_id=1, has_side_effects=True, vmem_limit_bytes=56 * 2**20
        ),
        cost_estimate=pl.CostEstimate(
            flops=10**10, bytes_accessed=300 * 2**20, transcendentals=0
        ),
    )(x, *shards, freq, parent, hits, dy)


def backward_kernel(
    gate_ref, gg_ref, x_any, dy_any, n1_any, q_any, kv_any, mixed_any, n2_any, lse_any,
    cos_any, sin_any, bias_any, middle_any, row_ref, w_full, wide_ref, down_ref,
    tok_ref, share_ref, wide_all, down_all,
    x_ref, dy_ref, n1_ref, q_ref, kv_ref, mixed_ref, n2_ref, lse_ref, cos_ref, sin_ref, bias_ref,
    middle, wbuf, wsmall, attended, mixed_grad, qg, dkv, kv_low, kv_in, w, wsib, legs, legs2, wz,
    load_sem, ag_local, ag_xs, ag_xr, ag_ys, ag_yr, ag_fs, ag_fr, kv_send, kv_recv,
    ws_send, ws_recv, a_send, a_recv, b_send, b_recv, a2_send, a2_recv, b2_send, b2_recv,
    wz_send, wz_recv,
):
    depth = lax.axis_size("expert") // 2
    rows, width = x_ref.shape
    heads = q_ref.shape[1] // HEAD_SIZE
    kv_width = kv_ref.shape[1]
    groups = kv_width // (2 * HEAD_SIZE)
    group = heads // groups
    wide = heads * HEAD_SIZE
    qkv_width = wide + kv_width
    split = qkv_width + 128
    shard, total = share_ref.shape
    me, mine = lax.axis_index("expert"), lax.axis_index("dp")
    z, core = me // 2, me % 2
    y, x = mine // 2, mine % 2
    xn, yn, diag = y * 2 + 1 - x, (1 - y) * 2 + x, (1 - y) * 2 + 1 - x
    sibling = {"expert": z * 2 + 1 - core}

    def at(zz):
        return {"expert": zz * 2 + core}

    def remote(src, dst, send, recv, target):
        return pltpu.make_async_remote_copy(
            src, dst, send, recv, device_id=target, device_id_type=MESH
        )

    def load(src, dst, i):
        return pltpu.make_async_copy(src, dst, load_sem.at[i])

    load_rows = load(row_ref, tok_ref, 0)
    load_out = load(w_full.at[:, pl.ds(split, width)], wbuf.at[:, pl.ds(0, width)], 1)
    load_small = load(w_full.at[:, pl.ds(qkv_width, 128)], wsmall, 2)
    load_qkv = load(w_full.at[:, pl.ds(0, qkv_width)], wbuf, 3)
    load_middle = load(middle_any, middle, 4)
    load_n2, load_dy, load_mixed, *load_rest = [
        load(src, dst, 5 + i)
        for i, (src, dst) in enumerate(
            (
                (n2_any, n2_ref), (dy_any, dy_ref), (mixed_any, mixed_ref), (q_any, q_ref),
                (kv_any, kv_ref), (lse_any, lse_ref), (bias_any, bias_ref), (cos_any, cos_ref),
                (sin_any, sin_ref), (n1_any, n1_ref), (x_any, x_ref),
            )
        )
    ]
    for first in (load_small, load_n2, load_rows, load_middle, load_dy, load_mixed, load_out):
        first.start()
    for rest in load_rest:
        rest.start()
    greet(depth, z, at, (sibling, {"dp": xn}, {"dp": yn}, {"dp": diag}))

    quarter = wide_ref.shape[1]
    down_half = down_ref.shape[0] // 2

    def quarter_of(piece, dp):
        span = pl.ds(pl.multiple_of(dp * quarter, 128), quarter)
        if piece < 2:
            return wide_all.at[piece, span]
        return down_all.at[pl.ds((piece - 2) * down_half, down_half), span]

    def own_quarter(piece):
        if piece < 2:
            return wide_ref.at[piece]
        return down_ref.at[pl.ds((piece - 2) * down_half, down_half)]

    def keep_quarter(piece):
        return pltpu.make_async_copy(own_quarter(piece), quarter_of(piece, mine), ag_local.at[piece])

    def quarter_x(piece, dp):
        return remote(own_quarter(piece), quarter_of(piece, dp), ag_xs.at[piece], ag_xr.at[piece], {"dp": xn})

    def quarter_y(piece, dp):
        return remote(own_quarter(piece), quarter_of(piece, dp), ag_ys.at[piece], ag_yr.at[piece], {"dp": yn})

    def quarter_on(piece, dp, target):
        ref = quarter_of(piece, dp)
        return remote(ref, ref, ag_fs.at[piece], ag_fr.at[piece], target)

    def quarters(piece):
        quarter_x(piece, mine).start()
        quarter_y(piece, mine).start()
        keep_quarter(piece).start()

    def quarters_on(piece):
        if piece % 2 == 0:
            quarter_x(piece, xn).wait_recv()
            quarter_on(piece, xn, {"dp": yn}).start()
        else:
            quarter_y(piece, yn).wait_recv()
            quarter_on(piece, yn, {"dp": xn}).start()

    quarters(0)

    bounds = ((split, total), (0, wide // 2), (wide // 2, wide), (wide, split))
    cuts = tuple(low + ((high - low) // 128 + 1) // 2 * 128 for low, high in bounds)

    def span(low, high):
        return pl.ds(low, high - low)

    def ws_copy(p, dp):
        cols = span(*bounds[p])
        return remote(
            w.at[dp, :, 1 - core, :, cols], wsib.at[dp, :, :, cols],
            ws_send.at[p, dp], ws_recv.at[p, dp], sibling,
        )

    def a_cols(p):
        return span(bounds[p][0], cuts[p])

    def b_cols(p):
        return span(cuts[p], bounds[p][1])

    def a_copy(p, yy):
        return remote(
            w.at[yy * 2 + 1 - x, :, core, :, a_cols(p)], legs.at[yy, :, :, a_cols(p)],
            a_send.at[p, yy], a_recv.at[p, yy], {"dp": xn},
        )

    def b_copy(p, xx):
        return remote(
            w.at[(1 - y) * 2 + xx, :, core, :, b_cols(p)], legs.at[xx, :, :, b_cols(p)],
            b_send.at[p, xx], b_recv.at[p, xx], {"dp": yn},
        )

    def a2_copy(p):
        return remote(
            w.at[yn, :, core, :, a_cols(p)], legs2.at[:, :, a_cols(p)], a2_send.at[p], a2_recv.at[p], {"dp": yn}
        )

    def b2_copy(p):
        return remote(
            w.at[xn, :, core, :, b_cols(p)], legs2.at[:, :, b_cols(p)], b2_send.at[p], b2_recv.at[p], {"dp": xn}
        )

    def wz_copy(p, zd, nxt, slot):
        cols = span(*bounds[p])
        return remote(
            w.at[mine, zd, core, :, cols], wz.at[slot, :, cols], wz_send.at[p, zd], wz_recv.at[p, slot], at(nxt)
        )

    block = 16
    steps = shard // block

    def add(dp, term, cols):
        def step(i, _):
            zz, rr = i // steps, pl.ds(pl.multiple_of(lax.rem(i, steps) * block, block), block)
            value = w[dp, zz, core, rr, cols].astype(F32) + term[zz, rr, cols].astype(F32)
            w[dp, zz, core, rr, cols] = value.astype(BF)
            return 0

        lax.fori_loop(0, depth * steps, step, 0)

    def begin(p):
        for dp in (xn, diag, yn, mine):
            ws_copy(p, dp).start()

    def first_legs(p):
        def combine(dp):
            ws_copy(p, dp).wait_recv()
            add(dp, wsib.at[dp], span(*bounds[p]))

        combine(xn)
        a_copy(p, y).start()
        combine(diag)
        a_copy(p, 1 - y).start()
        b_copy(p, 1 - x).start()
        combine(yn)
        b_copy(p, x).start()
        combine(mine)

    def second_legs(p):
        a_copy(p, 1 - y).wait_recv()
        add(yn, legs.at[1 - y], a_cols(p))
        a2_copy(p).start()
        b_copy(p, 1 - x).wait_recv()
        add(xn, legs.at[1 - x], b_cols(p))
        b2_copy(p).start()
        a_copy(p, y).wait_recv()
        add(mine, legs.at[y], a_cols(p))
        b_copy(p, x).wait_recv()
        add(mine, legs.at[x], b_cols(p))

    def slot_for(zd, nxt):
        return jnp.where((nxt == zd) & (nxt < z), depth, zd)

    def line(p):
        a2_copy(p).wait_recv()
        add(mine, legs2, a_cols(p))
        b2_copy(p).wait_recv()
        add(mine, legs2, b_cols(p))

        @pl.when((z == 0) | (z == depth - 1))
        def _():
            nxt = jnp.where(z == 0, 1, depth - 2)
            for d in range(1, depth):
                zd = jnp.where(z == 0, depth - d, d - 1)
                wz_copy(p, zd, nxt, slot_for(zd, nxt)).start()

    def line_on(p):
        cols = span(*bounds[p])
        for r in range(depth - 1, 1, -1):
            for first in (True, False):
                right = (z < depth - 1 - z) if first else (z >= depth - 1 - z)
                zd = jnp.where(right, r, depth - 1 - r)
                nxt = jnp.where(right, z + 1, z - 1)
                valid = jnp.where(right, (z < zd) & (z > 0), (z > zd) & (z < depth - 1))

                @pl.when(valid)
                def _():
                    wz_copy(p, zd, nxt, zd).wait_recv()

                    def step(i, _):
                        rr = pl.ds(pl.multiple_of(i * block, block), block)
                        value = w[mine, zd, core, rr, cols].astype(F32) + wz[zd, rr, cols].astype(F32)
                        w[mine, zd, core, rr, cols] = value.astype(BF)
                        return 0

                    lax.fori_loop(0, steps, step, 0)
                    wz_copy(p, zd, nxt, slot_for(zd, nxt)).start()

    def line_end(p):
        cols = span(*bounds[p])
        share_ref[:, cols] = w[mine, z, core, :, cols].astype(F32)

        @pl.when(z > 0)
        def _():
            wz_copy(p, z, z, z).wait_recv()
            share_ref[:, cols] += wz[z, :, cols].astype(F32)

        @pl.when(z < depth - 1)
        def _():
            wz_copy(p, z, z, depth).wait_recv()
            share_ref[:, cols] += wz[depth, :, cols].astype(F32)

    def weight_rows(left, right, low, size):
        quarter_rows = width // 4

        def step(i, _):
            cols = pl.ds(pl.multiple_of(i * quarter_rows, 128), quarter_rows)
            tile = mm_tn(left[:, cols], right).astype(BF)
            w[i, :, :, :, low : low + size] = tile.reshape(depth, 2, shard, size)
            return 0

        lax.fori_loop(0, 4, step, 0)

    experts = gate_ref.shape[0]
    gates, gate_grad = gate_ref[:, :rows], gg_ref[:, :rows]
    logit_grad = gates * (gate_grad - jnp.sum(gates * gate_grad, axis=0, keepdims=True))
    high = logit_grad.astype(BF)
    logit_two = jnp.concatenate([high.astype(F32), logit_grad - high.astype(F32)], axis=0).astype(BF)
    load_small.wait()
    small = jnp.transpose(wsmall[...].astype(F32))
    router = small[:experts].astype(BF).astype(F32)
    router_two = jnp.concatenate([router, router], axis=0).astype(BF)
    gain_one, gain_two = small[experts : experts + 1], small[experts + 1 : experts + 2]
    load_n2.wait()
    router_grad = mm(logit_two, n2_ref[...])
    router_grad = router_grad[:experts] + router_grad[experts:]
    load_rows.wait()
    load_middle.wait()
    load_dy.wait()
    tok_ref[...] += mm_tn(logit_two, router_two)

    def norm_back(value, grad, gain):
        scale = lax.rsqrt(jnp.mean(value * value, axis=1, keepdims=True) + EPS)
        unit = value * scale
        scaled = grad * gain
        back = scale * (scaled - unit * jnp.mean(scaled * unit, axis=1, keepdims=True))
        return back, jnp.sum(grad * unit, axis=0, keepdims=True)

    def second_norm(i, carry):
        rr = pl.ds(pl.multiple_of(i * block, block), block)
        back, gain = norm_back(middle[rr, :], tok_ref[rr, :], gain_two)
        back = back + dy_ref[rr, :].astype(F32)
        tok_ref[rr, :] = back
        attended[rr, :] = back.astype(BF)
        return carry + gain

    gain_two_grad = lax.fori_loop(0, rows // block, second_norm, jnp.zeros((1, width), F32))
    load_mixed.wait()
    weight_rows(mixed_ref, attended[...], split, width)
    begin(0)
    load_out.wait()
    tile = 512

    def mixed_step(i, _):
        out_rows = pl.ds(pl.multiple_of(i * tile, tile), tile)
        mixed_grad[:, out_rows] = mm_nt(attended[...], wbuf[out_rows, :width]).astype(BF)
        return 0

    lax.fori_loop(0, wide // tile, mixed_step, 0)
    load_qkv.start()
    first_legs(0)
    quarters(1)
    for rest in load_rest:
        rest.wait()

    lanes = lax.broadcasted_iota(jnp.int32, lse_ref.shape, 1)

    def turn_back(value):
        return value * cos_ref[...] - pltpu.roll(value, HEAD_SIZE // 2, 1) * sin_ref[...]

    def kv_copy(g, i):
        dp = (xn, diag, yn)[i]
        return remote(
            kv_low.at[g, pl.ds(pl.multiple_of(dp * rows, 16), rows)], kv_in.at[g, mine],
            kv_send.at[g, i], kv_recv.at[g, mine], {"dp": dp},
        )

    def attend_group(g, polls):
        low = 2 * g * HEAD_SIZE
        key, value = kv_ref[:, low : low + HEAD_SIZE], kv_ref[:, low + HEAD_SIZE : low + 2 * HEAD_SIZE]

        def attend(i, _):
            for j, job in polls.items():
                pl.when(i == j)(lambda job=job: (job(), None)[1])
            h = g * group + i
            cols = pl.ds(pl.multiple_of(h * HEAD_SIZE, HEAD_SIZE), HEAD_SIZE)
            query, grad = q_ref[:, cols], mixed_grad[:, cols]
            level = jnp.sum(jnp.where(lanes == h, lse_ref[...], 0.0), axis=1, keepdims=True)
            scores = mm_nt(query, key) * (HEAD_SIZE**-0.5 * LOG2E) + bias_ref[...]
            attn = jnp.exp2(scores - level)
            attn_grad = mm_nt(grad, value)
            mean = jnp.sum(attn * attn_grad, axis=1, keepdims=True)
            score_grad = (attn * (attn_grad - mean)).astype(BF)
            value_term = mm_tn(attn.astype(BF), grad)
            key_term = mm_tn(score_grad, query)
            qg[:, cols] = turn_back(mm(score_grad, key) * HEAD_SIZE**-0.5).astype(BF)

            @pl.when(i == 0)
            def _():
                dkv[:, :HEAD_SIZE] = key_term
                dkv[:, HEAD_SIZE:] = value_term

            @pl.when(i > 0)
            def _():
                dkv[:, :HEAD_SIZE] += key_term
                dkv[:, HEAD_SIZE:] += value_term

            return 0

        lax.fori_loop(0, group, attend, 0)
        kv_low[g, :, :HEAD_SIZE] = (dkv[:, :HEAD_SIZE] * HEAD_SIZE**-0.5).astype(BF)
        kv_low[g, :, HEAD_SIZE:] = dkv[:, HEAD_SIZE:].astype(BF)
        for i in range(3):
            kv_copy(g, i).start()
        weight_rows(n1_ref, qg[:, g * wide // 2 : (g + 1) * wide // 2], g * wide // 2, wide // 2)
        begin(1 + g)
        first_legs(1 + g)
        quarters(2 + g)

    attend_group(0, {3: lambda: quarters_on(0)})
    attend_group(1, {1: lambda: second_legs(0), 4: lambda: quarters_on(1)})

    def kv_sum(g):
        for i in range(3):
            dp = (xn, diag, yn)[i]
            remote(
                kv_low.at[g, pl.ds(0, rows)], kv_in.at[g, dp], kv_send.at[g, i], kv_recv.at[g, dp], {"dp": dp}
            ).wait_recv()
        terms = kv_low[g, pl.ds(pl.multiple_of(mine * rows, 16), rows), :].astype(F32)
        for dp in (xn, diag, yn):
            terms = terms + kv_in[g, dp].astype(F32)
        low = wide + 2 * g * HEAD_SIZE
        qg[:, low : low + HEAD_SIZE] = turn_back(terms[:, :HEAD_SIZE]).astype(BF)
        qg[:, low + HEAD_SIZE : low + 2 * HEAD_SIZE] = terms[:, HEAD_SIZE:].astype(BF)

    for g in range(groups):
        kv_sum(g)
    second_legs(1)
    weight_rows(n1_ref, qg[:, wide:], wide, kv_width)
    load_qkv.wait()

    def first_grad(i, _):
        out_rows = pl.ds(pl.multiple_of(i * tile, tile), tile)
        middle[:, out_rows] = mm_nt(qg[...], wbuf[out_rows, :])
        return 0

    lax.fori_loop(0, width // tile, first_grad, 0)
    quarters_on(2)

    def first_norm(i, carry):
        rr = pl.ds(pl.multiple_of(i * block, block), block)
        back, gain = norm_back(x_ref[rr, :].astype(F32), middle[rr, :], gain_one)
        tok_ref[rr, :] += back
        return carry + gain

    gain_one_grad = lax.fori_loop(0, rows // block, first_norm, jnp.zeros((1, width), F32))
    small_grad = jnp.concatenate(
        [
            router_grad,
            gain_one_grad,
            gain_two_grad,
            jnp.zeros((128 - experts - 2, width), F32),
        ],
        axis=0,
    )
    small_grad = jnp.transpose(small_grad).astype(BF)
    for i in range(4):
        part = small_grad[i * width // 4 : (i + 1) * width // 4]
        w[i, :, :, :, qkv_width:split] = part.reshape(depth, 2, shard, 128)
    begin(3)
    first_legs(3)
    line(0)
    second_legs(2)
    quarters_on(3)
    line_on(0)
    line(1)
    second_legs(3)
    line_on(1)
    line(2)
    line_on(2)
    line(3)
    line_on(3)
    for p in range(4):
        line_end(p)

    for piece in range(4):
        keep_quarter(piece).wait()
        quarter_x(piece, mine).wait_send()
        quarter_y(piece, mine).wait_send()
        if piece % 2 == 0:
            quarter_y(piece, yn).wait_recv()
        else:
            quarter_x(piece, xn).wait_recv()
        quarter_on(piece, diag, {"dp": xn}).wait()
    for g in range(groups):
        for i in range(3):
            kv_copy(g, i).wait_send()
    for p in range(4):
        for dp in range(4):
            ws_copy(p, dp).wait_send()
        for i in range(2):
            a_copy(p, i).wait_send()
            b_copy(p, i).wait_send()
        a2_copy(p).wait_send()
        b2_copy(p).wait_send()
        for zd in range(depth):

            @pl.when(zd != z)
            def _():
                wz_copy(p, zd, z, zd).wait_send()


def backward_pass(
    x, dy, middle, gates, gate_grads, n1, q, kv, mixed, n2, logs, cos, sin, bias, row_sum, w_full,
    wide_part, down_part,
):
    depth = lax.axis_size("expert") // 2
    rows, width = x.shape
    total = w_full.shape[1]
    shard = w_full.shape[0] // (4 * 2 * depth)
    kv_width = kv.shape[1]
    groups = kv_width // (2 * HEAD_SIZE)
    qkv_width = q.shape[1] + kv_width
    dma = pltpu.SemaphoreType.DMA
    vmem = pl.BlockSpec(memory_space=pltpu.VMEM)
    anywhere = pl.BlockSpec(memory_space=pl.ANY)
    shape = jax.ShapeDtypeStruct
    parts = 4
    return pl.pallas_call(
        backward_kernel,
        name="backward_pass",
        out_shape=(
            shape((rows, width), F32),
            shape((shard, total), F32),
            shape((2, 4 * wide_part.shape[1], wide_part.shape[2]), BF),
            shape((down_part.shape[0], 4 * down_part.shape[1]), BF),
        ),
        in_specs=[vmem] * 2 + [anywhere] * 16,
        out_specs=(vmem, vmem, anywhere, anywhere),
        scratch_shapes=[
            *[pltpu.VMEM(a.shape, a.dtype) for a in (x, dy, n1, q, kv, mixed, n2, logs, cos, sin, bias)],
            pltpu.VMEM((rows, width), F32),
            pltpu.VMEM((width, qkv_width), BF),
            pltpu.VMEM((width, 128), BF),
            pltpu.VMEM((rows, width), BF),
            pltpu.VMEM((rows, q.shape[1]), BF),
            pltpu.VMEM((rows, qkv_width), BF),
            pltpu.VMEM((kv.shape[0], 2 * HEAD_SIZE), F32),
            pltpu.VMEM((groups, kv.shape[0], 2 * HEAD_SIZE), BF),
            pltpu.VMEM((groups, 4, rows, 2 * HEAD_SIZE), BF),
            pltpu.VMEM((4, depth, 2, shard, total), BF),
            pltpu.VMEM((4, depth, shard, total), BF),
            pltpu.VMEM((2, depth, shard, total), BF),
            pltpu.VMEM((depth, shard, total), BF),
            pltpu.VMEM((depth + 1, shard, total), BF),
            dma((16,)), dma((4,)), dma((4,)), dma((4,)), dma((4,)), dma((4,)), dma((4,)), dma((4,)),
            dma((groups, 3)), dma((groups, 4)),
            dma((parts, 4)), dma((parts, 4)), dma((parts, 2)), dma((parts, 2)), dma((parts, 2)), dma((parts, 2)),
            dma((parts,)), dma((parts,)), dma((parts,)), dma((parts,)),
            dma((parts, depth)), dma((parts, depth + 1)),
        ],
        compiler_params=pltpu.CompilerParams(
            collective_id=3, has_side_effects=True, vmem_limit_bytes=63 * 2**20
        ),
        cost_estimate=pl.CostEstimate(
            flops=2 * 10**10, bytes_accessed=200 * 2**20, transcendentals=0
        ),
    )(
        gates, gate_grads, x, dy, n1, q, kv, mixed, n2, logs, cos, sin, bias,
        middle, row_sum, w_full, wide_part, down_part,
    )


def finish_kernel(
    wide_ref, down_ref, share_ref, middle_ref, sum_ref, tok_in,
    out_ref, tok_ref, first_ref, second_ref, query_ref, key_ref, value_ref, proj_ref, router_ref,
    gate_ref, up_ref, dgrad_ref,
):
    gate_ref[...] = wide_ref[0].astype(F32)
    up_ref[...] = wide_ref[1].astype(F32)
    dgrad_ref[...] = down_ref[...].astype(F32)
    out_ref[...] = (middle_ref[...] + sum_ref[...].astype(F32)).astype(BF)
    tok_ref[...] = tok_in[...]

    @pl.when(pl.program_id(0) == 0)
    def _():
        wide = query_ref.shape[1]
        groups = key_ref.shape[1] // HEAD_SIZE
        query_ref[...] = share_ref[:, :wide]
        for g in range(groups):
            low, head = wide + 2 * g * HEAD_SIZE, slice(g * HEAD_SIZE, (g + 1) * HEAD_SIZE)
            key_ref[:, head] = share_ref[:, low : low + HEAD_SIZE]
            value_ref[:, head] = share_ref[:, low + HEAD_SIZE : low + 2 * HEAD_SIZE]
        start = wide + 2 * groups * HEAD_SIZE
        small = share_ref[:, start : start + 128]
        experts = router_ref.shape[1]
        router_ref[...] = small[:, :experts]
        rows = small.shape[0]
        turned = jnp.transpose(
            jnp.concatenate([small, jnp.zeros((128 - rows, 128), F32)], axis=0)
        )
        first_ref[...] = turned[experts : experts + 1, :rows]
        second_ref[...] = turned[experts + 1 : experts + 2, :rows]
        proj_ref[...] = share_ref[:, start + 128 :]


def finish_pass(wide, down, share, middle, sums, tok, experts):
    steps = 3
    rows, width = middle.shape
    piece = rows // 2
    shard = share.shape[0]
    heads, kv = QUERY_HEADS * HEAD_SIZE, KEY_VALUE_HEADS * HEAD_SIZE
    _, tall, ff = wide.shape
    shape = jax.ShapeDtypeStruct

    def whole(*dims):
        return pl.BlockSpec(dims, lambda i: (0,) * len(dims))

    token_rows = pl.BlockSpec((piece, width), lambda i: (jnp.minimum(i, rows // piece - 1), 0))
    tall_rows = pl.BlockSpec((tall // steps, ff), lambda i: (i, 0))
    down_rows = pl.BlockSpec((ff // steps, tall), lambda i: (i, 0))
    return pl.pallas_call(
        finish_kernel,
        name="finish_pass",
        grid=(steps,),
        in_specs=[
            pl.BlockSpec((2, tall // steps, ff), lambda i: (0, i, 0)),
            down_rows, whole(*share.shape), token_rows, token_rows, token_rows,
        ],
        out_specs=(
            token_rows, token_rows, whole(1, shard), whole(1, shard), whole(shard, heads),
            whole(shard, kv), whole(shard, kv), whole(shard, width), whole(shard, experts),
            tall_rows, tall_rows, down_rows,
        ),
        out_shape=(
            shape((rows, width), BF), shape((rows, width), F32), shape((1, shard), F32),
            shape((1, shard), F32), shape((shard, heads), F32), shape((shard, kv), F32),
            shape((shard, kv), F32), shape((shard, width), F32), shape((shard, experts), F32),
            shape((tall, ff), F32), shape((tall, ff), F32), shape((ff, tall), F32),
        ),
        compiler_params=pltpu.CompilerParams(vmem_limit_bytes=62 * 2**20),
    )(wide, down, share, middle, sums, tok)


def dense_on_device(
    tokens,
    cotangent,
    parents,
    routes,
    first_gain,
    second_gain,
    query_weight,
    key_matrix,
    value_matrix,
    out_weight,
    router_weight,
    gate_weight,
    up_weight,
    down_weight,
):
    experts = router_weight.shape[1]
    small_shard = jnp.concatenate(
        [router_weight, first_gain[:, None], second_gain[:, None]], axis=1
    )
    small_shard = jnp.pad(small_shard, ((0, 0), (0, -small_shard.shape[1] % 128)))
    shards = (query_weight, key_matrix, value_matrix, small_shard, out_weight)
    dy_low = cotangent[0]
    inputs_low = tokens[0]
    half = HEAD_SIZE // 2
    frequency = THETA ** -(np.arange(half, dtype=np.float64) * 2.0 / HEAD_SIZE)
    freq = np.concatenate([frequency, frequency]).astype(np.float32)[None]
    expert_ids = jnp.arange(experts, dtype=jnp.int32)
    hit_rows = jnp.any(routes[0][None, :, :] == expert_ids[:, None, None], axis=2).astype(F32)
    n1, query_low, kv_all, mixed, logs, middle, n2, gate_rows, cos, sin, bias, full, dy_all = (
        attention_pass(inputs_low, shards, freq, parents, hit_rows, dy_low)
    )
    row_sum, gate_grads, sums, wide_part, down_part, _ = expert_pass(
        n2, gate_rows, dy_all, gate_weight[0], up_weight[0], down_weight[0]
    )
    combined = lax.psum_scatter(sums, "expert", scatter_dimension=0, tiled=True)[0]
    input_grad, share, wide_grads, down_grad = backward_pass(
        inputs_low, dy_low, middle, gate_rows, gate_grads, n1, query_low, kv_all, mixed, n2, logs,
        cos, sin, bias, row_sum, full, wide_part, down_part,
    )
    output, input_grad, gain_one, gain_two, query, key, value, proj, router, gate, up, down = finish_pass(
        wide_grads, down_grad, share, middle, combined, input_grad, experts
    )
    return (
        output[None],
        input_grad[None],
        gain_one[0],
        gain_two[0],
        query,
        key,
        value,
        proj,
        router,
        gate[None],
        up[None],
        down[None],
    )


def solution(mesh):
    dense = mesh.shape["expert"] <= 2 * TOPK and mesh.shape["dp"] == 4
    return jax.shard_map(
        dense_on_device if dense else on_device_routed,
        mesh=mesh,
        in_specs=(
            P("expert", "dp", None),
            P("expert", "dp", None),
            P("expert", None),
            P("expert", "dp", None),
            P(("dp", "expert")),
            P(("dp", "expert")),
            P(("dp", "expert"), None),
            P(("dp", "expert"), None),
            P(("dp", "expert"), None),
            P(("dp", "expert"), None),
            P(("dp", "expert"), None),
            P("expert", None, None),
            P("expert", None, None),
            P("expert", None, None),
        ),
        out_specs=(
            P("expert", "dp", None),
            P("expert", "dp", None),
            P(("dp", "expert")),
            P(("dp", "expert")),
            P(("dp", "expert"), None),
            P(("dp", "expert"), None),
            P(("dp", "expert"), None),
            P(("dp", "expert"), None),
            P(("dp", "expert"), None),
            P("expert", None, None),
            P("expert", None, None),
            P("expert", None, None),
        ),
        check_vma=False,
    )
```

```python
import jax
import jax.numpy as jnp
import numpy as np
from jax import lax
from jax.experimental import pallas as pl
from jax.experimental.pallas import tpu as pltpu
from jax.sharding import PartitionSpec as P

MESH = pl.DeviceIdType.MESH
BF = jnp.bfloat16
F32 = jnp.float32
MODEL_WIDTH = 1536
QUERY_HEADS = 12
KEY_VALUE_HEADS = 2
HEAD_SIZE = 128
FF = 768
TOPK = 4
SEG = 32
BRANCHES = 4
LEAVES = 8


EPS = 1e-06
THETA = 10000.0
HIGH_PRECISION = lax.Precision.HIGHEST
NEGATIVE = -1e30
LOG2E = 1.4426950408889634


def ancestry(parent_row):
    block_count = parent_row.shape[0]
    block_ids = jnp.arange(block_count, dtype=jnp.int32)

    def advance(counter, carried):
        current, ancestors = carried
        ancestors = jnp.maximum(
            ancestors, (current[:, None] == block_ids[None, :]).astype(jnp.float32)
        )
        return (jnp.take(parent_row, current), ancestors)

    start_pair = (block_ids, jnp.zeros((block_count, block_count), jnp.float32))
    current, ancestors = lax.fori_loop(0, block_count, advance, start_pair)
    depths = (jnp.sum(ancestors, axis=1) - 1.0).astype(jnp.int32)
    return (ancestors, depths)


def apply_rotation(values, positions):
    half_width = values.shape[-1] // 2
    frequency = jnp.power(
        THETA, -(jnp.arange(half_width, dtype=jnp.float32) * 2.0 / values.shape[-1])
    )
    angles = positions.astype(jnp.float32)[:, None] * frequency[None, :]
    cosine = jnp.cos(angles)[:, None, :]
    sine_part = jnp.sin(angles)[:, None, :]
    first_half = values[..., :half_width]
    second_half = values[..., half_width:]
    return jnp.concatenate(
        [
            first_half * cosine - second_half * sine_part,
            second_half * cosine + first_half * sine_part,
        ],
        axis=-1,
    )


def normalize(values, scales):
    return values * lax.rsqrt(jnp.mean(values * values, axis=-1, keepdims=True) + EPS) * scales


def place(route_ids, experts, capacity):
    one_hot = (route_ids[..., None] == jnp.arange(experts, dtype=jnp.int32)).astype(jnp.int32)
    pairs = one_hot.shape[-2]
    before = jnp.tri(pairs, pairs, -1, dtype=jnp.bfloat16)
    earlier = jnp.dot(before, one_hot.astype(jnp.bfloat16), preferred_element_type=jnp.float32)
    slot_rank = jnp.sum(earlier.astype(jnp.int32) * one_hot, axis=-1)
    return route_ids * capacity + slot_rank


def visibility(ancestors, depths, query_ids, key_ids):
    block_ids = jnp.arange(ancestors.shape[0], dtype=jnp.int32)
    query_hit = (query_ids // SEG)[:, None] == block_ids[None, :]
    key_hit = (key_ids // SEG)[:, None] == block_ids[None, :]
    query_positions = (
        jnp.sum(jnp.where(query_hit, depths[None, :], 0), axis=1) * SEG + query_ids % SEG
    )
    key_pos = jnp.sum(jnp.where(key_hit, depths[None, :], 0), axis=1) * SEG + key_ids % SEG
    reach = jnp.dot(query_hit.astype(jnp.float32), ancestors, precision=HIGH_PRECISION)
    reach_keys = jnp.repeat(reach, SEG, axis=1)
    visible = (reach_keys > 0.5) & (key_pos[None, :] <= query_positions[:, None])
    return (visible, query_positions)


def head_scores(query_rotated, keys_all, visible, key_value_head, query_group_width):
    query_part = query_rotated[
        :, key_value_head * query_group_width : (key_value_head + 1) * query_group_width, :
    ]
    key_part = keys_all[:, key_value_head * HEAD_SIZE : (key_value_head + 1) * HEAD_SIZE]
    scores = jnp.einsum(
        "rgd,kd->grk", query_part, key_part, preferred_element_type=jnp.float32
    ) * HEAD_SIZE ** (-0.5)
    return jnp.where(visible[None], scores, NEGATIVE)


def gelu_product(gate_pre, up_pre):
    return jax.nn.gelu(gate_pre, approximate=True) * up_pre


def expert_hidden(received, local_gate, local_up):
    local_count = local_gate.shape[0]
    slot_count = received.shape[1]
    grouped_queries = received.reshape(-1, local_count, slot_count, MODEL_WIDTH)
    gate_pre = jnp.einsum(
        "sjcd,jdf->sjcf", grouped_queries, local_gate, preferred_element_type=jnp.float32
    )
    up_pre = jnp.einsum(
        "sjcd,jdf->sjcf", grouped_queries, local_up, preferred_element_type=jnp.float32
    )
    hidden = gelu_product(gate_pre, up_pre).astype(jnp.bfloat16)
    flat_shape = (received.shape[0], slot_count, FF)
    return (gate_pre.reshape(flat_shape), up_pre.reshape(flat_shape), hidden.reshape(flat_shape))


def expert_result(hidden, local_down):
    local_count = local_down.shape[0]
    grouped_queries = hidden.reshape(-1, local_count, hidden.shape[1], FF)
    result = jnp.einsum(
        "sjcf,jfd->sjcd", grouped_queries, local_down, preferred_element_type=jnp.float32
    )
    return result.astype(jnp.bfloat16).reshape(hidden.shape[0], hidden.shape[1], MODEL_WIDTH)


def on_device_routed(
    tokens,
    cotangent,
    parents,
    routes,
    first_gain,
    second_gain,
    query_weight,
    key_matrix,
    value_matrix,
    out_weight,
    router_weight,
    gate_weight,
    up_weight,
    down_weight,
):
    gathered = (
        lax.all_gather(query_weight, ("dp", "expert"), axis=0, tiled=True),
        lax.all_gather(key_matrix, ("dp", "expert"), axis=0, tiled=True),
        lax.all_gather(value_matrix, ("dp", "expert"), axis=0, tiled=True),
        lax.all_gather(out_weight, ("dp", "expert"), axis=0, tiled=True),
        lax.all_gather(router_weight, ("dp", "expert"), axis=0, tiled=True),
        lax.all_gather(first_gain, ("dp", "expert"), axis=0, tiled=True),
        lax.all_gather(second_gain, ("dp", "expert"), axis=0, tiled=True),
    )
    query_full, key_complete, value_complete, out_full, router_full, gain_one, gain_two = gathered
    scale_one = gain_one.astype(jnp.float32)
    scale_two = gain_two.astype(jnp.float32)
    inputs = tokens[0].astype(jnp.float32)
    total_rows = inputs.shape[0]
    query_group_width = QUERY_HEADS // KEY_VALUE_HEADS
    ancestors, depths = ancestry(parents[0])
    tree_length = ancestors.shape[0] * SEG
    query_ids = lax.axis_index("dp") * total_rows + jnp.arange(total_rows, dtype=jnp.int32)
    key_ids = jnp.arange(tree_length, dtype=jnp.int32)
    visible, query_positions = visibility(ancestors, depths, query_ids, key_ids)
    first_normed = normalize(inputs, scale_one).astype(jnp.bfloat16)
    query_proj = jnp.dot(first_normed, query_full, preferred_element_type=jnp.float32).reshape(
        total_rows, QUERY_HEADS, HEAD_SIZE
    )
    key_projected = jnp.dot(first_normed, key_complete, preferred_element_type=jnp.float32).reshape(
        total_rows, KEY_VALUE_HEADS, HEAD_SIZE
    )
    value_projected = jnp.dot(first_normed, value_complete, preferred_element_type=jnp.float32)
    query_rotated = apply_rotation(query_proj, query_positions).astype(jnp.bfloat16)
    key_rotated = (
        apply_rotation(key_projected, query_positions)
        .astype(jnp.bfloat16)
        .reshape(total_rows, KEY_VALUE_HEADS * HEAD_SIZE)
    )
    value_low = value_projected.astype(jnp.bfloat16)
    keys_all, values_all = (
        lax.all_gather(key_rotated, "dp", axis=0, tiled=True),
        lax.all_gather(value_low, "dp", axis=0, tiled=True),
    )
    mixed_parts = []
    log_totals = []
    for key_value_head in range(KEY_VALUE_HEADS):
        scores = head_scores(query_rotated, keys_all, visible, key_value_head, query_group_width)
        row_max = jnp.max(scores, axis=-1, keepdims=True)
        exponent = jnp.exp(scores - row_max)
        row_total = jnp.sum(exponent, axis=-1, keepdims=True)
        log_totals.append(row_max + jnp.log(row_total))
        softmax_out = (exponent / row_total).astype(jnp.bfloat16)
        value_part = values_all[:, key_value_head * HEAD_SIZE : (key_value_head + 1) * HEAD_SIZE]
        mixed_parts.append(
            jnp.einsum("grk,kd->rgd", softmax_out, value_part, preferred_element_type=jnp.float32)
        )
    mixed_out = (
        jnp.concatenate(mixed_parts, axis=1)
        .reshape(total_rows, QUERY_HEADS * HEAD_SIZE)
        .astype(jnp.bfloat16)
    )
    middle = inputs + jnp.dot(mixed_out, out_full, preferred_element_type=jnp.float32)
    normed_two = normalize(middle, scale_two).astype(jnp.bfloat16)
    logits = jnp.dot(normed_two, router_full, preferred_element_type=jnp.float32)
    route_ids = routes[0]
    experts = gate_weight.shape[0] * lax.axis_size("expert")
    capacity = 3 * total_rows * TOPK // (2 * experts)
    expert_ids = jnp.arange(experts, dtype=jnp.int32)
    route_hits = route_ids[:, :, None] == expert_ids[None, None, :]
    chosen = jnp.sum(jnp.where(route_hits, logits[:, None, :], 0.0), axis=2)
    chosen_max = jnp.max(chosen, axis=1, keepdims=True)
    chosen_exp = jnp.exp(chosen - chosen_max)
    gate_weights = chosen_exp / jnp.sum(chosen_exp, axis=1, keepdims=True)
    pair_count = total_rows * TOPK
    slot_index = place(route_ids.reshape(pair_count), experts, capacity)
    slot_source = (
        jnp.full((experts * capacity,), pair_count, jnp.int32)
        .at[slot_index]
        .set(jnp.arange(pair_count, dtype=jnp.int32))
    )
    slot_used = slot_source < pair_count
    slot_pair = jnp.where(slot_used, slot_source, 0)
    slot_token = slot_pair // TOPK
    zero_low = jnp.zeros((), jnp.bfloat16)
    outgoing = jnp.where(slot_used[:, None], normed_two[slot_token], zero_low).reshape(
        experts, capacity, MODEL_WIDTH
    )
    gate_pre, up_pre, hidden = expert_hidden(
        lax.all_to_all(outgoing, "expert", split_axis=0, concat_axis=0, tiled=True),
        gate_weight,
        up_weight,
    )
    dispatched = expert_result(hidden, down_weight)
    returned = lax.all_to_all(dispatched, "expert", split_axis=0, concat_axis=0, tiled=True)
    expert_rows = (
        returned.reshape(experts * capacity, MODEL_WIDTH)[slot_index]
        .astype(jnp.float32)
        .reshape(total_rows, TOPK, MODEL_WIDTH)
    )
    final = middle + jnp.sum(gate_weights[:, :, None] * expert_rows, axis=1)
    output = final.astype(jnp.bfloat16)[None]
    upstream = cotangent[0].astype(jnp.float32)
    gate_grad = jnp.sum(upstream[:, None, :] * expert_rows, axis=2)
    chosen_grad = gate_weights * (
        gate_grad - jnp.sum(gate_weights * gate_grad, axis=1, keepdims=True)
    )
    logit_grad = jnp.sum(jnp.where(route_hits, chosen_grad[:, :, None], 0.0), axis=1)
    pair_grad = (
        (gate_weights[:, :, None] * upstream[:, None, :])
        .astype(jnp.bfloat16)
        .reshape(pair_count, MODEL_WIDTH)
    )
    grad_outgoing = jnp.where(slot_used[:, None], pair_grad[slot_pair], zero_low).reshape(
        experts, capacity, MODEL_WIDTH
    )
    received, grad_in = (
        lax.all_to_all(outgoing, "expert", split_axis=0, concat_axis=0, tiled=True),
        lax.all_to_all(grad_outgoing, "expert", split_axis=0, concat_axis=0, tiled=True),
    )
    gate_pre, up_pre, hidden = expert_hidden(received, gate_weight, up_weight)
    local_count = gate_weight.shape[0]
    slot_count = received.shape[1]
    grouped_rows = received.reshape(-1, local_count, slot_count, MODEL_WIDTH)
    grouped_hidden = hidden.reshape(-1, local_count, slot_count, FF)
    grouped_grad = grad_in.reshape(-1, local_count, slot_count, MODEL_WIDTH)
    down_grad = jnp.einsum(
        "sjcf,sjcd->jfd", grouped_hidden, grouped_grad, preferred_element_type=jnp.float32
    )
    hidden_grad = jnp.einsum(
        "sjcd,jfd->sjcf", grouped_grad, down_weight, preferred_element_type=jnp.float32
    )
    _, product_pull = jax.vjp(gelu_product, gate_pre, up_pre)
    gate_pre_grad, up_pre_grad = product_pull(hidden_grad.reshape(gate_pre.shape))
    gate_low = gate_pre_grad.astype(jnp.bfloat16).reshape(-1, local_count, slot_count, FF)
    up_low = up_pre_grad.astype(jnp.bfloat16).reshape(-1, local_count, slot_count, FF)
    gate_w_grad = jnp.einsum(
        "sjcd,sjcf->jdf", grouped_rows, gate_low, preferred_element_type=jnp.float32
    )
    up_w_grad = jnp.einsum(
        "sjcd,sjcf->jdf", grouped_rows, up_low, preferred_element_type=jnp.float32
    )
    row_grad = jnp.einsum(
        "sjcf,jdf->sjcd", gate_low, gate_weight, preferred_element_type=jnp.float32
    ) + jnp.einsum("sjcf,jdf->sjcd", up_low, up_weight, preferred_element_type=jnp.float32)
    row_grad = row_grad.astype(jnp.bfloat16).reshape(received.shape)
    returned_grad = lax.all_to_all(row_grad, "expert", split_axis=0, concat_axis=0, tiled=True)
    pair_rows = (
        returned_grad.reshape(experts * capacity, MODEL_WIDTH)[slot_index]
        .astype(jnp.float32)
        .reshape(total_rows, TOPK, MODEL_WIDTH)
    )
    summed_experts = (
        lax.psum(gate_w_grad.astype(jnp.bfloat16), "dp").astype(jnp.float32),
        lax.psum(up_w_grad.astype(jnp.bfloat16), "dp").astype(jnp.float32),
        lax.psum(down_grad.astype(jnp.bfloat16), "dp").astype(jnp.float32),
    )
    router_wide = router_full.astype(jnp.float32)
    normed_two_grad = jnp.dot(logit_grad, router_wide.T, precision=HIGH_PRECISION) + jnp.sum(
        pair_rows, axis=1
    )
    router_grad = jnp.dot(normed_two.astype(jnp.float32).T, logit_grad, precision=HIGH_PRECISION)
    _, second_pull = jax.vjp(normalize, middle, scale_two)
    middle_norm_grad, second_gain_grad = second_pull(normed_two_grad)
    middle_grad = upstream + middle_norm_grad
    attended_low = middle_grad.astype(jnp.bfloat16)
    out_grad = jnp.einsum("rd,re->de", mixed_out, attended_low, preferred_element_type=jnp.float32)
    mixed_grad = jnp.einsum("re,de->rd", attended_low, out_full, preferred_element_type=jnp.float32)
    mixed_grad = mixed_grad.astype(jnp.bfloat16).reshape(total_rows, QUERY_HEADS, HEAD_SIZE)
    query_parts = []
    key_parts = []
    value_parts = []
    for key_value_head in range(KEY_VALUE_HEADS):
        scores = head_scores(query_rotated, keys_all, visible, key_value_head, query_group_width)
        softmax_out = jnp.exp(scores - log_totals[key_value_head])
        query_part = query_rotated[
            :, key_value_head * query_group_width : (key_value_head + 1) * query_group_width, :
        ]
        key_part = keys_all[:, key_value_head * HEAD_SIZE : (key_value_head + 1) * HEAD_SIZE]
        value_part = values_all[:, key_value_head * HEAD_SIZE : (key_value_head + 1) * HEAD_SIZE]
        grad_part = mixed_grad[
            :, key_value_head * query_group_width : (key_value_head + 1) * query_group_width, :
        ]
        value_parts.append(
            jnp.einsum(
                "grk,rgd->kd",
                softmax_out.astype(jnp.bfloat16),
                grad_part,
                preferred_element_type=jnp.float32,
            )
        )
        attn_grad = jnp.einsum(
            "rgd,kd->grk", grad_part, value_part, preferred_element_type=jnp.float32
        )
        score_grad = softmax_out * (
            attn_grad - jnp.sum(softmax_out * attn_grad, axis=-1, keepdims=True)
        )
        score_low = score_grad.astype(jnp.bfloat16)
        query_parts.append(
            jnp.einsum("grk,kd->rgd", score_low, key_part, preferred_element_type=jnp.float32)
            * HEAD_SIZE ** (-0.5)
        )
        key_parts.append(
            jnp.einsum("grk,rgd->kd", score_low, query_part, preferred_element_type=jnp.float32)
            * HEAD_SIZE ** (-0.5)
        )
    key_total_sum, value_sum = (
        lax.psum_scatter(
            jnp.concatenate(key_parts, axis=1).astype(jnp.bfloat16),
            "dp",
            scatter_dimension=0,
            tiled=True,
        ).astype(jnp.float32),
        lax.psum_scatter(
            jnp.concatenate(value_parts, axis=1).astype(jnp.bfloat16),
            "dp",
            scatter_dimension=0,
            tiled=True,
        ).astype(jnp.float32),
    )
    _, query_pull = jax.vjp(lambda values: apply_rotation(values, query_positions), query_proj)
    _, key_pullback = jax.vjp(lambda values: apply_rotation(values, query_positions), key_projected)
    query_grad = (
        query_pull(jnp.concatenate(query_parts, axis=1))[0]
        .astype(jnp.bfloat16)
        .reshape(total_rows, QUERY_HEADS * HEAD_SIZE)
    )
    key_grad = (
        key_pullback(key_total_sum.reshape(total_rows, KEY_VALUE_HEADS, HEAD_SIZE))[0]
        .astype(jnp.bfloat16)
        .reshape(total_rows, KEY_VALUE_HEADS * HEAD_SIZE)
    )
    value_grad = value_sum.astype(jnp.bfloat16)
    query_w_grad = jnp.einsum(
        "rd,re->de", first_normed, query_grad, preferred_element_type=jnp.float32
    )
    key_w_grad = jnp.einsum("rd,re->de", first_normed, key_grad, preferred_element_type=jnp.float32)
    value_w_grad = jnp.einsum(
        "rd,re->de", first_normed, value_grad, preferred_element_type=jnp.float32
    )
    normed_one_grad = (
        jnp.einsum("re,de->rd", query_grad, query_full, preferred_element_type=jnp.float32)
        + jnp.einsum("re,de->rd", key_grad, key_complete, preferred_element_type=jnp.float32)
        + jnp.einsum("re,de->rd", value_grad, value_complete, preferred_element_type=jnp.float32)
    )
    _, first_pull = jax.vjp(normalize, inputs, scale_one)
    input_norm_grad, first_gain_grad = first_pull(normed_one_grad)
    input_grad = (middle_grad + input_norm_grad)[None]
    shares = (
        lax.psum_scatter(query_w_grad, ("dp", "expert"), scatter_dimension=0, tiled=True),
        lax.psum_scatter(key_w_grad, ("dp", "expert"), scatter_dimension=0, tiled=True),
        lax.psum_scatter(value_w_grad, ("dp", "expert"), scatter_dimension=0, tiled=True),
        lax.psum_scatter(out_grad, ("dp", "expert"), scatter_dimension=0, tiled=True),
        lax.psum_scatter(router_grad, ("dp", "expert"), scatter_dimension=0, tiled=True),
        lax.psum_scatter(first_gain_grad, ("dp", "expert"), scatter_dimension=0, tiled=True),
        lax.psum_scatter(second_gain_grad, ("dp", "expert"), scatter_dimension=0, tiled=True),
    )
    return (
        output,
        input_grad,
        shares[5],
        shares[6],
        shares[0],
        shares[1],
        shares[2],
        shares[3],
        shares[4],
        summed_experts[0],
        summed_experts[1],
        summed_experts[2],
    )


def mm(a, b):
    return jnp.dot(a, b, preferred_element_type=F32)


def mm_nt(a, b):
    return lax.dot_general(a, b, (((1,), (1,)), ((), ())), preferred_element_type=F32)


def mm_tn(a, b):
    return lax.dot_general(a, b, (((0,), (0,)), ((), ())), preferred_element_type=F32)


def gelu_both(value):
    scale = 0.7978845608028654
    square = value * value
    bend = jnp.tanh(scale * value * (1.0 + 0.044715 * square))
    half = 0.5 * (1.0 + bend)
    slope = half + 0.5 * value * (1.0 - bend * bend) * scale * (1.0 + 0.134145 * square)
    return value * half, slope


def expert_kernel(
    n2_ref, gate_ref, dy_ref, gw_any, uw_any, dw_any,
    row_ref, gg_ref, sum_ref, wide_ref, down_ref, landing,
    gw_ref, uw_ref, dw_ref, n2_all, gate_all, dy_buf, dy_cols, hs_all, gl_all, ul_all, own, sib, zin, gg_out, gg_in,
    gate_cols, gg_cols, stage, kept, down_kept,
    n2_send, n2_recv, gt_send, gt_recv, own_send, sib_recv, zin_send, zin_recv,
    gg_send, gg_recv, dy_sem, cols_sem, sum_sem, tile_send, tile_recv, load_sem, keep_sem, weight_sem,
):
    count = lax.axis_size("expert")
    depth = count // 2
    rows = n2_ref.shape[0]
    half = rows // 2
    width = n2_ref.shape[1]
    ff = gw_ref.shape[1]
    me = lax.axis_index("expert")
    z, core = me // 2, me % 2
    sibling = z * 2 + 1 - core
    mine = lax.axis_index("dp")
    y, x = mine // 2, mine % 2
    others = (y * 2 + 1 - x, (1 - y) * 2 + 1 - x, (1 - y) * 2 + x)

    def at(zz):
        return {"expert": zz * 2 + core}

    n2_load = pltpu.make_async_copy(
        n2_ref, n2_all.at[pl.ds(pl.multiple_of(me * rows, 16), rows)], cols_sem
    )
    n2_load.start()
    weight_loads = [
        pltpu.make_async_copy(src, dst, weight_sem.at[i])
        for i, (src, dst) in enumerate(((dw_any, dw_ref), (gw_any, gw_ref), (uw_any, uw_ref)))
    ]
    for load in weight_loads:
        load.start()
    barrier = pltpu.get_barrier_semaphore()
    for other in range(1, count):
        pl.semaphore_signal(
            barrier, 1, device_id={"expert": lax.rem(me + other, count)}, device_id_type=MESH
        )
    for dp in others:
        pl.semaphore_signal(barrier, 1, device_id={"dp": dp}, device_id_type=MESH)
    pl.semaphore_wait(barrier, count - 1 + len(others))

    def chunk(k):
        return pl.ds(pl.multiple_of(k * rows, 16), rows)

    def piece(k, h):
        return pl.ds(pl.multiple_of(k * rows + h * half, 16), half)

    def part(h):
        return pl.ds(h * half, half)

    def n2_copy(k, h, lane, target):
        return pltpu.make_async_remote_copy(
            n2_all.at[piece(k, h)], n2_all.at[piece(k, h)], n2_send.at[k, h, lane], n2_recv.at[k, h],
            device_id=target, device_id_type=MESH,
        )

    def gt_copy(k, lane, target):
        return pltpu.make_async_remote_copy(
            gate_all.at[k], gate_all.at[k], gt_send.at[k, lane], gt_recv.at[k],
            device_id=target, device_id_type=MESH,
        )

    def send_chunk(k, h, lane, target):
        n2_copy(k, h, lane, target).start()
        if h == 0:
            gt_copy(k, lane, target).start()

    def sent_chunk(k, h, lane, target):
        n2_copy(k, h, lane, target).wait_send()
        if h == 0:
            gt_copy(k, lane, target).wait_send()

    def arrived(k, h):
        n2_copy(k, h, 0, at(z)).wait_recv()
        if h == 0:
            gt_copy(k, 0, at(z)).wait_recv()

    def dy_copy(k, h, w, s):
        return pltpu.make_async_copy(dy_ref.at[k, part(h)], dy_buf.at[w, s], dy_sem.at[w, s])

    def gg_copy(k):
        return pltpu.make_async_remote_copy(
            gg_out.at[k], gg_in.at[me], gg_send.at[k], gg_recv.at[me],
            device_id={"expert": k}, device_id_type=MESH,
        )

    def own_copy(zs, h):
        return pltpu.make_async_remote_copy(
            own.at[2 * zs + 1 - core, part(h)], sib.at[zs, part(h)],
            own_send.at[zs, h], sib_recv.at[zs, h],
            device_id={"expert": sibling}, device_id_type=MESH,
        )

    def zin_copy(zd, h, nxt, slot):
        return pltpu.make_async_remote_copy(
            own.at[2 * zd + core, part(h)], zin.at[slot, part(h)],
            zin_send.at[zd, h], zin_recv.at[slot, h],
            device_id=at(nxt), device_id_type=MESH,
        )

    n2_load.wait()
    gate_all[me] = gate_ref[...]

    for h in range(2):

        @pl.when(z < depth - 1)
        def _():
            send_chunk(me, h, 0, at(z + 1))

        @pl.when(z > 0)
        def _():
            send_chunk(me, h, 1, at(z - 1))

        send_chunk(me, h, 2, {"expert": sibling})

    row_ids = lax.broadcasted_iota(jnp.int32, (count, gate_ref.shape[1]), 0)

    def hidden_part(k, h, w, s):
        r = piece(k, h)
        place = 2 * s + w
        if h == 0:
            gate_row = jnp.sum(jnp.where(row_ids == me, gate_all[k], 0.0), axis=0, keepdims=True)
            gate_cols[place] = jnp.transpose(jnp.broadcast_to(gate_row, (128, gate_row.shape[1])))
            gg_cols[place, rows:, :] = jnp.zeros((gate_ref.shape[1] - rows, 128), F32)
        gate_col = gate_cols[place, part(h), :]
        tile = 256
        gate_wide = jnp.concatenate([gate_col] * (tile // 128), axis=1)
        total = jnp.zeros((half, 128), F32)
        for j in range(ff // tile):
            cols = slice(j * tile, (j + 1) * tile)
            back = mm_nt(dy_buf[w, s], dw_ref[cols, :])
            gate_pre = mm(n2_all[r, :], gw_ref[:, cols])
            up_pre = mm(n2_all[r, :], uw_ref[:, cols])
            act, slope = gelu_both(gate_pre)
            hidden = act * up_pre
            hs_all[r, cols] = (gate_wide * hidden).astype(BF)
            product = hidden * back
            for i in range(tile // 128):
                total = total + product[:, i * 128 : (i + 1) * 128]
            back = gate_wide * back
            gl_all[r, cols] = (back * up_pre * slope).astype(BF)
            ul_all[r, cols] = (back * act).astype(BF)
        gg_cols[place, part(h), :] = total
        if h == 1:
            gg_row = jnp.sum(jnp.transpose(gg_cols[place]), axis=0, keepdims=True)
            gg_tile = jnp.where(row_ids == me, gg_row, 0.0)
            gg_out[k] = gg_tile

            @pl.when(k == me)
            def _():
                gg_in[me] = gg_tile

            @pl.when(k != me)
            def _():
                gg_copy(k).start()

    def row_part(k, h):
        r = piece(k, h)
        wide = 512
        for j in range(width // wide):
            cols = slice(j * wide, (j + 1) * wide)
            own[k, part(h), cols] = (
                mm_nt(gl_all[r, :], gw_ref[cols, :]) + mm_nt(ul_all[r, :], uw_ref[cols, :])
            ).astype(BF)

    block = 16

    def combine(zd, h, with_in):
        def step(i, _):
            rr = pl.ds(pl.multiple_of(h * half + i * block, block), block)
            value = own[2 * zd + core, rr, :].astype(F32) + sib[zd, rr, :].astype(F32)
            if with_in:
                value = value + zin[zd, rr, :].astype(F32)
            own[2 * zd + core, rr, :] = value.astype(BF)
            return 0

        lax.fori_loop(0, half // block, step, 0)

    def slot_for(zd, nxt):
        return jnp.where((nxt == zd) & (nxt < z), depth, zd)

    def pass_on(zd, h, nxt, with_in):
        own_copy(zd, h).wait_recv()
        if with_in:
            zin_copy(zd, h, nxt, zd).wait_recv()
        combine(zd, h, with_in)
        zin_copy(zd, h, nxt, slot_for(zd, nxt)).start()

    quarter = width // 4
    cut = ff // 2
    order = (others[1], others[0], others[2], mine)

    def owner(j):
        return jnp.where(
            j == 0, order[0], jnp.where(j == 1, order[1], jnp.where(j == 2, order[2], mine))
        )

    def cols_of(dp):
        return pl.ds(pl.multiple_of(dp * quarter, 128), quarter)

    def tile_slot(kind, j):
        if kind == 0:
            return stage.at[j]
        return (gl_all, ul_all)[kind - 1].at[pl.ds(pl.multiple_of(j * quarter, 16), quarter)]

    sides = (slice(0, cut), slice(cut, ff))
    ends = ({"dp": others[0]}, {"dp": others[2]})
    hops = ((0, 0, 1, 0), (0, 1, 1, 1), (1, 0, 0, 0), (2, 1, 0, 1), (2, 0, 2, 1), (1, 1, 2, 0))

    def hop(kind, n):
        j, side, slot, way = hops[n]
        return pltpu.make_async_remote_copy(
            tile_slot(kind, j).at[:, sides[side]], landing.at[kind, slot, :, sides[side]],
            tile_send.at[kind, n], tile_recv.at[kind, slot, side],
            device_id=ends[way], device_id_type=MESH,
        )

    def col_copy(j):
        return pltpu.make_async_copy(dy_ref.at[:, :, cols_of(owner(j))], dy_cols, cols_sem)

    def tiles(kind, low, high):
        def step(j, _):
            cols = cols_of(owner(j))
            if kind == 2:
                col_copy(j).wait()
                tile = mm_tn(dy_cols[...].reshape(count * rows, quarter), hs_all[...])

                @pl.when(j < 3)
                def _():
                    col_copy(j + 1).start()
            else:
                tile = mm_tn(n2_all[:, cols], (gl_all, ul_all)[kind][...])
            tile = tile.astype(BF)

            @pl.when(j < 3)
            def _():
                tile_slot(kind, j)[...] = tile

            for n in range(4):

                @pl.when(j == hops[n][0])
                def _():
                    hop(kind, n).start()

            @pl.when(j == 3)
            def _():
                kept[kind] = tile

            return 0

        lax.fori_loop(low, high, step, 0)

    def spare(kind, i):
        return (gl_all, ul_all, gl_all)[kind].at[pl.ds(6 * quarter, quarter)]

    def second_leg(kind):
        for side in range(2):
            n = side
            hop(kind, n).wait_recv()
        load = pltpu.make_async_copy(landing.at[kind, 1], spare(kind, 6), load_sem.at[kind, 2])
        load.start()
        load.wait()
        for n in (4, 5):
            j, side, _, _ = hops[n]

            def step(i, _):
                rr = pl.ds(pl.multiple_of(i * 32, 32), 32)
                into = tile_slot(kind, j)
                value = into[rr, sides[side]].astype(F32) + spare(kind, 6)[rr, sides[side]].astype(F32)
                into[rr, sides[side]] = value.astype(BF)
                return 0

            lax.fori_loop(0, quarter // 32, step, 0)
            hop(kind, n).start()

    def by_distance(d, _):
        left, right = z - d, z + d
        has_left, has_right = left >= 0, (right < depth) & (d > 0)

        def other_chunk(zs):
            return 2 * zs + 1 - core

        for h in range(2):
            for s, zs, there in ((0, left, has_left), (1, right, has_right)):

                @pl.when(there)
                def _():
                    dy_copy(other_chunk(zs), h, 0, s).start()
                    dy_copy(2 * zs + core, h, 1, s).start()

            @pl.when(has_left & (d > 0))
            def _():
                k = 2 * left + core
                arrived(k, h)

                @pl.when(z < depth - 1)
                def _():
                    send_chunk(k, h, 0, at(z + 1))

                send_chunk(k, h, 2, {"expert": sibling})

            @pl.when(has_right)
            def _():
                k = 2 * right + core
                arrived(k, h)

                @pl.when(z > 0)
                def _():
                    send_chunk(k, h, 1, at(z - 1))

                send_chunk(k, h, 2, {"expert": sibling})

            def side(s, _):
                zs = jnp.where(s == 0, left, right)

                @pl.when(jnp.where(s == 0, has_left, has_right))
                def _():
                    def first(w, _):
                        k = 2 * zs + jnp.where(w == 0, 1 - core, core)

                        @pl.when(w == 0)
                        def _():
                            arrived(k, h)

                        dy_copy(k, h, w, s).wait()
                        hidden_part(k, h, w, s)
                        return 0

                    lax.fori_loop(0, 2, first, 0)
                    if h == 1:
                        @pl.when(d == jnp.maximum(z, depth - 1 - z))
                        def _():
                            tiles(0, 0, 3)

                    def second(w, _):
                        row_part(2 * zs + jnp.where(w == 0, 1 - core, core), h)

                        @pl.when(w == 0)
                        def _():
                            own_copy(zs, h).start()

                        return 0

                    lax.fori_loop(0, 2, second, 0)

                    @pl.when((d > 0) & ((z == 0) | (z == depth - 1)))
                    def _():
                        pass_on(zs, h, jnp.where(z == 0, 1, depth - 2), False)

                return 0

            lax.fori_loop(0, 2, side, 0)
        return 0

    for load in weight_loads:
        load.wait()
    col_copy(0).start()
    lax.fori_loop(0, depth, by_distance, 0)

    def sum_copy(k, slot):
        return pltpu.make_async_copy(own.at[slot], sum_ref.at[k], sum_sem.at[slot])

    def sums(low, high):
        def step(i, _):
            slot = 2 * lax.rem(i, depth) + 1 - core

            @pl.when(i < depth)
            def _():
                for h in range(2):
                    own_copy(i, h).wait_send()

            @pl.when(i >= depth)
            def _():
                sum_copy(i, slot).wait()

            wide = 512
            for j in range(width // wide):
                cols = slice(j * wide, (j + 1) * wide)
                own[slot, :, cols] = mm(hs_all[chunk(i), :], dw_ref[:, cols]).astype(BF)
            sum_copy(i, slot).start()
            return 0

        lax.fori_loop(low, high, step, 0)

    def flow(r, first, h):
        right = (z < depth - 1 - z) if first else (z >= depth - 1 - z)
        zd = jnp.where(right, r, depth - 1 - r)
        valid = jnp.where(right, (z < zd) & (z > 0), (z > zd) & (z < depth - 1))

        @pl.when(valid)
        def _():
            pass_on(zd, h, jnp.where(right, z + 1, z - 1), True)

    eighth = count // 4
    jobs = [
        lambda: tiles(0, 3, 4),
        lambda: tiles(1, 0, 2),
        lambda: tiles(1, 2, 4),
        lambda: second_leg(0),
        lambda: tiles(2, 0, 2),
        lambda: tiles(2, 2, 4),
        lambda: second_leg(1),
        *[lambda i=i: sums(i * eighth, (i + 1) * eighth) for i in range(4)],
        lambda: second_leg(2),
    ]
    for r in range(2, depth):
        for first in (True, False):
            for h in range(2):
                if first or r == depth - 1:
                    for _ in range(2):
                        if jobs:
                            jobs.pop(0)()
                flow(r, first, h)
    while jobs:
        jobs.pop(0)()

    for h in range(2):
        own_copy(z, h).wait_recv()

        @pl.when(z > 0)
        def _():
            zin_copy(z, h, z, z).wait_recv()

        @pl.when(z < depth - 1)
        def _():
            zin_copy(z, h, z, depth).wait_recv()

    def last(i, _):
        rr = pl.ds(pl.multiple_of(i * block, block), block)
        row_ref[rr, :] = own[me, rr, :].astype(F32) + sib[z, rr, :].astype(F32)

        @pl.when(z > 0)
        def _():
            row_ref[rr, :] += zin[z, rr, :].astype(F32)

        @pl.when(z < depth - 1)
        def _():
            row_ref[rr, :] += zin[depth, rr, :].astype(F32)

        return 0

    lax.fori_loop(0, rows // block, last, 0)

    for e in range(count):

        @pl.when(e != me)
        def _():
            pltpu.make_async_remote_copy(
                gg_out.at[e], gg_in.at[e], gg_send.at[e], gg_recv.at[e],
                device_id={"expert": e}, device_id_type=MESH,
            ).wait_recv()

    gg_ref[...] = jnp.sum(gg_in[...], axis=0)

    def tile_load(kind, i):
        into = (gl_all, ul_all, hs_all)[kind]
        return pltpu.make_async_copy(
            landing.at[kind, 2 * i], into.at[pl.ds((3 + i) * quarter, quarter)], load_sem.at[kind, i]
        )

    keeps = [
        pltpu.make_async_copy(kept.at[pl.ds(0, 2)], wide_ref, keep_sem.at[0]),
        pltpu.make_async_copy(down_kept, down_ref, keep_sem.at[1]),
    ]
    for kind in range(3):
        for n in (2, 3, 4, 5):
            hop(kind, n).wait_recv()
        for i in range(2):
            tile_load(kind, i).start()
    for kind in range(3):
        for i in range(2):
            tile_load(kind, i).wait()
        into = (gl_all, ul_all, hs_all)[kind]

        def add_up(i, _):
            rr = pl.ds(pl.multiple_of(i * 128, 128), 128)
            total = kept[kind, rr, :].astype(F32)
            for j in range(2):
                total = total + into[pl.ds(pl.multiple_of((3 + j) * quarter + i * 128, 128), 128), :].astype(F32)
            if kind == 2:
                down_kept[:, rr] = jnp.transpose(total).astype(BF)
            else:
                kept[kind, rr, :] = total.astype(BF)
            return 0

        lax.fori_loop(0, quarter // 128, add_up, 0)
        if kind > 0:
            keeps[kind - 1].start()

    for e in range(count):

        @pl.when(e != me)
        def _():
            gg_copy(e).wait_send()

        zs = e // 2

        for h in range(2):

            @pl.when(((e == me) | ((zs < z) & (e % 2 == core))) & (z < depth - 1))
            def _():
                sent_chunk(e, h, 0, at(z + 1))

            @pl.when(((e == me) | ((zs > z) & (e % 2 == core))) & (z > 0))
            def _():
                sent_chunk(e, h, 1, at(z - 1))

            @pl.when(e % 2 == core)
            def _():
                sent_chunk(e, h, 2, {"expert": sibling})

    for zd in range(depth):
        sum_copy(zd, 2 * zd + 1 - core).wait()
        for h in range(2):

            @pl.when(zd != z)
            def _():
                zin_copy(zd, h, z, zd).wait_send()

    for kind in range(3):
        for n in range(len(hops)):
            hop(kind, n).wait_send()
    for keep in keeps:
        keep.wait()


def expert_pass(n2, gate_rows, dy_all, gate_w, up_w, down_w):
    count = lax.axis_size("expert")
    depth = count // 2
    rows, width = n2.shape
    ff = gate_w.shape[1]
    lanes = gate_rows.shape[1]
    dma = pltpu.SemaphoreType.DMA
    vmem = pl.BlockSpec(memory_space=pltpu.VMEM)
    anywhere = pl.BlockSpec(memory_space=pl.ANY)
    outs = (
        jax.ShapeDtypeStruct((rows, width), F32),
        jax.ShapeDtypeStruct((count, lanes), F32),
        jax.ShapeDtypeStruct((count, rows, width), BF),
        jax.ShapeDtypeStruct((2, width // 4, ff), BF),
        jax.ShapeDtypeStruct((ff, width // 4), BF),
        jax.ShapeDtypeStruct((3, 3, width // 4, ff), BF),
    )
    return pl.pallas_call(
        expert_kernel,
        name="expert_pass",
        out_shape=outs,
        in_specs=[anywhere, vmem] + [anywhere] * 4,
        out_specs=(vmem, vmem, anywhere, anywhere, anywhere, anywhere),
        scratch_shapes=[
            pltpu.VMEM((width, ff), BF),
            pltpu.VMEM((width, ff), BF),
            pltpu.VMEM((ff, width), BF),
            pltpu.VMEM((count * rows, width), BF),
            pltpu.VMEM((count, count, lanes), F32),
            pltpu.VMEM((2, 2, rows // 2, width), BF),
            pltpu.VMEM((count, rows, width // 4), BF),
            pltpu.VMEM((count * rows, ff), BF),
            pltpu.VMEM((count * rows, ff), BF),
            pltpu.VMEM((count * rows, ff), BF),
            pltpu.VMEM((count, rows, width), BF),
            pltpu.VMEM((depth, rows, width), BF),
            pltpu.VMEM((depth + 1, rows, width), BF),
            pltpu.VMEM((count, count, lanes), F32),
            pltpu.VMEM((count, count, lanes), F32),
            pltpu.VMEM((4, lanes, 128), F32),
            pltpu.VMEM((4, lanes, 128), F32),
            pltpu.VMEM((3, width // 4, ff), BF),
            pltpu.VMEM((3, width // 4, ff), BF),
            pltpu.VMEM((ff, width // 4), BF),
            dma((count, 2, 3)), dma((count, 2)), dma((count, 3)), dma((count,)),
            dma((depth, 2)), dma((depth, 2)), dma((depth, 2)), dma((depth + 1, 2)),
            dma((count,)), dma((count,)), dma((2, 2)), dma, dma((count,)), dma((3, 6)), dma((3, 3, 2)),
            dma((3, 3)), dma((2,)), dma((3,)),
        ],
        compiler_params=pltpu.CompilerParams(
            collective_id=2, has_side_effects=True, vmem_limit_bytes=62 * 2**20
        ),
        cost_estimate=pl.CostEstimate(
            flops=18 * count * rows * width * ff, bytes_accessed=60 * 2**20, transcendentals=0
        ),
    )(n2, gate_rows, dy_all, gate_w, up_w, down_w)


def greet(depth, z, at, targets):
    barrier = pltpu.get_barrier_semaphore()
    for target in targets:
        pl.semaphore_signal(barrier, 1, device_id=target, device_id_type=MESH)

    @pl.when(z > 0)
    def _():
        pl.semaphore_signal(barrier, 1, device_id=at(z - 1), device_id_type=MESH)

    @pl.when(z < depth - 1)
    def _():
        pl.semaphore_signal(barrier, 1, device_id=at(z + 1), device_id_type=MESH)

    ends = (z > 0).astype(jnp.int32) + (z < depth - 1).astype(jnp.int32)
    pl.semaphore_wait(barrier, len(targets) + ends)


def attention_kernel(
    x_ref, wq_ref, wk_ref, wv_ref, ws_ref, wo_ref, freq_ref, parent_ref, hits_ref, dy_ref,
    n1_ref, q_ref, kv_ref, mixed_ref, lse_ref, middle_ref, n2_ref, gate_ref, cos_ref, sin_ref,
    bias_ref, w_out, dy_all,
    w, n1, q, kv, mixed, bias,
    z_send, z_recv, x_send, x_recv, y_send, y_recv, a_send, a_recv, b_send, b_recv, s_send, s_recv,
    kx_send, kx_recv, ky_send, ky_recv, ka_send, ka_recv, kb_send, kb_recv, dy_send, dy_recv, out_sem, keep_sem, dy_sem,
):
    count = lax.axis_size("expert")
    depth = count // 2
    shard, total = wq_ref.shape[0], w.shape[1]
    rows, width = x_ref.shape
    heads = q.shape[1] // HEAD_SIZE
    kv_width = kv.shape[1]
    groups = kv_width // (2 * HEAD_SIZE)
    group = heads // groups
    wide = heads * HEAD_SIZE
    qkv_width = wide + kv_width
    split = qkv_width + 128
    me, mine = lax.axis_index("expert"), lax.axis_index("dp")
    z, core = me // 2, me % 2
    y, x = mine // 2, mine % 2
    xn, yn, diag = y * 2 + 1 - x, (1 - y) * 2 + x, (1 - y) * 2 + 1 - x
    sibling = {"expert": z * 2 + 1 - core}

    def at(zz):
        return {"expert": zz * 2 + core}

    greet(depth, z, at, (sibling, {"dp": xn}, {"dp": yn}))

    def remote(src, dst, send, recv, target):
        return pltpu.make_async_remote_copy(
            src, dst, send, recv, device_id=target, device_id_type=MESH
        )

    bounds = ((wide, split), (0, wide), (split, total))
    cuts = tuple(low + ((high - low) // 128 + 1) // 2 * 128 for low, high in bounds)

    def place(dp, zz, cc):
        return pl.ds(pl.multiple_of((dp * count + 2 * zz + cc) * shard, 16), shard)

    def w_copy(dp, zz, low, high, send, recv, target, cc=core):
        ref = w.at[place(dp, zz, cc), pl.ds(low, high - low)]
        return remote(ref, ref, send, recv, target)

    def z_copy(p, zz, lane, target):
        return w_copy(mine, zz, *bounds[p], z_send.at[p, zz, lane], z_recv.at[p, zz], target)

    def x_copy(p, zz, dp):
        return w_copy(dp, zz, *bounds[p], x_send.at[p, zz], x_recv.at[p, zz], {"dp": xn})

    def y_copy(p, zz, dp):
        return w_copy(dp, zz, *bounds[p], y_send.at[p, zz], y_recv.at[p, zz], {"dp": yn})

    def a_copy(p, zz, dp):
        return w_copy(dp, zz, bounds[p][0], cuts[p], a_send.at[p, zz], a_recv.at[p, zz], {"dp": yn})

    def b_copy(p, zz, dp):
        return w_copy(dp, zz, cuts[p], bounds[p][1], b_send.at[p, zz], b_recv.at[p, zz], {"dp": xn})

    def s_copy(p, dp, zz, cc=core):
        return w_copy(dp, zz, *bounds[p], s_send.at[p, dp, zz], s_recv.at[p, dp, zz], sibling, cc)

    def spread(p, zz):
        x_copy(p, zz, mine).start()
        y_copy(p, zz, mine).start()
        s_copy(p, mine, zz).start()

    def on_sides(d, action):
        @pl.when(z - d >= 0)
        def _():
            action(z - d, True)

        if d > 0:

            @pl.when(z + d < depth)
            def _():
                action(z + d, False)

    def z_step(p, d):
        if d == 0:

            @pl.when(z < depth - 1)
            def _():
                z_copy(p, z, 0, at(z + 1)).start()

            @pl.when(z > 0)
            def _():
                z_copy(p, z, 1, at(z - 1)).start()

            return

        def action(zz, from_left):
            z_copy(p, zz, 0, at(z)).wait_recv()
            if from_left:

                @pl.when(z < depth - 1)
                def _():
                    z_copy(p, zz, 0, at(z + 1)).start()
            else:

                @pl.when(z > 0)
                def _():
                    z_copy(p, zz, 1, at(z - 1)).start()

        on_sides(d, action)

    def spread_step(p, d):
        on_sides(d, lambda zz, _: spread(p, zz))

    def xy_step(p, d):
        def action(zz, _):
            x_copy(p, zz, xn).wait_recv()
            a_copy(p, zz, xn).start()
            s_copy(p, xn, zz).start()
            y_copy(p, zz, yn).wait_recv()
            b_copy(p, zz, yn).start()
            s_copy(p, yn, zz).start()

        on_sides(d, action)

    def diag_step(p, d):
        def action(zz, _):
            a_copy(p, zz, diag).wait_recv()
            b_copy(p, zz, diag).wait_recv()
            s_copy(p, diag, zz).start()

        on_sides(d, action)

    def all_here(p):
        for dp in range(4):
            for zz in range(depth):
                s_copy(p, dp, zz, 1 - core).wait_recv()

    def all_sent(p):
        for zz in range(depth):

            @pl.when((zz <= z) & (z < depth - 1))
            def _():
                z_copy(p, zz, 0, at(z)).wait_send()

            @pl.when((zz >= z) & (z > 0))
            def _():
                z_copy(p, zz, 1, at(z)).wait_send()

            x_copy(p, zz, mine).wait_send()
            y_copy(p, zz, mine).wait_send()
            a_copy(p, zz, xn).wait_send()
            b_copy(p, zz, yn).wait_send()
            for dp in range(4):
                s_copy(p, dp, zz).wait_send()

    def dy_copy(k, lane, target):
        return remote(dy_all.at[k], dy_all.at[k], dy_send.at[k, lane], dy_recv.at[k], target)

    def dy_own(lane, target):
        return remote(dy_ref, dy_all.at[me], dy_send.at[me, lane], dy_recv.at[me], target)

    dy_keep = pltpu.make_async_copy(dy_ref, dy_all.at[me], dy_sem)

    def dy_step(d):
        if d == 0:
            dy_own(2, sibling).start()
            dy_keep.start()

            @pl.when(z < depth - 1)
            def _():
                dy_own(0, at(z + 1)).start()

            @pl.when(z > 0)
            def _():
                dy_own(1, at(z - 1)).start()

            return

        def action(zz, from_left):
            k = 2 * zz + core
            dy_copy(k, 0, sibling).wait_recv()
            if from_left:

                @pl.when(z < depth - 1)
                def _():
                    dy_copy(k, 0, at(z + 1)).start()
            else:

                @pl.when(z > 0)
                def _():
                    dy_copy(k, 1, at(z - 1)).start()

            dy_copy(k, 2, sibling).start()

        on_sides(d, action)

    def dy_end():
        dy_keep.wait()
        for zz in range(depth):
            dy_copy(2 * zz + 1 - core, 2, sibling).wait_recv()
            k = 2 * zz + core
            dy_copy(k, 2, sibling).wait_send()

            @pl.when((zz <= z) & (z < depth - 1))
            def _():
                dy_copy(k, 0, sibling).wait_send()

            @pl.when((zz >= z) & (z > 0))
            def _():
                dy_copy(k, 1, sibling).wait_send()

    home = place(mine, z, core)
    w[home, 0:wide] = wq_ref[...]
    for g in range(groups):
        low, head = wide + 2 * g * HEAD_SIZE, slice(g * HEAD_SIZE, (g + 1) * HEAD_SIZE)
        w[home, low : low + HEAD_SIZE] = wk_ref[:, head]
        w[home, low + HEAD_SIZE : low + 2 * HEAD_SIZE] = wv_ref[:, head]
    w[home, qkv_width:split] = ws_ref[...]
    w[home, split:total] = wo_ref[...]
    z_step(0, 0)
    spread_step(0, 0)

    blocks = parent_ref.shape[1]
    trunk = blocks - BRANCHES - LEAVES
    ids = mine * rows + lax.broadcasted_iota(jnp.int32, (rows, 1), 0)
    query_block = lax.div(ids, SEG)
    level = jnp.minimum(query_block, trunk) + (query_block >= trunk + BRANCHES).astype(jnp.int32)
    positions = (level * SEG + lax.rem(ids, SEG)).astype(F32)
    angles = positions * freq_ref[...]
    cos_ref[...] = jnp.cos(angles)
    turned = lax.broadcasted_iota(jnp.int32, angles.shape, 1) < HEAD_SIZE // 2
    sine = jnp.sin(angles)
    sin_ref[...] = jnp.where(turned, -sine, sine)
    z_step(0, 1)
    spread_step(0, 1)
    xy_step(0, 0)
    block_ids = lax.broadcasted_iota(jnp.int32, (rows, blocks), 1)
    parent = jnp.sum(jnp.where(block_ids == query_block, parent_ref[...], 0), axis=1, keepdims=True)
    above = jnp.where(query_block >= trunk + BRANCHES, parent, query_block)
    keys = bias.shape[1] // 128

    def visible(i, _):
        cols = pl.ds(pl.multiple_of(i * 128, 128), 128)
        key_ids = i * 128 + lax.broadcasted_iota(jnp.int32, (rows, 128), 1)
        key_block = lax.div(key_ids, SEG)
        related = (key_block < trunk) | (key_block == query_block) | (key_block == above)
        bias[:, cols] = jnp.where(related & (key_ids <= ids), 0.0, NEGATIVE)
        return 0

    z_step(0, 2)
    spread_step(0, 2)
    z_step(1, 0)
    xy_step(0, 1)
    lax.fori_loop(0, keys, visible, 0)
    z_step(0, 3)
    spread_step(0, 3)
    z_step(2, 0)
    spread_step(1, 0)
    z_step(1, 1)
    spread_step(1, 1)
    xy_step(0, 2)
    z_step(2, 1)
    z_step(1, 2)
    spread_step(1, 2)
    z_step(2, 2)
    z_step(1, 3)
    spread_step(1, 3)
    z_step(2, 3)
    dy_step(0)
    xy_step(0, 3)
    for d in range(depth):
        diag_step(0, d)
    xy_step(1, 0)
    all_here(0)

    def keep(p):
        low, high = bounds[p]
        return pltpu.make_async_copy(
            w.at[:, pl.ds(low, high - low)], w_out.at[:, pl.ds(low, high - low)], keep_sem.at[p]
        )

    keep(0).start()
    small = jnp.transpose(w[:, qkv_width:split].astype(F32))
    experts = hits_ref.shape[0]
    gain_one, gain_two = small[experts : experts + 1], small[experts + 1 : experts + 2]

    block = 32

    def first_norm(i, _):
        rr = pl.ds(pl.multiple_of(i * block, block), block)
        value = x_ref[rr, :].astype(F32)
        scale = lax.rsqrt(jnp.mean(value * value, axis=1, keepdims=True) + EPS)
        n1[rr, :] = (value * scale * gain_one).astype(BF)
        return 0

    lax.fori_loop(0, rows // block, first_norm, 0)

    def turn(value):
        return value * cos_ref[...] + pltpu.roll(value, HEAD_SIZE // 2, 1) * sin_ref[...]

    own = pl.ds(pl.multiple_of(mine * rows, 16), rows)
    projected = mm(n1[...], w[:, wide:qkv_width])
    for g in range(groups):
        low = 2 * g * HEAD_SIZE
        kv[own, low : low + HEAD_SIZE] = turn(projected[:, low : low + HEAD_SIZE]).astype(BF)
        kv[own, low + HEAD_SIZE : low + 2 * HEAD_SIZE] = projected[
            :, low + HEAD_SIZE : low + 2 * HEAD_SIZE
        ].astype(BF)

    def kv_copy(g, dp, low, high, send, recv, target):
        ref = kv.at[
            pl.ds(pl.multiple_of(dp * rows, 16), rows),
            pl.ds((2 * g + low) * HEAD_SIZE, (high - low) * HEAD_SIZE),
        ]
        return remote(ref, ref, send.at[g], recv.at[g], target)

    def kx(g, dp):
        return kv_copy(g, dp, 0, 2, kx_send, kx_recv, {"dp": xn})

    def ky(g, dp):
        return kv_copy(g, dp, 0, 2, ky_send, ky_recv, {"dp": yn})

    def ka(g, dp):
        return kv_copy(g, dp, 0, 1, ka_send, ka_recv, {"dp": yn})

    def kb(g, dp):
        return kv_copy(g, dp, 1, 2, kb_send, kb_recv, {"dp": xn})

    def kv_on(g):
        kx(g, xn).wait_recv()
        ka(g, xn).start()
        ky(g, yn).wait_recv()
        kb(g, yn).start()

    def kv_here(g):
        ka(g, diag).wait_recv()
        kb(g, diag).wait_recv()

    for g in range(groups):
        kx(g, mine).start()
        ky(g, mine).start()
    xy_step(1, 1)
    xy_step(1, 2)
    kv_on(0)
    xy_step(1, 3)
    kv_on(1)
    for d in range(depth):
        diag_step(1, d)
        spread_step(2, d)
    kv_here(0)
    all_here(1)
    keep(1).start()
    dy_step(1)

    def project(h, _):
        cols = pl.ds(pl.multiple_of(h * 2 * HEAD_SIZE, 2 * HEAD_SIZE), 2 * HEAD_SIZE)
        value = mm(n1[...], w[:, cols])
        q[:, cols] = jnp.concatenate(
            [turn(value[:, :HEAD_SIZE]), turn(value[:, HEAD_SIZE:])], axis=1
        ).astype(BF)
        return 0

    lax.fori_loop(0, heads // 2, project, 0)
    later = [
        lambda: xy_step(2, 0),
        lambda: xy_step(2, 1),
        lambda: xy_step(2, 2),
        lambda: xy_step(2, 3),
        lambda: kv_here(1),
        lambda: (diag_step(2, 0), diag_step(2, 1)),
        lambda: (diag_step(2, 2), diag_step(2, 3)),
        lambda: (),
        lambda: dy_step(2),
    ]
    lse_ref[...] = jnp.zeros_like(lse_ref)
    lanes = lax.broadcasted_iota(jnp.int32, lse_ref.shape, 1)

    def attend(h, _):
        for i, job in enumerate(later):
            pl.when(h == i)(lambda job=job: (job(), None)[1])
        g = h // group
        cols = pl.ds(pl.multiple_of(h * HEAD_SIZE, HEAD_SIZE), HEAD_SIZE)
        k_cols = pl.ds(pl.multiple_of(g * 2 * HEAD_SIZE, HEAD_SIZE), HEAD_SIZE)
        v_cols = pl.ds(pl.multiple_of(g * 2 * HEAD_SIZE + HEAD_SIZE, HEAD_SIZE), HEAD_SIZE)
        scores = mm_nt(q[:, cols], kv[:, k_cols]) * (HEAD_SIZE**-0.5 * LOG2E) + bias[...]
        top = jnp.max(scores, axis=1, keepdims=True)
        power = jnp.exp2(scores - top)
        sums = jnp.sum(power, axis=1, keepdims=True)
        mixed[:, cols] = (mm(power.astype(BF), kv[:, v_cols]) / sums).astype(BF)
        lse_ref[...] = jnp.where(lanes == h, top + jnp.log2(sums), lse_ref[...])
        return 0

    lax.fori_loop(0, heads, attend, 0)
    keeps = [
        pltpu.make_async_copy(src, dst, out_sem.at[i])
        for i, (src, dst) in enumerate(
            ((n1, n1_ref), (q, q_ref), (kv, kv_ref), (mixed, mixed_ref), (bias, bias_ref))
        )
    ]
    for copy in keeps:
        copy.start()
    all_here(2)
    keep(2).start()
    tile = 512

    def project_out(i, _):
        cols = pl.ds(pl.multiple_of(i * tile, tile), tile)
        w_cols = pl.ds(pl.multiple_of(split + i * tile, 128), tile)
        middle_ref[:, cols] = x_ref[:, cols].astype(F32) + mm(mixed[...], w[:, w_cols])
        return 0

    lax.fori_loop(0, width // tile, project_out, 0)

    def second_norm(i, _):
        rr = pl.ds(pl.multiple_of(i * block, block), block)
        value = middle_ref[rr, :]
        scale = lax.rsqrt(jnp.mean(value * value, axis=1, keepdims=True) + EPS)
        n2_ref[rr, :] = (value * scale * gain_two).astype(BF)
        return 0

    lax.fori_loop(0, rows // block, second_norm, 0)
    logits = mm_nt(small.astype(BF), n2_ref[...])[:experts]
    hits = hits_ref[...] > 0.5
    chosen = jnp.where(hits, logits, NEGATIVE)
    power = jnp.where(hits, jnp.exp(chosen - jnp.max(chosen, axis=0, keepdims=True)), 0.0)
    gate_ref[...] = jnp.zeros_like(gate_ref)
    gate_ref[:, :rows] = power / jnp.sum(power, axis=0, keepdims=True)

    dy_step(3)
    dy_end()
    for g in range(groups):
        kx(g, mine).wait_send()
        ky(g, mine).wait_send()
        ka(g, xn).wait_send()
        kb(g, yn).wait_send()
    for p in range(3):
        all_sent(p)
        keep(p).wait()
    for copy in keeps:
        copy.wait()


def attention_pass(x, shards, freq, parent, hits, dy):
    count = lax.axis_size("expert")
    depth = count // 2
    rows, width = x.shape
    lanes = rows + -rows % 128
    shard = shards[0].shape[0]
    devices = 4 * count
    wide = shards[0].shape[1]
    kv_width = 2 * shards[1].shape[1]
    dma = pltpu.SemaphoreType.DMA
    vmem = pl.BlockSpec(memory_space=pltpu.VMEM)
    anywhere = pl.BlockSpec(memory_space=pl.ANY)
    shape = jax.ShapeDtypeStruct
    parts = 3
    pair = dma((parts, depth))
    groups = kv_width // (2 * HEAD_SIZE)
    tree = 4 * rows
    total = kv_width + sum(part.shape[1] for part in (shards[0], *shards[3:]))
    return pl.pallas_call(
        attention_kernel,
        name="attention_pass",
        out_shape=(
            shape((rows, width), BF),
            shape((rows, wide), BF),
            shape((tree, kv_width), BF),
            shape((rows, wide), BF),
            shape((rows, 128), F32),
            shape((rows, width), F32),
            shape((rows, width), BF),
            shape((hits.shape[0], lanes), F32),
            shape((rows, HEAD_SIZE), F32),
            shape((rows, HEAD_SIZE), F32),
            shape((rows, tree), F32),
            shape((devices * shard, total), BF),
            shape((count, rows, width), BF),
        ),
        in_specs=[vmem] * 9 + [anywhere],
        out_specs=(anywhere,) * 4 + (vmem,) * 6 + (anywhere,) * 3,
        scratch_shapes=[
            pltpu.VMEM((devices * shard, total), BF),
            pltpu.VMEM((rows, width), BF),
            pltpu.VMEM((rows, wide), BF),
            pltpu.VMEM((tree, kv_width), BF),
            pltpu.VMEM((rows, wide), BF),
            pltpu.VMEM((rows, tree), F32),
            dma((parts, depth, 2)), pair, pair, pair, pair, pair, pair, pair, pair, pair,
            dma((parts, 4, depth)), dma((parts, 4, depth)),
            *[dma((groups,)) for _ in range(8)],
            dma((count, 3)), dma((count,)), dma((5,)), dma((parts,)), dma,
        ],
        compiler_params=pltpu.CompilerParams(
            collective_id=1, has_side_effects=True, vmem_limit_bytes=56 * 2**20
        ),
        cost_estimate=pl.CostEstimate(
            flops=10**10, bytes_accessed=300 * 2**20, transcendentals=0
        ),
    )(x, *shards, freq, parent, hits, dy)


def backward_kernel(
    gate_ref, gg_ref, x_any, dy_any, n1_any, q_any, kv_any, mixed_any, n2_any, lse_any,
    cos_any, sin_any, bias_any, middle_any, row_ref, w_full, wide_ref, down_ref,
    tok_ref, share_ref, wide_all, down_all,
    x_ref, dy_ref, n1_ref, q_ref, kv_ref, mixed_ref, n2_ref, lse_ref, cos_ref, sin_ref, bias_ref,
    middle, wbuf, wsmall, attended, mixed_grad, qg, dkv, kv_low, kv_in, w, wsib, legs, legs2, wz,
    load_sem, ag_local, ag_xs, ag_xr, ag_ys, ag_yr, ag_fs, ag_fr, kv_send, kv_recv,
    ws_send, ws_recv, a_send, a_recv, b_send, b_recv, a2_send, a2_recv, b2_send, b2_recv,
    wz_send, wz_recv,
):
    depth = lax.axis_size("expert") // 2
    rows, width = x_ref.shape
    heads = q_ref.shape[1] // HEAD_SIZE
    kv_width = kv_ref.shape[1]
    groups = kv_width // (2 * HEAD_SIZE)
    group = heads // groups
    wide = heads * HEAD_SIZE
    qkv_width = wide + kv_width
    split = qkv_width + 128
    shard, total = share_ref.shape
    me, mine = lax.axis_index("expert"), lax.axis_index("dp")
    z, core = me // 2, me % 2
    y, x = mine // 2, mine % 2
    xn, yn, diag = y * 2 + 1 - x, (1 - y) * 2 + x, (1 - y) * 2 + 1 - x
    sibling = {"expert": z * 2 + 1 - core}

    def at(zz):
        return {"expert": zz * 2 + core}

    def remote(src, dst, send, recv, target):
        return pltpu.make_async_remote_copy(
            src, dst, send, recv, device_id=target, device_id_type=MESH
        )

    def load(src, dst, i):
        return pltpu.make_async_copy(src, dst, load_sem.at[i])

    load_rows = load(row_ref, tok_ref, 0)
    load_out = load(w_full.at[:, pl.ds(split, width)], wbuf.at[:, pl.ds(0, width)], 1)
    load_small = load(w_full.at[:, pl.ds(qkv_width, 128)], wsmall, 2)
    load_qkv = load(w_full.at[:, pl.ds(0, qkv_width)], wbuf, 3)
    load_middle = load(middle_any, middle, 4)
    load_n2, load_dy, load_mixed, *load_rest = [
        load(src, dst, 5 + i)
        for i, (src, dst) in enumerate(
            (
                (n2_any, n2_ref), (dy_any, dy_ref), (mixed_any, mixed_ref), (q_any, q_ref),
                (kv_any, kv_ref), (lse_any, lse_ref), (bias_any, bias_ref), (cos_any, cos_ref),
                (sin_any, sin_ref), (n1_any, n1_ref), (x_any, x_ref),
            )
        )
    ]
    for first in (load_small, load_n2, load_rows, load_middle, load_dy, load_mixed, load_out):
        first.start()
    for rest in load_rest:
        rest.start()
    greet(depth, z, at, (sibling, {"dp": xn}, {"dp": yn}, {"dp": diag}))

    quarter = wide_ref.shape[1]
    down_half = down_ref.shape[0] // 2

    def quarter_of(piece, dp):
        span = pl.ds(pl.multiple_of(dp * quarter, 128), quarter)
        if piece < 2:
            return wide_all.at[piece, span]
        return down_all.at[pl.ds((piece - 2) * down_half, down_half), span]

    def own_quarter(piece):
        if piece < 2:
            return wide_ref.at[piece]
        return down_ref.at[pl.ds((piece - 2) * down_half, down_half)]

    def keep_quarter(piece):
        return pltpu.make_async_copy(own_quarter(piece), quarter_of(piece, mine), ag_local.at[piece])

    def quarter_x(piece, dp):
        return remote(own_quarter(piece), quarter_of(piece, dp), ag_xs.at[piece], ag_xr.at[piece], {"dp": xn})

    def quarter_y(piece, dp):
        return remote(own_quarter(piece), quarter_of(piece, dp), ag_ys.at[piece], ag_yr.at[piece], {"dp": yn})

    def quarter_on(piece, dp, target):
        ref = quarter_of(piece, dp)
        return remote(ref, ref, ag_fs.at[piece], ag_fr.at[piece], target)

    def quarters(piece):
        quarter_x(piece, mine).start()
        quarter_y(piece, mine).start()
        keep_quarter(piece).start()

    def quarters_on(piece):
        if piece % 2 == 0:
            quarter_x(piece, xn).wait_recv()
            quarter_on(piece, xn, {"dp": yn}).start()
        else:
            quarter_y(piece, yn).wait_recv()
            quarter_on(piece, yn, {"dp": xn}).start()

    quarters(0)

    bounds = ((split, total), (0, wide // 2), (wide // 2, wide), (wide, split))
    cuts = tuple(low + ((high - low) // 128 + 1) // 2 * 128 for low, high in bounds)

    def span(low, high):
        return pl.ds(low, high - low)

    def ws_copy(p, dp):
        cols = span(*bounds[p])
        return remote(
            w.at[dp, :, 1 - core, :, cols], wsib.at[dp, :, :, cols],
            ws_send.at[p, dp], ws_recv.at[p, dp], sibling,
        )

    def a_cols(p):
        return span(bounds[p][0], cuts[p])

    def b_cols(p):
        return span(cuts[p], bounds[p][1])

    def a_copy(p, yy):
        return remote(
            w.at[yy * 2 + 1 - x, :, core, :, a_cols(p)], legs.at[yy, :, :, a_cols(p)],
            a_send.at[p, yy], a_recv.at[p, yy], {"dp": xn},
        )

    def b_copy(p, xx):
        return remote(
            w.at[(1 - y) * 2 + xx, :, core, :, b_cols(p)], legs.at[xx, :, :, b_cols(p)],
            b_send.at[p, xx], b_recv.at[p, xx], {"dp": yn},
        )

    def a2_copy(p):
        return remote(
            w.at[yn, :, core, :, a_cols(p)], legs2.at[:, :, a_cols(p)], a2_send.at[p], a2_recv.at[p], {"dp": yn}
        )

    def b2_copy(p):
        return remote(
            w.at[xn, :, core, :, b_cols(p)], legs2.at[:, :, b_cols(p)], b2_send.at[p], b2_recv.at[p], {"dp": xn}
        )

    def wz_copy(p, zd, nxt, slot):
        cols = span(*bounds[p])
        return remote(
            w.at[mine, zd, core, :, cols], wz.at[slot, :, cols], wz_send.at[p, zd], wz_recv.at[p, slot], at(nxt)
        )

    block = 16
    steps = shard // block

    def add(dp, term, cols):
        def step(i, _):
            zz, rr = i // steps, pl.ds(pl.multiple_of(lax.rem(i, steps) * block, block), block)
            value = w[dp, zz, core, rr, cols].astype(F32) + term[zz, rr, cols].astype(F32)
            w[dp, zz, core, rr, cols] = value.astype(BF)
            return 0

        lax.fori_loop(0, depth * steps, step, 0)

    def begin(p):
        for dp in (xn, diag, yn, mine):
            ws_copy(p, dp).start()

    def first_legs(p):
        def combine(dp):
            ws_copy(p, dp).wait_recv()
            add(dp, wsib.at[dp], span(*bounds[p]))

        combine(xn)
        a_copy(p, y).start()
        combine(diag)
        a_copy(p, 1 - y).start()
        b_copy(p, 1 - x).start()
        combine(yn)
        b_copy(p, x).start()
        combine(mine)

    def second_legs(p):
        a_copy(p, 1 - y).wait_recv()
        add(yn, legs.at[1 - y], a_cols(p))
        a2_copy(p).start()
        b_copy(p, 1 - x).wait_recv()
        add(xn, legs.at[1 - x], b_cols(p))
        b2_copy(p).start()
        a_copy(p, y).wait_recv()
        add(mine, legs.at[y], a_cols(p))
        b_copy(p, x).wait_recv()
        add(mine, legs.at[x], b_cols(p))

    def slot_for(zd, nxt):
        return jnp.where((nxt == zd) & (nxt < z), depth, zd)

    def line(p):
        a2_copy(p).wait_recv()
        add(mine, legs2, a_cols(p))
        b2_copy(p).wait_recv()
        add(mine, legs2, b_cols(p))

        @pl.when((z == 0) | (z == depth - 1))
        def _():
            nxt = jnp.where(z == 0, 1, depth - 2)
            for d in range(1, depth):
                zd = jnp.where(z == 0, depth - d, d - 1)
                wz_copy(p, zd, nxt, slot_for(zd, nxt)).start()

    def line_on(p):
        cols = span(*bounds[p])
        for r in range(depth - 1, 1, -1):
            for first in (True, False):
                right = (z < depth - 1 - z) if first else (z >= depth - 1 - z)
                zd = jnp.where(right, r, depth - 1 - r)
                nxt = jnp.where(right, z + 1, z - 1)
                valid = jnp.where(right, (z < zd) & (z > 0), (z > zd) & (z < depth - 1))

                @pl.when(valid)
                def _():
                    wz_copy(p, zd, nxt, zd).wait_recv()

                    def step(i, _):
                        rr = pl.ds(pl.multiple_of(i * block, block), block)
                        value = w[mine, zd, core, rr, cols].astype(F32) + wz[zd, rr, cols].astype(F32)
                        w[mine, zd, core, rr, cols] = value.astype(BF)
                        return 0

                    lax.fori_loop(0, steps, step, 0)
                    wz_copy(p, zd, nxt, slot_for(zd, nxt)).start()

    def line_end(p):
        cols = span(*bounds[p])
        share_ref[:, cols] = w[mine, z, core, :, cols].astype(F32)

        @pl.when(z > 0)
        def _():
            wz_copy(p, z, z, z).wait_recv()
            share_ref[:, cols] += wz[z, :, cols].astype(F32)

        @pl.when(z < depth - 1)
        def _():
            wz_copy(p, z, z, depth).wait_recv()
            share_ref[:, cols] += wz[depth, :, cols].astype(F32)

    def weight_rows(left, right, low, size):
        quarter_rows = width // 4

        def step(i, _):
            cols = pl.ds(pl.multiple_of(i * quarter_rows, 128), quarter_rows)
            tile = mm_tn(left[:, cols], right).astype(BF)
            w[i, :, :, :, low : low + size] = tile.reshape(depth, 2, shard, size)
            return 0

        lax.fori_loop(0, 4, step, 0)

    experts = gate_ref.shape[0]
    gates, gate_grad = gate_ref[:, :rows], gg_ref[:, :rows]
    logit_grad = gates * (gate_grad - jnp.sum(gates * gate_grad, axis=0, keepdims=True))
    high = logit_grad.astype(BF)
    logit_two = jnp.concatenate([high.astype(F32), logit_grad - high.astype(F32)], axis=0).astype(BF)
    load_small.wait()
    small = jnp.transpose(wsmall[...].astype(F32))
    router = small[:experts].astype(BF).astype(F32)
    router_two = jnp.concatenate([router, router], axis=0).astype(BF)
    gain_one, gain_two = small[experts : experts + 1], small[experts + 1 : experts + 2]
    load_n2.wait()
    router_grad = mm(logit_two, n2_ref[...])
    router_grad = router_grad[:experts] + router_grad[experts:]
    load_rows.wait()
    load_middle.wait()
    load_dy.wait()
    tok_ref[...] += mm_tn(logit_two, router_two)

    def norm_back(value, grad, gain):
        scale = lax.rsqrt(jnp.mean(value * value, axis=1, keepdims=True) + EPS)
        unit = value * scale
        scaled = grad * gain
        back = scale * (scaled - unit * jnp.mean(scaled * unit, axis=1, keepdims=True))
        return back, jnp.sum(grad * unit, axis=0, keepdims=True)

    def second_norm(i, carry):
        rr = pl.ds(pl.multiple_of(i * block, block), block)
        back, gain = norm_back(middle[rr, :], tok_ref[rr, :], gain_two)
        back = back + dy_ref[rr, :].astype(F32)
        tok_ref[rr, :] = back
        attended[rr, :] = back.astype(BF)
        return carry + gain

    gain_two_grad = lax.fori_loop(0, rows // block, second_norm, jnp.zeros((1, width), F32))
    load_mixed.wait()
    weight_rows(mixed_ref, attended[...], split, width)
    begin(0)
    load_out.wait()
    tile = 512

    def mixed_step(i, _):
        out_rows = pl.ds(pl.multiple_of(i * tile, tile), tile)
        mixed_grad[:, out_rows] = mm_nt(attended[...], wbuf[out_rows, :width]).astype(BF)
        return 0

    lax.fori_loop(0, wide // tile, mixed_step, 0)
    load_qkv.start()
    first_legs(0)
    quarters(1)
    for rest in load_rest:
        rest.wait()

    lanes = lax.broadcasted_iota(jnp.int32, lse_ref.shape, 1)

    def turn_back(value):
        return value * cos_ref[...] - pltpu.roll(value, HEAD_SIZE // 2, 1) * sin_ref[...]

    def kv_copy(g, i):
        dp = (xn, diag, yn)[i]
        return remote(
            kv_low.at[g, pl.ds(pl.multiple_of(dp * rows, 16), rows)], kv_in.at[g, mine],
            kv_send.at[g, i], kv_recv.at[g, mine], {"dp": dp},
        )

    def attend_group(g, polls):
        low = 2 * g * HEAD_SIZE
        key, value = kv_ref[:, low : low + HEAD_SIZE], kv_ref[:, low + HEAD_SIZE : low + 2 * HEAD_SIZE]

        def attend(i, _):
            for j, job in polls.items():
                pl.when(i == j)(lambda job=job: (job(), None)[1])
            h = g * group + i
            cols = pl.ds(pl.multiple_of(h * HEAD_SIZE, HEAD_SIZE), HEAD_SIZE)
            query, grad = q_ref[:, cols], mixed_grad[:, cols]
            level = jnp.sum(jnp.where(lanes == h, lse_ref[...], 0.0), axis=1, keepdims=True)
            scores = mm_nt(query, key) * (HEAD_SIZE**-0.5 * LOG2E) + bias_ref[...]
            attn = jnp.exp2(scores - level)
            attn_grad = mm_nt(grad, value)
            mean = jnp.sum(attn * attn_grad, axis=1, keepdims=True)
            score_grad = (attn * (attn_grad - mean)).astype(BF)
            value_term = mm_tn(attn.astype(BF), grad)
            key_term = mm_tn(score_grad, query)
            qg[:, cols] = turn_back(mm(score_grad, key) * HEAD_SIZE**-0.5).astype(BF)

            @pl.when(i == 0)
            def _():
                dkv[:, :HEAD_SIZE] = key_term
                dkv[:, HEAD_SIZE:] = value_term

            @pl.when(i > 0)
            def _():
                dkv[:, :HEAD_SIZE] += key_term
                dkv[:, HEAD_SIZE:] += value_term

            return 0

        lax.fori_loop(0, group, attend, 0)
        kv_low[g, :, :HEAD_SIZE] = (dkv[:, :HEAD_SIZE] * HEAD_SIZE**-0.5).astype(BF)
        kv_low[g, :, HEAD_SIZE:] = dkv[:, HEAD_SIZE:].astype(BF)
        for i in range(3):
            kv_copy(g, i).start()
        weight_rows(n1_ref, qg[:, g * wide // 2 : (g + 1) * wide // 2], g * wide // 2, wide // 2)
        begin(1 + g)
        first_legs(1 + g)
        quarters(2 + g)

    attend_group(0, {3: lambda: quarters_on(0)})
    attend_group(1, {1: lambda: second_legs(0), 4: lambda: quarters_on(1)})

    def kv_sum(g):
        for i in range(3):
            dp = (xn, diag, yn)[i]
            remote(
                kv_low.at[g, pl.ds(0, rows)], kv_in.at[g, dp], kv_send.at[g, i], kv_recv.at[g, dp], {"dp": dp}
            ).wait_recv()
        terms = kv_low[g, pl.ds(pl.multiple_of(mine * rows, 16), rows), :].astype(F32)
        for dp in (xn, diag, yn):
            terms = terms + kv_in[g, dp].astype(F32)
        low = wide + 2 * g * HEAD_SIZE
        qg[:, low : low + HEAD_SIZE] = turn_back(terms[:, :HEAD_SIZE]).astype(BF)
        qg[:, low + HEAD_SIZE : low + 2 * HEAD_SIZE] = terms[:, HEAD_SIZE:].astype(BF)

    for g in range(groups):
        kv_sum(g)
    second_legs(1)
    weight_rows(n1_ref, qg[:, wide:], wide, kv_width)
    load_qkv.wait()

    def first_grad(i, _):
        out_rows = pl.ds(pl.multiple_of(i * tile, tile), tile)
        middle[:, out_rows] = mm_nt(qg[...], wbuf[out_rows, :])
        return 0

    lax.fori_loop(0, width // tile, first_grad, 0)
    quarters_on(2)

    def first_norm(i, carry):
        rr = pl.ds(pl.multiple_of(i * block, block), block)
        back, gain = norm_back(x_ref[rr, :].astype(F32), middle[rr, :], gain_one)
        tok_ref[rr, :] += back
        return carry + gain

    gain_one_grad = lax.fori_loop(0, rows // block, first_norm, jnp.zeros((1, width), F32))
    small_grad = jnp.concatenate(
        [
            router_grad,
            gain_one_grad,
            gain_two_grad,
            jnp.zeros((128 - experts - 2, width), F32),
        ],
        axis=0,
    )
    small_grad = jnp.transpose(small_grad).astype(BF)
    for i in range(4):
        part = small_grad[i * width // 4 : (i + 1) * width // 4]
        w[i, :, :, :, qkv_width:split] = part.reshape(depth, 2, shard, 128)
    begin(3)
    first_legs(3)
    line(0)
    second_legs(2)
    quarters_on(3)
    line_on(0)
    line(1)
    second_legs(3)
    line_on(1)
    line(2)
    line_on(2)
    line(3)
    line_on(3)
    for p in range(4):
        line_end(p)

    for piece in range(4):
        keep_quarter(piece).wait()
        quarter_x(piece, mine).wait_send()
        quarter_y(piece, mine).wait_send()
        if piece % 2 == 0:
            quarter_y(piece, yn).wait_recv()
        else:
            quarter_x(piece, xn).wait_recv()
        quarter_on(piece, diag, {"dp": xn}).wait()
    for g in range(groups):
        for i in range(3):
            kv_copy(g, i).wait_send()
    for p in range(4):
        for dp in range(4):
            ws_copy(p, dp).wait_send()
        for i in range(2):
            a_copy(p, i).wait_send()
            b_copy(p, i).wait_send()
        a2_copy(p).wait_send()
        b2_copy(p).wait_send()
        for zd in range(depth):

            @pl.when(zd != z)
            def _():
                wz_copy(p, zd, z, zd).wait_send()


def backward_pass(
    x, dy, middle, gates, gate_grads, n1, q, kv, mixed, n2, logs, cos, sin, bias, row_sum, w_full,
    wide_part, down_part,
):
    depth = lax.axis_size("expert") // 2
    rows, width = x.shape
    total = w_full.shape[1]
    shard = w_full.shape[0] // (4 * 2 * depth)
    kv_width = kv.shape[1]
    groups = kv_width // (2 * HEAD_SIZE)
    qkv_width = q.shape[1] + kv_width
    dma = pltpu.SemaphoreType.DMA
    vmem = pl.BlockSpec(memory_space=pltpu.VMEM)
    anywhere = pl.BlockSpec(memory_space=pl.ANY)
    shape = jax.ShapeDtypeStruct
    parts = 4
    return pl.pallas_call(
        backward_kernel,
        name="backward_pass",
        out_shape=(
            shape((rows, width), F32),
            shape((shard, total), F32),
            shape((2, 4 * wide_part.shape[1], wide_part.shape[2]), BF),
            shape((down_part.shape[0], 4 * down_part.shape[1]), BF),
        ),
        in_specs=[vmem] * 2 + [anywhere] * 16,
        out_specs=(vmem, vmem, anywhere, anywhere),
        scratch_shapes=[
            *[pltpu.VMEM(a.shape, a.dtype) for a in (x, dy, n1, q, kv, mixed, n2, logs, cos, sin, bias)],
            pltpu.VMEM((rows, width), F32),
            pltpu.VMEM((width, qkv_width), BF),
            pltpu.VMEM((width, 128), BF),
            pltpu.VMEM((rows, width), BF),
            pltpu.VMEM((rows, q.shape[1]), BF),
            pltpu.VMEM((rows, qkv_width), BF),
            pltpu.VMEM((kv.shape[0], 2 * HEAD_SIZE), F32),
            pltpu.VMEM((groups, kv.shape[0], 2 * HEAD_SIZE), BF),
            pltpu.VMEM((groups, 4, rows, 2 * HEAD_SIZE), BF),
            pltpu.VMEM((4, depth, 2, shard, total), BF),
            pltpu.VMEM((4, depth, shard, total), BF),
            pltpu.VMEM((2, depth, shard, total), BF),
            pltpu.VMEM((depth, shard, total), BF),
            pltpu.VMEM((depth + 1, shard, total), BF),
            dma((16,)), dma((4,)), dma((4,)), dma((4,)), dma((4,)), dma((4,)), dma((4,)), dma((4,)),
            dma((groups, 3)), dma((groups, 4)),
            dma((parts, 4)), dma((parts, 4)), dma((parts, 2)), dma((parts, 2)), dma((parts, 2)), dma((parts, 2)),
            dma((parts,)), dma((parts,)), dma((parts,)), dma((parts,)),
            dma((parts, depth)), dma((parts, depth + 1)),
        ],
        compiler_params=pltpu.CompilerParams(
            collective_id=3, has_side_effects=True, vmem_limit_bytes=63 * 2**20
        ),
        cost_estimate=pl.CostEstimate(
            flops=2 * 10**10, bytes_accessed=200 * 2**20, transcendentals=0
        ),
    )(
        gates, gate_grads, x, dy, n1, q, kv, mixed, n2, logs, cos, sin, bias,
        middle, row_sum, w_full, wide_part, down_part,
    )


def finish_kernel(
    wide_ref, down_ref, share_ref, middle_ref, sum_ref, tok_in,
    out_ref, tok_ref, first_ref, second_ref, query_ref, key_ref, value_ref, proj_ref, router_ref,
    gate_ref, up_ref, dgrad_ref,
):
    gate_ref[...] = wide_ref[0].astype(F32)
    up_ref[...] = wide_ref[1].astype(F32)
    dgrad_ref[...] = down_ref[...].astype(F32)
    out_ref[...] = (middle_ref[...] + sum_ref[...].astype(F32)).astype(BF)
    tok_ref[...] = tok_in[...]

    @pl.when(pl.program_id(0) == 0)
    def _():
        wide = query_ref.shape[1]
        groups = key_ref.shape[1] // HEAD_SIZE
        query_ref[...] = share_ref[:, :wide]
        for g in range(groups):
            low, head = wide + 2 * g * HEAD_SIZE, slice(g * HEAD_SIZE, (g + 1) * HEAD_SIZE)
            key_ref[:, head] = share_ref[:, low : low + HEAD_SIZE]
            value_ref[:, head] = share_ref[:, low + HEAD_SIZE : low + 2 * HEAD_SIZE]
        start = wide + 2 * groups * HEAD_SIZE
        small = share_ref[:, start : start + 128]
        experts = router_ref.shape[1]
        router_ref[...] = small[:, :experts]
        rows = small.shape[0]
        turned = jnp.transpose(
            jnp.concatenate([small, jnp.zeros((128 - rows, 128), F32)], axis=0)
        )
        first_ref[...] = turned[experts : experts + 1, :rows]
        second_ref[...] = turned[experts + 1 : experts + 2, :rows]
        proj_ref[...] = share_ref[:, start + 128 :]


def finish_pass(wide, down, share, middle, sums, tok, experts):
    steps = 3
    rows, width = middle.shape
    piece = rows // 2
    shard = share.shape[0]
    heads, kv = QUERY_HEADS * HEAD_SIZE, KEY_VALUE_HEADS * HEAD_SIZE
    _, tall, ff = wide.shape
    shape = jax.ShapeDtypeStruct

    def whole(*dims):
        return pl.BlockSpec(dims, lambda i: (0,) * len(dims))

    token_rows = pl.BlockSpec((piece, width), lambda i: (jnp.minimum(i, rows // piece - 1), 0))
    tall_rows = pl.BlockSpec((tall // steps, ff), lambda i: (i, 0))
    down_rows = pl.BlockSpec((ff // steps, tall), lambda i: (i, 0))
    return pl.pallas_call(
        finish_kernel,
        name="finish_pass",
        grid=(steps,),
        in_specs=[
            pl.BlockSpec((2, tall // steps, ff), lambda i: (0, i, 0)),
            down_rows, whole(*share.shape), token_rows, token_rows, token_rows,
        ],
        out_specs=(
            token_rows, token_rows, whole(1, shard), whole(1, shard), whole(shard, heads),
            whole(shard, kv), whole(shard, kv), whole(shard, width), whole(shard, experts),
            tall_rows, tall_rows, down_rows,
        ),
        out_shape=(
            shape((rows, width), BF), shape((rows, width), F32), shape((1, shard), F32),
            shape((1, shard), F32), shape((shard, heads), F32), shape((shard, kv), F32),
            shape((shard, kv), F32), shape((shard, width), F32), shape((shard, experts), F32),
            shape((tall, ff), F32), shape((tall, ff), F32), shape((ff, tall), F32),
        ),
        compiler_params=pltpu.CompilerParams(vmem_limit_bytes=62 * 2**20),
    )(wide, down, share, middle, sums, tok)


def dense_on_device(
    tokens,
    cotangent,
    parents,
    routes,
    first_gain,
    second_gain,
    query_weight,
    key_matrix,
    value_matrix,
    out_weight,
    router_weight,
    gate_weight,
    up_weight,
    down_weight,
):
    experts = router_weight.shape[1]
    shard_rows = router_weight.shape[0]
    small_shard = jnp.concatenate(
        [
            router_weight,
            first_gain[:, None],
            second_gain[:, None],
            jnp.zeros((shard_rows, -(experts + 2) % 128), BF),
        ],
        axis=1,
    )
    shards = (query_weight, key_matrix, value_matrix, small_shard, out_weight)
    dy_low = cotangent[0]
    inputs_low = tokens[0]
    half = HEAD_SIZE // 2
    frequency = THETA ** -(np.arange(half, dtype=np.float64) * 2.0 / HEAD_SIZE)
    freq = np.concatenate([frequency, frequency]).astype(np.float32)[None]
    expert_ids = jnp.arange(experts, dtype=jnp.int32)
    hit_rows = jnp.sum((routes[0][None, :, :] == expert_ids[:, None, None]).astype(F32), axis=2)
    n1, query_low, kv_all, mixed, logs, middle, n2, gate_rows, cos, sin, bias, full, dy_all = (
        attention_pass(inputs_low, shards, freq, parents, hit_rows, dy_low)
    )
    row_sum, gate_grads, sums, wide_part, down_part, _ = expert_pass(
        n2, gate_rows, dy_all, gate_weight[0], up_weight[0], down_weight[0]
    )
    combined = lax.psum_scatter(sums, "expert", scatter_dimension=0, tiled=True)[0]
    input_grad, share, wide_grads, down_grad = backward_pass(
        inputs_low, dy_low, middle, gate_rows, gate_grads, n1, query_low, kv_all, mixed, n2, logs,
        cos, sin, bias, row_sum, full, wide_part, down_part,
    )
    output, input_grad, gain_one, gain_two, query, key, value, proj, router, gate, up, down = finish_pass(
        wide_grads, down_grad, share, middle, combined, input_grad, experts
    )
    return (
        output[None],
        input_grad[None],
        gain_one[0],
        gain_two[0],
        query,
        key,
        value,
        proj,
        router,
        gate[None],
        up[None],
        down[None],
    )


def solution(mesh):
    dense = mesh.shape["expert"] <= 2 * TOPK and mesh.shape["dp"] == 4
    return jax.shard_map(
        dense_on_device if dense else on_device_routed,
        mesh=mesh,
        in_specs=(
            P("expert", "dp", None),
            P("expert", "dp", None),
            P("expert", None),
            P("expert", "dp", None),
            P(("dp", "expert")),
            P(("dp", "expert")),
            P(("dp", "expert"), None),
            P(("dp", "expert"), None),
            P(("dp", "expert"), None),
            P(("dp", "expert"), None),
            P(("dp", "expert"), None),
            P("expert", None, None),
            P("expert", None, None),
            P("expert", None, None),
        ),
        out_specs=(
            P("expert", "dp", None),
            P("expert", "dp", None),
            P(("dp", "expert")),
            P(("dp", "expert")),
            P(("dp", "expert"), None),
            P(("dp", "expert"), None),
            P(("dp", "expert"), None),
            P(("dp", "expert"), None),
            P(("dp", "expert"), None),
            P("expert", None, None),
            P("expert", None, None),
            P("expert", None, None),
        ),
        check_vma=False,
    )
```
